128 devices in a mesh: seq: 32 (over x_hi, z, y), row: 4 (over x_lo, core).
Axes of the slice: x: 4 (x_hi: 2, x_lo: 2; x = x_hi * 2 + x_lo), y: 4, z: 4, core: 2. Of those that a mesh axis runs over, the one named last changes fastest.
Arguments:
- activations: bfloat16 [256, 256, 1024], P('seq', 'row'), may hold values from -6 to 6
- noise_embed: bfloat16 [256, 1024], P('seq'), may hold values from -6 to 6
- frame_position: int32 [256], P('seq'), may hold values from 0 to 7, as said below
- cotangent: bfloat16 [256, 256, 1024], P('seq', 'row'), may hold values from -6 to 6
- ada_weight: bfloat16 [1024, 6144], P('row'), may hold values from -0.1875 to 0.1875
- ada_bias: bfloat16 [6144], P('row'), may hold values from -3 to 3
- qkv_weight: bfloat16 [1024, 3072], P('row'), may hold values from -0.1875 to 0.1875
- qkv_bias: bfloat16 [3072], P('row'), may hold values from -3 to 3
- out_weight: bfloat16 [1024, 1024], P('row'), may hold values from -0.75 to 0.75
- out_bias: bfloat16 [1024], P('row'), may hold values from -3 to 3
- up_weight: bfloat16 [1024, 4096], P('row'), may hold values from -0.1875 to 0.1875
- up_bias: bfloat16 [4096], P('row'), may hold values from -3 to 3
- down_weight: bfloat16 [4096, 1024], P('row'), may hold values from -0.09375 to 0.09375
- down_bias: bfloat16 [1024], P('row'), may hold values from -3 to 3
Outputs:
- layer_output: bfloat16 [256, 256, 1024], P('seq', 'row')
- input_grad: float32 [256, 256, 1024], P('seq', 'row')
- embed_grad: float32 [256, 1024], P('seq')
- ada_weight_grad: float32 [1024, 6144], P('row')
- ada_bias_grad: float32 [6144], P('row')
- qkv_weight_grad: float32 [1024, 3072], P('row')
- qkv_bias_grad: float32 [3072], P('row')
- out_weight_grad: float32 [1024, 1024], P('row')
- out_bias_grad: float32 [1024], P('row')
- up_weight_grad: float32 [1024, 4096], P('row')
- up_bias_grad: float32 [4096], P('row')
- down_weight_grad: float32 [4096, 1024], P('row')
- down_bias_grad: float32 [1024], P('row')
The draws below stay inside these ranges and needn't reach their ends.
Inputs may be any that keep to these rules, and one draw needn't show every extreme that they name: frame_position[f] is the place of frame f in its clip: 0 where a clip begins, else one more than at frame f - 1; a clip holds 1 to 8 frames, and frames 0 to 7 form one clip.
All inputs are finite; a program needn't handle non-finite values.
Results may differ from the reference program's by a relative error of at most 0.028.
The reference program's roundings to bfloat16 on the way count: a program that leaves them out, or rounds other values in their place, can miss the bound.
Values may be sent and summed in bfloat16 or wider, within the bound.
No kernel may reach another device: no remote copies, remote signals or barrier semaphores. Data moves between devices by JAX's collectives and lax.ppermute only.
A program may use at most 320 MiB of HBM per device.

```python
import math
import jax
import jax.numpy as jnp
from jax import lax

D = 1024
H = 16
HD = 64
FF = 4096
GRID = 16
FPD = 8
MOST = 8
FRAMES = 256
P_SIZE = 256
N_SEQ = 32


def draw_frame_position(key, part):
    rolls = jax.random.randint(key, (FRAMES,), 0, 6)
    frame_index = jnp.arange(FRAMES, dtype=jnp.int32)
    begins = jnp.logical_and(rolls == 0, frame_index >= MOST)

    def advance(previous, begin_here):
        following = jnp.where(jnp.logical_or(begin_here, previous + 1 >= MOST), 0, previous + 1).astype(jnp.int32)
        return (following, following)
    unused, places = lax.scan(advance, jnp.int32(-1), begins)
    return places


def levels(key, dims, pieces, low, top_value):
    loudness, own = 1.0, jax.random.fold_in(key, 6)
    for dim, blocks in pieces:
        draws = jnp.exp(jax.random.uniform(jax.random.fold_in(own, dim), (blocks,), jnp.float32, low / len(pieces), top_value / len(pieces)))
        loudness = loudness * jnp.repeat(draws, dims[dim] // blocks).reshape([-1 if axis == dim else 1 for axis in range(len(dims))])
    return loudness


def gaussian(stream_key, shape, deviation, limit, pieces=(), kind=jnp.bfloat16):
    array = deviation * jax.random.normal(stream_key, shape, jnp.float32)
    if pieces:
        array = array * levels(stream_key, shape, pieces, -0.22, 0.18)
    return jnp.clip(array, -limit, limit).astype(kind)


def setup_inputs(seed: int = 0) -> dict:
    streams_of = jax.random.split(jax.random.key(seed), 15)
    return {
        "activations": gaussian(streams_of[0], (FRAMES, P_SIZE, D), 1.0, 6.0, ((0, 32), (1, 4))),
        "noise_embed": gaussian(streams_of[1], (FRAMES, D), 1.0, 6.0, ((0, 32),)),
        "frame_position": draw_frame_position(jax.random.fold_in(streams_of[14], 71), 0),
        "cotangent": gaussian(streams_of[3], (FRAMES, P_SIZE, D), 1.0, 6.0, ((0, 32), (1, 4))),
        "ada_weight": gaussian(streams_of[4], (D, 6 * D), D ** -0.5, 0.1875, ((0, 4),)),
        "ada_bias": gaussian(streams_of[5], (6 * D,), 0.5, 3.0, ((0, 4),)),
        "qkv_weight": gaussian(streams_of[6], (D, 3 * D), D ** -0.5, 0.1875, ((0, 4),)),
        "qkv_bias": gaussian(streams_of[7], (3 * D,), 0.5, 3.0, ((0, 4),)),
        "out_weight": gaussian(streams_of[8], (D, D), (D // 16) ** -0.5, 0.75, ((0, 4),)),
        "out_bias": gaussian(streams_of[9], (D,), 0.5, 3.0, ((0, 4),)),
        "up_weight": gaussian(streams_of[10], (D, FF), D ** -0.5, 0.1875, ((0, 4),)),
        "up_bias": gaussian(streams_of[11], (FF,), 0.5, 3.0, ((0, 4),)),
        "down_weight": gaussian(streams_of[12], (FF, D), FF ** -0.5, 0.09375, ((0, 4),)),
        "down_bias": gaussian(streams_of[13], (D,), 0.5, 3.0, ((0, 4),)),
    }


@jax.custom_vjp
def low(v):
    return lax.optimization_barrier(v.astype(jnp.bfloat16)).astype(jnp.float32)

@jax.custom_vjp
def low_back(v):
    return v

def low_keep(v):
    return (low(v), None)

def low_pass(kept, grad):
    return (grad,)

def back_keep(v):
    return (v, None)

def back_low(kept, grad):
    return (low(grad),)
low.defvjp(low_keep, low_pass)
low_back.defvjp(back_keep, back_low)

def layer_norm(values):
    center = values - lax.optimization_barrier(jnp.mean(values, axis=-1, keepdims=True))
    spread = lax.optimization_barrier(jnp.mean(center * center, axis=-1, keepdims=True))
    return center * lax.rsqrt(spread + 1e-06)

def modulate(values, shifts, scales):
    return layer_norm(values) * (1.0 + scales) + shifts

def gelu_tanh(values):
    return jax.nn.gelu(values, approximate=True)

def rotary_angles(frame_place, patch_row, patch_col, half_dim):
    pair_index = jnp.arange(half_dim).astype(jnp.float32)
    quarter = half_dim // 2
    eighth = half_dim // 4
    in_frame = pair_index < quarter
    in_row = jnp.logical_and(pair_index >= quarter, pair_index < quarter + eighth)
    offset = jnp.where(in_frame, pair_index, jnp.where(in_row, pair_index - quarter, pair_index - quarter - eighth))
    length = jnp.where(in_frame, 1.0 * quarter, 1.0 * eighth)
    frequency = jnp.exp(-math.log(10000.0) * offset / length)
    position = jnp.where(in_frame, frame_place[:, None], jnp.where(in_row, patch_row[:, None], patch_col[:, None]))
    angle_table = position * frequency
    return (jnp.cos(angle_table)[:, None, :], jnp.sin(angle_table)[:, None, :])

def rotate(values, cosine, sine):
    half_dim = values.shape[-1] // 2
    front_half = values[..., :half_dim]
    back_half = values[..., half_dim:]
    return jnp.concatenate([front_half * cosine - back_half * sine, front_half * sine + back_half * cosine], axis=-1)

def matmul(left, right):
    return jnp.dot(left, right, precision=lax.Precision.HIGHEST)

def reference(activations, noise_embed, frame_position, cotangent, ada_weight, ada_bias, qkv_weight, qkv_bias, out_weight, out_bias, up_weight, up_bias, down_weight, down_bias):
    weights = (ada_weight.astype(jnp.float32), ada_bias.astype(jnp.float32), qkv_weight.astype(jnp.float32), qkv_bias.astype(jnp.float32), out_weight.astype(jnp.float32), out_bias.astype(jnp.float32), up_weight.astype(jnp.float32), up_bias.astype(jnp.float32), down_weight.astype(jnp.float32), down_bias.astype(jnp.float32))
    inputs = activations.astype(jnp.float32)
    embedding = noise_embed.astype(jnp.float32)
    patches = GRID * GRID
    scale_factor = HD ** (-0.5)
    patch_index = jnp.arange(patches, dtype=jnp.int32)
    patch_row = jnp.tile(patch_index // GRID, FPD).astype(jnp.float32)
    patch_col = jnp.tile(patch_index % GRID, FPD).astype(jnp.float32)
    place_blocks = frame_position.reshape(N_SEQ, FPD)

    def forward(inputs, embedding, weights):
        ada_w, ada_b, qkv_w, qkv_b, out_w, out_b, up_w, up_b, down_w, down_b = weights
        silu_embed = low(jax.nn.silu(embedding))
        modulation = matmul(silu_embed, ada_w) + ada_b
        blocks = inputs.reshape(N_SEQ, FPD, patches, D)
        mod_blocks = modulation.reshape(N_SEQ, FPD, 6 * D)

        def project_block(block_inputs):
            block_values, mod_block, places = block_inputs
            shift_one = mod_block[:, None, 0:D]
            scale_one = mod_block[:, None, D:2 * D]
            hidden_one = low(modulate(block_values, shift_one, scale_one)).reshape(FPD * patches, D)
            projected = low_back(matmul(hidden_one, qkv_w) + qkv_b)
            frame_place = jnp.repeat(places, patches).astype(jnp.float32)
            cosine, sine = rotary_angles(frame_place, patch_row, patch_col, HD // 2)
            queries = low(rotate(projected[:, :D].reshape(-1, H, HD), cosine, sine))
            keys_now = low(rotate(projected[:, D:2 * D].reshape(-1, H, HD), cosine, sine))
            values_now = low(projected[:, 2 * D:].reshape(-1, H, HD))
            return (queries, keys_now, values_now)
        query_blocks, key_blocks, value_blocks = lax.map(jax.checkpoint(project_block), (blocks, mod_blocks, place_blocks))
        zero_block = jnp.zeros((1, FPD * patches, H, HD), jnp.float32)
        keys_prior = jnp.concatenate([zero_block, key_blocks[:-1]], axis=0)
        values_prior = jnp.concatenate([zero_block, value_blocks[:-1]], axis=0)

        def layer_block(block_inputs):
            block_values, mod_block, places, block_index, queries, keys_now, values_now, keys_before, values_before = block_inputs
            modulation_parts = [mod_block[:, None, segment * D:(segment + 1) * D] for segment in range(6)]
            shift_one, scale_one, gate_one, shift_two, scale_two, gate_two = modulation_parts
            key_all = jnp.concatenate([keys_before, keys_now], axis=0)
            value_all = jnp.concatenate([values_before, values_now], axis=0)
            query_frame = block_index * FPD + jnp.repeat(jnp.arange(FPD, dtype=jnp.int32), patches)
            key_frame = (block_index - 1) * FPD + jnp.repeat(jnp.arange(2 * FPD, dtype=jnp.int32), patches)
            query_place = jnp.repeat(places, patches)
            frame_gap = query_frame[:, None] - key_frame[None, :]
            allowed = (frame_gap >= 0) & (frame_gap <= query_place[:, None]) & (key_frame[None, :] >= 0)

            def one_head(head_inputs):
                head_query, head_key, head_value = head_inputs
                scores = low_back(matmul(head_query, head_key.T) * scale_factor)
                scores = jnp.where(allowed, scores, -1e+30)
                softmax_weights = jax.nn.softmax(scores, axis=-1)
                return matmul(low(softmax_weights), head_value)
            head_outputs = lax.map(jax.checkpoint(one_head), (jnp.transpose(queries, (1, 0, 2)), jnp.transpose(key_all, (1, 0, 2)), jnp.transpose(value_all, (1, 0, 2))))
            attended = low_back(low(jnp.transpose(head_outputs, (1, 0, 2)).reshape(-1, D)))
            branch = low_back(matmul(attended, out_w) + out_b).reshape(FPD, patches, D)
            middle = block_values + gate_one * branch
            hidden_two = low(modulate(middle, shift_two, scale_two)).reshape(-1, D)
            upward = low_back(matmul(hidden_two, up_w) + up_b)
            activated = low(gelu_tanh(upward))
            downward = low_back(matmul(activated, down_w) + down_b).reshape(FPD, patches, D)
            return middle + gate_two * downward
        outputs = lax.map(jax.checkpoint(layer_block), (blocks, mod_blocks, place_blocks, jnp.arange(N_SEQ, dtype=jnp.int32), query_blocks, key_blocks, value_blocks, keys_prior, values_prior))
        return outputs.reshape(FRAMES, patches, D)
    result, pullback = jax.vjp(forward, inputs, embedding, weights)
    input_grad, embed_grad, weight_grads = pullback(cotangent.astype(jnp.float32))
    return (result.astype(jnp.bfloat16), input_grad, embed_grad, weight_grads[0], weight_grads[1], weight_grads[2], weight_grads[3], weight_grads[4], weight_grads[5], weight_grads[6], weight_grads[7], weight_grads[8], weight_grads[9])
```

```python
import math

import jax
import jax.numpy as jnp
from jax import lax
from jax.experimental import pallas as pl
from jax.experimental.pallas import tpu as pltpu
from jax.sharding import Mesh, PartitionSpec as P

F32 = jnp.float32
BF16 = jnp.bfloat16
HD = 64
GRID = 16
FPD = 8
PR = 64
D = 1024
FF = 4096
HC = 256
TOK = 256
PREV = 7
AXES = ("xh", "z", "y", "xl", "c")
CORE, DIRECT, OTHER, FAR = 1, 2, 66, 64
MB = 1024 * 1024


def swap(value, mask):
    return lax.ppermute(value, AXES, [(i, i ^ mask) for i in range(128)])


def shift(value, steps):
    first, last = max(0, -4 * steps), min(128, 128 - 4 * steps)
    return lax.ppermute(value, AXES, [(i, i + 4 * steps) for i in range(first, last)])


def after(value, *others):
    return lax.optimization_barrier((value,) + others)[0]


def nt(left, right):
    return lax.dot_general(left, right, (((1,), (1,)), ((), ())), preferred_element_type=F32)


def tn(left, right):
    return lax.dot_general(left, right, (((0,), (0,)), ((), ())), preferred_element_type=F32)


def nn(left, right):
    return jnp.dot(left, right, preferred_element_type=F32)


def norm(values):
    center = values - jnp.mean(values, axis=-1, keepdims=True)
    spread = jnp.mean(center * center, axis=-1, keepdims=True)
    rate = lax.rsqrt(spread + 1e-06)
    return center * rate, rate


def norm_back(normal, rate, grad):
    mean_grad = jnp.mean(grad, axis=-1, keepdims=True)
    mean_both = jnp.mean(grad * normal, axis=-1, keepdims=True)
    return rate * (grad - mean_grad - normal * mean_both)


def turn(values, cosine, sine):
    lanes = lax.broadcasted_iota(jnp.int32, values.shape, 1)
    other = jnp.where(
        lanes % HD < HD // 2, pltpu.roll(values, HC - HD // 2, 1), pltpu.roll(values, HD // 2, 1)
    )
    return values * cosine + other * sine


def params(mib):
    return pltpu.CompilerParams(
        dimension_semantics=("arbitrary",), vmem_limit_bytes=mib * MB
    )


def cost(flops, moved, exps=0):
    return pl.CostEstimate(flops=int(flops), bytes_accessed=int(moved), transcendentals=int(exps))


def whole(shape):
    return pl.BlockSpec(shape, lambda i, *_: (0,) * len(shape))


def columns(row, j):
    return pl.ds(pl.multiple_of((row ^ j) * HC, HC), HC)


def project_kernel(with_query, row_ref, x0, x1, x2, x3, sh, sc, w0, w1, w2, w3, b, cp, sp, cf, sf, *outs):
    row = row_ref[0]
    if with_query:
        h_ref, q_ref, k_ref, v_ref = outs
        first = 0
    else:
        k_ref, v_ref, h_ref = outs
        first = HC
    x = jnp.concatenate([r[0] for r in (x0, x1, x2, x3)], axis=0).astype(F32)
    normal, _ = norm(x)
    hidden = (normal * (1.0 + sc[0]) + sh[0]).astype(BF16)
    where = (0,) if with_query else ()
    h_ref[where + (slice(None), slice(None))] = hidden
    total = b[:, first:]
    for j, w in enumerate((w0, w1, w2, w3)):
        total = total + nn(h_ref[where + (slice(None), columns(row, j))], w[:, first:])
    cosine = cp[...] + cf[0]
    sine = sp[...] + sf[0]
    if with_query:
        q_ref[0] = (turn(total[:, :HC], cosine, sine).astype(BF16).astype(F32) * 0.125).astype(BF16)
        total = total[:, HC:]
    k_ref[0] = turn(total[:, :HC], cosine, sine).astype(BF16)
    v_ref[0] = total[:, HC:].astype(BF16)


def project(with_query, row, xs, mod, weights, bias, tables):
    cp, sp, cf, sf = tables
    frames = xs[0].shape[0]
    segment = 0 if with_query else 6
    base = 0 if with_query else FPD - frames
    x_spec = pl.BlockSpec((1, PR, D), lambda f, *_: (f, 0, 0))
    mod_spec = lambda s: pl.BlockSpec((1, 1, D), lambda f, *_: (f + base, 0, s))
    frame_table = pl.BlockSpec((1, 1, HC), lambda f, *_: (f, 0, 0))
    out_spec = pl.BlockSpec((1, TOK, HC), lambda f, *_: (f, 0, 0))
    out = jax.ShapeDtypeStruct((frames, TOK, HC), BF16)
    if with_query:
        out_specs = [pl.BlockSpec((1, TOK, D), lambda f, *_: (f, 0, 0)), out_spec, out_spec, out_spec]
        out_shape = [jax.ShapeDtypeStruct((frames, TOK, D), BF16), out, out, out]
        scratch = []
    else:
        out_specs = [out_spec, out_spec]
        out_shape = [out, out]
        scratch = [pltpu.VMEM((TOK, D), BF16)]
    return pl.pallas_call(
        lambda *refs: project_kernel(with_query, *refs),
        out_shape=out_shape,
        grid_spec=pltpu.PrefetchScalarGridSpec(
            num_scalar_prefetch=1,
            grid=(frames,),
            in_specs=[x_spec] * 4
            + [mod_spec(segment), mod_spec(segment + 1)]
            + [whole((HC, 3 * HC))] * 4
            + [whole((1, 3 * HC)), whole((TOK, HC)), whole((TOK, HC)), frame_table, frame_table],
            out_specs=out_specs,
            scratch_shapes=scratch,
        ),
        compiler_params=params(32),
        cost_estimate=cost(2 * frames * TOK * D * 3 * HC, frames * TOK * D * 4 + 4 * MB),
        name="project_own" if with_query else "project_prev",
    )(row, *xs, mod, mod, *weights, bias, cp, sp, cf, sf)


def head_lanes():
    return lax.broadcasted_iota(jnp.int32, (TOK, HC), 1) // HD


def attend_kernel(pos_ref, q, k, v, kp, vp, o0, o1, o2, o3, lse, qs, scores, acc, top, low):
    f = pl.program_id(0)
    place = pos_ref[f]
    lanes = head_lanes()
    query = q[0]
    for h in range(4):
        qs[pl.ds(h * TOK, TOK), :] = jnp.where(lanes == h, query, jnp.zeros_like(query))
    top[...] = jnp.full_like(top, -1e30)
    low[...] = jnp.zeros_like(low)
    acc[...] = jnp.zeros_like(acc)
    before = jnp.maximum(place - f, 0)
    start = jnp.maximum(f - place, 0)

    def score(keys, slot):
        for h in range(4):
            rows = pl.ds(h * TOK, TOK)
            s = nt(qs[rows, :], keys)
            scores[slot, rows, :] = s
            top[rows, :] = jnp.maximum(top[rows, :], jnp.maximum(s[:, :128], s[:, 128:]))

    def mix(values, slot):
        for h in range(4):
            rows = pl.ds(h * TOK, TOK)
            p = jnp.exp(scores[slot, rows, :] - jnp.concatenate([top[rows, :]] * 2, axis=1))
            low[rows, :] = low[rows, :] + (p[:, :128] + p[:, 128:])
            acc[rows, :] = acc[rows, :] + nn(p.astype(BF16), values)

    def run(step):
        def prev(i, _):
            at = PREV - before + i
            step(kp[at] if step is score else vp[at], i)
            return 0

        def own(g, _):
            step(k[g] if step is score else v[g], g - f + place)
            return 0

        lax.fori_loop(0, before, prev, 0)
        lax.fori_loop(start, f + 1, own, 0)

    run(score)
    for h in range(4):
        rows = pl.ds(h * TOK, TOK)
        top[rows, :] = jnp.broadcast_to(jnp.max(top[rows, :], axis=1, keepdims=True), (TOK, 128))
    run(mix)
    result = jnp.zeros((TOK, HC), F32)
    logs = jnp.zeros((TOK, 128), F32)
    narrow = lax.broadcasted_iota(jnp.int32, (TOK, 128), 1)
    for h in range(4):
        rows = pl.ds(h * TOK, TOK)
        total = jnp.sum(low[rows, :], axis=1, keepdims=True)
        result = jnp.where(lanes == h, acc[rows, :] / total, result)
        logs = jnp.where(narrow == h, top[rows, :] + jnp.log(total), logs)
    lse[0] = logs.T[:8]
    result = result.astype(BF16)
    for j, o in enumerate((o0, o1, o2, o3)):
        o[0] = result[j * PR : (j + 1) * PR]


def attend(places, q, k, v, kp, vp):
    block = pl.BlockSpec((1, TOK, HC), lambda f, *_: (f, 0, 0))
    piece = pl.BlockSpec((1, PR, HC), lambda f, *_: (f, 0, 0))
    return pl.pallas_call(
        attend_kernel,
        out_shape=[jax.ShapeDtypeStruct((FPD, PR, HC), BF16)] * 4
        + [jax.ShapeDtypeStruct((FPD, 8, TOK), F32)],
        grid_spec=pltpu.PrefetchScalarGridSpec(
            num_scalar_prefetch=1,
            grid=(FPD,),
            in_specs=[block]
            + [whole((FPD, TOK, HC))] * 2
            + [whole((PREV, TOK, HC))] * 2,
            out_specs=[piece] * 4 + [pl.BlockSpec((1, 8, TOK), lambda f, *_: (f, 0, 0))],
            scratch_shapes=[
                pltpu.VMEM((4 * TOK, HC), BF16),
                pltpu.VMEM((8, 4 * TOK, TOK), F32),
                pltpu.VMEM((4 * TOK, HC), F32),
                pltpu.VMEM((4 * TOK, 128), F32),
                pltpu.VMEM((4 * TOK, 128), F32),
            ],
        ),
        compiler_params=params(40),
        cost_estimate=cost(36 * 4 * 2 * 2 * TOK**3, 6 * MB, 36 * 4 * TOK * TOK),
        name="attend",
    )(places, q, k, v, kp, vp)


def attend_back_kernel(
    pos_ref, q, k, v, kp, vp, g0, g1, g2, g3, o0, o1, o2, o3, lse, cp, sp, cf, sf,
    dq, dk, dv, dkp, dvp,
    qs, gs, ks, pl_scr, dl_scr, ds_scr, dq_acc, dkp_acc, dvp_acc,
):
    f = pl.program_id(0)
    place = pos_ref[f]
    lanes = head_lanes()

    @pl.when(f == 0)
    def _():
        for ref in (dk, dv, dkp_acc, dvp_acc):
            ref[...] = jnp.zeros_like(ref)

    query = q[0]
    grad = jnp.concatenate([r[0] for r in (g0, g1, g2, g3)], axis=0)
    mixed = jnp.concatenate([r[0] for r in (o0, o1, o2, o3)], axis=0)
    for h in range(4):
        rows = pl.ds(h * TOK, TOK)
        qs[rows, :] = jnp.where(lanes == h, query, jnp.zeros_like(query))
        gs[rows, :] = jnp.where(lanes == h, grad, jnp.zeros_like(grad))
    both = grad.astype(F32) * mixed.astype(F32)
    pick = (
        lax.broadcasted_iota(jnp.int32, (8, HC), 1) // HD
        == lax.broadcasted_iota(jnp.int32, (8, HC), 0)
    ).astype(F32)
    delta = lax.dot_general(
        pick, both, (((1,), (1,)), ((), ())),
        preferred_element_type=F32, precision=lax.Precision.HIGHEST,
    )
    logs = lse[0]
    dq_acc[...] = jnp.zeros_like(dq_acc)

    def step(keys, values, dk_ref, dv_ref, at):
        for h in range(4):
            rows = pl.ds(h * TOK, TOK)
            ks[rows, :] = jnp.where(lanes == h, keys, jnp.zeros_like(keys))
            p = jnp.exp(nt(keys, qs[rows, :]) - logs[h : h + 1])
            ds = (p * (nt(values, gs[rows, :]) - delta[h : h + 1])).astype(BF16)
            pl_scr[:, rows] = p.astype(BF16)
            dl_scr[:, rows] = ds
            ds_scr[rows, :] = ds
        dv_ref[at] = dv_ref[at] + nn(pl_scr[...], gs[...])
        dk_ref[at] = dk_ref[at] + nn(dl_scr[...], qs[...])
        dq_acc[...] = dq_acc[...] + tn(ds_scr[...], ks[...])

    before = jnp.maximum(place - f, 0)
    start = jnp.maximum(f - place, 0)

    def prev(i, _):
        at = PREV - before + i
        step(kp[at], vp[at], dkp_acc, dvp_acc, at)
        return 0

    def own(g, _):
        step(k[g], v[g], dk, dv, g)
        return 0

    lax.fori_loop(0, before, prev, 0)
    lax.fori_loop(start, f + 1, own, 0)
    dq[0] = turn(dq_acc[...] * 0.125, cp[...] + cf[0], -(sp[...] + sf[0])).astype(BF16)

    @pl.when(f == FPD - 1)
    def _():
        dkp[...] = dkp_acc[...].astype(BF16)
        dvp[...] = dvp_acc[...].astype(BF16)


def attend_back(places, q, k, v, kp, vp, grads, mixed, lse, tables):
    cp, sp, cf, sf = tables
    block = pl.BlockSpec((1, TOK, HC), lambda f, *_: (f, 0, 0))
    piece = pl.BlockSpec((1, PR, HC), lambda f, *_: (f, 0, 0))
    frame_table = pl.BlockSpec((1, 1, HC), lambda f, *_: (f, 0, 0))
    return pl.pallas_call(
        attend_back_kernel,
        out_shape=[
            jax.ShapeDtypeStruct((FPD, TOK, HC), BF16),
            jax.ShapeDtypeStruct((FPD, TOK, HC), F32),
            jax.ShapeDtypeStruct((FPD, TOK, HC), F32),
            jax.ShapeDtypeStruct((PREV, TOK, HC), BF16),
            jax.ShapeDtypeStruct((PREV, TOK, HC), BF16),
        ],
        grid_spec=pltpu.PrefetchScalarGridSpec(
            num_scalar_prefetch=1,
            grid=(FPD,),
            in_specs=[block]
            + [whole((FPD, TOK, HC))] * 2
            + [whole((PREV, TOK, HC))] * 2
            + [piece] * 8
            + [pl.BlockSpec((1, 8, TOK), lambda f, *_: (f, 0, 0))]
            + [whole((TOK, HC))] * 2
            + [frame_table] * 2,
            out_specs=[block]
            + [whole((FPD, TOK, HC))] * 2
            + [whole((PREV, TOK, HC))] * 2,
            scratch_shapes=[
                pltpu.VMEM((4 * TOK, HC), BF16),
                pltpu.VMEM((4 * TOK, HC), BF16),
                pltpu.VMEM((4 * TOK, HC), BF16),
                pltpu.VMEM((TOK, 4 * TOK), BF16),
                pltpu.VMEM((TOK, 4 * TOK), BF16),
                pltpu.VMEM((4 * TOK, TOK), BF16),
                pltpu.VMEM((TOK, HC), F32),
                pltpu.VMEM((PREV, TOK, HC), F32),
                pltpu.VMEM((PREV, TOK, HC), F32),
            ],
        ),
        compiler_params=params(44),
        cost_estimate=cost(36 * 4 * 5 * 2 * TOK**3, 16 * MB, 36 * 4 * TOK * TOK),
        name="attend_back",
    )(places, q, k, v, kp, vp, *grads, *mixed, lse, cp, sp, cf, sf)


HALF = 4


def flat(ref):
    return ref[...].reshape(HALF * PR, ref.shape[-1])


def frames_of(value):
    return value.reshape(HALF, PR, value.shape[-1])


def mid_kernel(o0, o1, o2, o3, w0, w1, w2, w3, ob, x, cot, g1, s2, c2, g2, branch, middle, hidden, down, dsum):
    total = ob[...]
    for o, w in zip((o0, o1, o2, o3), (w0, w1, w2, w3)):
        total = total + nn(flat(o), w[...])
    branched = frames_of(total)
    branch[...] = branched
    mid = x[...].astype(F32) + g1[...] * branched
    middle[...] = mid
    normal, _ = norm(mid)
    hidden[...] = (normal * (1.0 + c2[...]) + s2[...]).astype(BF16)
    grad = (g2[...] * cot[...].astype(F32)).astype(BF16)
    down[...] = grad
    sums = jnp.sum(grad.astype(F32).reshape(HALF * PR, D), axis=0, keepdims=True)

    @pl.when(pl.program_id(0) == 0)
    def _():
        dsum[...] = jnp.zeros_like(dsum)

    dsum[...] = dsum[...] + sums


def half_spec(width):
    return pl.BlockSpec((HALF, PR, width), lambda i, *_: (i, 0, 0))


def segment_spec(segment):
    return pl.BlockSpec((HALF, 1, D), lambda i, *_: (i, 0, segment))


def mid(pieces, weights, bias, x, cot, mod):
    return pl.pallas_call(
        mid_kernel,
        out_shape=[
            jax.ShapeDtypeStruct((FPD, PR, D), F32),
            jax.ShapeDtypeStruct((FPD, PR, D), F32),
            jax.ShapeDtypeStruct((FPD, PR, D), BF16),
            jax.ShapeDtypeStruct((FPD, PR, D), BF16),
            jax.ShapeDtypeStruct((1, D), F32),
        ],
        grid=(FPD // HALF,),
        in_specs=[half_spec(HC)] * 4
        + [whole((HC, D))] * 4
        + [whole((1, D)), half_spec(D), half_spec(D)]
        + [segment_spec(s) for s in (2, 3, 4, 5)],
        out_specs=[half_spec(D)] * 4 + [whole((1, D))],
        compiler_params=params(40),
        cost_estimate=cost(2 * 512 * D * D, 12 * MB),
        name="mid",
    )(*pieces, *weights, bias, x, cot, mod, mod, mod, mod)


def mid_back_kernel(hg, middle, branch, cot, g1, c2, w0, w1, w2, w3, mg, bg, a0, a1, a2, a3, sh, sc, ga, osum):
    grad = hg[...]
    normal, rate = norm(middle[...])
    sh[...] = jnp.sum(grad, axis=1, keepdims=True)
    sc[...] = jnp.sum(grad * normal, axis=1, keepdims=True)
    total = cot[...].astype(F32) + norm_back(normal, rate, grad * (1.0 + c2[...]))
    mg[...] = total
    ga[...] = jnp.sum(total * branch[...], axis=1, keepdims=True)
    low = (g1[...] * total).astype(BF16)
    bg[...] = low
    low = low.reshape(HALF * PR, D)
    sums = jnp.sum(low.astype(F32), axis=0, keepdims=True)

    @pl.when(pl.program_id(0) == 0)
    def _():
        osum[...] = jnp.zeros_like(osum)

    osum[...] = osum[...] + sums
    for a, w in zip((a0, a1, a2, a3), (w0, w1, w2, w3)):
        a[...] = frames_of(nt(low, w[...]).astype(BF16))


def mid_back(hg, middle, branch, cot, mod, weights):
    frame_sum = pl.BlockSpec((HALF, 1, D), lambda i, *_: (i, 0, 0))
    return pl.pallas_call(
        mid_back_kernel,
        out_shape=[
            jax.ShapeDtypeStruct((FPD, PR, D), F32),
            jax.ShapeDtypeStruct((FPD, PR, D), BF16),
        ]
        + [jax.ShapeDtypeStruct((FPD, PR, HC), BF16)] * 4
        + [jax.ShapeDtypeStruct((FPD, 1, D), F32)] * 3
        + [jax.ShapeDtypeStruct((1, D), F32)],
        grid=(FPD // HALF,),
        in_specs=[half_spec(D)] * 4
        + [segment_spec(2), segment_spec(4)]
        + [whole((HC, D))] * 4,
        out_specs=[half_spec(D)] * 2 + [half_spec(HC)] * 4 + [frame_sum] * 3 + [whole((1, D))],
        compiler_params=params(40),
        cost_estimate=cost(2 * 512 * D * D, 12 * MB),
        name="mid_back",
    )(hg, middle, branch, cot, mod, mod, *weights)


NB = 512
STEPS = FF // NB
PER = D // NB
TOKENS = FPD * PR


def up_column(t, row):
    return (row ^ (t // PER)) * PER + t % PER


def own_step(j):
    return lambda t: jnp.clip(t - j * PER, 0, PER - 1)


def down_spec(j):
    return pl.BlockSpec((NB, D), lambda t, row: (own_step(j)(t), 0))


def pick_down(d0, d1, d2, d3):
    j = pl.program_id(0) // PER
    return jnp.where(
        j < 2, jnp.where(j == 0, d0[...], d1[...]), jnp.where(j == 2, d2[...], d3[...])
    )


def feed_kernel(row_ref, h2, dg, u0, u1, u2, u3, ub, d0, d1, d2, d3, act, upg, hg, usum):
    row = row_ref[0]
    ups = (u0, u1, u2, u3)
    down = pick_down(d0, d1, d2, d3)
    u = ub[...]
    for j, w in enumerate(ups):
        u = u + nn(h2[:, columns(row, j)], w[...])
    rate = math.sqrt(2.0 / math.pi)
    square = u * u
    wave = jnp.tanh(rate * (u + 0.044715 * (u * square)))
    act[...] = (0.5 * u * (1.0 + wave)).astype(BF16)
    slope = 0.5 * (1.0 + wave) + 0.5 * u * (1.0 - wave * wave) * (
        rate * (1.0 + 3.0 * 0.044715 * square)
    )
    grad = (nt(dg[...], down) * slope).astype(BF16)
    upg[...] = grad
    usum[...] = jnp.sum(grad.astype(F32), axis=0, keepdims=True)

    @pl.when(pl.program_id(0) == 0)
    def _():
        hg[...] = jnp.zeros_like(hg)

    for j, w in enumerate(ups):
        hg[:, columns(row, j)] = hg[:, columns(row, j)] + nt(grad, w[...])


def feed(row, h2, dg, ups, up_bias, downs):
    tok = whole((TOKENS, D))
    block = pl.BlockSpec((TOKENS, NB), lambda t, row: (0, t))
    bias = pl.BlockSpec((1, NB), lambda t, row: (0, up_column(t, row[0])))
    return pl.pallas_call(
        feed_kernel,
        out_shape=[
            jax.ShapeDtypeStruct((TOKENS, FF), BF16),
            jax.ShapeDtypeStruct((TOKENS, FF), BF16),
            jax.ShapeDtypeStruct((TOKENS, D), F32),
            jax.ShapeDtypeStruct((1, FF), F32),
        ],
        grid_spec=pltpu.PrefetchScalarGridSpec(
            num_scalar_prefetch=1,
            grid=(STEPS,),
            in_specs=[tok, tok]
            + [pl.BlockSpec((HC, NB), lambda t, row: (0, up_column(t, row[0])))] * 4
            + [bias]
            + [down_spec(j) for j in range(4)],
            out_specs=[block, block, tok, bias],
        ),
        compiler_params=params(44),
        cost_estimate=cost(3 * 2 * TOKENS * D * FF, 30 * MB, TOKENS * FF),
        name="feed",
    )(row, h2, dg, *ups, up_bias, *downs)


def feed_back_kernel(row_ref, h2, dg, act, upg, d0, d1, d2, d3, dn, w0, w1, w2, w3, e0, e1, e2, e3):
    row = row_ref[0]
    j_now = pl.program_id(0) // PER
    down = pick_down(d0, d1, d2, d3)
    active = act[...]

    @pl.when(pl.program_id(0) == 0)
    def _():
        dn[...] = jnp.zeros_like(dn)

    dn[...] = dn[...] + nn(active, down)
    part = tn(active, dg[...]).astype(BF16)
    for j, e in enumerate((e0, e1, e2, e3)):

        @pl.when(j_now == j)
        def _():
            e[...] = part

    grad = upg[...]
    for j, w in enumerate((w0, w1, w2, w3)):
        w[0] = tn(h2[:, columns(row, j)], grad).astype(BF16)


def feed_back(row, h2, dg, act, upg, downs):
    tok = whole((TOKENS, D))
    block = pl.BlockSpec((TOKENS, NB), lambda t, row: (0, t))
    up_out = pl.BlockSpec(
        (1, HC, NB), lambda t, row: (up_column(t, row[0]) // PER, 0, up_column(t, row[0]) % PER)
    )
    return pl.pallas_call(
        feed_back_kernel,
        out_shape=[jax.ShapeDtypeStruct((TOKENS, D), F32)]
        + [jax.ShapeDtypeStruct((4, HC, D), BF16)] * 4
        + [jax.ShapeDtypeStruct((D, D), BF16)] * 4,
        grid_spec=pltpu.PrefetchScalarGridSpec(
            num_scalar_prefetch=1,
            grid=(STEPS,),
            in_specs=[tok, tok, block, block] + [down_spec(j) for j in range(4)],
            out_specs=[tok] + [up_out] * 4 + [down_spec(j) for j in range(4)],
        ),
        compiler_params=params(48),
        cost_estimate=cost(3 * 2 * TOKENS * D * FF, 40 * MB),
        name="feed_back",
    )(row, h2, dg, act, upg, *downs)


def project_back_kernel(row_ref, dq, dk, dv, rk, rv, w0, w1, w2, w3, cp, sp, cf, sf, dp, h0, h1, h2, h3, bsum):
    row = row_ref[0]
    f = pl.program_id(0)
    later = (f > 0).astype(F32)
    keys = dk[0] + later * rk[0].astype(F32)
    values = dv[0] + later * rv[0].astype(F32)
    dp[0, :, :HC] = dq[0]
    dp[0, :, HC : 2 * HC] = turn(keys, cp[...] + cf[0], -(sp[...] + sf[0])).astype(BF16)
    dp[0, :, 2 * HC :] = values.astype(BF16)
    grad = dp[0]
    sums = jnp.sum(grad.astype(F32), axis=0, keepdims=True)

    @pl.when(f == 0)
    def _():
        bsum[...] = jnp.zeros_like(bsum)

    bsum[...] = bsum[...] + sums
    for j, w in enumerate((w0, w1, w2, w3)):
        part = nt(grad, w[...]).astype(BF16)
        for i, h in enumerate((h0, h1, h2, h3)):
            h[0, :, columns(row, j)] = part[i * PR : (i + 1) * PR]


def project_back(row, dq, dk, dv, rk, rv, weights, tables):
    cp, sp, cf, sf = tables
    block = pl.BlockSpec((1, TOK, HC), lambda f, *_: (f, 0, 0))
    late = pl.BlockSpec((1, TOK, HC), lambda f, *_: (jnp.maximum(f - 1, 0), 0, 0))
    frame_table = pl.BlockSpec((1, 1, HC), lambda f, *_: (f, 0, 0))
    return pl.pallas_call(
        project_back_kernel,
        out_shape=[jax.ShapeDtypeStruct((FPD, TOK, 3 * HC), BF16)]
        + [jax.ShapeDtypeStruct((FPD, PR, D), BF16)] * 4
        + [jax.ShapeDtypeStruct((1, 3 * HC), F32)],
        grid_spec=pltpu.PrefetchScalarGridSpec(
            num_scalar_prefetch=1,
            grid=(FPD,),
            in_specs=[block] * 3
            + [late] * 2
            + [whole((HC, 3 * HC))] * 4
            + [whole((TOK, HC))] * 2
            + [frame_table] * 2,
            out_specs=[pl.BlockSpec((1, TOK, 3 * HC), lambda f, *_: (f, 0, 0))]
            + [pl.BlockSpec((1, PR, D), lambda f, *_: (f, 0, 0))] * 4
            + [whole((1, 3 * HC))],
        ),
        compiler_params=params(32),
        cost_estimate=cost(2 * FPD * TOK * D * 3 * HC, 14 * MB),
        name="project_back",
    )(row, dq, dk, dv, rk, rv, *weights, cp, sp, cf, sf)


def weight_kernel(row_ref, h, dp, w):
    w[0] = tn(h[...], dp[...]).astype(BF16)


def project_weight(row, hidden, dproj):
    tokens = FPD * TOK
    return pl.pallas_call(
        weight_kernel,
        out_shape=jax.ShapeDtypeStruct((4, HC, 3 * HC), BF16),
        grid_spec=pltpu.PrefetchScalarGridSpec(
            num_scalar_prefetch=1,
            grid=(4,),
            in_specs=[
                pl.BlockSpec((tokens, HC), lambda j, row: (0, row[0] ^ j)),
                whole((tokens, 3 * HC)),
            ],
            out_specs=pl.BlockSpec((1, HC, 3 * HC), lambda j, row: (j, 0, 0)),
        ),
        compiler_params=params(32),
        cost_estimate=cost(2 * tokens * D * 3 * HC, 9 * MB),
        name="project_weight",
    )(row, hidden.reshape(tokens, D), dproj.reshape(tokens, 3 * HC))


def input_back_kernel(x, near, far, c1, mg, out, sh, sc):
    grad = near[...] + far[...].astype(F32)
    normal, rate = norm(x[...].astype(F32))
    sh[...] = jnp.sum(grad, axis=1, keepdims=True)
    sc[...] = jnp.sum(grad * normal, axis=1, keepdims=True)
    out[...] = mg[...] + norm_back(normal, rate, grad * (1.0 + c1[...]))


def input_back(x, near, far, mod, mg):
    frame_sum = pl.BlockSpec((HALF, 1, D), lambda i, *_: (i, 0, 0))
    return pl.pallas_call(
        input_back_kernel,
        out_shape=[jax.ShapeDtypeStruct((FPD, PR, D), F32)]
        + [jax.ShapeDtypeStruct((FPD, 1, D), F32)] * 2,
        grid=(FPD // HALF,),
        in_specs=[half_spec(D)] * 3 + [segment_spec(1), half_spec(D)],
        out_specs=[half_spec(D)] + [frame_sum] * 2,
        compiler_params=params(32),
        cost_estimate=cost(20 * 512 * D, 10 * MB),
        name="input_back",
    )(x, near, far, mod, mg)


def row_sum(value):
    value = value + swap(value, CORE)
    return value + swap(value, DIRECT)


def row_pieces(value):
    return [value, swap(value, CORE), swap(value, DIRECT), swap(value, DIRECT ^ CORE)]


def seq_gather(value):
    value = jnp.stack([value, swap(value, FAR)])
    value = jnp.concatenate([value] + [swap(value, m) for m in (16, 32, 48)])
    return jnp.concatenate([value] + [swap(value, m) for m in (4, 8, 12)])


def by_row(pieces, row):
    a, b, c, d = pieces
    odd, high = row % 2 == 1, row >= 2
    a, b = jnp.where(odd, b, a), jnp.where(odd, a, b)
    c, d = jnp.where(odd, d, c), jnp.where(odd, c, d)
    return jnp.stack(
        [
            jnp.where(high, c, a),
            jnp.where(high, d, b),
            jnp.where(high, a, c),
            jnp.where(high, b, d),
        ]
    )


def angle_tables(row, places):
    index = jnp.arange(HC) % (HD // 2)
    quarter, eighth = HD // 4, HD // 8
    in_frame = index < quarter
    in_row = (index >= quarter) & (index < quarter + eighth)
    offset = jnp.where(
        in_frame, index, jnp.where(in_row, index - quarter, index - quarter - eighth)
    ).astype(F32)
    length = jnp.where(in_frame, 1.0 * quarter, 1.0 * eighth)
    frequency = jnp.exp(-math.log(10000.0) * offset / length)
    sign = jnp.where(jnp.arange(HC) % HD < HD // 2, -1.0, 1.0)
    slot = jnp.arange(TOK, dtype=jnp.int32)
    patch = ((slot // PR) ^ row) * PR + slot % PR
    position = jnp.where(in_row, (patch // GRID)[:, None], (patch % GRID)[:, None]).astype(F32)
    angle = position * frequency
    cp = jnp.where(in_frame, 0.0, jnp.cos(angle))
    sp = jnp.where(in_frame, 0.0, jnp.sin(angle) * sign)

    def frame_table(place):
        angle = place.astype(F32)[:, None] * frequency
        cf = jnp.where(in_frame, jnp.cos(angle), 0.0)
        sf = jnp.where(in_frame, jnp.sin(angle) * sign, 0.0)
        return cf[:, None, :], sf[:, None, :]

    return cp, sp, frame_table


def per_device(
    activations,
    noise_embed,
    frame_position,
    cotangent,
    ada_weight,
    ada_bias,
    qkv_weight,
    qkv_bias,
    out_weight,
    out_bias,
    up_weight,
    up_bias,
    down_weight,
    down_bias,
):
    row = lax.axis_index(("xl", "c"))
    row_arg = row.astype(jnp.int32).reshape(1)

    x0 = activations
    x2 = swap(x0, DIRECT)
    x1 = swap(x0, CORE)
    x3 = swap(x2, CORE)
    before = shift(activations[1:], 1)
    p0 = after(before, x2)
    p2 = swap(p0, DIRECT)
    p1 = swap(p0, CORE)
    p3 = swap(p2, CORE)

    heads = qkv_weight.reshape(HC, 3, 4, HC)
    masks = (0, CORE, OTHER, OTHER ^ CORE)
    qkv_pieces = []
    for j in range(4):
        piece = lax.dynamic_index_in_dim(heads, row ^ j, 2, keepdims=False).reshape(HC, 3 * HC)
        qkv_pieces.append(piece if j == 0 else swap(piece, masks[j]))

    pack = jnp.concatenate([ada_bias, qkv_bias, out_bias, up_bias, down_bias])[None]
    full = by_row(row_pieces(pack), row)[:, 0].astype(F32)
    ada_b = full[:, :1536].reshape(1, 6 * D)
    qkv_b = full[:, 1536:2304].reshape(3, 4, HC)
    qkv_b = lax.dynamic_index_in_dim(qkv_b, row, 1, keepdims=False).reshape(1, 3 * HC)
    out_b = full[:, 2304:2560].reshape(1, D)
    up_b = full[:, 2560:3584].reshape(1, FF)
    down_b = full[:, 3584:].reshape(1, D)

    embed = noise_embed.astype(F32)
    silu = jax.nn.silu(embed).astype(BF16)
    silu_own = lax.dynamic_slice_in_dim(silu, row * HC, HC, 1)
    silu_prev = shift(silu_own, 1)
    part = jnp.concatenate(
        [
            jnp.dot(silu_own, ada_weight, preferred_element_type=F32),
            jnp.dot(silu_prev, ada_weight[:, : 2 * D], preferred_element_type=F32),
        ],
        axis=1,
    )
    modulation = row_sum(part) + jnp.concatenate([ada_b, ada_b[:, : 2 * D]], axis=1)
    mod = modulation[:, None, :]

    cp, sp, frame_table = angle_tables(row, frame_position)
    own_tables = (cp, sp) + frame_table(frame_position)
    prev_tables = (cp, sp) + frame_table(shift(frame_position.astype(F32)[1:], 1))

    late = lambda value: after(value, p2)
    out_own = late(out_weight)
    up_own = late(up_weight)
    down_own = late(down_weight)
    outs2 = swap(out_own, OTHER)
    ups2 = jnp.concatenate([swap(up_own[:96], DIRECT), swap(up_own[96:], OTHER)])
    downs2 = jnp.concatenate([swap(down_own[:384], DIRECT), swap(down_own[384:], OTHER)])
    outs = [out_weight, swap(out_own, CORE), outs2, swap(outs2, CORE)]
    ups = [up_weight, swap(up_own, CORE), ups2, swap(ups2, CORE)]
    downs = [down_weight, swap(down_own, CORE), downs2, swap(downs2, CORE)]

    hidden1, q, k, v = project(True, row_arg, (x0, x1, x2, x3), mod, qkv_pieces, qkv_b, own_tables)
    kp, vp = project(False, row_arg, (p0, p1, p2, p3), mod, qkv_pieces, qkv_b, prev_tables)
    *mixed, lse = attend(frame_position, q, k, v, kp, vp)
    turned = [mixed[0]] + [swap(mixed[j], (0, CORE, DIRECT, DIRECT ^ CORE)[j]) for j in (1, 2, 3)]
    branch, middle, hidden2, down_grad, down_sum = mid(turned, outs, out_b, x0, cotangent, mod)
    h2 = hidden2.reshape(TOKENS, D)
    dg = down_grad.reshape(TOKENS, D)
    act, upg, hg, up_sum = feed(row_arg, h2, dg, ups, up_b, downs)
    mg, bg, *rest = mid_back(hg.reshape(FPD, PR, D), middle, branch, cotangent, mod, outs)
    ag, (shift2, scale2, gate1, out_sum) = rest[:4], rest[4:]
    back = [ag[0]] + [swap(ag[j], (0, CORE, DIRECT, DIRECT ^ CORE)[j]) for j in (1, 2, 3)]

    dn, *grads = feed_back(row_arg, h2, dg, act, upg, downs)
    up_parts, down_parts = grads[:4], grads[4:]
    downward = (dn + down_b).reshape(FPD, PR, D)
    layer_output = (middle + mod[:, :, 5 * D : 6 * D] * downward).astype(BF16)
    gate2 = jnp.sum(cotangent.astype(F32) * downward, axis=1)
    out_parts = [
        tn(t.reshape(TOKENS, HC), bg.reshape(TOKENS, D)).astype(BF16) for t in turned
    ]

    def core_sum(parts, j):
        own = parts[j].astype(F32)
        return (own + swap(parts[j + 1], CORE).astype(F32)).astype(BF16)

    packed = jnp.stack(
        [
            jnp.concatenate(
                [
                    core_sum(up_parts, j).reshape(D, D),
                    core_sum(down_parts, j),
                    core_sum(out_parts, j),
                ]
            )
            for j in (0, 2)
        ]
    )
    scattered = lax.psum_scatter(packed, ("z", "y"), scatter_dimension=1, tiled=True)
    share = scattered[0].astype(F32) + swap(scattered[1], DIRECT).astype(F32)
    share = (share + swap(share.astype(BF16), FAR).astype(F32)).astype(BF16)
    totals = lax.all_gather(share, ("z", "y"), axis=0, tiled=True)
    up_total = totals[:D].reshape(4, HC, D).transpose(1, 0, 2).reshape(HC, FF).astype(F32)
    down_total = totals[D : 2 * D].astype(F32)
    out_total = totals[2 * D :].astype(F32)

    dq, dk, dv, dkp, dvp = attend_back(
        frame_position, q, k, v, kp, vp, back, mixed, lse, own_tables
    )
    rk, rv = shift(dkp, -1), shift(dvp, -1)
    dproj, *pieces, qkv_sum = project_back(row_arg, dq, dk, dv, rk, rv, qkv_pieces, own_tables)
    near0 = pieces[0].astype(F32) + swap(pieces[1], CORE).astype(F32)
    near2 = pieces[2].astype(F32) + swap(pieces[3], CORE).astype(F32)
    far = swap(near2.astype(BF16), DIRECT)
    input_grad, shift1, scale1 = input_back(x0, near0, far, mod, mg)

    qkv_parts = project_weight(row_arg, hidden1, dproj)
    qkv_parts = lax.psum_scatter(qkv_parts, ("z", "y"), scatter_dimension=1, tiled=True)
    qkv_parts = (
        qkv_parts.astype(F32) + swap(qkv_parts, FAR).astype(F32)
    ).astype(BF16)
    qkv_turned = [qkv_parts[0]] + [
        swap(qkv_parts[j], (0, CORE, DIRECT, DIRECT ^ CORE)[j]) for j in (1, 2, 3)
    ]
    qkv_share = by_row(qkv_turned, row).reshape(4, 16, 3, HC).transpose(1, 2, 0, 3)
    qkv_total = lax.all_gather(
        qkv_share.reshape(16, 3 * D), ("z", "y"), axis=0, tiled=True
    ).astype(F32)

    early = jnp.concatenate(
        [
            gate1[:, 0],
            shift2[:, 0],
            scale2[:, 0],
            gate2,
            jnp.concatenate([down_sum, up_sum, out_sum], axis=1).reshape(FPD, 768),
        ],
        axis=1,
    )
    early = row_sum(early)
    early_all = seq_gather(early.astype(BF16))
    qkv_sum = lax.dynamic_update_slice(
        jnp.zeros((3, 4, HC), F32), qkv_sum.reshape(3, 1, HC), (0, row, 0)
    )
    final = jnp.concatenate([shift1[:, 0], scale1[:, 0], qkv_sum.reshape(FPD, 384)], axis=1)
    final = row_sum(final)
    final_all = seq_gather(final.astype(BF16))
    silu_all = seq_gather(silu_own).reshape(256, HC)

    mod_all = jnp.concatenate([final_all[:, :, : 2 * D], early_all[:, :, : 4 * D]], axis=2)
    mod_all = mod_all.reshape(256, 6 * D)
    ada_total = tn(silu_all, mod_all)
    ada_sum = jnp.sum(mod_all.astype(F32), axis=0)
    ada_sum = lax.dynamic_slice_in_dim(ada_sum, row * 1536, 1536)
    bias_sum = jnp.sum(early_all[:, :, 4 * D :].astype(F32), axis=0).reshape(6144)
    down_sum = lax.dynamic_slice_in_dim(bias_sum, row * HC, HC)
    up_sum = lax.dynamic_slice_in_dim(bias_sum, D + row * D, D)
    out_sum = lax.dynamic_slice_in_dim(bias_sum, 5 * D + row * HC, HC)
    qkv_sum = jnp.sum(final_all[:, :, 2 * D :].astype(F32), axis=0).reshape(3 * D)
    qkv_sum = lax.dynamic_slice_in_dim(qkv_sum, row * 768, 768)

    mod_own = jnp.concatenate([final[:, : 2 * D], early[:, : 4 * D]], axis=1).astype(BF16)
    silu_grad = nt(mod_own, ada_weight)
    silu_grad = by_row(row_pieces(silu_grad), row).transpose(1, 0, 2).reshape(FPD, D)
    gate = jax.nn.sigmoid(embed)
    embed_grad = silu_grad * (gate * (1.0 + embed * (1.0 - gate)))

    return (
        layer_output,
        input_grad,
        embed_grad,
        ada_total,
        ada_sum,
        qkv_total,
        qkv_sum,
        out_total,
        out_sum,
        up_total,
        up_sum,
        down_total,
        down_sum,
    )


def solution(mesh):
    fine = Mesh(mesh.devices.reshape(2, 4, 4, 2, 2), AXES)
    seq, row = ("xh", "z", "y"), ("xl", "c")
    token, weight, vector = P(seq, row, None), P(row, None), P(row)
    in_specs = (token, P(seq, None), P(seq), token) + (weight, vector) * 5
    out_specs = (token, token, P(seq, None)) + (weight, vector) * 5
    return jax.shard_map(
        per_device, mesh=fine, in_specs=in_specs, out_specs=out_specs, check_vma=False
    )
```

```python
import math

import jax
import jax.numpy as jnp
from jax import lax
from jax.experimental import pallas as pl
from jax.experimental.pallas import tpu as pltpu
from jax.sharding import Mesh, PartitionSpec as P

F32 = jnp.float32
BF16 = jnp.bfloat16
HD = 64
GRID = 16
FPD = 8
PR = 64
D = 1024
FF = 4096
HC = 256
TOK = 256
PREV = 7
AXES = ("xh", "z", "y", "xl", "c")
CORE, DIRECT, OTHER, FAR = 1, 2, 66, 64
MB = 1024 * 1024


def swap(value, mask):
    return lax.ppermute(value, AXES, [(i, i ^ mask) for i in range(128)])


def shift(value, steps):
    first, last = max(0, -4 * steps), min(128, 128 - 4 * steps)
    return lax.ppermute(value, AXES, [(i, i + 4 * steps) for i in range(first, last)])


def after(value, *others):
    return lax.optimization_barrier((value,) + others)[0]


def nt(left, right):
    return lax.dot_general(left, right, (((1,), (1,)), ((), ())), preferred_element_type=F32)


def tn(left, right):
    return lax.dot_general(left, right, (((0,), (0,)), ((), ())), preferred_element_type=F32)


def nn(left, right):
    return jnp.dot(left, right, preferred_element_type=F32)


def norm(values):
    center = values - jnp.mean(values, axis=-1, keepdims=True)
    spread = jnp.mean(center * center, axis=-1, keepdims=True)
    rate = lax.rsqrt(spread + 1e-06)
    return center * rate, rate


def norm_back(normal, rate, grad):
    mean_grad = jnp.mean(grad, axis=-1, keepdims=True)
    mean_both = jnp.mean(grad * normal, axis=-1, keepdims=True)
    return rate * (grad - mean_grad - normal * mean_both)


def turn(values, cosine, sine):
    lanes = lax.broadcasted_iota(jnp.int32, values.shape, 1)
    other = jnp.where(
        lanes % HD < HD // 2, pltpu.roll(values, HC - HD // 2, 1), pltpu.roll(values, HD // 2, 1)
    )
    return values * cosine + other * sine


def params(mib):
    return pltpu.CompilerParams(
        dimension_semantics=("arbitrary",), vmem_limit_bytes=mib * MB
    )


def cost(flops, moved, exps=0):
    return pl.CostEstimate(flops=int(flops), bytes_accessed=int(moved), transcendentals=int(exps))


def whole(shape):
    return pl.BlockSpec(shape, lambda i, *_: (0,) * len(shape))


def columns(row, j):
    return pl.ds(pl.multiple_of((row ^ j) * HC, HC), HC)


def shape(dims, kind=BF16):
    return jax.ShapeDtypeStruct(dims, kind)


UB, QB, OB, DB, WIDE = 6144, 6656, 7168, 7296, 7424


def put(ref, start, at, value):
    cols = slice(start, start + value.shape[1])
    number = lax.broadcasted_iota(jnp.int32, (8, value.shape[1]), 0)
    ref[:, cols] = jnp.where(number == at, value, ref[:, cols])


def take(value, at):
    number = lax.broadcasted_iota(jnp.int32, value.shape, 0)
    return jnp.sum(jnp.where(number == at, value, 0.0), axis=0, keepdims=True)


def put_half(ref, start, value):
    cols = slice(start, start + value.shape[1])
    number = lax.broadcasted_iota(jnp.int32, (8, value.shape[1]), 0)
    both = jnp.concatenate([value, value], axis=0)
    ref[:, cols] = jnp.where(number // 4 == pl.program_id(0), both, ref[:, cols])


def unfold(ref, start, width):
    return jnp.concatenate([ref[i : i + 1, start : start + width] for i in range(8)], axis=1)


def prepare_kernel(row_ref, pos_ref, noise, ada, ab, qb, ob, ub, db, pack, silu, cp, sp, frames):
    row = row_ref[0]
    embed = noise[...].astype(F32)
    value = (embed / (1.0 + jnp.exp(-embed))).astype(BF16)
    own = jnp.where(
        row < 2,
        jnp.where(row == 0, value[:, :HC], value[:, HC : 2 * HC]),
        jnp.where(row == 2, value[:, 2 * HC : 3 * HC], value[:, 3 * HC :]),
    )
    silu[...] = own
    pack[:, UB:] = jnp.zeros((FPD, WIDE - UB), F32)
    for segment in range(6):
        cols = slice(segment * D, (segment + 1) * D)
        pack[:, cols] = nn(own, ada[:, cols])
    bias = pl.ds(pl.multiple_of(row * 1536, 512), 1536)
    pack[:, bias] = pack[:, bias] + ab[...].astype(F32)
    for i in range(2):
        at = 2 * row + i
        put(pack, UB, at, ub[:, i * 512 : (i + 1) * 512].astype(F32))
        put(pack, OB, at, ob[:, i * 128 : (i + 1) * 128].astype(F32))
        put(pack, DB, at, db[:, i * 128 : (i + 1) * 128].astype(F32))
    for i in range(3):
        chunk = 3 * row + i
        at = jnp.where(chunk < 4, chunk, chunk - 4)
        second = (chunk >= 4) & (chunk < 8)
        value = qb[:, i * HC : (i + 1) * HC].astype(F32)
        put(pack, QB, jnp.where(second, -1, at), value)
        put(pack, QB + HC, jnp.where(second, at, -1), value)

    def parts(dims):
        lane = lax.broadcasted_iota(jnp.int32, dims, 1)
        index = lane % (HD // 2)
        quarter, eighth = HD // 4, HD // 8
        in_frame = index < quarter
        in_row = (index >= quarter) & (index < quarter + eighth)
        offset = jnp.where(
            in_frame, index, jnp.where(in_row, index - quarter, index - quarter - eighth)
        ).astype(F32)
        length = jnp.where(in_frame, 1.0 * quarter, 1.0 * eighth)
        frequency = jnp.exp(-math.log(10000.0) * offset / length)
        sign = jnp.where(lane % HD < HD // 2, -1.0, 1.0)
        return in_frame, in_row, frequency, sign

    in_frame, in_row, frequency, sign = parts((TOK, HC))
    slot = lax.broadcasted_iota(jnp.int32, (TOK, HC), 0)
    patch = ((slot // PR) ^ row) * PR + slot % PR
    angle = jnp.where(in_row, patch // GRID, patch % GRID).astype(F32) * frequency
    cp[...] = jnp.where(in_frame, 0.0, jnp.cos(angle))
    sp[...] = jnp.where(in_frame, 0.0, jnp.sin(angle) * sign)
    in_frame, _, frequency, sign = parts((16, HC))
    slot = lax.broadcasted_iota(jnp.int32, (16, HC), 0)
    place = pos_ref[0] - PREV + (slot - FPD)
    for f in range(FPD):
        place = jnp.where(slot == f, pos_ref[f], place)
    angle = place.astype(F32) * frequency
    frames[:, :HC] = jnp.where(in_frame, jnp.cos(angle), 0.0)
    frames[:, HC:] = jnp.where(in_frame, jnp.sin(angle) * sign, 0.0)


def prepare(row, places, noise, ada, biases):
    return pl.pallas_call(
        prepare_kernel,
        out_shape=[
            shape((FPD, WIDE), F32),
            shape((FPD, HC)),
            shape((TOK, HC), F32),
            shape((TOK, HC), F32),
            shape((16, 2 * HC), F32),
        ],
        grid_spec=pltpu.PrefetchScalarGridSpec(
            num_scalar_prefetch=2,
            grid=(1,),
            in_specs=[whole((FPD, D)), whole((HC, 6 * D))]
            + [whole((1, b.shape[0])) for b in biases],
            out_specs=[
                whole((FPD, WIDE)),
                whole((FPD, HC)),
                whole((TOK, HC)),
                whole((TOK, HC)),
                whole((16, 2 * HC)),
            ],
        ),
        compiler_params=params(32),
        cost_estimate=cost(2 * 8 * HC * 6 * D, 4 * MB, 4 * TOK * HC),
        name="prepare",
    )(row, places, noise, ada, *[b[None] for b in biases])


def split_heads_kernel(row_ref, q, k, v, p0, p1, p2, p3):
    for j, p in enumerate((p0, p1, p2, p3)):

        @pl.when(pl.program_id(0) == j)
        def _():
            p[:, :HC] = q[...]
            p[:, HC : 2 * HC] = k[...]
            p[:, 2 * HC :] = v[...]


def split_heads(row, weight):
    return pl.pallas_call(
        split_heads_kernel,
        out_shape=[shape((HC, 3 * HC))] * 4,
        grid_spec=pltpu.PrefetchScalarGridSpec(
            num_scalar_prefetch=1,
            grid=(4,),
            in_specs=[
                pl.BlockSpec((HC, HC), lambda j, row, s=s: (0, 4 * s + (row[0] ^ j)))
                for s in range(3)
            ],
            out_specs=[whole((HC, 3 * HC))] * 4,
        ),
        compiler_params=params(16),
        cost_estimate=cost(0, 3 * MB),
        name="split_heads",
    )(row, weight, weight, weight)


def cosines(cp, sp, frames, at):
    both = frames[pl.ds(at, 1), :]
    return cp[...] + both[:, :HC], sp[...] + both[:, HC:]


def project_kernel(own, row_ref, x0, x1, x2, x3, table, mods, w0, w1, w2, w3, cp, sp, fr, *outs):
    row = row_ref[0]
    f = pl.program_id(0)
    if own:
        h_ref, q_ref, k_ref, v_ref = outs
        first, at, angle = 0, f, f
    else:
        k_ref, v_ref, h_ref = outs
        first, at, angle = HC, f + FPD - PREV, f + FPD
    x = jnp.concatenate([r[0] for r in (x0, x1, x2, x3)], axis=0).astype(F32)
    normal, _ = norm(x)
    shift_row = mods[pl.ds(at, 1), :D]
    scale_row = mods[pl.ds(at, 1), D : 2 * D]
    hidden = (normal * (1.0 + scale_row) + shift_row).astype(BF16)
    where = (0,) if own else ()
    h_ref[where + (slice(None), slice(None))] = hidden
    low, high = table[pl.ds(row, 1), QB : QB + 2 * HC], table[pl.ds(row + 4, 1), QB : QB + HC]
    total = jnp.concatenate([low, high], axis=1)[:, first:]
    for j, w in enumerate((w0, w1, w2, w3)):
        total = total + nn(h_ref[where + (slice(None), columns(row, j))], w[:, first:])
    cosine, sine = cosines(cp, sp, fr, angle)
    if own:
        q_ref[0] = (turn(total[:, :HC], cosine, sine).astype(BF16).astype(F32) * 0.125).astype(BF16)
        total = total[:, HC:]
    k_ref[0] = turn(total[:, :HC], cosine, sine).astype(BF16)
    v_ref[0] = total[:, HC:].astype(BF16)


def project(own, row, xs, table, mods, weights, tables):
    frames = xs[0].shape[0]
    x_spec = pl.BlockSpec((1, PR, D), lambda f, *_: (f, 0, 0))
    out_spec = pl.BlockSpec((1, TOK, HC), lambda f, *_: (f, 0, 0))
    out = shape((frames, TOK, HC))
    if own:
        out_specs = [pl.BlockSpec((1, TOK, D), lambda f, *_: (f, 0, 0)), out_spec, out_spec, out_spec]
        out_shape = [shape((frames, TOK, D)), out, out, out]
        scratch = []
    else:
        out_specs = [out_spec, out_spec]
        out_shape = [out, out]
        scratch = [pltpu.VMEM((TOK, D), BF16)]
    return pl.pallas_call(
        lambda *refs: project_kernel(own, *refs),
        out_shape=out_shape,
        grid_spec=pltpu.PrefetchScalarGridSpec(
            num_scalar_prefetch=1,
            grid=(frames,),
            in_specs=[x_spec] * 4
            + [whole((FPD, WIDE)), whole(mods.shape)]
            + [whole((HC, 3 * HC))] * 4
            + [whole((TOK, HC)), whole((TOK, HC)), whole((16, 2 * HC))],
            out_specs=out_specs,
            scratch_shapes=scratch,
        ),
        compiler_params=params(32),
        cost_estimate=cost(2 * frames * TOK * D * 3 * HC, frames * TOK * D * 4 + 4 * MB),
        name="project_own" if own else "project_prev",
    )(row, *xs, table, mods, *weights, *tables)


def head_lanes():
    return lax.broadcasted_iota(jnp.int32, (TOK, HC), 1) // HD


def attend_kernel(pos_ref, q, k, v, kp, vp, o0, o1, o2, o3, lse, qs, scores, acc, top, low):
    f = pl.program_id(0)
    place = pos_ref[f]
    lanes = head_lanes()
    query = q[0]
    for h in range(4):
        qs[pl.ds(h * TOK, TOK), :] = jnp.where(lanes == h, query, jnp.zeros_like(query))
    top[...] = jnp.full_like(top, -1e30)
    low[...] = jnp.zeros_like(low)
    acc[...] = jnp.zeros_like(acc)
    before = jnp.maximum(place - f, 0)
    start = jnp.maximum(f - place, 0)

    def score(keys, slot):
        for h in range(4):
            rows = pl.ds(h * TOK, TOK)
            s = nt(qs[rows, :], keys)
            scores[slot, rows, :] = s
            top[rows, :] = jnp.maximum(top[rows, :], jnp.maximum(s[:, :128], s[:, 128:]))

    def mix(values, slot):
        for h in range(4):
            rows = pl.ds(h * TOK, TOK)
            p = jnp.exp(scores[slot, rows, :] - jnp.concatenate([top[rows, :]] * 2, axis=1))
            low[rows, :] = low[rows, :] + (p[:, :128] + p[:, 128:])
            acc[rows, :] = acc[rows, :] + nn(p.astype(BF16), values)

    def run(step):
        def prev(i, _):
            at = PREV - before + i
            step(kp[at] if step is score else vp[at], i)
            return 0

        def own(g, _):
            step(k[g] if step is score else v[g], g - f + place)
            return 0

        lax.fori_loop(0, before, prev, 0)
        lax.fori_loop(start, f + 1, own, 0)

    run(score)
    for h in range(4):
        rows = pl.ds(h * TOK, TOK)
        top[rows, :] = jnp.broadcast_to(jnp.max(top[rows, :], axis=1, keepdims=True), (TOK, 128))
    run(mix)
    result = jnp.zeros((TOK, HC), F32)
    logs = jnp.zeros((TOK, 128), F32)
    narrow = lax.broadcasted_iota(jnp.int32, (TOK, 128), 1)
    for h in range(4):
        rows = pl.ds(h * TOK, TOK)
        total = jnp.sum(low[rows, :], axis=1, keepdims=True)
        result = jnp.where(lanes == h, acc[rows, :] / total, result)
        logs = jnp.where(narrow == h, top[rows, :] + jnp.log(total), logs)
    lse[0] = logs.T[:8]
    result = result.astype(BF16)
    for j, o in enumerate((o0, o1, o2, o3)):
        o[0] = result[j * PR : (j + 1) * PR]


def attend(places, q, k, v, kp, vp):
    block = pl.BlockSpec((1, TOK, HC), lambda f, *_: (f, 0, 0))
    piece = pl.BlockSpec((1, PR, HC), lambda f, *_: (f, 0, 0))
    return pl.pallas_call(
        attend_kernel,
        out_shape=[jax.ShapeDtypeStruct((FPD, PR, HC), BF16)] * 4
        + [jax.ShapeDtypeStruct((FPD, 8, TOK), F32)],
        grid_spec=pltpu.PrefetchScalarGridSpec(
            num_scalar_prefetch=1,
            grid=(FPD,),
            in_specs=[block]
            + [whole((FPD, TOK, HC))] * 2
            + [whole((PREV, TOK, HC))] * 2,
            out_specs=[piece] * 4 + [pl.BlockSpec((1, 8, TOK), lambda f, *_: (f, 0, 0))],
            scratch_shapes=[
                pltpu.VMEM((4 * TOK, HC), BF16),
                pltpu.VMEM((8, 4 * TOK, TOK), F32),
                pltpu.VMEM((4 * TOK, HC), F32),
                pltpu.VMEM((4 * TOK, 128), F32),
                pltpu.VMEM((4 * TOK, 128), F32),
            ],
        ),
        compiler_params=params(40),
        cost_estimate=cost(36 * 4 * 2 * 2 * TOK**3, 6 * MB, 36 * 4 * TOK * TOK),
        name="attend",
    )(places, q, k, v, kp, vp)


def attend_back_kernel(own, pos_ref, q, k, v, g0, g1, g2, g3, o0, o1, o2, o3, lse, *rest):
    if own:
        cp, sp, fr, before_ref, dq, dk, dv, qs, gs, ks, pl_scr, dl_scr, ds_scr, dq_acc = rest
        dk_acc, dv_acc = dk, dv
    else:
        dq, dk, dv, qs, gs, ks, pl_scr, dl_scr, ds_scr, dq_acc, dk_acc, dv_acc = rest
    f = pl.program_id(0)
    place = pos_ref[f]
    lanes = head_lanes()

    @pl.when(f == 0)
    def _():
        for ref in (dk_acc, dv_acc):
            ref[...] = jnp.zeros_like(ref)

    def prelude():
        query = q[0]
        grad = jnp.concatenate([r[0] for r in (g0, g1, g2, g3)], axis=0)
        mixed = jnp.concatenate([r[0] for r in (o0, o1, o2, o3)], axis=0)
        for h in range(4):
            rows = pl.ds(h * TOK, TOK)
            qs[rows, :] = jnp.where(lanes == h, query, jnp.zeros_like(query))
            gs[rows, :] = jnp.where(lanes == h, grad, jnp.zeros_like(grad))
        both = grad.astype(F32) * mixed.astype(F32)
        pick = (
            lax.broadcasted_iota(jnp.int32, (8, HC), 1) // HD
            == lax.broadcasted_iota(jnp.int32, (8, HC), 0)
        ).astype(F32)
        return lax.dot_general(
            pick, both, (((1,), (1,)), ((), ())),
            preferred_element_type=F32, precision=lax.Precision.HIGHEST,
        )

    def step(delta, logs, at):
        keys, values = k[at], v[at]
        for h in range(4):
            rows = pl.ds(h * TOK, TOK)
            ks[rows, :] = jnp.where(lanes == h, keys, jnp.zeros_like(keys))
            p = jnp.exp(nt(keys, qs[rows, :]) - logs[h : h + 1])
            ds = (p * (nt(values, gs[rows, :]) - delta[h : h + 1])).astype(BF16)
            pl_scr[:, rows] = p.astype(BF16)
            dl_scr[:, rows] = ds
            ds_scr[rows, :] = ds
        dv_acc[at] = dv_acc[at] + nn(pl_scr[...], gs[...])
        dk_acc[at] = dk_acc[at] + nn(dl_scr[...], qs[...])
        dq_acc[...] = dq_acc[...] + tn(ds_scr[...], ks[...])

    def sweep(low, high):
        delta = prelude()
        logs = lse[0]
        dq_acc[...] = jnp.zeros_like(dq_acc)

        def one(at, _):
            step(delta, logs, at)
            return 0

        lax.fori_loop(low, high, one, 0)

    if own:
        sweep(jnp.maximum(f - place, 0), f + 1)
        cosine, sine = cosines(cp, sp, fr, f)
        dq[0] = turn((dq_acc[...] + before_ref[0]) * 0.125, cosine, -sine).astype(BF16)
    else:
        count = jnp.maximum(place - f, 0)

        @pl.when(count > 0)
        def _():
            sweep(PREV - count, PREV)
            dq[0] = dq_acc[...]

        @pl.when(count == 0)
        def _():
            dq[0] = jnp.zeros_like(dq_acc)

        @pl.when(f == FPD - 1)
        def _():
            dk[...] = dk_acc[...].astype(BF16)
            dv[...] = dv_acc[...].astype(BF16)


def attend_back(own, places, q, k, v, grads, mixed, lse, tables=None, before=None):
    block = pl.BlockSpec((1, TOK, HC), lambda f, *_: (f, 0, 0))
    piece = pl.BlockSpec((1, PR, HC), lambda f, *_: (f, 0, 0))
    count = FPD if own else PREV
    wide = pltpu.VMEM((4 * TOK, HC), BF16)
    tall = pltpu.VMEM((TOK, 4 * TOK), BF16)
    scratch = [wide, wide, wide, tall, tall, wide, pltpu.VMEM((TOK, HC), F32)]
    specs = []
    extra = ()
    if own:
        specs = [whole((TOK, HC)), whole((TOK, HC)), whole((16, 2 * HC)), block]
        extra = tuple(tables) + (before,)
    else:
        scratch += [pltpu.VMEM((PREV, TOK, HC), F32)] * 2
    return pl.pallas_call(
        lambda *refs: attend_back_kernel(own, *refs),
        out_shape=[shape((FPD, TOK, HC), BF16 if own else F32)]
        + [shape((count, TOK, HC), F32 if own else BF16)] * 2,
        grid_spec=pltpu.PrefetchScalarGridSpec(
            num_scalar_prefetch=1,
            grid=(FPD,),
            in_specs=[block]
            + [whole((count, TOK, HC))] * 2
            + [piece] * 8
            + [pl.BlockSpec((1, 8, TOK), lambda f, *_: (f, 0, 0))]
            + specs,
            out_specs=[block] + [whole((count, TOK, HC))] * 2,
            scratch_shapes=scratch,
        ),
        compiler_params=params(40),
        cost_estimate=cost((30 if own else 12) * 4 * 5 * 2 * TOK**3, 12 * MB, 30 * 4 * TOK * TOK),
        name="attend_back_own" if own else "attend_back_prev",
    )(places, q, k, v, *grads, *mixed, lse, *extra)


HALF = 4
RAW = HALF * PR


def flat(ref):
    return ref[...].reshape(RAW, ref.shape[-1])


def frames_of(value):
    return value.reshape(HALF, PR, value.shape[-1])


def segment(table, s):
    both = table[:, s * D : (s + 1) * D]
    return jnp.where(pl.program_id(0) == 0, both[:HALF], both[HALF:])[:, None, :]


def fold(out, start, width, row):
    @pl.when(pl.program_id(0) == 0)
    def _():
        out[:, start : start + width] = jnp.zeros((8, width), F32)

    for i in range(8):
        at = (slice(i, i + 1), slice(start, start + width))
        out[at] = out[at] + row[:, i * width : (i + 1) * width]


def mid_kernel(o0, o1, o2, o3, w0, w1, w2, w3, table, x, cot, branch, middle, hidden, down, dsum):
    total = unfold(table, OB, 128)
    for o, w in zip((o0, o1, o2, o3), (w0, w1, w2, w3)):
        total = total + nn(flat(o), w[...])
    branched = frames_of(total)
    branch[...] = branched
    mid_value = x[...].astype(F32) + segment(table, 2) * branched
    middle[...] = mid_value
    normal, _ = norm(mid_value)
    hidden[...] = (normal * (1.0 + segment(table, 4)) + segment(table, 3)).astype(BF16)
    grad = (segment(table, 5) * cot[...].astype(F32)).astype(BF16)
    down[...] = grad
    fold(dsum, 0, 128, jnp.sum(grad.astype(F32).reshape(RAW, D), axis=0, keepdims=True))


def half_spec(width):
    return pl.BlockSpec((HALF, PR, width), lambda i, *_: (i, 0, 0))


def mid(pieces, weights, table, x, cot):
    return pl.pallas_call(
        mid_kernel,
        out_shape=[
            shape((FPD, PR, D), F32),
            shape((FPD, PR, D), F32),
            shape((FPD, PR, D)),
            shape((FPD, PR, D)),
            shape((8, 128), F32),
        ],
        grid=(FPD // HALF,),
        in_specs=[half_spec(HC)] * 4
        + [whole((HC, D))] * 4
        + [whole((FPD, WIDE)), half_spec(D), half_spec(D)],
        out_specs=[half_spec(D)] * 4 + [whole((8, 128))],
        compiler_params=params(40),
        cost_estimate=cost(2 * 512 * D * D, 12 * MB),
        name="mid",
    )(*pieces, *weights, table, x, cot)


def mid_back_kernel(hg, middle, branch, cot, table, w0, w1, w2, w3, mg, bg, a0, a1, a2, a3, sums):
    grad = hg[...]
    normal, rate = norm(middle[...])
    put_half(sums, D, jnp.sum(grad, axis=1))
    put_half(sums, 2 * D, jnp.sum(grad * normal, axis=1))
    total = cot[...].astype(F32) + norm_back(normal, rate, grad * (1.0 + segment(table, 4)))
    mg[...] = total
    put_half(sums, 0, jnp.sum(total * branch[...], axis=1))
    low = (segment(table, 2) * total).astype(BF16)
    bg[...] = low
    low = low.reshape(RAW, D)
    fold(sums, 3 * D, 128, jnp.sum(low.astype(F32), axis=0, keepdims=True))
    for a, w in zip((a0, a1, a2, a3), (w0, w1, w2, w3)):
        a[...] = frames_of(nt(low, w[...]).astype(BF16))


def mid_back(hg, middle, branch, cot, table, weights):
    return pl.pallas_call(
        mid_back_kernel,
        out_shape=[shape((FPD, PR, D), F32), shape((FPD, PR, D))]
        + [shape((FPD, PR, HC))] * 4
        + [shape((8, 3 * D + 128), F32)],
        grid=(FPD // HALF,),
        in_specs=[half_spec(D)] * 4
        + [whole((FPD, WIDE))]
        + [whole((HC, D))] * 4,
        out_specs=[half_spec(D)] * 2 + [half_spec(HC)] * 4 + [whole((8, 3 * D + 128))],
        compiler_params=params(40),
        cost_estimate=cost(2 * 512 * D * D, 12 * MB),
        name="mid_back",
    )(hg, middle, branch, cot, table, *weights)


NB = 512
STEPS = FF // NB
PER = D // NB
TOKENS = FPD * PR


def block_of(t):
    phase = t // PER
    return ((phase % 2) * 2) ^ (phase // 2)


def up_column(t, row):
    return (row ^ block_of(t)) * PER + t % PER


def down_row(t):
    return block_of(t) * PER + t % PER


def down_spec(j):
    phase = (0, 2, 1, 3)[j]
    return pl.BlockSpec((NB, D), lambda t, row: (jnp.clip(t - phase * PER, 0, PER - 1), 0))


def pick_down(d0, d1, d2, d3):
    phase = pl.program_id(0) // PER
    return jnp.where(
        phase < 2,
        jnp.where(phase == 0, d0[...], d2[...]),
        jnp.where(phase == 2, d1[...], d3[...]),
    )


def feed_kernel(row_ref, h2, dg, u0, u1, u2, u3, table, d0, d1, d2, d3, act, upg, hg, usum):
    row = row_ref[0]
    ups = (u0, u1, u2, u3)
    down = pick_down(d0, d1, d2, d3)
    at = pl.ds(up_column(pl.program_id(0), row), 1)
    u = table[at, UB : UB + NB]
    for j, w in enumerate(ups):
        u = u + nn(h2[:, columns(row, j)], w[...])
    rate = math.sqrt(2.0 / math.pi)
    square = u * u
    half = 0.5 + 0.5 * jnp.tanh(u * (rate + (rate * 0.044715) * square))
    active = u * half
    act[...] = active.astype(BF16)
    slope = half + active * (1.0 - half) * (2.0 * rate + (6.0 * rate * 0.044715) * square)
    grad = (nt(dg[...], down) * slope).astype(BF16)
    upg[...] = grad
    put(usum, 0, up_column(pl.program_id(0), row), jnp.sum(grad.astype(F32), axis=0, keepdims=True))

    @pl.when(pl.program_id(0) == 0)
    def _():
        hg[...] = jnp.zeros_like(hg)

    for j, w in enumerate(ups):
        hg[:, columns(row, j)] = hg[:, columns(row, j)] + nt(grad, w[...])


def feed(row, h2, dg, ups, table, downs):
    tok = whole((TOKENS, D))
    block = pl.BlockSpec((TOKENS, NB), lambda t, row: (0, t))
    return pl.pallas_call(
        feed_kernel,
        out_shape=[
            shape((TOKENS, FF)),
            shape((TOKENS, FF)),
            shape((TOKENS, D), F32),
            shape((8, NB), F32),
        ],
        grid_spec=pltpu.PrefetchScalarGridSpec(
            num_scalar_prefetch=1,
            grid=(STEPS,),
            in_specs=[tok, tok]
            + [pl.BlockSpec((HC, NB), lambda t, row: (0, up_column(t, row[0])))] * 4
            + [whole((FPD, WIDE))]
            + [down_spec(j) for j in range(4)],
            out_specs=[block, block, tok, whole((8, NB))],
        ),
        compiler_params=params(44),
        cost_estimate=cost(3 * 2 * TOKENS * D * FF, 30 * MB, TOKENS * FF),
        name="feed",
    )(row, h2, dg, *ups, table, *downs)


def feed_back_kernel(
    row_ref, h2, dg, act, upg, d0, d1, d2, d3, table, middle, cot,
    uk, us, dk, ds, out, gate, dn,
):
    row = row_ref[0]
    t = pl.program_id(0)
    down = pick_down(d0, d1, d2, d3)
    active = act[...]

    @pl.when(t == 0)
    def _():
        dn[...] = jnp.zeros_like(dn)

    dn[...] = dn[...] + nn(active, down)
    part = tn(active, dg[...]).astype(BF16)

    @pl.when(t < STEPS // 2)
    def _():
        dk[0] = part

    @pl.when(t >= STEPS // 2)
    def _():
        ds[0] = part

    grad = upg[...]
    for j, ref in enumerate((uk, us, uk, us)):
        ref[j // 2, 0] = tn(h2[:, columns(row, j)], grad).astype(BF16)

    @pl.when(t == STEPS - 1)
    def _():
        bias = unfold(table, DB, 128)
        for f in range(FPD):
            rows = slice(f * PR, (f + 1) * PR)
            value = dn[rows, :] + bias
            out[f] = (middle[f] + table[f : f + 1, 5 * D : 6 * D] * value).astype(BF16)
            gate[f : f + 1, :] = jnp.sum(cot[f].astype(F32) * value, axis=0, keepdims=True)


def feed_back(row, h2, dg, act, upg, downs, table, middle, cot):
    tok = whole((TOKENS, D))
    full = whole((FPD, PR, D))
    block = pl.BlockSpec((TOKENS, NB), lambda t, row: (0, t))
    up_out = pl.BlockSpec(
        (2, 1, HC, NB),
        lambda t, row: (0, up_column(t, row[0]) // PER, 0, up_column(t, row[0]) % PER),
    )

    def down_out(first):
        def index(t, row):
            at = jnp.clip(t - first, 0, STEPS // 2 - 1)
            return (at // PER, at % PER, 0)

        return pl.BlockSpec((1, NB, D), index)

    return pl.pallas_call(
        feed_back_kernel,
        out_shape=[shape((2, 4, HC, D))] * 2
        + [shape((2, D, D))] * 2
        + [shape((FPD, PR, D)), shape((8, D), F32)],
        grid_spec=pltpu.PrefetchScalarGridSpec(
            num_scalar_prefetch=1,
            grid=(STEPS,),
            in_specs=[tok, tok, block, block]
            + [down_spec(j) for j in range(4)]
            + [whole((FPD, WIDE)), full, full],
            out_specs=[up_out, up_out, down_out(0), down_out(STEPS // 2), full, whole((8, D))],
            scratch_shapes=[pltpu.VMEM((TOKENS, D), F32)],
        ),
        compiler_params=params(48),
        cost_estimate=cost(3 * 2 * TOKENS * D * FF, 40 * MB),
        name="feed_back",
    )(row, h2, dg, act, upg, *downs, table, middle, cot)


def out_weight_kernel(t0, t1, t2, t3, bg, keep, send):
    grad = bg[...].reshape(TOKENS, D)
    for j, t in enumerate((t0, t1, t2, t3)):
        ref = (keep, send)[j % 2]
        ref[j // 2] = tn(t[...].reshape(TOKENS, HC), grad).astype(BF16)


def out_weight_grad(pieces, bg):
    return pl.pallas_call(
        out_weight_kernel,
        out_shape=[shape((2, HC, D))] * 2,
        grid=(1,),
        in_specs=[whole((FPD, PR, HC))] * 4 + [whole((FPD, PR, D))],
        out_specs=[whole((2, HC, D))] * 2,
        compiler_params=params(24),
        cost_estimate=cost(2 * TOKENS * D * D, 4 * MB),
        name="out_weight_grad",
    )(*pieces, bg)


ROWS = 2 * D + HC
BLOCKS = ROWS // HC


def core_sum_kernel(ua, ub, da, db, oa, ob, out):
    i = pl.program_id(1)
    for low, high, a, b in ((0, 4, ua, ub), (4, 8, da, db), (8, 9, oa, ob)):

        @pl.when((i >= low) & (i < high))
        def _():
            out[0] = (a[0].astype(F32) + b[0].astype(F32)).astype(BF16)


def core_sum(up, down, out):
    def spec(low, count):
        return pl.BlockSpec((1, HC, D), lambda j, i: (j, jnp.clip(i - low, 0, count - 1), 0))

    up = [u.reshape(2, D, D) for u in up]
    return pl.pallas_call(
        core_sum_kernel,
        out_shape=shape((2, ROWS, D)),
        grid=(2, BLOCKS),
        in_specs=[spec(0, 4)] * 2 + [spec(4, 4)] * 2 + [spec(8, 1)] * 2,
        out_specs=pl.BlockSpec((1, HC, D), lambda j, i: (j, i, 0)),
        compiler_params=pltpu.CompilerParams(
            dimension_semantics=("arbitrary", "arbitrary"), vmem_limit_bytes=24 * MB
        ),
        cost_estimate=cost(2 * ROWS * D, 28 * MB),
        name="core_sum",
    )(*up, *down, *out)


def unpack_kernel(total, up, down, out):
    i = pl.program_id(0)
    value = total[...].astype(F32)
    for low, high, ref in ((0, 4, up), (4, 8, down), (8, 9, out)):

        @pl.when((i >= low) & (i < high))
        def _():
            ref[...] = value


def unpack(total):
    return pl.pallas_call(
        unpack_kernel,
        out_shape=[shape((HC, FF), F32), shape((D, D), F32), shape((HC, D), F32)],
        grid=(BLOCKS,),
        in_specs=[pl.BlockSpec((HC, D), lambda i: (i, 0))],
        out_specs=[
            pl.BlockSpec((HC, D), lambda i: (0, jnp.clip(i, 0, 3))),
            pl.BlockSpec((HC, D), lambda i: (jnp.clip(i - 4, 0, 3), 0)),
            pl.BlockSpec((HC, D), lambda i: (0, 0)),
        ],
        compiler_params=params(24),
        cost_estimate=cost(0, 14 * MB),
        name="unpack",
    )(total)


def project_back_kernel(row_ref, dq, dk, dv, rk, rv, w0, w1, w2, w3, cp, sp, fr, dp, h0, h2, hs, bsum):
    row = row_ref[0]
    f = pl.program_id(0)
    later = (f > 0).astype(F32)
    keys = dk[0] + later * rk[0].astype(F32)
    values = dv[0] + later * rv[0].astype(F32)
    cosine, sine = cosines(cp, sp, fr, f)
    dp[0, :, :HC] = dq[0]
    dp[0, :, HC : 2 * HC] = turn(keys, cosine, -sine).astype(BF16)
    dp[0, :, 2 * HC :] = values.astype(BF16)
    grad = dp[0]
    sums = jnp.sum(grad.astype(F32), axis=0, keepdims=True)

    @pl.when(f == 0)
    def _():
        bsum[...] = jnp.zeros_like(bsum)

    number = lax.broadcasted_iota(jnp.int32, (8, 2 * HC), 0)
    bsum[...] = bsum[...] + jnp.where(number == row, sums[:, : 2 * HC], 0.0)
    bsum[:, :HC] = bsum[:, :HC] + jnp.where(number[:, :HC] == row + 4, sums[:, 2 * HC :], 0.0)
    for j, w in enumerate((w0, w1, w2, w3)):
        part = nt(grad, w[...]).astype(BF16)
        at = (0, slice(None), columns(row, j))
        h0[at] = part[:PR]
        hs[(0,) + at] = part[PR : 2 * PR]
        h2[at] = part[2 * PR : 3 * PR]
        hs[(1,) + at] = part[3 * PR :]


def project_back(row, dq, dk, dv, rk, rv, weights, tables):
    block = pl.BlockSpec((1, TOK, HC), lambda f, *_: (f, 0, 0))
    late = pl.BlockSpec((1, TOK, HC), lambda f, *_: (jnp.maximum(f - 1, 0), 0, 0))
    piece = pl.BlockSpec((1, PR, D), lambda f, *_: (f, 0, 0))
    return pl.pallas_call(
        project_back_kernel,
        out_shape=[
            shape((FPD, TOK, 3 * HC)),
            shape((FPD, PR, D)),
            shape((FPD, PR, D)),
            shape((2, FPD, PR, D)),
            shape((8, 2 * HC), F32),
        ],
        grid_spec=pltpu.PrefetchScalarGridSpec(
            num_scalar_prefetch=1,
            grid=(FPD,),
            in_specs=[block] * 3
            + [late] * 2
            + [whole((HC, 3 * HC))] * 4
            + [whole((TOK, HC)), whole((TOK, HC)), whole((16, 2 * HC))],
            out_specs=[
                pl.BlockSpec((1, TOK, 3 * HC), lambda f, *_: (f, 0, 0)),
                piece,
                piece,
                pl.BlockSpec((2, 1, PR, D), lambda f, *_: (0, f, 0, 0)),
                whole((8, 2 * HC)),
            ],
        ),
        compiler_params=params(32),
        cost_estimate=cost(2 * FPD * TOK * D * 3 * HC, 14 * MB),
        name="project_back",
    )(row, dq, dk, dv, rk, rv, *weights, *tables)


def weight_kernel(row_ref, h, dp, w):
    w[0] = tn(h[...], dp[...]).astype(BF16)


def project_weight(row, hidden, dproj):
    tokens = FPD * TOK
    return pl.pallas_call(
        weight_kernel,
        out_shape=shape((4, HC, 3 * HC)),
        grid_spec=pltpu.PrefetchScalarGridSpec(
            num_scalar_prefetch=1,
            grid=(4,),
            in_specs=[
                pl.BlockSpec((tokens, HC), lambda j, row: (0, row[0] ^ j)),
                whole((tokens, 3 * HC)),
            ],
            out_specs=pl.BlockSpec((1, HC, 3 * HC), lambda j, row: (j, 0, 0)),
        ),
        compiler_params=params(32),
        cost_estimate=cost(2 * tokens * D * 3 * HC, 9 * MB),
        name="project_weight",
    )(row, hidden.reshape(tokens, D), dproj.reshape(tokens, 3 * HC))


def input_back_kernel(x, h0, near, far, table, mg, bsum, out, sums):
    grad = h0[...].astype(F32) + near[0].astype(F32) + far[...].astype(F32)
    normal, rate = norm(x[...].astype(F32))
    put_half(sums, 0, jnp.sum(grad, axis=1))
    put_half(sums, D, jnp.sum(grad * normal, axis=1))
    sums[:, 2 * D :] = bsum[...]
    out[...] = mg[...] + norm_back(normal, rate, grad * (1.0 + segment(table, 1)))


LATE = 2 * D + 2 * HC
EARLY = 4 * D + NB + 256


def input_back(x, h0, near, far, table, mg, bsum):
    return pl.pallas_call(
        input_back_kernel,
        out_shape=[shape((FPD, PR, D), F32), shape((8, LATE), F32)],
        grid=(FPD // HALF,),
        in_specs=[half_spec(D)] * 2
        + [pl.BlockSpec((1, HALF, PR, D), lambda i: (0, i, 0, 0))]
        + [half_spec(D), whole((FPD, WIDE)), half_spec(D), whole((8, 2 * HC))],
        out_specs=[half_spec(D), whole((8, LATE))],
        compiler_params=params(32),
        cost_estimate=cost(20 * 512 * D, 10 * MB),
        name="input_back",
    )(x, h0, near, far, table, mg, bsum)


def early_kernel(m, g, u, d, out):
    out[:, : 3 * D] = m[:, : 3 * D]
    out[:, 3 * D : 4 * D] = g[...]
    out[:, 4 * D : 4 * D + NB] = u[...]
    out[:, 4 * D + NB : 4 * D + NB + 128] = d[...]
    out[:, 4 * D + NB + 128 :] = m[:, 3 * D :]


def early_sums(sums, gate, usum, dsum):
    return pl.pallas_call(
        early_kernel,
        out_shape=shape((8, EARLY), F32),
        grid=(1,),
        in_specs=[whole(a.shape) for a in (sums, gate, usum, dsum)],
        out_specs=whole((8, EARLY)),
        cost_estimate=cost(0, MB),
        name="early_sums",
    )(sums, gate, usum, dsum)


def final_kernel(row_ref, *refs):
    row = row_ref[0]
    late, early, silu = refs[:4], refs[4:8], refs[8:12]
    ada, ab, qb, ob, ub, db, asum = refs[12:]

    def rows(ref, cols):
        value = ref[:, :, cols].astype(F32)
        return value.reshape(64, value.shape[-1])

    left = [rows(s, slice(None)).astype(BF16) for s in silu]
    for segment in range(6):
        source, start = (late, segment) if segment < 2 else (early, segment - 2)
        cols = slice(start * D, (start + 1) * D)
        product, total = 0.0, 0.0
        for s, ref in zip(left, source):
            right = rows(ref, cols)
            total = total + jnp.sum(right, axis=0, keepdims=True)
            product = product + tn(s, right.astype(BF16))
        at = segment * D
        ada[:, at : at + D] = product
        asum[0:1, at : at + D] = total

    def bias(source, start, stop):
        return sum(
            jnp.sum(ref[:, :, start:stop].astype(F32), axis=0) for ref in source
        )

    ab[...] = asum[0:1, pl.ds(pl.multiple_of(row * 1536, 512), 1536)]
    folded = bias(late, 2 * D, LATE)
    for i in range(3):
        chunk = 3 * row + i
        at = jnp.where(chunk < 4, chunk, chunk - 4)
        second = (chunk >= 4) & (chunk < 8)
        value = jnp.where(second, folded[:, HC:], folded[:, :HC])
        qb[:, i * HC : (i + 1) * HC] = take(value, at)
    folded = bias(early, 4 * D, EARLY)
    for i in range(2):
        at = 2 * row + i
        ub[:, i * NB : (i + 1) * NB] = take(folded[:, :NB], at)
        db[:, i * 128 : (i + 1) * 128] = take(folded[:, NB : NB + 128], at)
        ob[:, i * 128 : (i + 1) * 128] = take(folded[:, NB + 128 :], at)


def final_sums(row, late, early, silu):
    sizes = (1536, 768, 256, 1024, 256)
    return pl.pallas_call(
        final_kernel,
        out_shape=[shape((HC, 6 * D), F32)] + [shape((1, n), F32) for n in sizes],
        grid_spec=pltpu.PrefetchScalarGridSpec(
            num_scalar_prefetch=1,
            grid=(1,),
            in_specs=[whole((8, 8, LATE))] * 4
            + [whole((8, 8, EARLY))] * 4
            + [whole((8, 8, HC))] * 4,
            out_specs=[whole((HC, 6 * D))] + [whole((1, n)) for n in sizes],
            scratch_shapes=[pltpu.VMEM((8, 6 * D), F32)],
        ),
        compiler_params=params(44),
        cost_estimate=cost(2 * 256 * HC * 6 * D, 10 * MB),
        name="final_sums",
    )(row, *late, *early, *silu)


def row_sum(value):
    value = value + swap(value, CORE)
    return value + swap(value, DIRECT)


def row_pieces(value):
    return [value, swap(value, CORE), swap(value, DIRECT), swap(value, DIRECT ^ CORE)]


def seq_gather(value):
    value = jnp.stack([value, swap(value, FAR)])
    value = jnp.concatenate([value] + [swap(value, m) for m in (16, 32, 48)])
    return [value] + [swap(value, m) for m in (4, 8, 12)]


def by_row(pieces, row):
    a, b, c, d = pieces
    odd, high = row % 2 == 1, row >= 2
    a, b = jnp.where(odd, b, a), jnp.where(odd, a, b)
    c, d = jnp.where(odd, d, c), jnp.where(odd, c, d)
    return jnp.stack(
        [
            jnp.where(high, c, a),
            jnp.where(high, d, b),
            jnp.where(high, a, c),
            jnp.where(high, b, d),
        ]
    )


def turn_heads(pieces):
    return [pieces[0]] + [
        swap(piece, mask) for piece, mask in zip(pieces[1:], (CORE, DIRECT, DIRECT ^ CORE))
    ]


def per_device(
    activations,
    noise_embed,
    frame_position,
    cotangent,
    ada_weight,
    ada_bias,
    qkv_weight,
    qkv_bias,
    out_weight,
    out_bias,
    up_weight,
    up_bias,
    down_weight,
    down_bias,
):
    row = lax.axis_index(("xl", "c")).astype(jnp.int32)
    row_arg = row.reshape(1)

    x0 = activations
    x2 = swap(x0, DIRECT)
    x1 = swap(x0, CORE)
    x3 = swap(x2, CORE)
    p0 = after(shift(activations[1:], 1), x2)
    p2 = swap(p0, DIRECT)
    p1 = swap(p0, CORE)
    p3 = swap(p2, CORE)

    biases = (ada_bias, qkv_bias, out_bias, up_bias, down_bias)
    part, silu_own, *tables = prepare(row_arg, frame_position, noise_embed, ada_weight, biases)
    table = row_sum(part)
    before_mods = shift(table[:, : 2 * D], 1)
    heads = split_heads(row_arg, qkv_weight)
    qkv_pieces = [heads[0], swap(heads[1], CORE), swap(heads[2], OTHER), swap(heads[3], OTHER ^ CORE)]

    out_own = after(out_weight, qkv_pieces[3])
    up_own = after(up_weight, qkv_pieces[3])
    down_own = after(down_weight, p2)
    outs2 = swap(out_own, OTHER)
    ups2 = swap(up_own, OTHER)
    downs2 = swap(down_own, DIRECT)
    outs = [out_weight, swap(out_own, CORE), outs2, swap(outs2, CORE)]
    ups = [up_weight, swap(up_own, CORE), ups2, swap(ups2, CORE)]
    downs = [down_weight, swap(down_own, CORE), downs2, swap(downs2, CORE)]

    hidden1, q, k, v = project(True, row_arg, (x0, x1, x2, x3), table, table, qkv_pieces, tables)
    kp, vp = project(
        False, row_arg, (p0, p1, p2, p3), table, before_mods, qkv_pieces, tables
    )
    *mixed, lse = attend(frame_position, q, k, v, kp, vp)
    turned = turn_heads(mixed)
    branch, middle, hidden2, down_grad, dsum = mid(turned, outs, table, x0, cotangent)
    h2 = hidden2.reshape(TOKENS, D)
    dg = down_grad.reshape(TOKENS, D)
    act, upg, hg, usum = feed(row_arg, h2, dg, ups, table, downs)
    mg, bg, *ag, sums = mid_back(hg.reshape(FPD, PR, D), middle, branch, cotangent, table, outs)
    back = turn_heads(ag)

    uk, us, dk_part, ds_part, layer_output, gate = feed_back(
        row_arg, h2, dg, act, upg, downs, table, middle, cotangent
    )
    ok, os = out_weight_grad(turned, bg)
    back = list(lax.optimization_barrier(tuple(back) + (gate, ok))[:4])
    dq_before, dkp, dvp = attend_back(False, frame_position, q, kp, vp, back, mixed, lse)
    rk, rv = shift(dkp, -1), shift(dvp, -1)
    packed = core_sum(
        (uk, swap(us, CORE)), (dk_part, swap(ds_part, CORE)), (ok, swap(os, CORE))
    )
    dq_before = after(dq_before, packed)
    scattered = lax.psum_scatter(packed, ("z", "y"), scatter_dimension=1, tiled=True)
    dq, dk, dv = attend_back(
        True, frame_position, q, k, v, back, mixed, lse, tables, dq_before
    )
    share = scattered[0].astype(F32) + swap(scattered[1], DIRECT).astype(F32)
    share = (share + swap(share.astype(BF16), FAR).astype(F32)).astype(BF16)
    totals = lax.all_gather(share, ("z", "y"), axis=0, tiled=True)
    up_total, down_total, out_total = unpack(totals)

    early = row_sum(early_sums(sums, gate, usum, dsum))
    early_all = seq_gather(early.astype(BF16))
    silu_all = seq_gather(silu_own)

    dproj, h0, h2_part, send, bsum = project_back(row_arg, dq, dk, dv, rk, rv, qkv_pieces, tables)
    near = swap(send, CORE)
    far = swap((h2_part.astype(F32) + near[1].astype(F32)).astype(BF16), DIRECT)
    qkv_parts = project_weight(row_arg, hidden1, dproj)
    input_grad, late = input_back(x0, h0, near, far, table, mg, bsum)
    late = row_sum(late)
    late_all = seq_gather(late.astype(BF16))

    qkv_parts = lax.psum_scatter(qkv_parts, ("z", "y"), scatter_dimension=1, tiled=True)
    qkv_parts = (qkv_parts.astype(F32) + swap(qkv_parts, FAR).astype(F32)).astype(BF16)
    qkv_turned = turn_heads([qkv_parts[j] for j in range(4)])
    qkv_share = by_row(qkv_turned, row).reshape(4, 16, 3, HC).transpose(1, 2, 0, 3)
    qkv_total = lax.all_gather(
        qkv_share.reshape(16, 3 * D), ("z", "y"), axis=0, tiled=True
    ).astype(F32)

    ada_total, *bias_sums = final_sums(row_arg, late_all, early_all, silu_all)
    ada_sum, qkv_sum, out_sum, up_sum, down_sum = [b[0] for b in bias_sums]
    mod_own = jnp.concatenate([late[:, : 2 * D], early[:, : 4 * D]], axis=1).astype(BF16)
    silu_grad = nt(mod_own, ada_weight)
    silu_grad = by_row(row_pieces(silu_grad), row).transpose(1, 0, 2).reshape(FPD, D)
    embed = noise_embed.astype(F32)
    sigma = jax.nn.sigmoid(embed)
    embed_grad = silu_grad * (sigma * (1.0 + embed * (1.0 - sigma)))

    return (
        layer_output,
        input_grad,
        embed_grad,
        ada_total,
        ada_sum,
        qkv_total,
        qkv_sum,
        out_total,
        out_sum,
        up_total,
        up_sum,
        down_total,
        down_sum,
    )


def solution(mesh):
    fine = Mesh(mesh.devices.reshape(2, 4, 4, 2, 2), AXES)
    seq, row = ("xh", "z", "y"), ("xl", "c")
    token, weight, vector = P(seq, row, None), P(row, None), P(row)
    in_specs = (token, P(seq, None), P(seq), token) + (weight, vector) * 5
    out_specs = (token, token, P(seq, None)) + (weight, vector) * 5
    return jax.shard_map(
        per_device, mesh=fine, in_specs=in_specs, out_specs=out_specs, check_vma=False
    )
```

```python
import math

import jax
import jax.numpy as jnp
from jax import lax
from jax.experimental import pallas as pl
from jax.experimental.pallas import tpu as pltpu
from jax.sharding import Mesh, PartitionSpec as P

F32 = jnp.float32
BF16 = jnp.bfloat16
HD = 64
GRID = 16
FPD = 8
PR = 64
D = 1024
FF = 4096
HC = 256
TOK = 256
PREV = 7
AXES = ("xh", "z", "y", "xl", "c")
CORE, DIRECT, OTHER, FAR = 1, 2, 66, 64
MB = 1024 * 1024


def swap(value, mask):
    return lax.ppermute(value, AXES, [(i, i ^ mask) for i in range(128)])


def shift(value, steps):
    first, last = max(0, -4 * steps), min(128, 128 - 4 * steps)
    return lax.ppermute(value, AXES, [(i, i + 4 * steps) for i in range(first, last)])


def after(value, *others):
    return lax.optimization_barrier((value,) + others)[0]


def nt(left, right):
    return lax.dot_general(left, right, (((1,), (1,)), ((), ())), preferred_element_type=F32)


def tn(left, right):
    return lax.dot_general(left, right, (((0,), (0,)), ((), ())), preferred_element_type=F32)


def nn(left, right):
    return jnp.dot(left, right, preferred_element_type=F32)


def norm(values):
    center = values - jnp.mean(values, axis=-1, keepdims=True)
    spread = jnp.mean(center * center, axis=-1, keepdims=True)
    rate = lax.rsqrt(spread + 1e-06)
    return center * rate, rate


def norm_back(normal, rate, grad):
    mean_grad = jnp.mean(grad, axis=-1, keepdims=True)
    mean_both = jnp.mean(grad * normal, axis=-1, keepdims=True)
    return rate * (grad - mean_grad - normal * mean_both)


def turn(values, cosine, sine):
    lanes = lax.broadcasted_iota(jnp.int32, values.shape, 1)
    other = jnp.where(
        lanes % HD < HD // 2, pltpu.roll(values, HC - HD // 2, 1), pltpu.roll(values, HD // 2, 1)
    )
    return values * cosine + other * sine


def params(mib):
    del mib
    return pltpu.CompilerParams(vmem_limit_bytes=58 * MB)


def cost(flops, moved, exps=0):
    return pl.CostEstimate(flops=int(flops), bytes_accessed=int(moved), transcendentals=int(exps))


def whole(shape):
    return pl.BlockSpec(shape, lambda i, *_: (0,) * len(shape))


def columns(row, j):
    return pl.ds(pl.multiple_of((row ^ j) * HC, HC), HC)


def shape(dims, kind=BF16):
    return jax.ShapeDtypeStruct(dims, kind)


UB, QB, OB, DB, WIDE = 6144, 6656, 7168, 7296, 7424


def put(ref, start, at, value):
    cols = slice(start, start + value.shape[1])
    number = lax.broadcasted_iota(jnp.int32, (8, value.shape[1]), 0)
    ref[:, cols] = jnp.where(number == at, value, ref[:, cols])


def take(value, at):
    number = lax.broadcasted_iota(jnp.int32, value.shape, 0)
    return jnp.sum(jnp.where(number == at, value, 0.0), axis=0, keepdims=True)


def put_half(ref, start, value):
    cols = slice(start, start + value.shape[1])
    number = lax.broadcasted_iota(jnp.int32, (8, value.shape[1]), 0)
    both = jnp.concatenate([value, value], axis=0)
    ref[:, cols] = jnp.where(number // 4 == pl.program_id(0), both, ref[:, cols])


def unfold(ref, start, width):
    return jnp.concatenate([ref[i : i + 1, start : start + width] for i in range(8)], axis=1)


def prepare_kernel(row_ref, pos_ref, noise, ada, ab, qb, ob, ub, db, pack, silu, cp, sp, frames):
    row = row_ref[0]
    embed = noise[...].astype(F32)
    value = (embed / (1.0 + jnp.exp(-embed))).astype(BF16)
    own = jnp.where(
        row < 2,
        jnp.where(row == 0, value[:, :HC], value[:, HC : 2 * HC]),
        jnp.where(row == 2, value[:, 2 * HC : 3 * HC], value[:, 3 * HC :]),
    )
    silu[...] = own
    pack[:, UB:] = jnp.zeros((FPD, WIDE - UB), F32)
    for segment in range(6):
        cols = slice(segment * D, (segment + 1) * D)
        pack[:, cols] = nn(own, ada[:, cols])
    bias = pl.ds(pl.multiple_of(row * 1536, 512), 1536)
    pack[:, bias] = pack[:, bias] + ab[...].astype(F32)
    for i in range(2):
        at = 2 * row + i
        put(pack, UB, at, ub[:, i * 512 : (i + 1) * 512].astype(F32))
        put(pack, OB, at, ob[:, i * 128 : (i + 1) * 128].astype(F32))
        put(pack, DB, at, db[:, i * 128 : (i + 1) * 128].astype(F32))
    for i in range(3):
        chunk = 3 * row + i
        at = jnp.where(chunk < 4, chunk, chunk - 4)
        second = (chunk >= 4) & (chunk < 8)
        value = qb[:, i * HC : (i + 1) * HC].astype(F32)
        put(pack, QB, jnp.where(second, -1, at), value)
        put(pack, QB + HC, jnp.where(second, at, -1), value)

    def parts(dims):
        lane = lax.broadcasted_iota(jnp.int32, dims, 1)
        index = lane % (HD // 2)
        quarter, eighth = HD // 4, HD // 8
        in_frame = index < quarter
        in_row = (index >= quarter) & (index < quarter + eighth)
        offset = jnp.where(
            in_frame, index, jnp.where(in_row, index - quarter, index - quarter - eighth)
        ).astype(F32)
        length = jnp.where(in_frame, 1.0 * quarter, 1.0 * eighth)
        frequency = jnp.exp(-math.log(10000.0) * offset / length)
        sign = jnp.where(lane % HD < HD // 2, -1.0, 1.0)
        return in_frame, in_row, frequency, sign

    in_frame, in_row, frequency, sign = parts((TOK, HC))
    slot = lax.broadcasted_iota(jnp.int32, (TOK, HC), 0)
    patch = ((slot // PR) ^ row) * PR + slot % PR
    angle = jnp.where(in_row, patch // GRID, patch % GRID).astype(F32) * frequency
    cp[...] = jnp.where(in_frame, 0.0, jnp.cos(angle))
    sp[...] = jnp.where(in_frame, 0.0, jnp.sin(angle) * sign)
    in_frame, _, frequency, sign = parts((16, HC))
    slot = lax.broadcasted_iota(jnp.int32, (16, HC), 0)
    place = pos_ref[0] - PREV + (slot - FPD)
    for f in range(FPD):
        place = jnp.where(slot == f, pos_ref[f], place)
    angle = place.astype(F32) * frequency
    frames[:, :HC] = jnp.where(in_frame, jnp.cos(angle), 0.0)
    frames[:, HC:] = jnp.where(in_frame, jnp.sin(angle) * sign, 0.0)


def prepare(row, places, noise, ada, biases):
    return pl.pallas_call(
        prepare_kernel,
        out_shape=[
            shape((FPD, WIDE), F32),
            shape((FPD, HC)),
            shape((TOK, HC), F32),
            shape((TOK, HC), F32),
            shape((16, 2 * HC), F32),
        ],
        grid_spec=pltpu.PrefetchScalarGridSpec(
            num_scalar_prefetch=2,
            grid=(1,),
            in_specs=[whole((FPD, D)), whole((HC, 6 * D))]
            + [whole((1, b.shape[0])) for b in biases],
            out_specs=[
                whole((FPD, WIDE)),
                whole((FPD, HC)),
                whole((TOK, HC)),
                whole((TOK, HC)),
                whole((16, 2 * HC)),
            ],
        ),
        compiler_params=params(32),
        cost_estimate=cost(2 * 8 * HC * 6 * D, 4 * MB, 4 * TOK * HC),
        name="prepare",
    )(row, places, noise, ada, *[b[None] for b in biases])


def split_heads_kernel(row_ref, q, k, v, p0, p1, p2, p3):
    for j, p in enumerate((p0, p1, p2, p3)):

        @pl.when(pl.program_id(0) == j)
        def _():
            p[:, :HC] = q[...]
            p[:, HC : 2 * HC] = k[...]
            p[:, 2 * HC :] = v[...]


def split_heads(row, weight):
    return pl.pallas_call(
        split_heads_kernel,
        out_shape=[shape((HC, 3 * HC))] * 4,
        grid_spec=pltpu.PrefetchScalarGridSpec(
            num_scalar_prefetch=1,
            grid=(4,),
            in_specs=[
                pl.BlockSpec((HC, HC), lambda j, row, s=s: (0, 4 * s + (row[0] ^ j)))
                for s in range(3)
            ],
            out_specs=[whole((HC, 3 * HC))] * 4,
        ),
        compiler_params=params(16),
        cost_estimate=cost(0, 3 * MB),
        name="split_heads",
    )(row, weight, weight, weight)


def cosines(cp, sp, frames, at):
    both = frames[pl.ds(at, 1), :]
    return cp[...] + both[:, :HC], sp[...] + both[:, HC:]


def project_kernel(own, row_ref, x0, x1, x2, x3, table, mods, w0, w1, w2, w3, cp, sp, fr, *outs):
    row = row_ref[0]
    f = pl.program_id(0)
    if own:
        h_ref, q_ref, k_ref, v_ref = outs
        first, at, angle = 0, f, f
    else:
        k_ref, v_ref, h_ref = outs
        first, at, angle = HC, f + FPD - PREV, f + FPD
    x = jnp.concatenate([r[0] for r in (x0, x1, x2, x3)], axis=0).astype(F32)
    normal, _ = norm(x)
    shift_row = mods[pl.ds(at, 1), :D]
    scale_row = mods[pl.ds(at, 1), D : 2 * D]
    hidden = (normal * (1.0 + scale_row) + shift_row).astype(BF16)
    where = (0,) if own else ()
    h_ref[where + (slice(None), slice(None))] = hidden
    low, high = table[pl.ds(row, 1), QB : QB + 2 * HC], table[pl.ds(row + 4, 1), QB : QB + HC]
    total = jnp.concatenate([low, high], axis=1)[:, first:]
    for j, w in enumerate((w0, w1, w2, w3)):
        total = total + nn(h_ref[where + (slice(None), columns(row, j))], w[:, first:])
    cosine, sine = cosines(cp, sp, fr, angle)
    if own:
        q_ref[0] = (turn(total[:, :HC], cosine, sine).astype(BF16).astype(F32) * 0.125).astype(BF16)
        total = total[:, HC:]
    k_ref[0] = turn(total[:, :HC], cosine, sine).astype(BF16)
    v_ref[0] = total[:, HC:].astype(BF16)


def project(own, row, xs, table, mods, weights, tables):
    frames = xs[0].shape[0]
    x_spec = pl.BlockSpec((1, PR, D), lambda f, *_: (f, 0, 0))
    out_spec = pl.BlockSpec((1, TOK, HC), lambda f, *_: (f, 0, 0))
    out = shape((frames, TOK, HC))
    if own:
        out_specs = [pl.BlockSpec((1, TOK, D), lambda f, *_: (f, 0, 0)), out_spec, out_spec, out_spec]
        out_shape = [shape((frames, TOK, D)), out, out, out]
        scratch = []
    else:
        out_specs = [out_spec, out_spec]
        out_shape = [out, out]
        scratch = [pltpu.VMEM((TOK, D), BF16)]
    return pl.pallas_call(
        lambda *refs: project_kernel(own, *refs),
        out_shape=out_shape,
        grid_spec=pltpu.PrefetchScalarGridSpec(
            num_scalar_prefetch=1,
            grid=(frames,),
            in_specs=[x_spec] * 4
            + [whole((FPD, WIDE)), whole(mods.shape)]
            + [whole((HC, 3 * HC))] * 4
            + [whole((TOK, HC)), whole((TOK, HC)), whole((16, 2 * HC))],
            out_specs=out_specs,
            scratch_shapes=scratch,
        ),
        compiler_params=params(32),
        cost_estimate=cost(2 * frames * TOK * D * 3 * HC, frames * TOK * D * 4 + 4 * MB),
        name="project_own" if own else "project_prev",
    )(row, *xs, table, mods, *weights, *tables)


def head_lanes():
    return lax.broadcasted_iota(jnp.int32, (TOK, HC), 1) // HD


def attend_kernel(pos_ref, q, k, v, kp, vp, o0, o1, o2, o3, lse, qs, scores, acc, top, low):
    f = pl.program_id(0)
    place = pos_ref[f]
    lanes = head_lanes()
    query = q[0]
    for h in range(4):
        qs[pl.ds(h * TOK, TOK), :] = jnp.where(lanes == h, query, jnp.zeros_like(query))
    top[...] = jnp.full_like(top, -1e30)
    low[...] = jnp.zeros_like(low)
    acc[...] = jnp.zeros_like(acc)
    before = jnp.maximum(place - f, 0)
    start = jnp.maximum(f - place, 0)

    def score(keys, slot):
        for h in range(4):
            rows = pl.ds(h * TOK, TOK)
            s = nt(qs[rows, :], keys)
            scores[slot, rows, :] = s
            top[rows, :] = jnp.maximum(top[rows, :], jnp.maximum(s[:, :128], s[:, 128:]))

    def mix(values, slot):
        for h in range(4):
            rows = pl.ds(h * TOK, TOK)
            p = jnp.exp(scores[slot, rows, :] - jnp.concatenate([top[rows, :]] * 2, axis=1))
            low[rows, :] = low[rows, :] + (p[:, :128] + p[:, 128:])
            acc[rows, :] = acc[rows, :] + nn(p.astype(BF16), values)

    def run(step):
        def prev(i, _):
            at = PREV - before + i
            step(kp[at] if step is score else vp[at], i)
            return 0

        def own(g, _):
            step(k[g] if step is score else v[g], g - f + place)
            return 0

        lax.fori_loop(0, before, prev, 0)
        lax.fori_loop(start, f + 1, own, 0)

    run(score)
    for h in range(4):
        rows = pl.ds(h * TOK, TOK)
        top[rows, :] = jnp.broadcast_to(jnp.max(top[rows, :], axis=1, keepdims=True), (TOK, 128))
    run(mix)
    result = jnp.zeros((TOK, HC), F32)
    logs = jnp.zeros((TOK, 128), F32)
    narrow = lax.broadcasted_iota(jnp.int32, (TOK, 128), 1)
    for h in range(4):
        rows = pl.ds(h * TOK, TOK)
        total = jnp.sum(low[rows, :], axis=1, keepdims=True)
        result = jnp.where(lanes == h, acc[rows, :] / total, result)
        logs = jnp.where(narrow == h, top[rows, :] + jnp.log(total), logs)
    lse[0] = logs.T[:8]
    result = result.astype(BF16)
    for j, o in enumerate((o0, o1, o2, o3)):
        o[0] = result[j * PR : (j + 1) * PR]


def attend(places, q, k, v, kp, vp):
    block = pl.BlockSpec((1, TOK, HC), lambda f, *_: (f, 0, 0))
    piece = pl.BlockSpec((1, PR, HC), lambda f, *_: (f, 0, 0))
    return pl.pallas_call(
        attend_kernel,
        out_shape=[jax.ShapeDtypeStruct((FPD, PR, HC), BF16)] * 4
        + [jax.ShapeDtypeStruct((FPD, 8, TOK), F32)],
        grid_spec=pltpu.PrefetchScalarGridSpec(
            num_scalar_prefetch=1,
            grid=(FPD,),
            in_specs=[block]
            + [whole((FPD, TOK, HC))] * 2
            + [whole((PREV, TOK, HC))] * 2,
            out_specs=[piece] * 4 + [pl.BlockSpec((1, 8, TOK), lambda f, *_: (f, 0, 0))],
            scratch_shapes=[
                pltpu.VMEM((4 * TOK, HC), BF16),
                pltpu.VMEM((8, 4 * TOK, TOK), F32),
                pltpu.VMEM((4 * TOK, HC), F32),
                pltpu.VMEM((4 * TOK, 128), F32),
                pltpu.VMEM((4 * TOK, 128), F32),
            ],
        ),
        compiler_params=params(40),
        cost_estimate=cost(36 * 4 * 2 * 2 * TOK**3, 6 * MB, 36 * 4 * TOK * TOK),
        name="attend",
    )(places, q, k, v, kp, vp)


def attend_back_kernel(own, pos_ref, q, k, v, g0, g1, g2, g3, o0, o1, o2, o3, lse, *rest):
    if own:
        cp, sp, fr, before_ref, dq, dk, dv, qs, gs, ks, pl_scr, dl_scr, ds_scr, dq_acc = rest
        dk_acc, dv_acc = dk, dv
    else:
        dq, both_ref, qs, gs, ks, pl_scr, dl_scr, ds_scr, dq_acc, dk_acc, dv_acc = rest
    f = pl.program_id(0)
    place = pos_ref[f]
    lanes = head_lanes()

    @pl.when(f == 0)
    def _():
        for ref in (dk_acc, dv_acc):
            ref[...] = jnp.zeros_like(ref)

    def prelude():
        query = q[0]
        grad = jnp.concatenate([r[0] for r in (g0, g1, g2, g3)], axis=0)
        mixed = jnp.concatenate([r[0] for r in (o0, o1, o2, o3)], axis=0)
        for h in range(4):
            rows = pl.ds(h * TOK, TOK)
            qs[rows, :] = jnp.where(lanes == h, query, jnp.zeros_like(query))
            gs[rows, :] = jnp.where(lanes == h, grad, jnp.zeros_like(grad))
        both = grad.astype(F32) * mixed.astype(F32)
        pick = (
            lax.broadcasted_iota(jnp.int32, (8, HC), 1) // HD
            == lax.broadcasted_iota(jnp.int32, (8, HC), 0)
        ).astype(F32)
        return lax.dot_general(
            pick, both, (((1,), (1,)), ((), ())),
            preferred_element_type=F32, precision=lax.Precision.HIGHEST,
        )

    def step(delta, logs, at):
        keys, values = k[at], v[at]
        for h in range(4):
            rows = pl.ds(h * TOK, TOK)
            ks[rows, :] = jnp.where(lanes == h, keys, jnp.zeros_like(keys))
            p = jnp.exp(nt(keys, qs[rows, :]) - logs[h : h + 1])
            ds = (p * (nt(values, gs[rows, :]) - delta[h : h + 1])).astype(BF16)
            pl_scr[:, rows] = p.astype(BF16)
            dl_scr[:, rows] = ds
            ds_scr[rows, :] = ds
        dv_acc[at] = dv_acc[at] + nn(pl_scr[...], gs[...])
        dk_acc[at] = dk_acc[at] + nn(dl_scr[...], qs[...])
        dq_acc[...] = dq_acc[...] + tn(ds_scr[...], ks[...])

    def sweep(low, high):
        delta = prelude()
        logs = lse[0]
        dq_acc[...] = jnp.zeros_like(dq_acc)

        def one(at, _):
            step(delta, logs, at)
            return 0

        lax.fori_loop(low, high, one, 0)

    if own:
        sweep(jnp.maximum(f - place, 0), f + 1)
        cosine, sine = cosines(cp, sp, fr, f)
        dq[0] = turn((dq_acc[...] + before_ref[0]) * 0.125, cosine, -sine).astype(BF16)
    else:
        count = jnp.maximum(place - f, 0)

        @pl.when(count > 0)
        def _():
            sweep(PREV - count, PREV)
            dq[0] = dq_acc[...]

        @pl.when(count == 0)
        def _():
            dq[0] = jnp.zeros_like(dq_acc)

        @pl.when(f == FPD - 1)
        def _():
            both_ref[0] = dk_acc[...].astype(BF16)
            both_ref[1] = dv_acc[...].astype(BF16)


def attend_back(own, places, q, k, v, grads, mixed, lse, tables=None, before=None):
    block = pl.BlockSpec((1, TOK, HC), lambda f, *_: (f, 0, 0))
    piece = pl.BlockSpec((1, PR, HC), lambda f, *_: (f, 0, 0))
    count = FPD if own else PREV
    wide = pltpu.VMEM((4 * TOK, HC), BF16)
    tall = pltpu.VMEM((TOK, 4 * TOK), BF16)
    scratch = [wide, wide, wide, tall, tall, wide, pltpu.VMEM((TOK, HC), F32)]
    specs = []
    extra = ()
    if own:
        specs = [whole((TOK, HC)), whole((TOK, HC)), whole((16, 2 * HC)), block]
        extra = tuple(tables) + (before,)
    else:
        scratch += [pltpu.VMEM((PREV, TOK, HC), F32)] * 2
    return pl.pallas_call(
        lambda *refs: attend_back_kernel(own, *refs),
        out_shape=[shape((FPD, TOK, HC), BF16 if own else F32)]
        + ([shape((FPD, TOK, HC), F32)] * 2 if own else [shape((2, PREV, TOK, HC))]),
        grid_spec=pltpu.PrefetchScalarGridSpec(
            num_scalar_prefetch=1,
            grid=(FPD,),
            in_specs=[block]
            + [whole((count, TOK, HC))] * 2
            + [piece] * 8
            + [pl.BlockSpec((1, 8, TOK), lambda f, *_: (f, 0, 0))]
            + specs,
            out_specs=[block]
            + ([whole((FPD, TOK, HC))] * 2 if own else [whole((2, PREV, TOK, HC))]),
            scratch_shapes=scratch,
        ),
        compiler_params=params(40),
        cost_estimate=cost(1000 if own else 12 * 4 * 5 * 2 * TOK**3, 1000 if own else 12 * MB),
        name="attend_back_own" if own else "attend_back_prev",
    )(places, q, k, v, *grads, *mixed, lse, *extra)


HALF = 4
RAW = HALF * PR


def flat(ref):
    return ref[...].reshape(RAW, ref.shape[-1])


def frames_of(value):
    return value.reshape(HALF, PR, value.shape[-1])


def segment(table, s):
    both = table[:, s * D : (s + 1) * D]
    return jnp.where(pl.program_id(0) == 0, both[:HALF], both[HALF:])[:, None, :]


def fold(out, start, width, row):
    @pl.when(pl.program_id(0) == 0)
    def _():
        out[:, start : start + width] = jnp.zeros((8, width), F32)

    for i in range(8):
        at = (slice(i, i + 1), slice(start, start + width))
        out[at] = out[at] + row[:, i * width : (i + 1) * width]


def mid_kernel(o0, o1, o2, o3, w0, w1, w2, w3, table, x, cot, branch, middle, hidden, down, dsum):
    total = unfold(table, OB, 128)
    for o, w in zip((o0, o1, o2, o3), (w0, w1, w2, w3)):
        total = total + nn(flat(o), w[...])
    branched = frames_of(total)
    branch[...] = branched
    mid_value = x[...].astype(F32) + segment(table, 2) * branched
    middle[...] = mid_value
    normal, _ = norm(mid_value)
    hidden[...] = (normal * (1.0 + segment(table, 4)) + segment(table, 3)).astype(BF16)
    grad = (segment(table, 5) * cot[...].astype(F32)).astype(BF16)
    down[...] = grad
    fold(dsum, 0, 128, jnp.sum(grad.astype(F32).reshape(RAW, D), axis=0, keepdims=True))


def half_spec(width):
    return pl.BlockSpec((HALF, PR, width), lambda i, *_: (i, 0, 0))


def mid(pieces, weights, table, x, cot):
    return pl.pallas_call(
        mid_kernel,
        out_shape=[
            shape((FPD, PR, D), F32),
            shape((FPD, PR, D), F32),
            shape((FPD, PR, D)),
            shape((FPD, PR, D)),
            shape((8, 128), F32),
        ],
        grid=(FPD // HALF,),
        in_specs=[half_spec(HC)] * 4
        + [whole((HC, D))] * 4
        + [whole((FPD, WIDE)), half_spec(D), half_spec(D)],
        out_specs=[half_spec(D)] * 4 + [whole((8, 128))],
        compiler_params=params(40),
        cost_estimate=cost(2 * 512 * D * D, 12 * MB),
        name="mid",
    )(*pieces, *weights, table, x, cot)


def mid_back_kernel(hg, middle, branch, cot, table, w0, w1, w2, w3, mg, bg, a0, a1, a2, a3, sums):
    grad = hg[...]
    normal, rate = norm(middle[...])
    put_half(sums, D, jnp.sum(grad, axis=1))
    put_half(sums, 2 * D, jnp.sum(grad * normal, axis=1))
    total = cot[...].astype(F32) + norm_back(normal, rate, grad * (1.0 + segment(table, 4)))
    mg[...] = total
    put_half(sums, 0, jnp.sum(total * branch[...], axis=1))
    low = (segment(table, 2) * total).astype(BF16)
    bg[...] = low
    low = low.reshape(RAW, D)
    fold(sums, 3 * D, 128, jnp.sum(low.astype(F32), axis=0, keepdims=True))
    for a, w in zip((a0, a1, a2, a3), (w0, w1, w2, w3)):
        a[...] = frames_of(nt(low, w[...]).astype(BF16))


def mid_back(hg, middle, branch, cot, table, weights):
    return pl.pallas_call(
        mid_back_kernel,
        out_shape=[shape((FPD, PR, D), F32), shape((FPD, PR, D))]
        + [shape((FPD, PR, HC))] * 4
        + [shape((8, 3 * D + 128), F32)],
        grid=(FPD // HALF,),
        in_specs=[half_spec(D)] * 4
        + [whole((FPD, WIDE))]
        + [whole((HC, D))] * 4,
        out_specs=[half_spec(D)] * 2 + [half_spec(HC)] * 4 + [whole((8, 3 * D + 128))],
        compiler_params=params(40),
        cost_estimate=cost(2 * 512 * D * D, 12 * MB),
        name="mid_back",
    )(hg, middle, branch, cot, table, *weights)


NB = 512
STEPS = FF // NB
PER = D // NB
TOKENS = FPD * PR


def block_of(t):
    phase = t // PER
    return ((phase % 2) * 2) ^ (phase // 2)


def up_column(t, row):
    return (row ^ block_of(t)) * PER + t % PER


def down_row(t):
    return block_of(t) * PER + t % PER


def down_spec(j):
    phase = (0, 2, 1, 3)[j]
    return pl.BlockSpec((NB, D), lambda t, row: (jnp.clip(t - phase * PER, 0, PER - 1), 0))


def pick_down(d0, d1, d2, d3):
    phase = pl.program_id(0) // PER
    return jnp.where(
        phase < 2,
        jnp.where(phase == 0, d0[...], d2[...]),
        jnp.where(phase == 2, d1[...], d3[...]),
    )


def feed_kernel(row_ref, h2, dg, u0, u1, u2, u3, table, d0, d1, d2, d3, act, upg, hg, usum):
    row = row_ref[0]
    ups = (u0, u1, u2, u3)
    down = pick_down(d0, d1, d2, d3)
    at = pl.ds(up_column(pl.program_id(0), row), 1)
    u = table[at, UB : UB + NB]
    for j, w in enumerate(ups):
        u = u + nn(h2[:, columns(row, j)], w[...])
    rate = math.sqrt(2.0 / math.pi)
    square = u * u
    half = 0.5 + 0.5 * jnp.tanh(u * (rate + (rate * 0.044715) * square))
    active = u * half
    act[...] = active.astype(BF16)
    slope = half + active * (1.0 - half) * (2.0 * rate + (6.0 * rate * 0.044715) * square)
    grad = (nt(dg[...], down) * slope).astype(BF16)
    upg[...] = grad
    put(usum, 0, up_column(pl.program_id(0), row), jnp.sum(grad.astype(F32), axis=0, keepdims=True))

    @pl.when(pl.program_id(0) == 0)
    def _():
        hg[...] = jnp.zeros_like(hg)

    for j, w in enumerate(ups):
        hg[:, columns(row, j)] = hg[:, columns(row, j)] + nt(grad, w[...])


def feed(row, h2, dg, ups, table, downs):
    tok = whole((TOKENS, D))
    block = pl.BlockSpec((TOKENS, NB), lambda t, row: (0, t))
    return pl.pallas_call(
        feed_kernel,
        out_shape=[
            shape((TOKENS, FF)),
            shape((TOKENS, FF)),
            shape((TOKENS, D), F32),
            shape((8, NB), F32),
        ],
        grid_spec=pltpu.PrefetchScalarGridSpec(
            num_scalar_prefetch=1,
            grid=(STEPS,),
            in_specs=[tok, tok]
            + [pl.BlockSpec((HC, NB), lambda t, row: (0, up_column(t, row[0])))] * 4
            + [whole((FPD, WIDE))]
            + [down_spec(j) for j in range(4)],
            out_specs=[block, block, tok, whole((8, NB))],
        ),
        compiler_params=params(44),
        cost_estimate=cost(3 * 2 * TOKENS * D * FF, 30 * MB, TOKENS * FF),
        name="feed",
    )(row, h2, dg, *ups, table, *downs)


def down_weight_kernel(row_ref, dg, act, d0, d1, d2, d3, table, middle, cot, dk, ds, out, gate, dn):
    t = pl.program_id(0)
    down = pick_down(d0, d1, d2, d3)
    active = act[...]

    @pl.when(t == 0)
    def _():
        dn[...] = jnp.zeros_like(dn)

    dn[...] = dn[...] + nn(active, down)
    part = tn(active, dg[...]).astype(BF16)

    @pl.when(t < STEPS // 2)
    def _():
        dk[0] = part

    @pl.when(t >= STEPS // 2)
    def _():
        ds[0] = part

    @pl.when(t == STEPS - 1)
    def _():
        bias = unfold(table, DB, 128)
        for f in range(FPD):
            rows = slice(f * PR, (f + 1) * PR)
            value = dn[rows, :] + bias
            out[f] = (middle[f] + table[f : f + 1, 5 * D : 6 * D] * value).astype(BF16)
            gate[f : f + 1, :] = jnp.sum(cot[f].astype(F32) * value, axis=0, keepdims=True)


def down_weight_grad(row, dg, act, downs, table, middle, cot):
    tok = whole((TOKENS, D))
    full = whole((FPD, PR, D))
    block = pl.BlockSpec((TOKENS, NB), lambda t, row: (0, t))

    def down_out(first):
        def index(t, row):
            at = jnp.clip(t - first, 0, STEPS // 2 - 1)
            return (at // PER, at % PER, 0)

        return pl.BlockSpec((1, NB, D), index)

    return pl.pallas_call(
        down_weight_kernel,
        out_shape=[shape((2, D, D))] * 2 + [shape((FPD, PR, D)), shape((8, D), F32)],
        grid_spec=pltpu.PrefetchScalarGridSpec(
            num_scalar_prefetch=1,
            grid=(STEPS,),
            in_specs=[tok, block]
            + [down_spec(j) for j in range(4)]
            + [whole((FPD, WIDE)), full, full],
            out_specs=[down_out(0), down_out(STEPS // 2), full, whole((8, D))],
            scratch_shapes=[pltpu.VMEM((TOKENS, D), F32)],
        ),
        compiler_params=params(48),
        cost_estimate=cost(2 * 2 * TOKENS * D * FF, 24 * MB),
        name="down_weight_grad",
    )(row, dg, act, *downs, table, middle, cot)


def up_weight_kernel(row_ref, h2, upg, uk, us):
    row = row_ref[0]
    grad = upg[...]
    for j, ref in enumerate((uk, us, uk, us)):
        ref[j // 2, 0] = tn(h2[:, columns(row, j)], grad).astype(BF16)


def up_weight_grad(row, h2, upg):
    up_out = pl.BlockSpec(
        (2, 1, HC, NB),
        lambda t, row: (0, up_column(t, row[0]) // PER, 0, up_column(t, row[0]) % PER),
    )
    return pl.pallas_call(
        up_weight_kernel,
        out_shape=[shape((2, 4, HC, D))] * 2,
        grid_spec=pltpu.PrefetchScalarGridSpec(
            num_scalar_prefetch=1,
            grid=(STEPS,),
            in_specs=[whole((TOKENS, D)), pl.BlockSpec((TOKENS, NB), lambda t, row: (0, t))],
            out_specs=[up_out, up_out],
        ),
        compiler_params=params(48),
        cost_estimate=cost(2 * TOKENS * D * FF, 14 * MB),
        name="up_weight_grad",
    )(row, h2, upg)


def out_weight_kernel(t0, t1, t2, t3, bg, keep, send):
    grad = bg[...].reshape(TOKENS, D)
    for j, t in enumerate((t0, t1, t2, t3)):
        ref = (keep, send)[j % 2]
        ref[j // 2] = tn(t[...].reshape(TOKENS, HC), grad).astype(BF16)


def out_weight_grad(pieces, bg):
    return pl.pallas_call(
        out_weight_kernel,
        out_shape=[shape((2, HC, D))] * 2,
        grid=(1,),
        in_specs=[whole((FPD, PR, HC))] * 4 + [whole((FPD, PR, D))],
        out_specs=[whole((2, HC, D))] * 2,
        compiler_params=params(24),
        cost_estimate=cost(2 * TOKENS * D * D, 4 * MB),
        name="out_weight_grad",
    )(*pieces, bg)


CHUNKS = 16
UP_ROWS, OUT_ROWS, DOWN_ROWS = D // CHUNKS, HC // CHUNKS, D // CHUNKS
FIRST = UP_ROWS + OUT_ROWS
ROWS = FIRST + DOWN_ROWS


def core_sum_kernel(ua, ub, da, db, oa, ob, out):
    def both(a, b):
        return (a.astype(F32) + b.astype(F32)).astype(BF16)

    for i in range(4):
        out[0, i * OUT_ROWS : (i + 1) * OUT_ROWS] = both(ua[0, i], ub[0, i])
    out[0, UP_ROWS:FIRST] = both(oa[0], ob[0])
    out[0, FIRST:] = both(da[0], db[0])


def core_sum(up, down, out):
    ups = pl.BlockSpec((1, 4, OUT_ROWS, D), lambda j, c: (j, 0, c, 0))
    outs = pl.BlockSpec((1, OUT_ROWS, D), lambda j, c: (j, c, 0))
    downs = pl.BlockSpec((1, DOWN_ROWS, D), lambda j, c: (j, c, 0))
    return pl.pallas_call(
        core_sum_kernel,
        out_shape=shape((2, CHUNKS * ROWS, D)),
        grid=(2, CHUNKS),
        in_specs=[ups, ups, downs, downs, outs, outs],
        out_specs=pl.BlockSpec((1, ROWS, D), lambda j, c: (j, c, 0)),
        compiler_params=params(24),
        cost_estimate=cost(1000, 1000),
        name="core_sum",
    )(*up, *down, *out)


def piece_spec(m, rows):
    return pl.BlockSpec(
        (1, rows, D), lambda i, k, *_: (jnp.where(i == m, k, jnp.where(i < m, 0, 3)), 0, 0)
    )


def spread_kernel(index_ref, a0, a1, a2, a3, *outs):
    for m, a in enumerate((a0, a1, a2, a3)):

        @pl.when(pl.program_id(0) == m)
        def _():
            value = a[0].astype(F32)
            if len(outs) == 2:
                for i in range(4):
                    outs[0][:, i * D : (i + 1) * D] = value[i * OUT_ROWS : (i + 1) * OUT_ROWS]
                outs[1][...] = value[UP_ROWS:]
            else:
                outs[0][...] = value


def spread_first(index, pieces):
    def at(i, k, index):
        return ((index[1] ^ k) * 4 + (index[0] ^ i), 0)

    return pl.pallas_call(
        spread_kernel,
        out_shape=[shape((HC, FF), F32), shape((HC, D), F32)],
        grid_spec=pltpu.PrefetchScalarGridSpec(
            num_scalar_prefetch=1,
            grid=(4, 4),
            in_specs=[piece_spec(m, FIRST) for m in range(4)],
            out_specs=[pl.BlockSpec((OUT_ROWS, FF), at), pl.BlockSpec((OUT_ROWS, D), at)],
        ),
        compiler_params=params(24),
        cost_estimate=cost(0, 8 * MB),
        name="spread_up_out",
    )(index, *pieces)


def spread_second(index, pieces):
    def at(i, k, index):
        return ((index[1] ^ i) * 4 + (index[0] ^ k), 0)

    return pl.pallas_call(
        spread_kernel,
        out_shape=shape((D, D), F32),
        grid_spec=pltpu.PrefetchScalarGridSpec(
            num_scalar_prefetch=1,
            grid=(4, 4),
            in_specs=[piece_spec(m, DOWN_ROWS) for m in range(4)],
            out_specs=pl.BlockSpec((DOWN_ROWS, D), at),
        ),
        compiler_params=params(24),
        cost_estimate=cost(0, 6 * MB),
        name="spread_down",
    )(index, *pieces)


def place_kernel(axis, index_ref, a0, a1, a2, a3, out):
    for m, a in enumerate((a0, a1, a2, a3)):

        @pl.when(pl.program_id(0) == m)
        def _():
            out[...] = a[...].astype(out.dtype)


def place(index, axis, pieces, kind):
    rows, width = pieces[0].shape
    return pl.pallas_call(
        lambda *refs: place_kernel(axis, *refs),
        out_shape=shape((4 * rows, width), kind),
        grid_spec=pltpu.PrefetchScalarGridSpec(
            num_scalar_prefetch=1,
            grid=(4,),
            in_specs=[whole((rows, width))] * 4,
            out_specs=pl.BlockSpec((rows, width), lambda i, index: (index[axis] ^ i, 0)),
        ),
        compiler_params=params(24),
        cost_estimate=cost(0, 24 * rows * width),
        name="place",
    )(index, *pieces)


def arrange_kernel(row_ref, a0, a1, a2, a3, out):
    row = row_ref[0]
    for j, a in enumerate((a0, a1, a2, a3)):
        for s in range(3):
            lanes = pl.ds(pl.multiple_of(s * D + (row ^ j) * HC, HC), HC)
            out[:, lanes] = a[:, s * HC : (s + 1) * HC]


def arrange(row, pieces):
    rows = pieces[0].shape[0]
    return pl.pallas_call(
        arrange_kernel,
        out_shape=shape((rows, 3 * D)),
        grid_spec=pltpu.PrefetchScalarGridSpec(
            num_scalar_prefetch=1,
            grid=(1,),
            in_specs=[whole((rows, 3 * HC))] * 4,
            out_specs=whole((rows, 3 * D)),
        ),
        compiler_params=params(16),
        cost_estimate=cost(0, 8 * rows * D),
        name="arrange",
    )(row, *pieces)


def project_back_kernel(row_ref, dq, dk, dv, rk, rv, w0, w1, w2, w3, cp, sp, fr, dp, h0, h2, hs, bsum):
    row = row_ref[0]
    f = pl.program_id(0)
    later = (f > 0).astype(F32)
    keys = dk[0] + later * rk[0, 0].astype(F32)
    values = dv[0] + later * rv[0, 0].astype(F32)
    cosine, sine = cosines(cp, sp, fr, f)
    dp[0, :, :HC] = dq[0]
    dp[0, :, HC : 2 * HC] = turn(keys, cosine, -sine).astype(BF16)
    dp[0, :, 2 * HC :] = values.astype(BF16)
    grad = dp[0]
    sums = jnp.sum(grad.astype(F32), axis=0, keepdims=True)

    @pl.when(f == 0)
    def _():
        bsum[...] = jnp.zeros_like(bsum)

    number = lax.broadcasted_iota(jnp.int32, (8, 2 * HC), 0)
    bsum[...] = bsum[...] + jnp.where(number == row, sums[:, : 2 * HC], 0.0)
    bsum[:, :HC] = bsum[:, :HC] + jnp.where(number[:, :HC] == row + 4, sums[:, 2 * HC :], 0.0)
    for j, w in enumerate((w0, w1, w2, w3)):
        part = nt(grad, w[...]).astype(BF16)
        at = (0, slice(None), columns(row, j))
        h0[at] = part[:PR]
        hs[(0,) + at] = part[PR : 2 * PR]
        h2[at] = part[2 * PR : 3 * PR]
        hs[(1,) + at] = part[3 * PR :]


def project_back(row, dq, dk, dv, returned, weights, tables):
    block = pl.BlockSpec((1, TOK, HC), lambda f, *_: (f, 0, 0))
    late = [
        pl.BlockSpec((1, 1, TOK, HC), lambda f, *_, i=i: (i, jnp.maximum(f - 1, 0), 0, 0))
        for i in range(2)
    ]
    piece = pl.BlockSpec((1, PR, D), lambda f, *_: (f, 0, 0))
    return pl.pallas_call(
        project_back_kernel,
        out_shape=[
            shape((FPD, TOK, 3 * HC)),
            shape((FPD, PR, D)),
            shape((FPD, PR, D)),
            shape((2, FPD, PR, D)),
            shape((8, 2 * HC), F32),
        ],
        grid_spec=pltpu.PrefetchScalarGridSpec(
            num_scalar_prefetch=1,
            grid=(FPD,),
            in_specs=[block] * 3
            + late
            + [whole((HC, 3 * HC))] * 4
            + [whole((TOK, HC)), whole((TOK, HC)), whole((16, 2 * HC))],
            out_specs=[
                pl.BlockSpec((1, TOK, 3 * HC), lambda f, *_: (f, 0, 0)),
                piece,
                piece,
                pl.BlockSpec((2, 1, PR, D), lambda f, *_: (0, f, 0, 0)),
                whole((8, 2 * HC)),
            ],
        ),
        compiler_params=params(32),
        cost_estimate=cost(2 * FPD * TOK * D * 3 * HC, 14 * MB),
        name="project_back",
    )(row, dq, dk, dv, returned, returned, *weights, *tables)


def weight_kernel(row_ref, h, dp, w):
    w[0] = tn(h[...], dp[...]).astype(BF16)


def project_weight(row, hidden, dproj):
    tokens = FPD * TOK
    return pl.pallas_call(
        weight_kernel,
        out_shape=shape((4, HC, 3 * HC)),
        grid_spec=pltpu.PrefetchScalarGridSpec(
            num_scalar_prefetch=1,
            grid=(4,),
            in_specs=[
                pl.BlockSpec((tokens, HC), lambda j, row: (0, row[0] ^ j)),
                whole((tokens, 3 * HC)),
            ],
            out_specs=pl.BlockSpec((1, HC, 3 * HC), lambda j, row: (j, 0, 0)),
        ),
        compiler_params=params(32),
        cost_estimate=cost(2 * tokens * D * 3 * HC, 9 * MB),
        name="project_weight",
    )(row, hidden.reshape(tokens, D), dproj.reshape(tokens, 3 * HC))


def input_back_kernel(x, h0, near, far, table, mg, bsum, gate, out, sums):
    grad = h0[...].astype(F32) + near[0].astype(F32) + far[...].astype(F32)
    normal, rate = norm(x[...].astype(F32))
    put_half(sums, 0, jnp.sum(grad, axis=1))
    put_half(sums, D, jnp.sum(grad * normal, axis=1))
    sums[:, 2 * D : 3 * D] = gate[...]
    sums[:, 3 * D :] = bsum[...]
    out[...] = mg[...] + norm_back(normal, rate, grad * (1.0 + segment(table, 1)))


LATE = 3 * D + 2 * HC
EARLY = 3 * D + NB + 256


def input_back(x, h0, near, far, table, mg, bsum, gate):
    return pl.pallas_call(
        input_back_kernel,
        out_shape=[shape((FPD, PR, D), F32), shape((8, LATE), F32)],
        grid=(FPD // HALF,),
        in_specs=[half_spec(D)] * 2
        + [pl.BlockSpec((1, HALF, PR, D), lambda i: (0, i, 0, 0))]
        + [half_spec(D), whole((FPD, WIDE)), half_spec(D), whole((8, 2 * HC)), whole((8, D))],
        out_specs=[half_spec(D), whole((8, LATE))],
        compiler_params=params(32),
        cost_estimate=cost(20 * 512 * D, 10 * MB),
        name="input_back",
    )(x, h0, near, far, table, mg, bsum, gate)


def early_kernel(m, u, d, out):
    out[:, : 3 * D] = m[:, : 3 * D]
    out[:, 3 * D : 3 * D + NB] = u[...]
    out[:, 3 * D + NB : 3 * D + NB + 128] = d[...]
    out[:, 3 * D + NB + 128 :] = m[:, 3 * D :]


def early_sums(sums, usum, dsum):
    return pl.pallas_call(
        early_kernel,
        out_shape=shape((8, EARLY), F32),
        grid=(1,),
        in_specs=[whole(a.shape) for a in (sums, usum, dsum)],
        out_specs=whole((8, EARLY)),
        cost_estimate=cost(0, MB),
        name="early_sums",
    )(sums, usum, dsum)


def final_kernel(row_ref, *refs):
    row = row_ref[0]
    late, early = refs[:4], refs[4:8]
    ada, ab, qb, ob, ub, db, asum = refs[8:]

    def rows(ref, cols):
        value = ref[:, :, cols].astype(F32)
        return value.reshape(64, value.shape[-1])

    left = [rows(s, slice(EARLY, EARLY + HC)).astype(BF16) for s in early]
    for segment in range(6):
        source, start = ((late, 0), (late, 1), (early, 0), (early, 1), (early, 2), (late, 2))[segment]
        cols = slice(start * D, (start + 1) * D)
        product, total = 0.0, 0.0
        for s, ref in zip(left, source):
            right = rows(ref, cols)
            total = total + jnp.sum(right, axis=0, keepdims=True)
            product = product + tn(s, right.astype(BF16))
        at = segment * D
        ada[:, at : at + D] = product
        asum[0:1, at : at + D] = total

    def bias(source, start, stop):
        return sum(
            jnp.sum(ref[:, :, start:stop].astype(F32), axis=0) for ref in source
        )

    ab[...] = asum[0:1, pl.ds(pl.multiple_of(row * 1536, 512), 1536)]
    folded = bias(late, 3 * D, LATE)
    for i in range(3):
        chunk = 3 * row + i
        at = jnp.where(chunk < 4, chunk, chunk - 4)
        second = (chunk >= 4) & (chunk < 8)
        value = jnp.where(second, folded[:, HC:], folded[:, :HC])
        qb[:, i * HC : (i + 1) * HC] = take(value, at)
    folded = bias(early, 3 * D, EARLY)
    for i in range(2):
        at = 2 * row + i
        ub[:, i * NB : (i + 1) * NB] = take(folded[:, :NB], at)
        db[:, i * 128 : (i + 1) * 128] = take(folded[:, NB : NB + 128], at)
        ob[:, i * 128 : (i + 1) * 128] = take(folded[:, NB + 128 :], at)


def final_sums(row, late, early):
    sizes = (1536, 768, 256, 1024, 256)
    return pl.pallas_call(
        final_kernel,
        out_shape=[shape((HC, 6 * D), F32)] + [shape((1, n), F32) for n in sizes],
        grid_spec=pltpu.PrefetchScalarGridSpec(
            num_scalar_prefetch=1,
            grid=(1,),
            in_specs=[whole((8, 8, LATE))] * 4
            + [whole((8, 8, EARLY + HC))] * 4,
            out_specs=[whole((HC, 6 * D))] + [whole((1, n)) for n in sizes],
            scratch_shapes=[pltpu.VMEM((8, 6 * D), F32)],
        ),
        compiler_params=params(44),
        cost_estimate=cost(2 * 256 * HC * 6 * D, 10 * MB),
        name="final_sums",
    )(row, *late, *early)


def row_sum(value):
    value = value + swap(value, CORE)
    return value + swap(value, DIRECT)


def row_pieces(value):
    return [value, swap(value, CORE), swap(value, DIRECT), swap(value, DIRECT ^ CORE)]


def seq_gather(value):
    value = jnp.stack([value, swap(value, FAR)])
    value = jnp.concatenate([value] + [swap(value, m) for m in (16, 32, 48)])
    return [value] + [swap(value, m) for m in (4, 8, 12)]


def by_row(pieces, row):
    a, b, c, d = pieces
    odd, high = row % 2 == 1, row >= 2
    a, b = jnp.where(odd, b, a), jnp.where(odd, a, b)
    c, d = jnp.where(odd, d, c), jnp.where(odd, c, d)
    return jnp.stack(
        [
            jnp.where(high, c, a),
            jnp.where(high, d, b),
            jnp.where(high, a, c),
            jnp.where(high, b, d),
        ]
    )


def exchange_rows(value, bit, index, axis):
    rows = value.shape[1] // 4
    at = lambda m: lax.dynamic_slice_in_dim(value, (index[axis] ^ m) * rows, rows, 1)
    parts = [at(0)] + [swap(at(m), bit * m) for m in (1, 2, 3)]
    return sum(part.astype(F32) for part in parts).astype(BF16)


def turn_heads(pieces):
    return [pieces[0]] + [
        swap(piece, mask) for piece, mask in zip(pieces[1:], (CORE, DIRECT, DIRECT ^ CORE))
    ]


def per_device(
    activations,
    noise_embed,
    frame_position,
    cotangent,
    ada_weight,
    ada_bias,
    qkv_weight,
    qkv_bias,
    out_weight,
    out_bias,
    up_weight,
    up_bias,
    down_weight,
    down_bias,
):
    row = lax.axis_index(("xl", "c")).astype(jnp.int32)
    row_arg = row.reshape(1)
    index = [lax.axis_index("y").astype(jnp.int32), lax.axis_index("z").astype(jnp.int32)]
    index_arg = jnp.stack(index)

    x0 = activations
    x2 = swap(x0, DIRECT)
    x1 = swap(x0, CORE)
    p0 = shift(activations[1:], 1)
    biases = (ada_bias, qkv_bias, out_bias, up_bias, down_bias)
    part, silu_own, *tables = prepare(row_arg, frame_position, noise_embed, ada_weight, biases)
    heads = split_heads(row_arg, after(qkv_weight, silu_own))
    qkv_pieces = [heads[0], swap(heads[1], CORE), swap(heads[2], OTHER), swap(heads[3], OTHER ^ CORE)]
    part = part + swap(part, CORE)
    part = after(part, heads[0])
    table = part + swap(part, DIRECT)
    x2, p0, table, *qkv_pieces = lax.optimization_barrier((x2, p0, table, *qkv_pieces))

    x3 = swap(x2, CORE)
    p2 = swap(p0, DIRECT)
    p1 = swap(p0, CORE)
    before_mods = shift(table[:, : 2 * D], 1)

    out_own, up_own, _ = lax.optimization_barrier((out_weight, up_weight, table))
    outs2 = swap(out_own, OTHER)
    ups2 = swap(up_own, OTHER)

    hidden1, q, k, v = project(True, row_arg, (x0, x1, x2, x3), table, table, qkv_pieces, tables)
    p2, down_own, q = lax.optimization_barrier((p2, down_weight, q))
    p3 = swap(p2, CORE)
    downs2 = swap(down_own, DIRECT)
    kp, vp = project(
        False, row_arg, (p0, p1, p2, p3), table, before_mods, qkv_pieces, tables
    )
    *mixed, lse = attend(frame_position, q, k, v, kp, vp)
    outs2, ups2, downs2, lse = lax.optimization_barrier((outs2, ups2, downs2, lse))
    outs = [out_weight, swap(out_own, CORE), outs2, swap(outs2, CORE)]
    ups = [up_weight, swap(up_own, CORE), ups2, swap(ups2, CORE)]
    downs = [down_weight, swap(down_own, CORE), downs2, swap(downs2, CORE)]
    turned = turn_heads(mixed)
    branch, middle, hidden2, down_grad, dsum = mid(turned, outs, table, x0, cotangent)
    h2 = hidden2.reshape(TOKENS, D)
    dg = down_grad.reshape(TOKENS, D)
    act, upg, hg, usum = feed(row_arg, h2, dg, ups, table, downs)
    mg, bg, *ag, sums = mid_back(hg.reshape(FPD, PR, D), middle, branch, cotangent, table, outs)
    back = turn_heads(ag)

    early = early_sums(sums, usum, dsum)
    early = early + swap(early, CORE)
    dk_part, ds_part, layer_output, gate = down_weight_grad(
        row_arg, after(dg, bg), act, downs, table, middle, cotangent
    )
    upg, early, gate, *back = lax.optimization_barrier((upg, early, gate, *back))
    early = early + swap(early, DIRECT)
    uk, us = up_weight_grad(row_arg, h2, upg)
    ok, os = out_weight_grad(turned, bg)

    early = jnp.concatenate([early.astype(BF16), silu_own], axis=1)
    early, uk, ok, *back = lax.optimization_barrier((early, uk, ok, *back))
    dq_before, both = attend_back(False, frame_position, q, kp, vp, back, mixed, lse)
    returned = shift(both, -1)
    early = jnp.stack([early, swap(early, FAR)])
    uk, early, dq_before = lax.optimization_barrier((uk, early, dq_before))
    packed = core_sum(
        (uk, swap(us, CORE)), (dk_part, swap(ds_part, CORE)), (ok, swap(os, CORE))
    )
    early = jnp.concatenate([early] + [swap(early, m) for m in (16, 32, 48)])
    dq_before, packed, early = lax.optimization_barrier((dq_before, packed, early))
    scattered = lax.psum_scatter(packed, ("z", "y"), scatter_dimension=1, tiled=True)
    early_all = [early] + [swap(early, m) for m in (4, 8, 12)]
    dq, dk, dv = attend_back(
        True, frame_position, q, k, v, back, mixed, lse, tables, dq_before
    )
    dq, *early_all = lax.optimization_barrier((dq, *early_all))
    early = early_all[0][0].astype(F32)

    dproj, h0, h2_part, send, bsum = project_back(row_arg, dq, dk, dv, returned, qkv_pieces, tables)
    near = swap(send, CORE)
    far_part = (h2_part.astype(F32) + near[1].astype(F32)).astype(BF16)
    far = swap(far_part, DIRECT)
    qkv_parts = project_weight(row_arg, hidden1, dproj)
    input_grad, late = input_back(x0, h0, near, far, table, mg, bsum, gate)
    late = row_sum(late)
    late_all = seq_gather(late.astype(BF16))

    qkv_parts = after(qkv_parts, far_part)
    qkv_parts = exchange_rows(qkv_parts, 4, index, 0)
    qkv_parts = exchange_rows(qkv_parts, 16, index, 1)
    qkv_parts = (qkv_parts.astype(F32) + swap(qkv_parts, FAR).astype(F32)).astype(BF16)
    qkv_share = arrange(row_arg, turn_heads([qkv_parts[j] for j in range(4)]))
    qkv_share = place(
        index_arg, 1, [qkv_share] + [swap(qkv_share, 16 * m) for m in (1, 2, 3)], BF16
    )
    qkv_total = place(
        index_arg, 0, [qkv_share] + [swap(qkv_share, 4 * m) for m in (1, 2, 3)], F32
    )

    share = scattered[0].astype(F32) + swap(scattered[1], DIRECT).astype(F32)
    share = (share + swap(share.astype(BF16), FAR).astype(F32)).astype(BF16)
    one, two = share[:FIRST], share[FIRST:]
    one = jnp.stack([one] + [swap(one, 16 * m) for m in (1, 2, 3)])
    two = jnp.stack([two] + [swap(two, 4 * m) for m in (1, 2, 3)])
    up_total, out_total = spread_first(index_arg, [one] + [swap(one, 4 * m) for m in (1, 2, 3)])
    down_total = spread_second(index_arg, [two] + [swap(two, 16 * m) for m in (1, 2, 3)])

    ada_total, *bias_sums = final_sums(row_arg, late_all, early_all)
    ada_sum, qkv_sum, out_sum, up_sum, down_sum = [b[0] for b in bias_sums]
    mod_own = jnp.concatenate(
        [late[:, : 2 * D], early[:, : 3 * D], late[:, 2 * D : 3 * D]], axis=1
    ).astype(BF16)
    silu_grad = nt(mod_own, ada_weight)
    silu_grad = by_row(row_pieces(silu_grad), row).transpose(1, 0, 2).reshape(FPD, D)
    embed = noise_embed.astype(F32)
    sigma = jax.nn.sigmoid(embed)
    embed_grad = silu_grad * (sigma * (1.0 + embed * (1.0 - sigma)))

    return (
        layer_output,
        input_grad,
        embed_grad,
        ada_total,
        ada_sum,
        qkv_total,
        qkv_sum,
        out_total,
        out_sum,
        up_total,
        up_sum,
        down_total,
        down_sum,
    )


def solution(mesh):
    fine = Mesh(mesh.devices.reshape(2, 4, 4, 2, 2), AXES)
    seq, row = ("xh", "z", "y"), ("xl", "c")
    token, weight, vector = P(seq, row, None), P(row, None), P(row)
    in_specs = (token, P(seq, None), P(seq), token) + (weight, vector) * 5
    out_specs = (token, token, P(seq, None)) + (weight, vector) * 5
    return jax.shard_map(
        per_device, mesh=fine, in_specs=in_specs, out_specs=out_specs, check_vma=False
    )
```

```python
import math

import jax
import jax.numpy as jnp
from jax import lax
from jax.experimental import pallas as pl
from jax.experimental.pallas import tpu as pltpu
from jax.sharding import Mesh, PartitionSpec as P

F32 = jnp.float32
BF16 = jnp.bfloat16
HD = 64
GRID = 16
FPD = 8
PR = 64
D = 1024
FF = 4096
HC = 256
TOK = 256
PREV = 7
AXES = ("xh", "z", "y", "xl", "c")
CORE, DIRECT, OTHER, FAR = 1, 2, 66, 64
MB = 1024 * 1024


def swap(value, mask):
    return lax.ppermute(value, AXES, [(i, i ^ mask) for i in range(128)])


def shift(value, steps):
    return lax.ppermute(value, AXES, [(i, (i + 4 * steps) % 128) for i in range(128)])


def after(value, *others):
    return lax.optimization_barrier((value,) + others)[0]


def nt(left, right):
    return lax.dot_general(left, right, (((1,), (1,)), ((), ())), preferred_element_type=F32)


def tn(left, right):
    return lax.dot_general(left, right, (((0,), (0,)), ((), ())), preferred_element_type=F32)


def nn(left, right):
    return jnp.dot(left, right, preferred_element_type=F32)


def norm(values):
    center = values - jnp.mean(values, axis=-1, keepdims=True)
    spread = jnp.mean(center * center, axis=-1, keepdims=True)
    rate = lax.rsqrt(spread + 1e-06)
    return center * rate, rate


def norm_back(normal, rate, grad):
    mean_grad = jnp.mean(grad, axis=-1, keepdims=True)
    mean_both = jnp.mean(grad * normal, axis=-1, keepdims=True)
    return rate * (grad - mean_grad - normal * mean_both)


def turn(values, cosine, sine):
    lanes = lax.broadcasted_iota(jnp.int32, values.shape, 1)
    other = jnp.where(
        lanes % HD < HD // 2, pltpu.roll(values, HC - HD // 2, 1), pltpu.roll(values, HD // 2, 1)
    )
    return values * cosine + other * sine


def params(mib):
    return pltpu.CompilerParams(vmem_limit_bytes=mib * MB)


def cost(flops, moved, exps=0):
    return pl.CostEstimate(flops=int(flops), bytes_accessed=int(moved), transcendentals=int(exps))


def whole(shape):
    return pl.BlockSpec(shape, lambda i, *_: (0,) * len(shape))


def columns(row, j):
    return pl.ds(pl.multiple_of((row ^ j) * HC, HC), HC)


def shape(dims, kind=BF16):
    return jax.ShapeDtypeStruct(dims, kind)


UB, QB, OB, DB, WIDE = 6144, 6656, 7168, 7296, 7424


def put(ref, start, at, value):
    cols = slice(start, start + value.shape[1])
    number = lax.broadcasted_iota(jnp.int32, (8, value.shape[1]), 0)
    ref[:, cols] = jnp.where(number == at, value, ref[:, cols])


def take(value, at):
    number = lax.broadcasted_iota(jnp.int32, value.shape, 0)
    return jnp.sum(jnp.where(number == at, value, 0.0), axis=0, keepdims=True)


def put_half(ref, start, value):
    cols = slice(start, start + value.shape[1])
    number = lax.broadcasted_iota(jnp.int32, (8, value.shape[1]), 0)
    both = jnp.concatenate([value, value], axis=0)
    ref[:, cols] = jnp.where(number // 4 == pl.program_id(0), both, ref[:, cols])


def unfold(ref, start, width):
    return jnp.concatenate([ref[i : i + 1, start : start + width] for i in range(8)], axis=1)


def prepare_kernel(row_ref, pos_ref, noise, ada, ab, qb, ob, ub, db, pack, silu, cp, sp, frames):
    row = row_ref[0]
    embed = noise[...].astype(F32)
    value = (embed / (1.0 + jnp.exp(-embed))).astype(BF16)
    own = jnp.where(
        row < 2,
        jnp.where(row == 0, value[:, :HC], value[:, HC : 2 * HC]),
        jnp.where(row == 2, value[:, 2 * HC : 3 * HC], value[:, 3 * HC :]),
    )
    silu[...] = own
    pack[:, UB:] = jnp.zeros((FPD, WIDE - UB), F32)
    for segment in range(6):
        cols = slice(segment * D, (segment + 1) * D)
        pack[:, cols] = nn(own, ada[:, cols])
    bias = pl.ds(pl.multiple_of(row * 1536, 512), 1536)
    pack[:, bias] = pack[:, bias] + ab[...].astype(F32)
    for i in range(2):
        at = 2 * row + i
        put(pack, UB, at, ub[:, i * 512 : (i + 1) * 512].astype(F32))
        put(pack, OB, at, ob[:, i * 128 : (i + 1) * 128].astype(F32))
        put(pack, DB, at, db[:, i * 128 : (i + 1) * 128].astype(F32))
    for i in range(3):
        chunk = 3 * row + i
        at = jnp.where(chunk < 4, chunk, chunk - 4)
        second = (chunk >= 4) & (chunk < 8)
        value = qb[:, i * HC : (i + 1) * HC].astype(F32)
        put(pack, QB, jnp.where(second, -1, at), value)
        put(pack, QB + HC, jnp.where(second, at, -1), value)

    def parts(dims):
        lane = lax.broadcasted_iota(jnp.int32, dims, 1)
        index = lane % (HD // 2)
        quarter, eighth = HD // 4, HD // 8
        in_frame = index < quarter
        in_row = (index >= quarter) & (index < quarter + eighth)
        offset = jnp.where(
            in_frame, index, jnp.where(in_row, index - quarter, index - quarter - eighth)
        ).astype(F32)
        length = jnp.where(in_frame, 1.0 * quarter, 1.0 * eighth)
        frequency = jnp.exp(-math.log(10000.0) * offset / length)
        sign = jnp.where(lane % HD < HD // 2, -1.0, 1.0)
        return in_frame, in_row, frequency, sign

    in_frame, in_row, frequency, sign = parts((TOK, HC))
    slot = lax.broadcasted_iota(jnp.int32, (TOK, HC), 0)
    patch = ((slot // PR) ^ row) * PR + slot % PR
    angle = jnp.where(in_row, patch // GRID, patch % GRID).astype(F32) * frequency
    cp[...] = jnp.where(in_frame, 0.0, jnp.cos(angle))
    sp[...] = jnp.where(in_frame, 0.0, jnp.sin(angle) * sign)
    in_frame, _, frequency, sign = parts((16, HC))
    slot = lax.broadcasted_iota(jnp.int32, (16, HC), 0)
    place = pos_ref[0] - PREV + (slot - FPD)
    for f in range(FPD):
        place = jnp.where(slot == f, pos_ref[f], place)
    angle = place.astype(F32) * frequency
    frames[:, :HC] = jnp.where(in_frame, jnp.cos(angle), 0.0)
    frames[:, HC:] = jnp.where(in_frame, jnp.sin(angle) * sign, 0.0)


def prepare(row, places, noise, ada, biases):
    return pl.pallas_call(
        prepare_kernel,
        out_shape=[
            shape((FPD, WIDE), F32),
            shape((FPD, HC)),
            shape((TOK, HC), F32),
            shape((TOK, HC), F32),
            shape((16, 2 * HC), F32),
        ],
        grid_spec=pltpu.PrefetchScalarGridSpec(
            num_scalar_prefetch=2,
            grid=(1,),
            in_specs=[whole((FPD, D)), whole((HC, 6 * D))]
            + [whole((1, b.shape[0])) for b in biases],
            out_specs=[
                whole((FPD, WIDE)),
                whole((FPD, HC)),
                whole((TOK, HC)),
                whole((TOK, HC)),
                whole((16, 2 * HC)),
            ],
        ),
        compiler_params=params(24),
        cost_estimate=cost(2 * 8 * HC * 6 * D, 4 * MB, 4 * TOK * HC),
        name="prepare",
    )(row, places, noise, ada, *[b[None] for b in biases])


def split_heads_kernel(row_ref, q, k, v, p0, p1, p2, p3):
    for j, p in enumerate((p0, p1, p2, p3)):

        @pl.when(pl.program_id(0) == j)
        def _():
            p[:, :HC] = q[...]
            p[:, HC : 2 * HC] = k[...]
            p[:, 2 * HC :] = v[...]


def split_heads(row, weight):
    return pl.pallas_call(
        split_heads_kernel,
        out_shape=[shape((HC, 3 * HC))] * 4,
        grid_spec=pltpu.PrefetchScalarGridSpec(
            num_scalar_prefetch=1,
            grid=(4,),
            in_specs=[
                pl.BlockSpec((HC, HC), lambda j, row, s=s: (0, 4 * s + (row[0] ^ j)))
                for s in range(3)
            ],
            out_specs=[whole((HC, 3 * HC))] * 4,
        ),
        compiler_params=params(12),
        cost_estimate=cost(0, 3 * MB),
        name="split_heads",
    )(row, weight, weight, weight)


def cosines(cp, sp, frames, at):
    both = frames[pl.ds(at, 1), :]
    return cp[...] + both[:, :HC], sp[...] + both[:, HC:]


def project_kernel(own, row_ref, x0, x1, x2, x3, table, mods, w0, w1, w2, w3, cp, sp, fr, *outs):
    row = row_ref[0]
    f = pl.program_id(0)
    if own:
        h_ref, q_ref, k_ref, v_ref = outs
        first, at, angle = 0, f, f
    else:
        k_ref, v_ref, h_ref = outs
        first, at, angle = HC, f + FPD - PREV, f + FPD
    x = jnp.concatenate([r[0] for r in (x0, x1, x2, x3)], axis=0).astype(F32)
    normal, _ = norm(x)
    shift_row = mods[pl.ds(at, 1), :D]
    scale_row = mods[pl.ds(at, 1), D : 2 * D]
    hidden = (normal * (1.0 + scale_row) + shift_row).astype(BF16)
    where = (0,) if own else ()
    h_ref[where + (slice(None), slice(None))] = hidden
    low, high = table[pl.ds(row, 1), QB : QB + 2 * HC], table[pl.ds(row + 4, 1), QB : QB + HC]
    total = jnp.concatenate([low, high], axis=1)[:, first:]
    for j, w in enumerate((w0, w1, w2, w3)):
        total = total + nn(h_ref[where + (slice(None), columns(row, j))], w[:, first:])
    cosine, sine = cosines(cp, sp, fr, angle)
    if own:
        q_ref[0] = (turn(total[:, :HC], cosine, sine).astype(BF16).astype(F32) * 0.125).astype(BF16)
        total = total[:, HC:]
    k_ref[0] = turn(total[:, :HC], cosine, sine).astype(BF16)
    v_ref[0] = total[:, HC:].astype(BF16)


def project(own, row, xs, table, mods, weights, tables):
    frames = xs[0].shape[0]
    x_spec = pl.BlockSpec((1, PR, D), lambda f, *_: (f, 0, 0))
    out_spec = pl.BlockSpec((1, TOK, HC), lambda f, *_: (f, 0, 0))
    out = shape((frames, TOK, HC))
    if own:
        out_specs = [pl.BlockSpec((1, TOK, D), lambda f, *_: (f, 0, 0)), out_spec, out_spec, out_spec]
        out_shape = [shape((frames, TOK, D)), out, out, out]
        scratch = []
    else:
        out_specs = [out_spec, out_spec]
        out_shape = [out, out]
        scratch = [pltpu.VMEM((TOK, D), BF16)]
    return pl.pallas_call(
        lambda *refs: project_kernel(own, *refs),
        out_shape=out_shape,
        grid_spec=pltpu.PrefetchScalarGridSpec(
            num_scalar_prefetch=1,
            grid=(frames,),
            in_specs=[x_spec] * 4
            + [whole((FPD, WIDE)), whole(mods.shape)]
            + [whole((HC, 3 * HC))] * 4
            + [whole((TOK, HC)), whole((TOK, HC)), whole((16, 2 * HC))],
            out_specs=out_specs,
            scratch_shapes=scratch,
        ),
        compiler_params=params(20),
        cost_estimate=cost(2 * frames * TOK * D * 3 * HC, frames * TOK * D * 4 + 4 * MB),
        name="project_own" if own else "project_prev",
    )(row, *xs, table, mods, *weights, *tables)


def head_lanes():
    return lax.broadcasted_iota(jnp.int32, (TOK, HC), 1) // HD


def attend_kernel(pos_ref, q, k, v, kp, vp, o0, o1, o23, lse, qs, scores, acc, top, low):
    f = pl.program_id(0)
    place = pos_ref[f]
    lanes = head_lanes()
    query = q[0]
    for h in range(4):
        qs[pl.ds(h * TOK, TOK), :] = jnp.where(lanes == h, query, jnp.zeros_like(query))
    top[...] = jnp.full_like(top, -1e30)
    low[...] = jnp.zeros_like(low)
    acc[...] = jnp.zeros_like(acc)
    before = jnp.maximum(place - f, 0)
    start = jnp.maximum(f - place, 0)

    def score(keys, slot):
        for h in range(4):
            rows = pl.ds(h * TOK, TOK)
            s = nt(qs[rows, :], keys)
            scores[slot, rows, :] = s
            top[rows, :] = jnp.maximum(top[rows, :], jnp.maximum(s[:, :128], s[:, 128:]))

    def mix(values, slot):
        for h in range(4):
            rows = pl.ds(h * TOK, TOK)
            p = jnp.exp(scores[slot, rows, :] - jnp.concatenate([top[rows, :]] * 2, axis=1))
            low[rows, :] = low[rows, :] + (p[:, :128] + p[:, 128:])
            acc[rows, :] = acc[rows, :] + nn(p.astype(BF16), values)

    def run(step):
        def prev(i, _):
            at = PREV - before + i
            step(kp[at] if step is score else vp[at], i)
            return 0

        def own(g, _):
            step(k[g] if step is score else v[g], g - f + place)
            return 0

        lax.fori_loop(0, before, prev, 0)
        lax.fori_loop(start, f + 1, own, 0)

    run(score)
    for h in range(4):
        rows = pl.ds(h * TOK, TOK)
        top[rows, :] = jnp.broadcast_to(jnp.max(top[rows, :], axis=1, keepdims=True), (TOK, 128))
    run(mix)
    result = jnp.zeros((TOK, HC), F32)
    logs = jnp.zeros((TOK, 128), F32)
    narrow = lax.broadcasted_iota(jnp.int32, (TOK, 128), 1)
    for h in range(4):
        rows = pl.ds(h * TOK, TOK)
        total = jnp.sum(low[rows, :], axis=1, keepdims=True)
        result = jnp.where(lanes == h, acc[rows, :] / total, result)
        logs = jnp.where(narrow == h, top[rows, :] + jnp.log(total), logs)
    lse[0] = logs.T[:8]
    result = result.astype(BF16)
    o0[0] = result[:PR]
    o1[0] = result[PR : 2 * PR]
    o23[0, 0] = result[2 * PR : 3 * PR]
    o23[1, 0] = result[3 * PR :]


def attend(places, q, k, v, kp, vp):
    block = pl.BlockSpec((1, TOK, HC), lambda f, *_: (f, 0, 0))
    piece = pl.BlockSpec((1, PR, HC), lambda f, *_: (f, 0, 0))
    return pl.pallas_call(
        attend_kernel,
        out_shape=[shape((FPD, PR, HC))] * 2
        + [shape((2, FPD, PR, HC)), shape((FPD, 8, TOK), F32)],
        grid_spec=pltpu.PrefetchScalarGridSpec(
            num_scalar_prefetch=1,
            grid=(FPD,),
            in_specs=[block]
            + [whole((FPD, TOK, HC))] * 2
            + [whole((PREV, TOK, HC))] * 2,
            out_specs=[piece] * 2
            + [
                pl.BlockSpec((2, 1, PR, HC), lambda f, *_: (0, f, 0, 0)),
                pl.BlockSpec((1, 8, TOK), lambda f, *_: (f, 0, 0)),
            ],
            scratch_shapes=[
                pltpu.VMEM((4 * TOK, HC), BF16),
                pltpu.VMEM((8, 4 * TOK, TOK), F32),
                pltpu.VMEM((4 * TOK, HC), F32),
                pltpu.VMEM((4 * TOK, 128), F32),
                pltpu.VMEM((4 * TOK, 128), F32),
            ],
        ),
        compiler_params=params(58),
        cost_estimate=cost(36 * 4 * 2 * 2 * TOK**3, 6 * MB, 36 * 4 * TOK * TOK),
        name="attend",
    )(places, q, k, v, kp, vp)


def attend_back_kernel(own, pos_ref, q, k, v, g0, g1, g2, g3, o0, o1, o23, lse, *rest):
    if own:
        cp, sp, fr, before_ref, dq, dk, dv, qs, gs, ks, pl_scr, dl_scr, ds_scr, dq_acc = rest
        dk_acc, dv_acc = dk, dv
    else:
        dq, both_ref, qs, gs, ks, pl_scr, dl_scr, ds_scr, dq_acc, dk_acc, dv_acc = rest
    f = pl.program_id(0)
    place = pos_ref[f]
    lanes = head_lanes()

    @pl.when(f == 0)
    def _():
        for ref in (dk_acc, dv_acc):
            ref[...] = jnp.zeros_like(ref)

    def prelude():
        query = q[0]
        grad = jnp.concatenate([r[0] for r in (g0, g1, g2, g3)], axis=0)
        mixed = jnp.concatenate([o0[0], o1[0], o23[0, 0], o23[1, 0]], axis=0)
        for h in range(4):
            rows = pl.ds(h * TOK, TOK)
            qs[rows, :] = jnp.where(lanes == h, query, jnp.zeros_like(query))
            gs[rows, :] = jnp.where(lanes == h, grad, jnp.zeros_like(grad))
        both = grad.astype(F32) * mixed.astype(F32)
        pick = (
            lax.broadcasted_iota(jnp.int32, (8, HC), 1) // HD
            == lax.broadcasted_iota(jnp.int32, (8, HC), 0)
        ).astype(F32)
        return lax.dot_general(
            pick, both, (((1,), (1,)), ((), ())),
            preferred_element_type=F32, precision=lax.Precision.HIGHEST,
        )

    def step(delta, logs, at):
        keys, values = k[at], v[at]
        for h in range(4):
            rows = pl.ds(h * TOK, TOK)
            ks[rows, :] = jnp.where(lanes == h, keys, jnp.zeros_like(keys))
            p = jnp.exp(nt(keys, qs[rows, :]) - logs[h : h + 1])
            ds = (p * (nt(values, gs[rows, :]) - delta[h : h + 1])).astype(BF16)
            pl_scr[:, rows] = p.astype(BF16)
            dl_scr[:, rows] = ds
            ds_scr[rows, :] = ds
        dv_acc[at] = dv_acc[at] + nn(pl_scr[...], gs[...])
        dk_acc[at] = dk_acc[at] + nn(dl_scr[...], qs[...])
        dq_acc[...] = dq_acc[...] + tn(ds_scr[...], ks[...])

    def sweep(low, high):
        delta = prelude()
        logs = lse[0]
        dq_acc[...] = jnp.zeros_like(dq_acc)

        def one(at, _):
            step(delta, logs, at)
            return 0

        lax.fori_loop(low, high, one, 0)

    if own:
        sweep(jnp.maximum(f - place, 0), f + 1)
        cosine, sine = cosines(cp, sp, fr, f)
        dq[0] = turn((dq_acc[...] + before_ref[0]) * 0.125, cosine, -sine).astype(BF16)
    else:
        count = jnp.maximum(place - f, 0)

        @pl.when(count > 0)
        def _():
            sweep(PREV - count, PREV)
            dq[0] = dq_acc[...]

        @pl.when(count == 0)
        def _():
            dq[0] = jnp.zeros_like(dq_acc)

        @pl.when(f == FPD - 1)
        def _():
            both_ref[0] = dk_acc[...].astype(BF16)
            both_ref[1] = dv_acc[...].astype(BF16)


def attend_back(own, places, q, k, v, grads, mixed, lse, tables=None, before=None):
    block = pl.BlockSpec((1, TOK, HC), lambda f, *_: (f, 0, 0))
    piece = pl.BlockSpec((1, PR, HC), lambda f, *_: (f, 0, 0))
    count = FPD if own else PREV
    wide = pltpu.VMEM((4 * TOK, HC), BF16)
    tall = pltpu.VMEM((TOK, 4 * TOK), BF16)
    scratch = [wide, wide, wide, tall, tall, wide, pltpu.VMEM((TOK, HC), F32)]
    specs = []
    extra = ()
    if own:
        specs = [whole((TOK, HC)), whole((TOK, HC)), whole((16, 2 * HC)), block]
        extra = tuple(tables) + (before,)
    else:
        scratch += [pltpu.VMEM((PREV, TOK, HC), F32)] * 2
    return pl.pallas_call(
        lambda *refs: attend_back_kernel(own, *refs),
        out_shape=[shape((FPD, TOK, HC), BF16 if own else F32)]
        + ([shape((FPD, TOK, HC), F32)] * 2 if own else [shape((2, PREV, TOK, HC))]),
        grid_spec=pltpu.PrefetchScalarGridSpec(
            num_scalar_prefetch=1,
            grid=(FPD,),
            in_specs=[block]
            + [whole((count, TOK, HC))] * 2
            + [piece] * 6
            + [pl.BlockSpec((2, 1, PR, HC), lambda f, *_: (0, f, 0, 0))]
            + [pl.BlockSpec((1, 8, TOK), lambda f, *_: (f, 0, 0))]
            + specs,
            out_specs=[block]
            + ([whole((FPD, TOK, HC))] * 2 if own else [whole((2, PREV, TOK, HC))]),
            scratch_shapes=scratch,
        ),
        compiler_params=params(58),
        cost_estimate=cost(1000 if own else 12 * 4 * 5 * 2 * TOK**3, 1000 if own else 12 * MB),
        name="attend_back_own" if own else "attend_back_prev",
    )(places, q, k, v, *grads, *mixed, lse, *extra)


HALF = 4
RAW = HALF * PR


def flat(ref):
    return ref[...].reshape(RAW, ref.shape[-1])


def frames_of(value):
    return value.reshape(HALF, PR, value.shape[-1])


def segment(table, s):
    both = table[:, s * D : (s + 1) * D]
    return jnp.where(pl.program_id(0) == 0, both[:HALF], both[HALF:])[:, None, :]


def fold(out, start, width, row):
    @pl.when(pl.program_id(0) == 0)
    def _():
        out[:, start : start + width] = jnp.zeros((8, width), F32)

    for i in range(8):
        at = (slice(i, i + 1), slice(start, start + width))
        out[at] = out[at] + row[:, i * width : (i + 1) * width]


def mid_kernel(o0, o1, o2, o3, w0, w1, w2, w3, table, x, cot, branch, middle, hidden, down, dsum):
    total = unfold(table, OB, 128)
    for o, w in zip((o0, o1, o2, o3), (w0, w1, w2, w3)):
        total = total + nn(flat(o), w[...])
    branched = frames_of(total)
    branch[...] = branched
    mid_value = x[...].astype(F32) + segment(table, 2) * branched
    middle[...] = mid_value
    normal, _ = norm(mid_value)
    hidden[...] = (normal * (1.0 + segment(table, 4)) + segment(table, 3)).astype(BF16)
    grad = (segment(table, 5) * cot[...].astype(F32)).astype(BF16)
    down[...] = grad
    fold(dsum, 0, 128, jnp.sum(grad.astype(F32).reshape(RAW, D), axis=0, keepdims=True))


def half_spec(width):
    return pl.BlockSpec((HALF, PR, width), lambda i, *_: (i, 0, 0))


def mid(pieces, weights, table, x, cot):
    return pl.pallas_call(
        mid_kernel,
        out_shape=[
            shape((FPD, PR, D), F32),
            shape((FPD, PR, D), F32),
            shape((FPD, PR, D)),
            shape((FPD, PR, D)),
            shape((8, 128), F32),
        ],
        grid=(FPD // HALF,),
        in_specs=[half_spec(HC)] * 4
        + [whole((HC, D))] * 4
        + [whole((FPD, WIDE)), half_spec(D), half_spec(D)],
        out_specs=[half_spec(D)] * 4 + [whole((8, 128))],
        compiler_params=params(26),
        cost_estimate=cost(2 * 512 * D * D, 12 * MB),
        name="mid",
    )(*pieces, *weights, table, x, cot)


def mid_back_kernel(hg, middle, branch, cot, table, w0, w1, w2, w3, mg, bg, a0, a1, a23, sums):
    grad = hg[...]
    normal, rate = norm(middle[...])
    put_half(sums, D, jnp.sum(grad, axis=1))
    put_half(sums, 2 * D, jnp.sum(grad * normal, axis=1))
    total = cot[...].astype(F32) + norm_back(normal, rate, grad * (1.0 + segment(table, 4)))
    mg[...] = total
    put_half(sums, 0, jnp.sum(total * branch[...], axis=1))
    low = (segment(table, 2) * total).astype(BF16)
    bg[...] = low
    low = low.reshape(RAW, D)
    fold(sums, 3 * D, 128, jnp.sum(low.astype(F32), axis=0, keepdims=True))
    for j, w in enumerate((w0, w1, w2, w3)):
        value = frames_of(nt(low, w[...]).astype(BF16))
        if j < 2:
            (a0, a1)[j][...] = value
        else:
            a23[j - 2] = value


def mid_back(hg, middle, branch, cot, table, weights):
    return pl.pallas_call(
        mid_back_kernel,
        out_shape=[shape((FPD, PR, D), F32), shape((FPD, PR, D))]
        + [shape((FPD, PR, HC))] * 2
        + [shape((2, FPD, PR, HC)), shape((8, 3 * D + 128), F32)],
        grid=(FPD // HALF,),
        in_specs=[half_spec(D)] * 4
        + [whole((FPD, WIDE))]
        + [whole((HC, D))] * 4,
        out_specs=[half_spec(D)] * 2
        + [half_spec(HC)] * 2
        + [pl.BlockSpec((2, HALF, PR, HC), lambda i: (0, i, 0, 0)), whole((8, 3 * D + 128))],
        compiler_params=params(26),
        cost_estimate=cost(2 * 512 * D * D, 12 * MB),
        name="mid_back",
    )(hg, middle, branch, cot, table, *weights)


NB = 512
STEPS = FF // NB
PER = D // NB
TOKENS = FPD * PR


def block_of(t):
    phase = t // PER
    return ((phase % 2) * 2) ^ (phase // 2)


def up_column(t, row):
    return (row ^ block_of(t)) * PER + t % PER


def down_row(t):
    return block_of(t) * PER + t % PER


def down_spec(j):
    phase = (0, 2, 1, 3)[j]
    return pl.BlockSpec((NB, D), lambda t, row: (jnp.clip(t - phase * PER, 0, PER - 1), 0))


def pick_down(d0, d1, d2, d3):
    phase = pl.program_id(0) // PER
    return jnp.where(
        phase < 2,
        jnp.where(phase == 0, d0[...], d2[...]),
        jnp.where(phase == 2, d1[...], d3[...]),
    )


def feed_kernel(row_ref, h2, dg, u0, u1, u2, u3, table, d0, d1, d2, d3, act, upg, hg, usum):
    row = row_ref[0]
    ups = (u0, u1, u2, u3)
    down = pick_down(d0, d1, d2, d3)
    at = pl.ds(up_column(pl.program_id(0), row), 1)
    u = table[at, UB : UB + NB]
    for j, w in enumerate(ups):
        u = u + nn(h2[:, columns(row, j)], w[...])
    rate = math.sqrt(2.0 / math.pi)
    square = u * u
    half = 0.5 + 0.5 * jnp.tanh(u * (rate + (rate * 0.044715) * square))
    active = u * half
    act[...] = active.astype(BF16)
    slope = half + active * (1.0 - half) * (2.0 * rate + (6.0 * rate * 0.044715) * square)
    grad = (nt(dg[...], down) * slope).astype(BF16)
    upg[...] = grad
    put(usum, 0, up_column(pl.program_id(0), row), jnp.sum(grad.astype(F32), axis=0, keepdims=True))

    @pl.when(pl.program_id(0) == 0)
    def _():
        hg[...] = jnp.zeros_like(hg)

    for j, w in enumerate(ups):
        hg[:, columns(row, j)] = hg[:, columns(row, j)] + nt(grad, w[...])


def feed(row, h2, dg, ups, table, downs):
    tok = whole((TOKENS, D))
    block = pl.BlockSpec((TOKENS, NB), lambda t, row: (0, t))
    return pl.pallas_call(
        feed_kernel,
        out_shape=[
            shape((TOKENS, FF)),
            shape((TOKENS, FF)),
            shape((TOKENS, D), F32),
            shape((8, NB), F32),
        ],
        grid_spec=pltpu.PrefetchScalarGridSpec(
            num_scalar_prefetch=1,
            grid=(STEPS,),
            in_specs=[tok, tok]
            + [pl.BlockSpec((HC, NB), lambda t, row: (0, up_column(t, row[0])))] * 4
            + [whole((FPD, WIDE))]
            + [down_spec(j) for j in range(4)],
            out_specs=[block, block, tok, whole((8, NB))],
        ),
        compiler_params=params(58),
        cost_estimate=cost(3 * 2 * TOKENS * D * FF, 30 * MB, TOKENS * FF),
        name="feed",
    )(row, h2, dg, *ups, table, *downs)


def down_weight_kernel(row_ref, dg, act, d0, d1, d2, d3, table, middle, cot, dk, ds, out, gate, dn):
    t = pl.program_id(0)
    down = pick_down(d0, d1, d2, d3)
    active = act[...]

    @pl.when(t == 0)
    def _():
        dn[...] = jnp.zeros_like(dn)

    dn[...] = dn[...] + nn(active, down)
    part = tn(active, dg[...]).astype(BF16)

    @pl.when(t < STEPS // 2)
    def _():
        dk[0] = part

    @pl.when(t >= STEPS // 2)
    def _():
        ds[0] = part

    @pl.when(t == STEPS - 1)
    def _():
        bias = unfold(table, DB, 128)
        for f in range(FPD):
            rows = slice(f * PR, (f + 1) * PR)
            value = dn[rows, :] + bias
            out[f] = (middle[f] + table[f : f + 1, 5 * D : 6 * D] * value).astype(BF16)
            gate[f : f + 1, :] = jnp.sum(cot[f].astype(F32) * value, axis=0, keepdims=True)


def down_weight_grad(row, dg, act, downs, table, middle, cot):
    tok = whole((TOKENS, D))
    full = whole((FPD, PR, D))
    block = pl.BlockSpec((TOKENS, NB), lambda t, row: (0, t))

    def down_out(first):
        def index(t, row):
            at = jnp.clip(t - first, 0, STEPS // 2 - 1)
            return (at // PER, at % PER, 0)

        return pl.BlockSpec((1, NB, D), index)

    return pl.pallas_call(
        down_weight_kernel,
        out_shape=[shape((2, D, D))] * 2 + [shape((FPD, PR, D)), shape((8, D), F32)],
        grid_spec=pltpu.PrefetchScalarGridSpec(
            num_scalar_prefetch=1,
            grid=(STEPS,),
            in_specs=[tok, block]
            + [down_spec(j) for j in range(4)]
            + [whole((FPD, WIDE)), full, full],
            out_specs=[down_out(0), down_out(STEPS // 2), full, whole((8, D))],
            scratch_shapes=[pltpu.VMEM((TOKENS, D), F32)],
        ),
        compiler_params=params(58),
        cost_estimate=cost(2 * 2 * TOKENS * D * FF, 24 * MB),
        name="down_weight_grad",
    )(row, dg, act, *downs, table, middle, cot)


def up_weight_kernel(row_ref, h2, upg, uk, us):
    row = row_ref[0]
    grad = upg[...]
    for j, ref in enumerate((uk, us, uk, us)):
        ref[j // 2, 0] = tn(h2[:, columns(row, j)], grad).astype(BF16)


def up_weight_grad(row, h2, upg):
    up_out = pl.BlockSpec(
        (2, 1, HC, NB),
        lambda t, row: (0, up_column(t, row[0]) // PER, 0, up_column(t, row[0]) % PER),
    )
    return pl.pallas_call(
        up_weight_kernel,
        out_shape=[shape((2, 4, HC, D))] * 2,
        grid_spec=pltpu.PrefetchScalarGridSpec(
            num_scalar_prefetch=1,
            grid=(STEPS,),
            in_specs=[whole((TOKENS, D)), pl.BlockSpec((TOKENS, NB), lambda t, row: (0, t))],
            out_specs=[up_out, up_out],
        ),
        compiler_params=params(58),
        cost_estimate=cost(2 * TOKENS * D * FF, 14 * MB),
        name="up_weight_grad",
    )(row, h2, upg)


def out_weight_kernel(t0, t1, t2, t3, bg, keep, send):
    grad = bg[...].reshape(TOKENS, D)
    for j, t in enumerate((t0, t1, t2, t3)):
        ref = (keep, send)[j % 2]
        ref[j // 2] = tn(t[...].reshape(TOKENS, HC), grad).astype(BF16)


def out_weight_grad(pieces, bg):
    return pl.pallas_call(
        out_weight_kernel,
        out_shape=[shape((2, HC, D))] * 2,
        grid=(1,),
        in_specs=[whole((FPD, PR, HC))] * 4 + [whole((FPD, PR, D))],
        out_specs=[whole((2, HC, D))] * 2,
        compiler_params=params(14),
        cost_estimate=cost(2 * TOKENS * D * D, 4 * MB),
        name="out_weight_grad",
    )(*pieces, bg)


CHUNKS = 16
UP_ROWS, OUT_ROWS, DOWN_ROWS = D // CHUNKS, HC // CHUNKS, D // CHUNKS
FIRST = UP_ROWS + OUT_ROWS
ROWS = FIRST + DOWN_ROWS


def core_sum_kernel(ua, ub, da, db, oa, ob, out):
    def both(a, b):
        return (a.astype(F32) + b.astype(F32)).astype(BF16)

    for c in range(4):
        at = c * ROWS
        low, high = c * OUT_ROWS, (c + 1) * OUT_ROWS
        for i in range(4):
            to = at + i * OUT_ROWS
            out[0, to : to + OUT_ROWS] = both(ua[0, i, low:high], ub[0, i, low:high])
        out[0, at + UP_ROWS : at + FIRST] = both(oa[0, low:high], ob[0, low:high])
        low, high = c * DOWN_ROWS, (c + 1) * DOWN_ROWS
        out[0, at + FIRST : at + ROWS] = both(da[0, low:high], db[0, low:high])


def core_sum(up, down, out):
    ups = pl.BlockSpec((1, 4, 4 * OUT_ROWS, D), lambda j, c: (j, 0, c, 0))
    outs = pl.BlockSpec((1, 4 * OUT_ROWS, D), lambda j, c: (j, c, 0))
    downs = pl.BlockSpec((1, 4 * DOWN_ROWS, D), lambda j, c: (j, c, 0))
    return pl.pallas_call(
        core_sum_kernel,
        out_shape=shape((2, CHUNKS * ROWS, D)),
        grid=(2, CHUNKS // 4),
        in_specs=[ups, ups, downs, downs, outs, outs],
        out_specs=pl.BlockSpec((1, 4 * ROWS, D), lambda j, c: (j, c, 0)),
        compiler_params=params(20),
        cost_estimate=cost(1000, 1000),
        name="core_sum",
    )(*up, *down, *out)


def spread_first_kernel(index_ref, a0, a1, a2, a3, up, out):
    for m, a in enumerate((a0, a1, a2, a3)):

        @pl.when(pl.program_id(0) == m)
        def _():
            for k in range(4):
                at = index_ref[1] ^ k
                for i in range(4):
                    rows = slice(i * OUT_ROWS, (i + 1) * OUT_ROWS)
                    up[0, at, :, i * D : (i + 1) * D] = a[k, rows].astype(F32)
                out[0, at] = a[k, UP_ROWS:].astype(F32)


def spread_first(index, pieces):
    def at(i, index):
        return (index[0] ^ i, 0, 0, 0)

    up, out = pl.pallas_call(
        spread_first_kernel,
        out_shape=[shape((4, 4, OUT_ROWS, FF), F32), shape((4, 4, OUT_ROWS, D), F32)],
        grid_spec=pltpu.PrefetchScalarGridSpec(
            num_scalar_prefetch=1,
            grid=(4,),
            in_specs=[whole((4, FIRST, D))] * 4,
            out_specs=[
                pl.BlockSpec((1, 4, OUT_ROWS, FF), at),
                pl.BlockSpec((1, 4, OUT_ROWS, D), at),
            ],
        ),
        compiler_params=params(24),
        cost_estimate=cost(0, 8 * MB),
        name="spread_up_out",
    )(index, *pieces)
    return up.reshape(HC, FF), out.reshape(HC, D)


def spread_second_kernel(index_ref, a0, a1, a2, a3, down):
    for m, a in enumerate((a0, a1, a2, a3)):

        @pl.when(pl.program_id(0) == m)
        def _():
            for k in range(4):
                down[index_ref[0] ^ k, 0] = a[k].astype(F32)


def spread_second(index, pieces):
    return pl.pallas_call(
        spread_second_kernel,
        out_shape=shape((4, 4, DOWN_ROWS, D), F32),
        grid_spec=pltpu.PrefetchScalarGridSpec(
            num_scalar_prefetch=1,
            grid=(4,),
            in_specs=[whole((4, DOWN_ROWS, D))] * 4,
            out_specs=pl.BlockSpec(
                (4, 1, DOWN_ROWS, D), lambda i, index: (0, index[1] ^ i, 0, 0)
            ),
        ),
        compiler_params=params(24),
        cost_estimate=cost(0, 6 * MB),
        name="spread_down",
    )(index, *pieces).reshape(D, D)


def place_kernel(axis, index_ref, a0, a1, a2, a3, out):
    for m, a in enumerate((a0, a1, a2, a3)):

        @pl.when(pl.program_id(0) == m)
        def _():
            out[...] = a[...].astype(out.dtype)


def place(index, axis, pieces, kind):
    rows, width = pieces[0].shape
    return pl.pallas_call(
        lambda *refs: place_kernel(axis, *refs),
        out_shape=shape((4 * rows, width), kind),
        grid_spec=pltpu.PrefetchScalarGridSpec(
            num_scalar_prefetch=1,
            grid=(4,),
            in_specs=[whole((rows, width))] * 4,
            out_specs=pl.BlockSpec((rows, width), lambda i, index: (index[axis] ^ i, 0)),
        ),
        compiler_params=params(24),
        cost_estimate=cost(0, 24 * rows * width),
        name="place",
    )(index, *pieces)


def arrange_kernel(row_ref, a0, a1, a2, a3, out):
    row = row_ref[0]
    for j, a in enumerate((a0, a1, a2, a3)):
        for s in range(3):
            lanes = pl.ds(pl.multiple_of(s * D + (row ^ j) * HC, HC), HC)
            out[:, lanes] = a[:, s * HC : (s + 1) * HC]


def arrange(row, pieces):
    rows = pieces[0].shape[0]
    return pl.pallas_call(
        arrange_kernel,
        out_shape=shape((rows, 3 * D)),
        grid_spec=pltpu.PrefetchScalarGridSpec(
            num_scalar_prefetch=1,
            grid=(1,),
            in_specs=[whole((rows, 3 * HC))] * 4,
            out_specs=whole((rows, 3 * D)),
        ),
        compiler_params=params(16),
        cost_estimate=cost(0, 8 * rows * D),
        name="arrange",
    )(row, *pieces)


def project_back_kernel(row_ref, dq, dk, dv, rk, rv, w0, w1, w2, w3, cp, sp, fr, dp, h0, h2, hs, bsum):
    row = row_ref[0]
    f = pl.program_id(0)
    later = (f > 0).astype(F32)
    keys = dk[0] + later * rk[0, 0].astype(F32)
    values = dv[0] + later * rv[0, 0].astype(F32)
    cosine, sine = cosines(cp, sp, fr, f)
    dp[0, :, :HC] = dq[0]
    dp[0, :, HC : 2 * HC] = turn(keys, cosine, -sine).astype(BF16)
    dp[0, :, 2 * HC :] = values.astype(BF16)
    grad = dp[0]
    sums = jnp.sum(grad.astype(F32), axis=0, keepdims=True)

    @pl.when(f == 0)
    def _():
        bsum[...] = jnp.zeros_like(bsum)

    number = lax.broadcasted_iota(jnp.int32, (8, 2 * HC), 0)
    bsum[...] = bsum[...] + jnp.where(number == row, sums[:, : 2 * HC], 0.0)
    bsum[:, :HC] = bsum[:, :HC] + jnp.where(number[:, :HC] == row + 4, sums[:, 2 * HC :], 0.0)
    for j, w in enumerate((w0, w1, w2, w3)):
        part = nt(grad, w[...]).astype(BF16)
        at = (0, slice(None), columns(row, j))
        h0[at] = part[:PR]
        hs[(0,) + at] = part[PR : 2 * PR]
        h2[at] = part[2 * PR : 3 * PR]
        hs[(1,) + at] = part[3 * PR :]


def project_back(row, dq, dk, dv, returned, weights, tables):
    block = pl.BlockSpec((1, TOK, HC), lambda f, *_: (f, 0, 0))
    late = [
        pl.BlockSpec((1, 1, TOK, HC), lambda f, *_, i=i: (i, jnp.maximum(f - 1, 0), 0, 0))
        for i in range(2)
    ]
    piece = pl.BlockSpec((1, PR, D), lambda f, *_: (f, 0, 0))
    return pl.pallas_call(
        project_back_kernel,
        out_shape=[
            shape((FPD, TOK, 3 * HC)),
            shape((FPD, PR, D)),
            shape((FPD, PR, D)),
            shape((2, FPD, PR, D)),
            shape((8, 2 * HC), F32),
        ],
        grid_spec=pltpu.PrefetchScalarGridSpec(
            num_scalar_prefetch=1,
            grid=(FPD,),
            in_specs=[block] * 3
            + late
            + [whole((HC, 3 * HC))] * 4
            + [whole((TOK, HC)), whole((TOK, HC)), whole((16, 2 * HC))],
            out_specs=[
                pl.BlockSpec((1, TOK, 3 * HC), lambda f, *_: (f, 0, 0)),
                piece,
                piece,
                pl.BlockSpec((2, 1, PR, D), lambda f, *_: (0, f, 0, 0)),
                whole((8, 2 * HC)),
            ],
        ),
        compiler_params=params(20),
        cost_estimate=cost(2 * FPD * TOK * D * 3 * HC, 14 * MB),
        name="project_back",
    )(row, dq, dk, dv, returned, returned, *weights, *tables)


def weight_kernel(row_ref, h, dp, w):
    w[0] = tn(h[...], dp[...]).astype(BF16)


def project_weight(row, hidden, dproj):
    tokens = FPD * TOK
    return pl.pallas_call(
        weight_kernel,
        out_shape=shape((4, HC, 3 * HC)),
        grid_spec=pltpu.PrefetchScalarGridSpec(
            num_scalar_prefetch=1,
            grid=(4,),
            in_specs=[
                pl.BlockSpec((tokens, HC), lambda j, row: (0, row[0] ^ j)),
                whole((tokens, 3 * HC)),
            ],
            out_specs=pl.BlockSpec((1, HC, 3 * HC), lambda j, row: (j, 0, 0)),
        ),
        compiler_params=params(20),
        cost_estimate=cost(2 * tokens * D * 3 * HC, 9 * MB),
        name="project_weight",
    )(row, hidden.reshape(tokens, D), dproj.reshape(tokens, 3 * HC))


def input_back_kernel(x, h0, near, far, table, mg, bsum, gate, out, sums):
    grad = h0[...].astype(F32) + near[0].astype(F32) + far[...].astype(F32)
    normal, rate = norm(x[...].astype(F32))
    put_half(sums, 0, jnp.sum(grad, axis=1))
    put_half(sums, D, jnp.sum(grad * normal, axis=1))
    sums[:, 2 * D : 3 * D] = gate[...]
    sums[:, 3 * D :] = bsum[...]
    out[...] = mg[...] + norm_back(normal, rate, grad * (1.0 + segment(table, 1)))


LATE = 3 * D + 2 * HC
EARLY = 3 * D + NB + 256


def input_back(x, h0, near, far, table, mg, bsum, gate):
    return pl.pallas_call(
        input_back_kernel,
        out_shape=[shape((FPD, PR, D), F32), shape((8, LATE), F32)],
        grid=(FPD // HALF,),
        in_specs=[half_spec(D)] * 2
        + [pl.BlockSpec((1, HALF, PR, D), lambda i: (0, i, 0, 0))]
        + [half_spec(D), whole((FPD, WIDE)), half_spec(D), whole((8, 2 * HC)), whole((8, D))],
        out_specs=[half_spec(D), whole((8, LATE))],
        compiler_params=params(20),
        cost_estimate=cost(20 * 512 * D, 10 * MB),
        name="input_back",
    )(x, h0, near, far, table, mg, bsum, gate)


def early_kernel(m, u, d, out):
    out[:, : 3 * D] = m[:, : 3 * D]
    out[:, 3 * D : 3 * D + NB] = u[...]
    out[:, 3 * D + NB : 3 * D + NB + 128] = d[...]
    out[:, 3 * D + NB + 128 :] = m[:, 3 * D :]


def early_sums(sums, usum, dsum):
    return pl.pallas_call(
        early_kernel,
        out_shape=shape((8, EARLY), F32),
        grid=(1,),
        in_specs=[whole(a.shape) for a in (sums, usum, dsum)],
        out_specs=whole((8, EARLY)),
        cost_estimate=cost(0, MB),
        name="early_sums",
    )(sums, usum, dsum)


def final_kernel(row_ref, *refs):
    row = row_ref[0]
    late, early = refs[:4], refs[4:8]
    ada, ab, qb, ob, ub, db, asum = refs[8:]

    def rows(ref, cols):
        value = ref[:, :, cols].astype(F32)
        return value.reshape(64, value.shape[-1])

    left = [rows(s, slice(EARLY, EARLY + HC)).astype(BF16) for s in early]
    for segment in range(6):
        source, start = ((late, 0), (late, 1), (early, 0), (early, 1), (early, 2), (late, 2))[segment]
        cols = slice(start * D, (start + 1) * D)
        product, total = 0.0, 0.0
        for s, ref in zip(left, source):
            right = rows(ref, cols)
            total = total + jnp.sum(right, axis=0, keepdims=True)
            product = product + tn(s, right.astype(BF16))
        at = segment * D
        ada[:, at : at + D] = product
        asum[0:1, at : at + D] = total

    def bias(source, start, stop):
        return sum(
            jnp.sum(ref[:, :, start:stop].astype(F32), axis=0) for ref in source
        )

    ab[...] = asum[0:1, pl.ds(pl.multiple_of(row * 1536, 512), 1536)]
    folded = bias(late, 3 * D, LATE)
    for i in range(3):
        chunk = 3 * row + i
        at = jnp.where(chunk < 4, chunk, chunk - 4)
        second = (chunk >= 4) & (chunk < 8)
        value = jnp.where(second, folded[:, HC:], folded[:, :HC])
        qb[:, i * HC : (i + 1) * HC] = take(value, at)
    folded = bias(early, 3 * D, EARLY)
    for i in range(2):
        at = 2 * row + i
        ub[:, i * NB : (i + 1) * NB] = take(folded[:, :NB], at)
        db[:, i * 128 : (i + 1) * 128] = take(folded[:, NB : NB + 128], at)
        ob[:, i * 128 : (i + 1) * 128] = take(folded[:, NB + 128 :], at)


def final_sums(row, late, early):
    sizes = (1536, 768, 256, 1024, 256)
    return pl.pallas_call(
        final_kernel,
        out_shape=[shape((HC, 6 * D), F32)] + [shape((1, n), F32) for n in sizes],
        grid_spec=pltpu.PrefetchScalarGridSpec(
            num_scalar_prefetch=1,
            grid=(1,),
            in_specs=[whole((8, 8, LATE))] * 4
            + [whole((8, 8, EARLY + HC))] * 4,
            out_specs=[whole((HC, 6 * D))] + [whole((1, n)) for n in sizes],
            scratch_shapes=[pltpu.VMEM((8, 6 * D), F32)],
        ),
        compiler_params=params(28),
        cost_estimate=cost(2 * 256 * HC * 6 * D, 10 * MB),
        name="final_sums",
    )(row, *late, *early)


def row_sum(value):
    value = value + swap(value, CORE)
    return value + swap(value, DIRECT)


def row_pieces(value):
    return [value, swap(value, CORE), swap(value, DIRECT), swap(value, DIRECT ^ CORE)]


def seq_gather(value):
    value = jnp.stack([value, swap(value, FAR)])
    value = jnp.concatenate([value] + [swap(value, m) for m in (16, 32, 48)])
    return [value] + [swap(value, m) for m in (4, 8, 12)]


def by_row(pieces, row):
    a, b, c, d = pieces
    odd, high = row % 2 == 1, row >= 2
    a, b = jnp.where(odd, b, a), jnp.where(odd, a, b)
    c, d = jnp.where(odd, d, c), jnp.where(odd, c, d)
    return jnp.stack(
        [
            jnp.where(high, c, a),
            jnp.where(high, d, b),
            jnp.where(high, a, c),
            jnp.where(high, b, d),
        ]
    )


def exchange_rows(value, bit, index, axis):
    rows = value.shape[1] // 4
    at = lambda m: lax.dynamic_slice_in_dim(value, (index[axis] ^ m) * rows, rows, 1)
    parts = [at(0)] + [swap(at(m), bit * m) for m in (1, 2, 3)]
    return sum(part.astype(F32) for part in parts).astype(BF16)


def turn_heads(own, beside, across, order=lambda piece: piece):
    across = swap(across, DIRECT)
    return [own, swap(beside, CORE), across[0], swap(order(across)[1], CORE)]


def per_device(
    activations,
    noise_embed,
    frame_position,
    cotangent,
    ada_weight,
    ada_bias,
    qkv_weight,
    qkv_bias,
    out_weight,
    out_bias,
    up_weight,
    up_bias,
    down_weight,
    down_bias,
):
    row = lax.axis_index(("xl", "c")).astype(jnp.int32)
    row_arg = row.reshape(1)
    index = [lax.axis_index("y").astype(jnp.int32), lax.axis_index("z").astype(jnp.int32)]
    index_arg = jnp.stack(index)

    x0 = activations
    x2 = swap(x0, DIRECT)
    x1 = swap(x0, CORE)
    p0 = shift(activations[1:], 1)
    biases = (ada_bias, qkv_bias, out_bias, up_bias, down_bias)
    heads = list(split_heads(row_arg, qkv_weight))
    noise, heads[1] = lax.optimization_barrier((noise_embed, heads[1]))
    part, silu_own, *tables = prepare(row_arg, frame_position, noise, ada_weight, biases)
    qkv_pieces = [heads[0], swap(heads[1], CORE), swap(heads[2], OTHER), swap(heads[3], OTHER ^ CORE)]
    part = part + swap(part, CORE)
    table = part + swap(part, DIRECT)
    x2, p0, table, *qkv_pieces = lax.optimization_barrier((x2, p0, table, *qkv_pieces))

    x3 = swap(x2, CORE)
    p2 = swap(p0, DIRECT)
    p1 = swap(p0, CORE)
    before_mods = shift(table[:, : 2 * D], 1)

    out_own, up_own, _ = lax.optimization_barrier((out_weight, up_weight, table))
    outs2 = swap(out_own, OTHER)
    ups2 = swap(up_own, OTHER)

    hidden1, q, k, v = project(True, row_arg, (x0, x1, x2, x3), table, table, qkv_pieces, tables)
    p2, down_own, q, before_mods = lax.optimization_barrier((p2, down_weight, q, before_mods))
    p3 = swap(p2, CORE)
    downs2 = swap(down_own, DIRECT)
    kp, vp = project(
        False, row_arg, (p0, p1, p2, p3), table, before_mods, qkv_pieces, tables
    )
    *mixed, lse = attend(frame_position, q, k, v, kp, vp)
    outs2, ups2, downs2, lse = lax.optimization_barrier((outs2, ups2, downs2, lse))
    outs = [out_weight, swap(out_own, CORE), outs2, swap(outs2, CORE)]
    ups = [up_weight, swap(up_own, CORE), ups2, swap(ups2, CORE)]
    downs = [down_weight, swap(down_own, CORE), downs2, swap(downs2, CORE)]
    turned = turn_heads(*mixed)
    branch, middle, hidden2, down_grad, dsum = mid(turned, outs, table, x0, cotangent)
    h2 = hidden2.reshape(TOKENS, D)
    dg = down_grad.reshape(TOKENS, D)
    act, upg, hg, usum = feed(row_arg, h2, dg, ups, table, downs)
    mg, bg, *ag, sums = mid_back(hg.reshape(FPD, PR, D), middle, branch, cotangent, table, outs)
    late = []
    back = turn_heads(*ag[:2], ag[2], order=lambda piece: late.append(piece) or piece)[:2]

    early = early_sums(sums, usum, dsum)
    early = early + swap(early, CORE)
    dk_part, ds_part, layer_output, gate = down_weight_grad(
        row_arg, after(dg, bg), act, downs, table, middle, cotangent
    )
    upg, early, gate, far_back, *back = lax.optimization_barrier((upg, early, gate, *late, *back))
    back += [far_back[0], swap(far_back[1], CORE)]
    early = early + swap(early, DIRECT)
    uk, us = up_weight_grad(row_arg, h2, upg)
    ok, os = out_weight_grad(turned, bg)

    early = jnp.concatenate([early.astype(BF16), silu_own], axis=1)
    early, uk, ok, *back = lax.optimization_barrier((early, uk, ok, *back))
    dq_before, both = attend_back(False, frame_position, q, kp, vp, back, mixed, lse)
    returned = shift(both, -1)
    early = jnp.stack([early, swap(early, FAR)])
    uk, early, dq_before = lax.optimization_barrier((uk, early, dq_before))
    packed = core_sum(
        (uk, swap(us, CORE)), (dk_part, swap(ds_part, CORE)), (ok, swap(os, CORE))
    )
    early = jnp.concatenate([early] + [swap(early, m) for m in (16, 32, 48)])
    dq_before, packed, early = lax.optimization_barrier((dq_before, packed, early))
    scattered = lax.psum_scatter(packed, ("y", "z"), scatter_dimension=1, tiled=True)
    early_all = [early] + [swap(early, m) for m in (4, 8, 12)]
    dq, dk, dv = attend_back(
        True, frame_position, q, k, v, back, mixed, lse, tables, dq_before
    )
    dq, *early_all = lax.optimization_barrier((dq, *early_all))
    early = early_all[0][0].astype(F32)

    dproj, h0, h2_part, send, bsum = project_back(row_arg, dq, dk, dv, returned, qkv_pieces, tables)
    near = swap(send, CORE)
    far_part = (h2_part.astype(F32) + near[1].astype(F32)).astype(BF16)
    far = swap(far_part, DIRECT)
    qkv_parts = project_weight(row_arg, hidden1, dproj)
    input_grad, late = input_back(x0, h0, near, far, table, mg, bsum, gate)
    late = row_sum(late)
    late_all = seq_gather(late.astype(BF16))

    qkv_parts = after(qkv_parts, far_part)
    qkv_parts = exchange_rows(qkv_parts, 4, index, 0)
    qkv_parts = exchange_rows(qkv_parts, 16, index, 1)
    qkv_parts = (qkv_parts.astype(F32) + swap(qkv_parts, FAR).astype(F32)).astype(BF16)
    qkv_share = arrange(row_arg, turn_heads(qkv_parts[0], qkv_parts[1], qkv_parts[2:]))
    qkv_share = place(
        index_arg, 1, [qkv_share] + [swap(qkv_share, 16 * m) for m in (1, 2, 3)], BF16
    )
    qkv_total = place(
        index_arg, 0, [qkv_share] + [swap(qkv_share, 4 * m) for m in (1, 2, 3)], F32
    )

    share = scattered[0].astype(F32) + swap(scattered[1], DIRECT).astype(F32)
    share = (share + swap(share.astype(BF16), FAR).astype(F32)).astype(BF16)
    one, two = share[:FIRST], share[FIRST:]
    one = jnp.stack([one] + [swap(one, 16 * m) for m in (1, 2, 3)])
    two = jnp.stack([two] + [swap(two, 4 * m) for m in (1, 2, 3)])
    up_total, out_total = spread_first(index_arg, [one] + [swap(one, 4 * m) for m in (1, 2, 3)])
    down_total = spread_second(index_arg, [two] + [swap(two, 16 * m) for m in (1, 2, 3)])

    ada_total, *bias_sums = final_sums(row_arg, late_all, early_all)
    ada_sum, qkv_sum, out_sum, up_sum, down_sum = [b[0] for b in bias_sums]
    mod_own = jnp.concatenate(
        [late[:, : 2 * D], early[:, : 3 * D], late[:, 2 * D : 3 * D]], axis=1
    ).astype(BF16)
    silu_grad = nt(mod_own, ada_weight)
    silu_grad = by_row(row_pieces(silu_grad), row).transpose(1, 0, 2).reshape(FPD, D)
    embed = noise_embed.astype(F32)
    sigma = jax.nn.sigmoid(embed)
    embed_grad = silu_grad * (sigma * (1.0 + embed * (1.0 - sigma)))

    return (
        layer_output,
        input_grad,
        embed_grad,
        ada_total,
        ada_sum,
        qkv_total,
        qkv_sum,
        out_total,
        out_sum,
        up_total,
        up_sum,
        down_total,
        down_sum,
    )


def solution(mesh):
    fine = Mesh(mesh.devices.reshape(2, 4, 4, 2, 2), AXES)
    seq, row = ("xh", "z", "y"), ("xl", "c")
    token, weight, vector = P(seq, row, None), P(row, None), P(row)
    in_specs = (token, P(seq, None), P(seq), token) + (weight, vector) * 5
    out_specs = (token, token, P(seq, None)) + (weight, vector) * 5
    return jax.shard_map(
        per_device, mesh=fine, in_specs=in_specs, out_specs=out_specs, check_vma=False
    )
```

```python
import math

import jax
import jax.numpy as jnp
from jax import lax
from jax.experimental import pallas as pl
from jax.experimental.pallas import tpu as pltpu
from jax.sharding import Mesh, PartitionSpec as P

F32 = jnp.float32
BF16 = jnp.bfloat16
HD = 64
GRID = 16
FPD = 8
PR = 64
D = 1024
FF = 4096
HC = 256
TOK = 256
PREV = 7
AXES = ("xh", "z", "y", "xl", "c")
CORE, DIRECT, OTHER, FAR = 1, 2, 66, 64
MB = 1024 * 1024


def swap(value, mask):
    return lax.ppermute(value, AXES, [(i, i ^ mask) for i in range(128)])


def shift(value, steps):
    return lax.ppermute(value, AXES, [(i, (i + 4 * steps) % 128) for i in range(128)])


def after(value, *others):
    return lax.optimization_barrier((value,) + others)[0]


def nt(left, right):
    return lax.dot_general(left, right, (((1,), (1,)), ((), ())), preferred_element_type=F32)


def tn(left, right):
    return lax.dot_general(left, right, (((0,), (0,)), ((), ())), preferred_element_type=F32)


def nn(left, right):
    return jnp.dot(left, right, preferred_element_type=F32)


def norm(values):
    center = values - jnp.mean(values, axis=-1, keepdims=True)
    spread = jnp.mean(center * center, axis=-1, keepdims=True)
    rate = lax.rsqrt(spread + 1e-06)
    return center * rate, rate


def norm_back(normal, rate, grad):
    mean_grad = jnp.mean(grad, axis=-1, keepdims=True)
    mean_both = jnp.mean(grad * normal, axis=-1, keepdims=True)
    return rate * (grad - mean_grad - normal * mean_both)


def turn(values, cosine, sine):
    lanes = lax.broadcasted_iota(jnp.int32, values.shape, 1)
    other = jnp.where(
        lanes % HD < HD // 2, pltpu.roll(values, HC - HD // 2, 1), pltpu.roll(values, HD // 2, 1)
    )
    return values * cosine + other * sine


def params(mib):
    return pltpu.CompilerParams(vmem_limit_bytes=mib * MB)


def cost(flops, moved, exps=0):
    return pl.CostEstimate(flops=int(flops), bytes_accessed=int(moved), transcendentals=int(exps))


def whole(shape):
    return pl.BlockSpec(shape, lambda i, *_: (0,) * len(shape))


def columns(row, j):
    return pl.ds(pl.multiple_of((row ^ j) * HC, HC), HC)


def shape(dims, kind=BF16):
    return jax.ShapeDtypeStruct(dims, kind)


UB, QB, OB, DB, WIDE = 6144, 6656, 7168, 7296, 7424


def put(ref, start, at, value):
    cols = slice(start, start + value.shape[1])
    number = lax.broadcasted_iota(jnp.int32, (8, value.shape[1]), 0)
    ref[:, cols] = jnp.where(number == at, value, ref[:, cols])


def take(value, at):
    number = lax.broadcasted_iota(jnp.int32, value.shape, 0)
    return jnp.sum(jnp.where(number == at, value, 0.0), axis=0, keepdims=True)


def put_half(ref, start, value):
    cols = slice(start, start + value.shape[1])
    number = lax.broadcasted_iota(jnp.int32, (8, value.shape[1]), 0)
    both = jnp.concatenate([value, value], axis=0)
    ref[:, cols] = jnp.where(number // 4 == pl.program_id(0), both, ref[:, cols])


def unfold(ref, start, width):
    return jnp.concatenate([ref[i : i + 1, start : start + width] for i in range(8)], axis=1)


def prepare_kernel(row_ref, pos_ref, noise, ada, ab, qb, ob, ub, db, pack, silu, cp, sp, frames):
    row = row_ref[0]
    embed = noise[...].astype(F32)
    value = (embed / (1.0 + jnp.exp(-embed))).astype(BF16)
    own = jnp.where(
        row < 2,
        jnp.where(row == 0, value[:, :HC], value[:, HC : 2 * HC]),
        jnp.where(row == 2, value[:, 2 * HC : 3 * HC], value[:, 3 * HC :]),
    )
    silu[...] = own
    pack[:, UB:] = jnp.zeros((FPD, WIDE - UB), F32)
    for segment in range(6):
        cols = slice(segment * D, (segment + 1) * D)
        pack[:, cols] = nn(own, ada[:, cols])
    bias = pl.ds(pl.multiple_of(row * 1536, 512), 1536)
    pack[:, bias] = pack[:, bias] + ab[...].astype(F32)
    for i in range(2):
        at = 2 * row + i
        put(pack, UB, at, ub[:, i * 512 : (i + 1) * 512].astype(F32))
        put(pack, OB, at, ob[:, i * 128 : (i + 1) * 128].astype(F32))
        put(pack, DB, at, db[:, i * 128 : (i + 1) * 128].astype(F32))
    for i in range(3):
        chunk = 3 * row + i
        at = jnp.where(chunk < 4, chunk, chunk - 4)
        second = (chunk >= 4) & (chunk < 8)
        value = qb[:, i * HC : (i + 1) * HC].astype(F32)
        put(pack, QB, jnp.where(second, -1, at), value)
        put(pack, QB + HC, jnp.where(second, at, -1), value)

    def parts(dims):
        lane = lax.broadcasted_iota(jnp.int32, dims, 1)
        index = lane % (HD // 2)
        quarter, eighth = HD // 4, HD // 8
        in_frame = index < quarter
        in_row = (index >= quarter) & (index < quarter + eighth)
        offset = jnp.where(
            in_frame, index, jnp.where(in_row, index - quarter, index - quarter - eighth)
        ).astype(F32)
        length = jnp.where(in_frame, 1.0 * quarter, 1.0 * eighth)
        frequency = jnp.exp(-math.log(10000.0) * offset / length)
        sign = jnp.where(lane % HD < HD // 2, -1.0, 1.0)
        return in_frame, in_row, frequency, sign

    in_frame, in_row, frequency, sign = parts((TOK, HC))
    slot = lax.broadcasted_iota(jnp.int32, (TOK, HC), 0)
    patch = ((slot // PR) ^ row) * PR + slot % PR
    angle = jnp.where(in_row, patch // GRID, patch % GRID).astype(F32) * frequency
    cp[...] = jnp.where(in_frame, 0.0, jnp.cos(angle))
    sp[...] = jnp.where(in_frame, 0.0, jnp.sin(angle) * sign)
    in_frame, _, frequency, sign = parts((16, HC))
    slot = lax.broadcasted_iota(jnp.int32, (16, HC), 0)
    place = pos_ref[0] - PREV + (slot - FPD)
    for f in range(FPD):
        place = jnp.where(slot == f, pos_ref[f], place)
    angle = place.astype(F32) * frequency
    frames[:, :HC] = jnp.where(in_frame, jnp.cos(angle), 0.0)
    frames[:, HC:] = jnp.where(in_frame, jnp.sin(angle) * sign, 0.0)


def prepare(row, places, noise, ada, biases):
    return pl.pallas_call(
        prepare_kernel,
        out_shape=[
            shape((FPD, WIDE), F32),
            shape((FPD, HC)),
            shape((TOK, HC), F32),
            shape((TOK, HC), F32),
            shape((16, 2 * HC), F32),
        ],
        grid_spec=pltpu.PrefetchScalarGridSpec(
            num_scalar_prefetch=2,
            grid=(1,),
            in_specs=[whole((FPD, D)), whole((HC, 6 * D))]
            + [whole((1, b.shape[0])) for b in biases],
            out_specs=[
                whole((FPD, WIDE)),
                whole((FPD, HC)),
                whole((TOK, HC)),
                whole((TOK, HC)),
                whole((16, 2 * HC)),
            ],
        ),
        compiler_params=params(24),
        cost_estimate=cost(2 * 8 * HC * 6 * D, 4 * MB, 4 * TOK * HC),
        name="prepare",
    )(row, places, noise, ada, *[b[None] for b in biases])


def split_heads_kernel(row_ref, q, k, v, p0, p1, p23):
    for j, p in enumerate((p0, p1, p23.at[0], p23.at[1])):

        @pl.when(pl.program_id(0) == j)
        def _():
            p[:, :HC] = q[...]
            p[:, HC : 2 * HC] = k[...]
            p[:, 2 * HC :] = v[...]


def split_heads(row, weight):
    piece = (HC, 3 * HC)
    return pl.pallas_call(
        split_heads_kernel,
        out_shape=[shape(piece), shape(piece), shape((2,) + piece)],
        grid_spec=pltpu.PrefetchScalarGridSpec(
            num_scalar_prefetch=1,
            grid=(4,),
            in_specs=[
                pl.BlockSpec((HC, HC), lambda j, row, s=s: (0, 4 * s + (row[0] ^ j)))
                for s in range(3)
            ],
            out_specs=[whole(piece), whole(piece), whole((2,) + piece)],
        ),
        compiler_params=params(12),
        cost_estimate=cost(0, 3 * MB),
        name="split_heads",
    )(row, weight, weight, weight)


def cosines(cp, sp, frames, at):
    both = frames[pl.ds(at, 1), :]
    return cp[...] + both[:, :HC], sp[...] + both[:, HC:]


def project_kernel(own, row_ref, x0, x1, x2, x3, table, mods, w0, w1, w2, w3, cp, sp, fr, *outs):
    row = row_ref[0]
    f = pl.program_id(0)
    if own:
        h_ref, q_ref, k_ref, v_ref = outs
        first, at, angle = 0, f, f
    else:
        k_ref, v_ref, h_ref = outs
        first, at, angle = HC, f + FPD - PREV, f + FPD
    x = jnp.concatenate([r[0] for r in (x0, x1, x2, x3)], axis=0).astype(F32)
    normal, _ = norm(x)
    shift_row = mods[pl.ds(at, 1), :D]
    scale_row = mods[pl.ds(at, 1), D : 2 * D]
    hidden = (normal * (1.0 + scale_row) + shift_row).astype(BF16)
    where = (0,) if own else ()
    h_ref[where + (slice(None), slice(None))] = hidden
    low, high = table[pl.ds(row, 1), QB : QB + 2 * HC], table[pl.ds(row + 4, 1), QB : QB + HC]
    total = jnp.concatenate([low, high], axis=1)[:, first:]
    for j, w in enumerate((w0, w1, w2, w3)):
        total = total + nn(h_ref[where + (slice(None), columns(row, j))], w[:, first:])
    cosine, sine = cosines(cp, sp, fr, angle)
    if own:
        q_ref[0] = (turn(total[:, :HC], cosine, sine).astype(BF16).astype(F32) * 0.125).astype(BF16)
        total = total[:, HC:]
    k_ref[0] = turn(total[:, :HC], cosine, sine).astype(BF16)
    v_ref[0] = total[:, HC:].astype(BF16)


def project(own, row, xs, table, mods, weights, tables):
    frames = xs[0].shape[0]
    x_spec = pl.BlockSpec((1, PR, D), lambda f, *_: (f, 0, 0))
    out_spec = pl.BlockSpec((1, TOK, HC), lambda f, *_: (f, 0, 0))
    out = shape((frames, TOK, HC))
    if own:
        out_specs = [pl.BlockSpec((1, TOK, D), lambda f, *_: (f, 0, 0)), out_spec, out_spec, out_spec]
        out_shape = [shape((frames, TOK, D)), out, out, out]
        scratch = []
    else:
        out_specs = [out_spec, out_spec]
        out_shape = [out, out]
        scratch = [pltpu.VMEM((TOK, D), BF16)]
    return pl.pallas_call(
        lambda *refs: project_kernel(own, *refs),
        out_shape=out_shape,
        grid_spec=pltpu.PrefetchScalarGridSpec(
            num_scalar_prefetch=1,
            grid=(frames,),
            in_specs=[x_spec] * 4
            + [whole((FPD, WIDE)), whole(mods.shape)]
            + [whole((HC, 3 * HC))] * 4
            + [whole((TOK, HC)), whole((TOK, HC)), whole((16, 2 * HC))],
            out_specs=out_specs,
            scratch_shapes=scratch,
        ),
        compiler_params=params(20),
        cost_estimate=cost(2 * frames * TOK * D * 3 * HC, frames * TOK * D * 4 + 4 * MB),
        name="project_own" if own else "project_prev",
    )(row, *xs, table, mods, *weights, *tables)


def head_lanes():
    return lax.broadcasted_iota(jnp.int32, (TOK, HC), 1) // HD


def attend_kernel(pos_ref, q, k, v, kp, vp, o0, o1, o23, lse, qs, scores, acc, top, low):
    f = pl.program_id(0)
    place = pos_ref[f]
    lanes = head_lanes()
    query = q[0]
    for h in range(4):
        qs[pl.ds(h * TOK, TOK), :] = jnp.where(lanes == h, query, jnp.zeros_like(query))
    top[...] = jnp.full_like(top, -1e30)
    low[...] = jnp.zeros_like(low)
    acc[...] = jnp.zeros_like(acc)
    before = jnp.maximum(place - f, 0)
    start = jnp.maximum(f - place, 0)

    def score(keys, slot):
        for h in range(4):
            rows = pl.ds(h * TOK, TOK)
            s = nt(qs[rows, :], keys)
            scores[slot, rows, :] = s
            top[rows, :] = jnp.maximum(top[rows, :], jnp.maximum(s[:, :128], s[:, 128:]))

    def mix(values, slot):
        for h in range(4):
            rows = pl.ds(h * TOK, TOK)
            p = jnp.exp(scores[slot, rows, :] - jnp.concatenate([top[rows, :]] * 2, axis=1))
            low[rows, :] = low[rows, :] + (p[:, :128] + p[:, 128:])
            acc[rows, :] = acc[rows, :] + nn(p.astype(BF16), values)

    def run(step):
        def prev(i, _):
            at = PREV - before + i
            step(kp[at] if step is score else vp[at], i)
            return 0

        def own(g, _):
            step(k[g] if step is score else v[g], g - f + place)
            return 0

        lax.fori_loop(0, before, prev, 0)
        lax.fori_loop(start, f + 1, own, 0)

    run(score)
    for h in range(4):
        rows = pl.ds(h * TOK, TOK)
        top[rows, :] = jnp.broadcast_to(jnp.max(top[rows, :], axis=1, keepdims=True), (TOK, 128))
    run(mix)
    result = jnp.zeros((TOK, HC), F32)
    logs = jnp.zeros((TOK, 128), F32)
    narrow = lax.broadcasted_iota(jnp.int32, (TOK, 128), 1)
    for h in range(4):
        rows = pl.ds(h * TOK, TOK)
        total = jnp.sum(low[rows, :], axis=1, keepdims=True)
        result = jnp.where(lanes == h, acc[rows, :] / total, result)
        logs = jnp.where(narrow == h, top[rows, :] + jnp.log(total), logs)
    lse[0] = logs.T[:8]
    result = result.astype(BF16)
    o0[0] = result[:PR]
    o1[0] = result[PR : 2 * PR]
    o23[0, 0] = result[2 * PR : 3 * PR]
    o23[1, 0] = result[3 * PR :]


def attend(places, q, k, v, kp, vp):
    block = pl.BlockSpec((1, TOK, HC), lambda f, *_: (f, 0, 0))
    piece = pl.BlockSpec((1, PR, HC), lambda f, *_: (f, 0, 0))
    return pl.pallas_call(
        attend_kernel,
        out_shape=[shape((FPD, PR, HC))] * 2
        + [shape((2, FPD, PR, HC)), shape((FPD, 8, TOK), F32)],
        grid_spec=pltpu.PrefetchScalarGridSpec(
            num_scalar_prefetch=1,
            grid=(FPD,),
            in_specs=[block]
            + [whole((FPD, TOK, HC))] * 2
            + [whole((PREV, TOK, HC))] * 2,
            out_specs=[piece] * 2
            + [
                pl.BlockSpec((2, 1, PR, HC), lambda f, *_: (0, f, 0, 0)),
                pl.BlockSpec((1, 8, TOK), lambda f, *_: (f, 0, 0)),
            ],
            scratch_shapes=[
                pltpu.VMEM((4 * TOK, HC), BF16),
                pltpu.VMEM((8, 4 * TOK, TOK), F32),
                pltpu.VMEM((4 * TOK, HC), F32),
                pltpu.VMEM((4 * TOK, 128), F32),
                pltpu.VMEM((4 * TOK, 128), F32),
            ],
        ),
        compiler_params=params(58),
        cost_estimate=cost(36 * 4 * 2 * 2 * TOK**3, 6 * MB, 36 * 4 * TOK * TOK),
        name="attend",
    )(places, q, k, v, kp, vp)


def attend_back_kernel(own, pos_ref, q, k, v, g0, g1, g2, g3, o0, o1, o23, lse, *rest):
    if own:
        cp, sp, fr, before_ref, dq, dk, dv, qs, gs, ks, pl_scr, dl_scr, ds_scr, dq_acc = rest
        dk_acc, dv_acc = dk, dv
    else:
        dq, both_ref, qs, gs, ks, pl_scr, dl_scr, ds_scr, dq_acc, dk_acc, dv_acc = rest
    f = pl.program_id(0)
    place = pos_ref[f]
    lanes = head_lanes()

    @pl.when(f == 0)
    def _():
        for ref in (dk_acc, dv_acc):
            ref[...] = jnp.zeros_like(ref)

    def prelude():
        query = q[0]
        grad = jnp.concatenate([r[0] for r in (g0, g1, g2, g3)], axis=0)
        mixed = jnp.concatenate([o0[0], o1[0], o23[0, 0], o23[1, 0]], axis=0)
        for h in range(4):
            rows = pl.ds(h * TOK, TOK)
            qs[rows, :] = jnp.where(lanes == h, query, jnp.zeros_like(query))
            gs[rows, :] = jnp.where(lanes == h, grad, jnp.zeros_like(grad))
        both = grad.astype(F32) * mixed.astype(F32)
        pick = (
            lax.broadcasted_iota(jnp.int32, (8, HC), 1) // HD
            == lax.broadcasted_iota(jnp.int32, (8, HC), 0)
        ).astype(F32)
        return lax.dot_general(
            pick, both, (((1,), (1,)), ((), ())),
            preferred_element_type=F32, precision=lax.Precision.HIGHEST,
        )

    def step(delta, logs, at):
        keys, values = k[at], v[at]
        for h in range(4):
            rows = pl.ds(h * TOK, TOK)
            ks[rows, :] = jnp.where(lanes == h, keys, jnp.zeros_like(keys))
            p = jnp.exp(nt(keys, qs[rows, :]) - logs[h : h + 1])
            ds = (p * (nt(values, gs[rows, :]) - delta[h : h + 1])).astype(BF16)
            pl_scr[:, rows] = p.astype(BF16)
            dl_scr[:, rows] = ds
            ds_scr[rows, :] = ds
        dv_acc[at] = dv_acc[at] + nn(pl_scr[...], gs[...])
        dk_acc[at] = dk_acc[at] + nn(dl_scr[...], qs[...])
        dq_acc[...] = dq_acc[...] + tn(ds_scr[...], ks[...])

    def sweep(low, high):
        delta = prelude()
        logs = lse[0]
        dq_acc[...] = jnp.zeros_like(dq_acc)

        def one(at, _):
            step(delta, logs, at)
            return 0

        lax.fori_loop(low, high, one, 0)

    if own:
        sweep(jnp.maximum(f - place, 0), f + 1)
        cosine, sine = cosines(cp, sp, fr, f)
        dq[0] = turn((dq_acc[...] + before_ref[0]) * 0.125, cosine, -sine).astype(BF16)
    else:
        count = jnp.maximum(place - f, 0)

        @pl.when(count > 0)
        def _():
            sweep(PREV - count, PREV)
            dq[0] = dq_acc[...]

        @pl.when(count == 0)
        def _():
            dq[0] = jnp.zeros_like(dq_acc)

        @pl.when(f == FPD - 1)
        def _():
            both_ref[0] = dk_acc[...].astype(BF16)
            both_ref[1] = dv_acc[...].astype(BF16)


def attend_back(own, places, q, k, v, grads, mixed, lse, tables=None, before=None):
    block = pl.BlockSpec((1, TOK, HC), lambda f, *_: (f, 0, 0))
    piece = pl.BlockSpec((1, PR, HC), lambda f, *_: (f, 0, 0))
    count = FPD if own else PREV
    wide = pltpu.VMEM((4 * TOK, HC), BF16)
    tall = pltpu.VMEM((TOK, 4 * TOK), BF16)
    scratch = [wide, wide, wide, tall, tall, wide, pltpu.VMEM((TOK, HC), F32)]
    specs = []
    extra = ()
    if own:
        specs = [whole((TOK, HC)), whole((TOK, HC)), whole((16, 2 * HC)), block]
        extra = tuple(tables) + (before,)
    else:
        scratch += [pltpu.VMEM((PREV, TOK, HC), F32)] * 2
    return pl.pallas_call(
        lambda *refs: attend_back_kernel(own, *refs),
        out_shape=[shape((FPD, TOK, HC), BF16 if own else F32)]
        + ([shape((FPD, TOK, HC), F32)] * 2 if own else [shape((2, PREV, TOK, HC))]),
        grid_spec=pltpu.PrefetchScalarGridSpec(
            num_scalar_prefetch=1,
            grid=(FPD,),
            in_specs=[block]
            + [whole((count, TOK, HC))] * 2
            + [piece] * 6
            + [pl.BlockSpec((2, 1, PR, HC), lambda f, *_: (0, f, 0, 0))]
            + [pl.BlockSpec((1, 8, TOK), lambda f, *_: (f, 0, 0))]
            + specs,
            out_specs=[block]
            + ([whole((FPD, TOK, HC))] * 2 if own else [whole((2, PREV, TOK, HC))]),
            scratch_shapes=scratch,
        ),
        compiler_params=params(58),
        cost_estimate=cost(1000 if own else 12 * 4 * 5 * 2 * TOK**3, 1000 if own else 12 * MB),
        name="attend_back_own" if own else "attend_back_prev",
    )(places, q, k, v, *grads, *mixed, lse, *extra)


HALF = 4
RAW = HALF * PR


def flat(ref):
    return ref[...].reshape(RAW, ref.shape[-1])


def frames_of(value):
    return value.reshape(HALF, PR, value.shape[-1])


def segment(table, s):
    both = table[:, s * D : (s + 1) * D]
    return jnp.where(pl.program_id(0) == 0, both[:HALF], both[HALF:])[:, None, :]


def fold(out, start, width, row):
    @pl.when(pl.program_id(0) == 0)
    def _():
        out[:, start : start + width] = jnp.zeros((8, width), F32)

    for i in range(8):
        at = (slice(i, i + 1), slice(start, start + width))
        out[at] = out[at] + row[:, i * width : (i + 1) * width]


def mid_kernel(o0, o1, o2, o3, w0, w1, w2, w3, table, x, cot, branch, middle, hidden, down, dsum):
    total = unfold(table, OB, 128)
    for o, w in zip((o0, o1, o2, o3), (w0, w1, w2, w3)):
        total = total + nn(flat(o), w[...])
    branched = frames_of(total)
    branch[...] = branched
    mid_value = x[...].astype(F32) + segment(table, 2) * branched
    middle[...] = mid_value
    normal, _ = norm(mid_value)
    hidden[...] = (normal * (1.0 + segment(table, 4)) + segment(table, 3)).astype(BF16)
    grad = (segment(table, 5) * cot[...].astype(F32)).astype(BF16)
    down[...] = grad
    fold(dsum, 0, 128, jnp.sum(grad.astype(F32).reshape(RAW, D), axis=0, keepdims=True))


def half_spec(width):
    return pl.BlockSpec((HALF, PR, width), lambda i, *_: (i, 0, 0))


def mid(pieces, weights, table, x, cot):
    return pl.pallas_call(
        mid_kernel,
        out_shape=[
            shape((FPD, PR, D), F32),
            shape((FPD, PR, D), F32),
            shape((FPD, PR, D)),
            shape((FPD, PR, D)),
            shape((8, 128), F32),
        ],
        grid=(FPD // HALF,),
        in_specs=[half_spec(HC)] * 4
        + [whole((HC, D))] * 4
        + [whole((FPD, WIDE)), half_spec(D), half_spec(D)],
        out_specs=[half_spec(D)] * 4 + [whole((8, 128))],
        compiler_params=params(26),
        cost_estimate=cost(2 * 512 * D * D, 12 * MB),
        name="mid",
    )(*pieces, *weights, table, x, cot)


def mid_back_kernel(hg, middle, branch, cot, table, w0, w1, w2, w3, mg, bg, a0, a1, a23, sums):
    grad = hg[...]
    normal, rate = norm(middle[...])
    put_half(sums, D, jnp.sum(grad, axis=1))
    put_half(sums, 2 * D, jnp.sum(grad * normal, axis=1))
    total = cot[...].astype(F32) + norm_back(normal, rate, grad * (1.0 + segment(table, 4)))
    mg[...] = total
    put_half(sums, 0, jnp.sum(total * branch[...], axis=1))
    low = (segment(table, 2) * total).astype(BF16)
    bg[...] = low
    low = low.reshape(RAW, D)
    fold(sums, 3 * D, 128, jnp.sum(low.astype(F32), axis=0, keepdims=True))
    for j, w in enumerate((w0, w1, w2, w3)):
        value = frames_of(nt(low, w[...]).astype(BF16))
        if j < 2:
            (a0, a1)[j][...] = value
        else:
            a23[j - 2] = value


def mid_back(hg, middle, branch, cot, table, weights):
    return pl.pallas_call(
        mid_back_kernel,
        out_shape=[shape((FPD, PR, D), F32), shape((FPD, PR, D))]
        + [shape((FPD, PR, HC))] * 2
        + [shape((2, FPD, PR, HC)), shape((8, 3 * D + 128), F32)],
        grid=(FPD // HALF,),
        in_specs=[half_spec(D)] * 4
        + [whole((FPD, WIDE))]
        + [whole((HC, D))] * 4,
        out_specs=[half_spec(D)] * 2
        + [half_spec(HC)] * 2
        + [pl.BlockSpec((2, HALF, PR, HC), lambda i: (0, i, 0, 0)), whole((8, 3 * D + 128))],
        compiler_params=params(26),
        cost_estimate=cost(2 * 512 * D * D, 12 * MB),
        name="mid_back",
    )(hg, middle, branch, cot, table, *weights)


NB = 512
STEPS = FF // NB
PER = D // NB
TOKENS = FPD * PR


def block_of(t):
    phase = t // PER
    return ((phase % 2) * 2) ^ (phase // 2)


def up_column(t, row):
    return (row ^ block_of(t)) * PER + t % PER


def down_row(t):
    return block_of(t) * PER + t % PER


def down_spec(j):
    phase = (0, 2, 1, 3)[j]
    return pl.BlockSpec((NB, D), lambda t, row: (jnp.clip(t - phase * PER, 0, PER - 1), 0))


def pick_down(d0, d1, d2, d3):
    phase = pl.program_id(0) // PER
    return jnp.where(
        phase < 2,
        jnp.where(phase == 0, d0[...], d2[...]),
        jnp.where(phase == 2, d1[...], d3[...]),
    )


def feed_kernel(row_ref, h2, dg, u0, u1, u2, u3, table, d0, d1, d2, d3, act, upg, hg, usum):
    row = row_ref[0]
    ups = (u0, u1, u2, u3)
    down = pick_down(d0, d1, d2, d3)
    at = pl.ds(up_column(pl.program_id(0), row), 1)
    u = table[at, UB : UB + NB]
    for j, w in enumerate(ups):
        u = u + nn(h2[:, columns(row, j)], w[...])
    rate = math.sqrt(2.0 / math.pi)
    square = u * u
    half = 0.5 + 0.5 * jnp.tanh(u * (rate + (rate * 0.044715) * square))
    active = u * half
    act[...] = active.astype(BF16)
    slope = half + active * (1.0 - half) * (2.0 * rate + (6.0 * rate * 0.044715) * square)
    grad = (nt(dg[...], down) * slope).astype(BF16)
    upg[...] = grad
    put(usum, 0, up_column(pl.program_id(0), row), jnp.sum(grad.astype(F32), axis=0, keepdims=True))

    @pl.when(pl.program_id(0) == 0)
    def _():
        hg[...] = jnp.zeros_like(hg)

    for j, w in enumerate(ups):
        hg[:, columns(row, j)] = hg[:, columns(row, j)] + nt(grad, w[...])


def feed(row, h2, dg, ups, table, downs):
    tok = whole((TOKENS, D))
    block = pl.BlockSpec((TOKENS, NB), lambda t, row: (0, t))
    return pl.pallas_call(
        feed_kernel,
        out_shape=[
            shape((TOKENS, FF)),
            shape((TOKENS, FF)),
            shape((TOKENS, D), F32),
            shape((8, NB), F32),
        ],
        grid_spec=pltpu.PrefetchScalarGridSpec(
            num_scalar_prefetch=1,
            grid=(STEPS,),
            in_specs=[tok, tok]
            + [pl.BlockSpec((HC, NB), lambda t, row: (0, up_column(t, row[0])))] * 4
            + [whole((FPD, WIDE))]
            + [down_spec(j) for j in range(4)],
            out_specs=[block, block, tok, whole((8, NB))],
        ),
        compiler_params=params(58),
        cost_estimate=cost(3 * 2 * TOKENS * D * FF, 30 * MB, TOKENS * FF),
        name="feed",
    )(row, h2, dg, *ups, table, *downs)


def down_weight_kernel(row_ref, dg, act, d0, d1, d2, d3, table, middle, cot, dk, ds, out, gate, dn):
    t = pl.program_id(0)
    down = pick_down(d0, d1, d2, d3)
    active = act[...]

    @pl.when(t == 0)
    def _():
        dn[...] = jnp.zeros_like(dn)

    dn[...] = dn[...] + nn(active, down)
    part = tn(active, dg[...]).astype(BF16)

    @pl.when(t < STEPS // 2)
    def _():
        dk[0] = part

    @pl.when(t >= STEPS // 2)
    def _():
        ds[0] = part

    @pl.when(t == STEPS - 1)
    def _():
        bias = unfold(table, DB, 128)
        for f in range(FPD):
            rows = slice(f * PR, (f + 1) * PR)
            value = dn[rows, :] + bias
            out[f] = (middle[f] + table[f : f + 1, 5 * D : 6 * D] * value).astype(BF16)
            gate[f : f + 1, :] = jnp.sum(cot[f].astype(F32) * value, axis=0, keepdims=True)


def down_weight_grad(row, dg, act, downs, table, middle, cot):
    tok = whole((TOKENS, D))
    full = whole((FPD, PR, D))
    block = pl.BlockSpec((TOKENS, NB), lambda t, row: (0, t))

    def down_out(first):
        def index(t, row):
            at = jnp.clip(t - first, 0, STEPS // 2 - 1)
            return (at // PER, at % PER, 0)

        return pl.BlockSpec((1, NB, D), index)

    return pl.pallas_call(
        down_weight_kernel,
        out_shape=[shape((2, D, D))] * 2 + [shape((FPD, PR, D)), shape((8, D), F32)],
        grid_spec=pltpu.PrefetchScalarGridSpec(
            num_scalar_prefetch=1,
            grid=(STEPS,),
            in_specs=[tok, block]
            + [down_spec(j) for j in range(4)]
            + [whole((FPD, WIDE)), full, full],
            out_specs=[down_out(0), down_out(STEPS // 2), full, whole((8, D))],
            scratch_shapes=[pltpu.VMEM((TOKENS, D), F32)],
        ),
        compiler_params=params(58),
        cost_estimate=cost(2 * 2 * TOKENS * D * FF, 24 * MB),
        name="down_weight_grad",
    )(row, dg, act, *downs, table, middle, cot)


def up_weight_kernel(row_ref, h2, upg, uk, us):
    row = row_ref[0]
    grad = upg[...]
    for j, ref in enumerate((uk, us, uk, us)):
        ref[j // 2, 0] = tn(h2[:, columns(row, j)], grad).astype(BF16)


def up_weight_grad(row, h2, upg):
    up_out = pl.BlockSpec(
        (2, 1, HC, NB),
        lambda t, row: (0, up_column(t, row[0]) // PER, 0, up_column(t, row[0]) % PER),
    )
    return pl.pallas_call(
        up_weight_kernel,
        out_shape=[shape((2, 4, HC, D))] * 2,
        grid_spec=pltpu.PrefetchScalarGridSpec(
            num_scalar_prefetch=1,
            grid=(STEPS,),
            in_specs=[whole((TOKENS, D)), pl.BlockSpec((TOKENS, NB), lambda t, row: (0, t))],
            out_specs=[up_out, up_out],
        ),
        compiler_params=params(58),
        cost_estimate=cost(2 * TOKENS * D * FF, 14 * MB),
        name="up_weight_grad",
    )(row, h2, upg)


def out_weight_kernel(t0, t1, t2, t3, bg, keep, send):
    grad = bg[...].reshape(TOKENS, D)
    for j, t in enumerate((t0, t1, t2, t3)):
        ref = (keep, send)[j % 2]
        ref[j // 2] = tn(t[...].reshape(TOKENS, HC), grad).astype(BF16)


def out_weight_grad(pieces, bg):
    return pl.pallas_call(
        out_weight_kernel,
        out_shape=[shape((2, HC, D))] * 2,
        grid=(1,),
        in_specs=[whole((FPD, PR, HC))] * 4 + [whole((FPD, PR, D))],
        out_specs=[whole((2, HC, D))] * 2,
        compiler_params=params(14),
        cost_estimate=cost(2 * TOKENS * D * D, 4 * MB),
        name="out_weight_grad",
    )(*pieces, bg)


CHUNKS = 16
UP_ROWS, OUT_ROWS, DOWN_ROWS = D // CHUNKS, HC // CHUNKS, D // CHUNKS
FIRST = UP_ROWS + OUT_ROWS
ROWS = FIRST + DOWN_ROWS


def core_sum_kernel(ua, ub, da, db, oa, ob, out):
    def both(a, b):
        return (a.astype(F32) + b.astype(F32)).astype(BF16)

    for c in range(4):
        at = c * ROWS
        low, high = c * OUT_ROWS, (c + 1) * OUT_ROWS
        for i in range(4):
            to = at + i * OUT_ROWS
            out[0, to : to + OUT_ROWS] = both(ua[0, i, low:high], ub[0, i, low:high])
        out[0, at + UP_ROWS : at + FIRST] = both(oa[0, low:high], ob[0, low:high])
        low, high = c * DOWN_ROWS, (c + 1) * DOWN_ROWS
        out[0, at + FIRST : at + ROWS] = both(da[0, low:high], db[0, low:high])


def core_sum(up, down, out):
    ups = pl.BlockSpec((1, 4, 4 * OUT_ROWS, D), lambda j, c: (j, 0, c, 0))
    outs = pl.BlockSpec((1, 4 * OUT_ROWS, D), lambda j, c: (j, c, 0))
    downs = pl.BlockSpec((1, 4 * DOWN_ROWS, D), lambda j, c: (j, c, 0))
    return pl.pallas_call(
        core_sum_kernel,
        out_shape=shape((2, CHUNKS * ROWS, D)),
        grid=(2, CHUNKS // 4),
        in_specs=[ups, ups, downs, downs, outs, outs],
        out_specs=pl.BlockSpec((1, 4 * ROWS, D), lambda j, c: (j, c, 0)),
        compiler_params=params(58),
        cost_estimate=cost(1000, 1000),
        name="core_sum",
    )(*up, *down, *out)


def unpack_kernel(total, up, out, down):
    for k in range(4):
        at = k * ROWS
        for i in range(4):
            rows = slice(at + i * OUT_ROWS, at + (i + 1) * OUT_ROWS)
            up[k * OUT_ROWS : (k + 1) * OUT_ROWS, i * D : (i + 1) * D] = total[rows].astype(F32)
        out[k * OUT_ROWS : (k + 1) * OUT_ROWS] = total[at + UP_ROWS : at + FIRST].astype(F32)
        down[k * DOWN_ROWS : (k + 1) * DOWN_ROWS] = total[at + FIRST : at + ROWS].astype(F32)


def unpack(total):
    block = lambda i: (i, 0)
    return pl.pallas_call(
        unpack_kernel,
        out_shape=[shape((HC, FF), F32), shape((HC, D), F32), shape((D, D), F32)],
        grid=(4,),
        in_specs=[pl.BlockSpec((4 * ROWS, D), block)],
        out_specs=[
            pl.BlockSpec((4 * OUT_ROWS, FF), block),
            pl.BlockSpec((4 * OUT_ROWS, D), block),
            pl.BlockSpec((4 * DOWN_ROWS, D), block),
        ],
        compiler_params=params(24),
        cost_estimate=cost(0, 14 * MB),
        name="unpack",
    )(total)


LATE = 3 * D + 2 * HC
EARLY = 3 * D + NB + 256


def arrange_kernel(row_ref, a0, a1, a2, a3, late, far, out):
    row = row_ref[0]
    for j, a in enumerate((a0, a1, a2, a3)):
        for s in range(3):
            lanes = pl.ds(pl.multiple_of(s * D + (row ^ j) * HC, HC), HC)
            out[:, lanes] = a[:, s * HC : (s + 1) * HC]
    both = jnp.concatenate([late[...].astype(F32), far[...].astype(F32)], axis=0)
    out[:, 3 * D :] = both.astype(BF16)


def arrange(row, pieces, late, far):
    rows = pieces[0].shape[0]
    return pl.pallas_call(
        arrange_kernel,
        out_shape=shape((rows, 3 * D + LATE)),
        grid_spec=pltpu.PrefetchScalarGridSpec(
            num_scalar_prefetch=1,
            grid=(1,),
            in_specs=[whole((rows, 3 * HC))] * 4 + [whole((8, LATE))] * 2,
            out_specs=whole((rows, 3 * D + LATE)),
        ),
        compiler_params=params(16),
        cost_estimate=cost(0, 8 * rows * D),
        name="arrange",
    )(row, *pieces, late, far)


def place_kernel(index_ref, a0, a1, a2, a3, out):
    for m, a in enumerate((a0, a1, a2, a3)):

        @pl.when(pl.program_id(0) == m)
        def _():
            for k in range(4):
                out[0, index_ref[1] ^ k] = a[k, :, : 3 * D].astype(F32)


def place(index, pieces):
    rows = pieces[0].shape[1]
    return pl.pallas_call(
        place_kernel,
        out_shape=shape((4, 4, rows, 3 * D), F32),
        grid_spec=pltpu.PrefetchScalarGridSpec(
            num_scalar_prefetch=1,
            grid=(4,),
            in_specs=[whole(a.shape) for a in pieces],
            out_specs=pl.BlockSpec((1, 4, rows, 3 * D), lambda i, index: (index[0] ^ i, 0, 0, 0)),
        ),
        compiler_params=params(24),
        cost_estimate=cost(0, 24 * rows * D),
        name="place",
    )(index, *pieces).reshape(HC, 3 * D)


def project_back_kernel(row_ref, dq, dk, dv, rk, rv, w0, w1, w2, w3, cp, sp, fr, dp, h0, h2, hs, bsum):
    row = row_ref[0]
    f = pl.program_id(0)
    later = (f > 0).astype(F32)
    keys = dk[0] + later * rk[0, 0].astype(F32)
    values = dv[0] + later * rv[0, 0].astype(F32)
    cosine, sine = cosines(cp, sp, fr, f)
    dp[0, :, :HC] = dq[0]
    dp[0, :, HC : 2 * HC] = turn(keys, cosine, -sine).astype(BF16)
    dp[0, :, 2 * HC :] = values.astype(BF16)
    grad = dp[0]
    sums = jnp.sum(grad.astype(F32), axis=0, keepdims=True)

    @pl.when(f == 0)
    def _():
        bsum[...] = jnp.zeros_like(bsum)

    number = lax.broadcasted_iota(jnp.int32, (8, 2 * HC), 0)
    bsum[...] = bsum[...] + jnp.where(number == row, sums[:, : 2 * HC], 0.0)
    bsum[:, :HC] = bsum[:, :HC] + jnp.where(number[:, :HC] == row + 4, sums[:, 2 * HC :], 0.0)
    for j, w in enumerate((w0, w1, w2, w3)):
        part = nt(grad, w[...]).astype(BF16)
        at = (0, slice(None), columns(row, j))
        h0[at] = part[:PR]
        hs[(0,) + at] = part[PR : 2 * PR]
        h2[at] = part[2 * PR : 3 * PR]
        hs[(1,) + at] = part[3 * PR :]


def project_back(row, dq, dk, dv, returned, weights, tables):
    block = pl.BlockSpec((1, TOK, HC), lambda f, *_: (f, 0, 0))
    late = [
        pl.BlockSpec((1, 1, TOK, HC), lambda f, *_, i=i: (i, jnp.maximum(f - 1, 0), 0, 0))
        for i in range(2)
    ]
    piece = pl.BlockSpec((1, PR, D), lambda f, *_: (f, 0, 0))
    return pl.pallas_call(
        project_back_kernel,
        out_shape=[
            shape((FPD, TOK, 3 * HC)),
            shape((FPD, PR, D)),
            shape((FPD, PR, D)),
            shape((2, FPD, PR, D)),
            shape((8, 2 * HC), F32),
        ],
        grid_spec=pltpu.PrefetchScalarGridSpec(
            num_scalar_prefetch=1,
            grid=(FPD,),
            in_specs=[block] * 3
            + late
            + [whole((HC, 3 * HC))] * 4
            + [whole((TOK, HC)), whole((TOK, HC)), whole((16, 2 * HC))],
            out_specs=[
                pl.BlockSpec((1, TOK, 3 * HC), lambda f, *_: (f, 0, 0)),
                piece,
                piece,
                pl.BlockSpec((2, 1, PR, D), lambda f, *_: (0, f, 0, 0)),
                whole((8, 2 * HC)),
            ],
        ),
        compiler_params=params(20),
        cost_estimate=cost(2 * FPD * TOK * D * 3 * HC, 14 * MB),
        name="project_back",
    )(row, dq, dk, dv, returned, returned, *weights, *tables)


def weight_kernel(row_ref, h, dp, w):
    w[0] = tn(h[...], dp[...]).astype(BF16)


def project_weight(row, hidden, dproj):
    tokens = FPD * TOK
    return pl.pallas_call(
        weight_kernel,
        out_shape=shape((4, HC, 3 * HC)),
        grid_spec=pltpu.PrefetchScalarGridSpec(
            num_scalar_prefetch=1,
            grid=(4,),
            in_specs=[
                pl.BlockSpec((tokens, HC), lambda j, row: (0, row[0] ^ j)),
                whole((tokens, 3 * HC)),
            ],
            out_specs=pl.BlockSpec((1, HC, 3 * HC), lambda j, row: (j, 0, 0)),
        ),
        compiler_params=params(20),
        cost_estimate=cost(2 * tokens * D * 3 * HC, 9 * MB),
        name="project_weight",
    )(row, hidden.reshape(tokens, D), dproj.reshape(tokens, 3 * HC))


def input_back_kernel(x, h0, near, far, table, mg, bsum, gate, out, sums):
    grad = h0[...].astype(F32) + near[0].astype(F32) + far[...].astype(F32)
    normal, rate = norm(x[...].astype(F32))
    put_half(sums, 0, jnp.sum(grad, axis=1))
    put_half(sums, D, jnp.sum(grad * normal, axis=1))
    sums[:, 2 * D : 3 * D] = gate[...]
    sums[:, 3 * D :] = bsum[...]
    out[...] = mg[...] + norm_back(normal, rate, grad * (1.0 + segment(table, 1)))


def input_back(x, h0, near, far, table, mg, bsum, gate):
    return pl.pallas_call(
        input_back_kernel,
        out_shape=[shape((FPD, PR, D), F32), shape((8, LATE), F32)],
        grid=(FPD // HALF,),
        in_specs=[half_spec(D)] * 2
        + [pl.BlockSpec((1, HALF, PR, D), lambda i: (0, i, 0, 0))]
        + [half_spec(D), whole((FPD, WIDE)), half_spec(D), whole((8, 2 * HC)), whole((8, D))],
        out_specs=[half_spec(D), whole((8, LATE))],
        compiler_params=params(20),
        cost_estimate=cost(20 * 512 * D, 10 * MB),
        name="input_back",
    )(x, h0, near, far, table, mg, bsum, gate)


def early_kernel(m, u, d, out):
    out[:, : 3 * D] = m[:, : 3 * D]
    out[:, 3 * D : 3 * D + NB] = u[...]
    out[:, 3 * D + NB : 3 * D + NB + 128] = d[...]
    out[:, 3 * D + NB + 128 :] = m[:, 3 * D :]


def early_sums(sums, usum, dsum):
    return pl.pallas_call(
        early_kernel,
        out_shape=shape((8, EARLY), F32),
        grid=(1,),
        in_specs=[whole(a.shape) for a in (sums, usum, dsum)],
        out_specs=whole((8, EARLY)),
        cost_estimate=cost(0, MB),
        name="early_sums",
    )(sums, usum, dsum)


def final_kernel(row_ref, *refs):
    row = row_ref[0]
    late, early = refs[:4], refs[4:8]
    ada, ab, qb, ob, ub, db, asum = refs[8:]

    def rows(ref, cols):
        value = ref[:, :, cols].astype(F32)
        return value.reshape(64, value.shape[-1])

    late = [ref.at[:, :, 3 * D :] for ref in late]
    left = [rows(s, slice(EARLY, EARLY + HC)).astype(BF16) for s in early]
    for segment in range(6):
        source, start = ((late, 0), (late, 1), (early, 0), (early, 1), (early, 2), (late, 2))[segment]
        cols = slice(start * D, (start + 1) * D)
        product, total = 0.0, 0.0
        for s, ref in zip(left, source):
            right = rows(ref, cols)
            total = total + jnp.sum(right, axis=0, keepdims=True)
            product = product + tn(s, right.astype(BF16))
        at = segment * D
        ada[:, at : at + D] = product
        asum[0:1, at : at + D] = total

    def fold8(value):
        value = jnp.sum(value, axis=0)
        return value if value.shape[0] == 8 else value[:8] + value[8:]

    def bias(source, start, stop):
        return sum(
            fold8(ref[:, :, start:stop].astype(F32)) for ref in source
        )

    ab[...] = asum[0:1, pl.ds(pl.multiple_of(row * 1536, 512), 1536)]
    folded = bias(late, 3 * D, LATE)
    for i in range(3):
        chunk = 3 * row + i
        at = jnp.where(chunk < 4, chunk, chunk - 4)
        second = (chunk >= 4) & (chunk < 8)
        value = jnp.where(second, folded[:, HC:], folded[:, :HC])
        qb[:, i * HC : (i + 1) * HC] = take(value, at)
    folded = bias(early, 3 * D, EARLY)
    for i in range(2):
        at = 2 * row + i
        ub[:, i * NB : (i + 1) * NB] = take(folded[:, :NB], at)
        db[:, i * 128 : (i + 1) * 128] = take(folded[:, NB : NB + 128], at)
        ob[:, i * 128 : (i + 1) * 128] = take(folded[:, NB + 128 :], at)


def final_sums(row, late, early):
    sizes = (1536, 768, 256, 1024, 256)
    return pl.pallas_call(
        final_kernel,
        out_shape=[shape((HC, 6 * D), F32)] + [shape((1, n), F32) for n in sizes],
        grid_spec=pltpu.PrefetchScalarGridSpec(
            num_scalar_prefetch=1,
            grid=(1,),
            in_specs=[whole((4, 16, 3 * D + LATE))] * 4
            + [whole((8, 8, EARLY + HC))] * 4,
            out_specs=[whole((HC, 6 * D))] + [whole((1, n)) for n in sizes],
            scratch_shapes=[pltpu.VMEM((8, 6 * D), F32)],
        ),
        compiler_params=params(28),
        cost_estimate=cost(2 * 256 * HC * 6 * D, 10 * MB),
        name="final_sums",
    )(row, *late, *early)


def row_sum(value):
    value = value + swap(value, CORE)
    return value + swap(value, DIRECT)


def row_pieces(value):
    return [value, swap(value, CORE), swap(value, DIRECT), swap(value, DIRECT ^ CORE)]


def by_row(pieces, row):
    a, b, c, d = pieces
    odd, high = row % 2 == 1, row >= 2
    a, b = jnp.where(odd, b, a), jnp.where(odd, a, b)
    c, d = jnp.where(odd, d, c), jnp.where(odd, c, d)
    return jnp.stack(
        [
            jnp.where(high, c, a),
            jnp.where(high, d, b),
            jnp.where(high, a, c),
            jnp.where(high, b, d),
        ]
    )


def quarter_rows(value, bit, index, axis):
    rows = value.shape[1] // 4
    at = lambda m: lax.dynamic_slice_in_dim(value, (index[axis] ^ m) * rows, rows, 1)
    return [at(0)] + [swap(at(m), bit * m) for m in (1, 2, 3)]


def add_all(parts):
    return sum(part.astype(F32) for part in parts).astype(BF16)


def exchange_rows(value, bit, index, axis):
    return add_all(quarter_rows(value, bit, index, axis))


def turn_heads(own, beside, across, order=lambda piece: piece):
    across = swap(across, DIRECT)
    return [own, swap(beside, CORE), across[0], swap(order(across)[1], CORE)]


def per_device(
    activations,
    noise_embed,
    frame_position,
    cotangent,
    ada_weight,
    ada_bias,
    qkv_weight,
    qkv_bias,
    out_weight,
    out_bias,
    up_weight,
    up_bias,
    down_weight,
    down_bias,
):
    row = lax.axis_index(("xl", "c")).astype(jnp.int32)
    row_arg = row.reshape(1)
    index = [lax.axis_index("y").astype(jnp.int32), lax.axis_index("z").astype(jnp.int32)]
    index_arg = jnp.stack(index)

    x0 = activations
    x2 = swap(x0, DIRECT)
    x1 = swap(x0, CORE)
    p0 = shift(activations[1:], 1)
    biases = (ada_bias, qkv_bias, out_bias, up_bias, down_bias)
    heads = list(split_heads(row_arg, qkv_weight))
    noise, heads[1] = lax.optimization_barrier((noise_embed, heads[1]))
    part, silu_own, *tables = prepare(row_arg, frame_position, noise, ada_weight, biases)
    across = swap(heads[2], OTHER)
    qkv_pieces = [heads[0], swap(heads[1], CORE), across]
    part = part + swap(part, CORE)
    table = part + swap(part, DIRECT)
    x2, p0, table, *qkv_pieces = lax.optimization_barrier((x2, p0, table, *qkv_pieces))

    qkv_pieces = qkv_pieces[:2] + [qkv_pieces[2][0], swap(qkv_pieces[2][1], CORE)]
    x3 = swap(x2, CORE)
    p2 = swap(p0, DIRECT)
    p1 = swap(p0, CORE)
    before_mods = shift(table[:, : 2 * D], 1)

    out_own, up_own, _ = lax.optimization_barrier((out_weight, up_weight, table))
    outs2 = swap(out_own, OTHER)
    ups2 = swap(up_own, OTHER)

    hidden1, q, k, v = project(True, row_arg, (x0, x1, x2, x3), table, table, qkv_pieces, tables)
    p2, down_own, q, before_mods = lax.optimization_barrier((p2, down_weight, q, before_mods))
    p3 = swap(p2, CORE)
    downs2 = swap(down_own, DIRECT)
    kp, vp = project(
        False, row_arg, (p0, p1, p2, p3), table, before_mods, qkv_pieces, tables
    )
    *mixed, lse = attend(frame_position, q, k, v, kp, vp)
    outs2, ups2, downs2, lse = lax.optimization_barrier((outs2, ups2, downs2, lse))
    outs = [out_weight, swap(out_own, CORE), outs2, swap(outs2, CORE)]
    ups = [up_weight, swap(up_own, CORE), ups2, swap(ups2, CORE)]
    downs = [down_weight, swap(down_own, CORE), downs2, swap(downs2, CORE)]
    turned = turn_heads(*mixed)
    branch, middle, hidden2, down_grad, dsum = mid(turned, outs, table, x0, cotangent)
    h2 = hidden2.reshape(TOKENS, D)
    dg = down_grad.reshape(TOKENS, D)
    act, upg, hg, usum = feed(row_arg, h2, dg, ups, table, downs)
    mg, bg, *ag, sums = mid_back(hg.reshape(FPD, PR, D), middle, branch, cotangent, table, outs)
    late = []
    back = turn_heads(*ag[:2], ag[2], order=lambda piece: late.append(piece) or piece)[:2]

    early = early_sums(sums, usum, dsum)
    early = early + swap(early, CORE)
    dk_part, ds_part, layer_output, gate = down_weight_grad(
        row_arg, after(dg, bg), act, downs, table, middle, cotangent
    )
    upg, early, gate, far_back, *back = lax.optimization_barrier((upg, early, gate, *late, *back))
    back += [far_back[0], swap(far_back[1], CORE)]
    early = early + swap(early, DIRECT)
    uk, us = up_weight_grad(row_arg, h2, upg)
    ok, os = out_weight_grad(turned, bg)

    early = jnp.concatenate([early.astype(BF16), silu_own], axis=1)
    early, uk = lax.optimization_barrier((early, uk))
    early = jnp.stack([early, swap(early, FAR)])
    early, uk, ok, *back = lax.optimization_barrier((early, uk, ok, *back))
    early_parts = [early] + [swap(early, m) for m in (16, 32, 48)]
    dq_before, both = attend_back(False, frame_position, q, kp, vp, back, mixed, lse)
    returned = shift(both, -1)
    uk, dq_before = lax.optimization_barrier((uk, dq_before))
    packed = core_sum(
        (uk, swap(us, CORE)), (dk_part, swap(ds_part, CORE)), (ok, swap(os, CORE))
    )
    dq_before, packed = lax.optimization_barrier((dq_before, packed))
    scattered = lax.psum_scatter(packed, ("y", "z"), scatter_dimension=1, tiled=True)
    dq, dk, dv = attend_back(
        True, frame_position, q, k, v, back, mixed, lse, tables, dq_before
    )
    dq, *early_parts = lax.optimization_barrier((dq, *early_parts))
    early = jnp.concatenate(early_parts)
    early_high = early
    early = early[0].astype(F32)

    dproj, h0, h2_part, send, bsum = project_back(row_arg, dq, dk, dv, returned, qkv_pieces, tables)
    near = swap(send, CORE)
    qkv_parts = project_weight(row_arg, hidden1, dproj)
    far = swap((h2_part.astype(F32) + near[1].astype(F32)).astype(BF16), DIRECT)
    qkv_parts = exchange_rows(qkv_parts, 4, index, 0)
    far, qkv_parts, early_high = lax.optimization_barrier((far, qkv_parts, early_high))
    early_all = [early_high] + [swap(early_high, m) for m in (4, 8, 12)]
    quarters = quarter_rows(qkv_parts, 16, index, 1)
    input_grad, late = input_back(x0, h0, near, far, table, mg, bsum, gate)
    late, *quarters = lax.optimization_barrier((late, *quarters))
    qkv_parts = add_all(quarters)
    late_near = swap(late, CORE)
    late, late_near, qkv_parts = lax.optimization_barrier((late, late_near, qkv_parts))
    late = late + late_near
    late_far = swap(late, DIRECT)
    qkv_far = swap(qkv_parts, FAR)
    late, late_far, qkv_parts, qkv_far = lax.optimization_barrier(
        (late, late_far, qkv_parts, qkv_far)
    )
    late = late + late_far
    qkv_parts = add_all([qkv_parts, qkv_far])
    late_low = late.astype(BF16)
    late_far = swap(late_low, FAR)
    turned = turn_heads(qkv_parts[0], qkv_parts[1], qkv_parts[2:])
    last = arrange(row_arg, turned, late_low, late_far)

    scattered, last, *early_all = lax.optimization_barrier((scattered, last, *early_all))
    last = jnp.stack([last] + [swap(last, m) for m in (16, 32, 48)])
    share = scattered[0].astype(F32) + swap(scattered[1], DIRECT).astype(F32)
    share = (share + swap(share.astype(BF16), FAR).astype(F32)).astype(BF16)
    share, last = lax.optimization_barrier((share, last))
    last_all = [last] + [swap(last, m) for m in (4, 8, 12)]
    totals = lax.all_gather(share, ("y", "z"), axis=0, tiled=True)
    up_total, out_total, down_total = unpack(totals)
    qkv_total = place(index_arg, last_all)

    ada_total, *bias_sums = final_sums(row_arg, last_all, early_all)
    ada_sum, qkv_sum, out_sum, up_sum, down_sum = [b[0] for b in bias_sums]
    mod_own = jnp.concatenate(
        [late[:, : 2 * D], early[:, : 3 * D], late[:, 2 * D : 3 * D]], axis=1
    ).astype(BF16)
    silu_grad = nt(mod_own, ada_weight)
    silu_grad = by_row(row_pieces(silu_grad), row).transpose(1, 0, 2).reshape(FPD, D)
    embed = noise_embed.astype(F32)
    sigma = jax.nn.sigmoid(embed)
    embed_grad = silu_grad * (sigma * (1.0 + embed * (1.0 - sigma)))

    return (
        layer_output,
        input_grad,
        embed_grad,
        ada_total,
        ada_sum,
        qkv_total,
        qkv_sum,
        out_total,
        out_sum,
        up_total,
        up_sum,
        down_total,
        down_sum,
    )


def solution(mesh):
    fine = Mesh(mesh.devices.reshape(2, 4, 4, 2, 2), AXES)
    seq, row = ("xh", "z", "y"), ("xl", "c")
    token, weight, vector = P(seq, row, None), P(row, None), P(row)
    in_specs = (token, P(seq, None), P(seq), token) + (weight, vector) * 5
    out_specs = (token, token, P(seq, None)) + (weight, vector) * 5
    return jax.shard_map(
        per_device, mesh=fine, in_specs=in_specs, out_specs=out_specs, check_vma=False
    )
```

```python
import math

import jax
import jax.numpy as jnp
from jax import lax
from jax.experimental import pallas as pl
from jax.experimental.pallas import tpu as pltpu
from jax.sharding import Mesh, PartitionSpec as P

F32 = jnp.float32
BF16 = jnp.bfloat16
HD = 64
GRID = 16
FPD = 8
PR = 64
D = 1024
FF = 4096
HC = 256
TOK = 256
PREV = 7
AXES = ("xh", "z", "y", "xl", "c")
CORE, DIRECT, OTHER, FAR = 1, 2, 66, 64
MB = 1024 * 1024


def swap(value, mask):
    return lax.ppermute(value, AXES, [(i, i ^ mask) for i in range(128)])


def shift(value, steps):
    return lax.ppermute(value, AXES, [(i, (i + 4 * steps) % 128) for i in range(128)])


def after(value, *others):
    return lax.optimization_barrier((value,) + others)[0]


def nt(left, right):
    return lax.dot_general(left, right, (((1,), (1,)), ((), ())), preferred_element_type=F32)


def tn(left, right):
    return lax.dot_general(left, right, (((0,), (0,)), ((), ())), preferred_element_type=F32)


def nn(left, right):
    return jnp.dot(left, right, preferred_element_type=F32)


def norm(values):
    center = values - jnp.mean(values, axis=-1, keepdims=True)
    spread = jnp.mean(center * center, axis=-1, keepdims=True)
    rate = lax.rsqrt(spread + 1e-06)
    return center * rate, rate


def norm_back(normal, rate, grad):
    mean_grad = jnp.mean(grad, axis=-1, keepdims=True)
    mean_both = jnp.mean(grad * normal, axis=-1, keepdims=True)
    return rate * (grad - mean_grad - normal * mean_both)


def turn(values, cosine, sine):
    lanes = lax.broadcasted_iota(jnp.int32, values.shape, 1)
    other = jnp.where(
        lanes % HD < HD // 2, pltpu.roll(values, HC - HD // 2, 1), pltpu.roll(values, HD // 2, 1)
    )
    return values * cosine + other * sine


def params(mib):
    return pltpu.CompilerParams(vmem_limit_bytes=mib * MB)


def cost(flops, moved, exps=0):
    return pl.CostEstimate(flops=int(flops), bytes_accessed=int(moved), transcendentals=int(exps))


def whole(shape):
    return pl.BlockSpec(shape, lambda i, *_: (0,) * len(shape))


def columns(row, j):
    return pl.ds(pl.multiple_of((row ^ j) * HC, HC), HC)


def shape(dims, kind=BF16):
    return jax.ShapeDtypeStruct(dims, kind)


UB, QB, OB, DB, WIDE = 6144, 6656, 7168, 7296, 7424


def put(ref, start, at, value):
    cols = slice(start, start + value.shape[1])
    number = lax.broadcasted_iota(jnp.int32, (8, value.shape[1]), 0)
    ref[:, cols] = jnp.where(number == at, value, ref[:, cols])


def take(value, at):
    number = lax.broadcasted_iota(jnp.int32, value.shape, 0)
    return jnp.sum(jnp.where(number == at, value, 0.0), axis=0, keepdims=True)


def put_half(ref, start, value):
    cols = slice(start, start + value.shape[1])
    number = lax.broadcasted_iota(jnp.int32, (8, value.shape[1]), 0)
    both = jnp.concatenate([value, value], axis=0)
    ref[:, cols] = jnp.where(number // 4 == pl.program_id(0), both, ref[:, cols])


def unfold(ref, start, width):
    return jnp.concatenate([ref[i : i + 1, start : start + width] for i in range(8)], axis=1)


def prepare_kernel(row_ref, pos_ref, noise, ada, ab, qb, ob, ub, db, pack, silu, cp, sp, frames):
    row = row_ref[0]
    embed = noise[...].astype(F32)
    value = (embed / (1.0 + jnp.exp(-embed))).astype(BF16)
    own = jnp.where(
        row < 2,
        jnp.where(row == 0, value[:, :HC], value[:, HC : 2 * HC]),
        jnp.where(row == 2, value[:, 2 * HC : 3 * HC], value[:, 3 * HC :]),
    )
    silu[...] = own
    pack[:, UB:] = jnp.zeros((FPD, WIDE - UB), F32)
    for segment in range(6):
        cols = slice(segment * D, (segment + 1) * D)
        pack[:, cols] = nn(own, ada[:, cols])
    bias = pl.ds(pl.multiple_of(row * 1536, 512), 1536)
    pack[:, bias] = pack[:, bias] + ab[...].astype(F32)
    for i in range(2):
        at = 2 * row + i
        put(pack, UB, at, ub[:, i * 512 : (i + 1) * 512].astype(F32))
        put(pack, OB, at, ob[:, i * 128 : (i + 1) * 128].astype(F32))
        put(pack, DB, at, db[:, i * 128 : (i + 1) * 128].astype(F32))
    for i in range(3):
        chunk = 3 * row + i
        at = jnp.where(chunk < 4, chunk, chunk - 4)
        second = (chunk >= 4) & (chunk < 8)
        value = qb[:, i * HC : (i + 1) * HC].astype(F32)
        put(pack, QB, jnp.where(second, -1, at), value)
        put(pack, QB + HC, jnp.where(second, at, -1), value)

    def parts(dims):
        lane = lax.broadcasted_iota(jnp.int32, dims, 1)
        index = lane % (HD // 2)
        quarter, eighth = HD // 4, HD // 8
        in_frame = index < quarter
        in_row = (index >= quarter) & (index < quarter + eighth)
        offset = jnp.where(
            in_frame, index, jnp.where(in_row, index - quarter, index - quarter - eighth)
        ).astype(F32)
        length = jnp.where(in_frame, 1.0 * quarter, 1.0 * eighth)
        frequency = jnp.exp(-math.log(10000.0) * offset / length)
        sign = jnp.where(lane % HD < HD // 2, -1.0, 1.0)
        return in_frame, in_row, frequency, sign

    in_frame, in_row, frequency, sign = parts((TOK, HC))
    slot = lax.broadcasted_iota(jnp.int32, (TOK, HC), 0)
    patch = ((slot // PR) ^ row) * PR + slot % PR
    angle = jnp.where(in_row, patch // GRID, patch % GRID).astype(F32) * frequency
    cp[...] = jnp.where(in_frame, 0.0, jnp.cos(angle))
    sp[...] = jnp.where(in_frame, 0.0, jnp.sin(angle) * sign)
    in_frame, _, frequency, sign = parts((16, HC))
    slot = lax.broadcasted_iota(jnp.int32, (16, HC), 0)
    place = pos_ref[0] - PREV + (slot - FPD)
    for f in range(FPD):
        place = jnp.where(slot == f, pos_ref[f], place)
    angle = place.astype(F32) * frequency
    frames[:, :HC] = jnp.where(in_frame, jnp.cos(angle), 0.0)
    frames[:, HC:] = jnp.where(in_frame, jnp.sin(angle) * sign, 0.0)


def prepare(row, places, noise, ada, biases):
    return pl.pallas_call(
        prepare_kernel,
        out_shape=[
            shape((FPD, WIDE), F32),
            shape((FPD, HC)),
            shape((TOK, HC), F32),
            shape((TOK, HC), F32),
            shape((16, 2 * HC), F32),
        ],
        grid_spec=pltpu.PrefetchScalarGridSpec(
            num_scalar_prefetch=2,
            grid=(1,),
            in_specs=[whole((FPD, D)), whole((HC, 6 * D))]
            + [whole((1, b.shape[0])) for b in biases],
            out_specs=[
                whole((FPD, WIDE)),
                whole((FPD, HC)),
                whole((TOK, HC)),
                whole((TOK, HC)),
                whole((16, 2 * HC)),
            ],
        ),
        compiler_params=params(24),
        cost_estimate=cost(2 * 8 * HC * 6 * D, 4 * MB, 4 * TOK * HC),
        name="prepare",
    )(row, places, noise, ada, *[b[None] for b in biases])


def split_heads_kernel(row_ref, q, k, v, p0, p1, p23):
    for j, p in enumerate((p0, p1, p23.at[0], p23.at[1])):

        @pl.when(pl.program_id(0) == j)
        def _():
            p[:, :HC] = q[...]
            p[:, HC : 2 * HC] = k[...]
            p[:, 2 * HC :] = v[...]


def split_heads(row, weight):
    piece = (HC, 3 * HC)
    return pl.pallas_call(
        split_heads_kernel,
        out_shape=[shape(piece), shape(piece), shape((2,) + piece)],
        grid_spec=pltpu.PrefetchScalarGridSpec(
            num_scalar_prefetch=1,
            grid=(4,),
            in_specs=[
                pl.BlockSpec((HC, HC), lambda j, row, s=s: (0, 4 * s + (row[0] ^ j)))
                for s in range(3)
            ],
            out_specs=[whole(piece), whole(piece), whole((2,) + piece)],
        ),
        compiler_params=params(12),
        cost_estimate=cost(0, 3 * MB),
        name="split_heads",
    )(row, weight, weight, weight)


def cosines(cp, sp, frames, at):
    both = frames[pl.ds(at, 1), :]
    return cp[...] + both[:, :HC], sp[...] + both[:, HC:]


def project_kernel(own, row_ref, x0, x1, x2, x3, table, mods, w0, w1, w2, w3, cp, sp, fr, *outs):
    row = row_ref[0]
    f = pl.program_id(0)
    if own:
        h_ref, q_ref, k_ref, v_ref = outs
        first, at, angle = 0, f, f
    else:
        k_ref, v_ref, h_ref = outs
        first, at, angle = HC, f + FPD - PREV, f + FPD
    x = jnp.concatenate([r[0] for r in (x0, x1, x2, x3)], axis=0).astype(F32)
    normal, _ = norm(x)
    shift_row = mods[pl.ds(at, 1), :D]
    scale_row = mods[pl.ds(at, 1), D : 2 * D]
    hidden = (normal * (1.0 + scale_row) + shift_row).astype(BF16)
    where = (0,) if own else ()
    h_ref[where + (slice(None), slice(None))] = hidden
    low, high = table[pl.ds(row, 1), QB : QB + 2 * HC], table[pl.ds(row + 4, 1), QB : QB + HC]
    total = jnp.concatenate([low, high], axis=1)[:, first:]
    for j, w in enumerate((w0, w1, w2, w3)):
        total = total + nn(h_ref[where + (slice(None), columns(row, j))], w[:, first:])
    cosine, sine = cosines(cp, sp, fr, angle)
    if own:
        q_ref[0] = (turn(total[:, :HC], cosine, sine).astype(BF16).astype(F32) * 0.125).astype(BF16)
        total = total[:, HC:]
    k_ref[0] = turn(total[:, :HC], cosine, sine).astype(BF16)
    v_ref[0] = total[:, HC:].astype(BF16)


def project(own, row, xs, table, mods, weights, tables):
    frames = xs[0].shape[0]
    x_spec = pl.BlockSpec((1, PR, D), lambda f, *_: (f, 0, 0))
    out_spec = pl.BlockSpec((1, TOK, HC), lambda f, *_: (f, 0, 0))
    out = shape((frames, TOK, HC))
    if own:
        out_specs = [pl.BlockSpec((1, TOK, D), lambda f, *_: (f, 0, 0)), out_spec, out_spec, out_spec]
        out_shape = [shape((frames, TOK, D)), out, out, out]
        scratch = []
    else:
        out_specs = [out_spec, out_spec]
        out_shape = [out, out]
        scratch = [pltpu.VMEM((TOK, D), BF16)]
    return pl.pallas_call(
        lambda *refs: project_kernel(own, *refs),
        out_shape=out_shape,
        grid_spec=pltpu.PrefetchScalarGridSpec(
            num_scalar_prefetch=1,
            grid=(frames,),
            in_specs=[x_spec] * 4
            + [whole((FPD, WIDE)), whole(mods.shape)]
            + [whole((HC, 3 * HC))] * 4
            + [whole((TOK, HC)), whole((TOK, HC)), whole((16, 2 * HC))],
            out_specs=out_specs,
            scratch_shapes=scratch,
        ),
        compiler_params=params(20),
        cost_estimate=cost(2 * frames * TOK * D * 3 * HC, frames * TOK * D * 4 + 4 * MB),
        name="project_own" if own else "project_prev",
    )(row, *xs, table, mods, *weights, *tables)


def head_lanes():
    return lax.broadcasted_iota(jnp.int32, (TOK, HC), 1) // HD


def attend_kernel(pos_ref, q, k, v, kp, vp, o0, o1, o23, lse, qs, scores, acc, top, low):
    f = pl.program_id(0)
    place = pos_ref[f]
    lanes = head_lanes()
    query = q[0]
    for h in range(4):
        qs[pl.ds(h * TOK, TOK), :] = jnp.where(lanes == h, query, jnp.zeros_like(query))
    top[...] = jnp.full_like(top, -1e30)
    low[...] = jnp.zeros_like(low)
    acc[...] = jnp.zeros_like(acc)
    before = jnp.maximum(place - f, 0)
    start = jnp.maximum(f - place, 0)

    def score(keys, slot):
        for h in range(4):
            rows = pl.ds(h * TOK, TOK)
            s = nt(qs[rows, :], keys)
            scores[slot, rows, :] = s
            top[rows, :] = jnp.maximum(top[rows, :], jnp.maximum(s[:, :128], s[:, 128:]))

    def mix(values, slot):
        for h in range(4):
            rows = pl.ds(h * TOK, TOK)
            p = jnp.exp(scores[slot, rows, :] - jnp.concatenate([top[rows, :]] * 2, axis=1))
            low[rows, :] = low[rows, :] + (p[:, :128] + p[:, 128:])
            acc[rows, :] = acc[rows, :] + nn(p.astype(BF16), values)

    def run(step):
        def prev(i, _):
            at = PREV - before + i
            step(kp[at] if step is score else vp[at], i)
            return 0

        def own(g, _):
            step(k[g] if step is score else v[g], g - f + place)
            return 0

        lax.fori_loop(0, before, prev, 0)
        lax.fori_loop(start, f + 1, own, 0)

    run(score)
    for h in range(4):
        rows = pl.ds(h * TOK, TOK)
        top[rows, :] = jnp.broadcast_to(jnp.max(top[rows, :], axis=1, keepdims=True), (TOK, 128))
    run(mix)
    result = jnp.zeros((TOK, HC), F32)
    logs = jnp.zeros((TOK, 128), F32)
    narrow = lax.broadcasted_iota(jnp.int32, (TOK, 128), 1)
    for h in range(4):
        rows = pl.ds(h * TOK, TOK)
        total = jnp.sum(low[rows, :], axis=1, keepdims=True)
        result = jnp.where(lanes == h, acc[rows, :] / total, result)
        logs = jnp.where(narrow == h, top[rows, :] + jnp.log(total), logs)
    lse[0] = logs.T[:8]
    result = result.astype(BF16)
    o0[0] = result[:PR]
    o1[0] = result[PR : 2 * PR]
    o23[0, 0] = result[2 * PR : 3 * PR]
    o23[1, 0] = result[3 * PR :]


def attend(places, q, k, v, kp, vp):
    block = pl.BlockSpec((1, TOK, HC), lambda f, *_: (f, 0, 0))
    piece = pl.BlockSpec((1, PR, HC), lambda f, *_: (f, 0, 0))
    return pl.pallas_call(
        attend_kernel,
        out_shape=[shape((FPD, PR, HC))] * 2
        + [shape((2, FPD, PR, HC)), shape((FPD, 8, TOK), F32)],
        grid_spec=pltpu.PrefetchScalarGridSpec(
            num_scalar_prefetch=1,
            grid=(FPD,),
            in_specs=[block]
            + [whole((FPD, TOK, HC))] * 2
            + [whole((PREV, TOK, HC))] * 2,
            out_specs=[piece] * 2
            + [
                pl.BlockSpec((2, 1, PR, HC), lambda f, *_: (0, f, 0, 0)),
                pl.BlockSpec((1, 8, TOK), lambda f, *_: (f, 0, 0)),
            ],
            scratch_shapes=[
                pltpu.VMEM((4 * TOK, HC), BF16),
                pltpu.VMEM((8, 4 * TOK, TOK), F32),
                pltpu.VMEM((4 * TOK, HC), F32),
                pltpu.VMEM((4 * TOK, 128), F32),
                pltpu.VMEM((4 * TOK, 128), F32),
            ],
        ),
        compiler_params=params(58),
        cost_estimate=cost(36 * 4 * 2 * 2 * TOK**3, 6 * MB, 36 * 4 * TOK * TOK),
        name="attend",
    )(places, q, k, v, kp, vp)


def attend_back_kernel(own, pos_ref, q, k, v, g0, g1, g2, g3, o0, o1, o23, lse, *rest):
    if own:
        cp, sp, fr, before_ref, dq, dk, dv, qs, gs, ks, pl_scr, dl_scr, ds_scr, dq_acc = rest
        dk_acc, dv_acc = dk, dv
    else:
        dq, both_ref, qs, gs, ks, pl_scr, dl_scr, ds_scr, dq_acc, dk_acc, dv_acc = rest
    f = pl.program_id(0)
    place = pos_ref[f]
    lanes = head_lanes()

    @pl.when(f == 0)
    def _():
        for ref in (dk_acc, dv_acc):
            ref[...] = jnp.zeros_like(ref)

    def prelude():
        query = q[0]
        grad = jnp.concatenate([r[0] for r in (g0, g1, g2, g3)], axis=0)
        mixed = jnp.concatenate([o0[0], o1[0], o23[0, 0], o23[1, 0]], axis=0)
        for h in range(4):
            rows = pl.ds(h * TOK, TOK)
            qs[rows, :] = jnp.where(lanes == h, query, jnp.zeros_like(query))
            gs[rows, :] = jnp.where(lanes == h, grad, jnp.zeros_like(grad))
        both = grad.astype(F32) * mixed.astype(F32)
        pick = (
            lax.broadcasted_iota(jnp.int32, (8, HC), 1) // HD
            == lax.broadcasted_iota(jnp.int32, (8, HC), 0)
        ).astype(F32)
        return lax.dot_general(
            pick, both, (((1,), (1,)), ((), ())),
            preferred_element_type=F32, precision=lax.Precision.HIGHEST,
        )

    def step(delta, logs, at):
        keys, values = k[at], v[at]
        for h in range(4):
            rows = pl.ds(h * TOK, TOK)
            ks[rows, :] = jnp.where(lanes == h, keys, jnp.zeros_like(keys))
            p = jnp.exp(nt(keys, qs[rows, :]) - logs[h : h + 1])
            ds = (p * (nt(values, gs[rows, :]) - delta[h : h + 1])).astype(BF16)
            pl_scr[:, rows] = p.astype(BF16)
            dl_scr[:, rows] = ds
            ds_scr[rows, :] = ds
        dv_acc[at] = dv_acc[at] + nn(pl_scr[...], gs[...])
        dk_acc[at] = dk_acc[at] + nn(dl_scr[...], qs[...])
        dq_acc[...] = dq_acc[...] + tn(ds_scr[...], ks[...])

    def sweep(low, high):
        delta = prelude()
        logs = lse[0]
        dq_acc[...] = jnp.zeros_like(dq_acc)

        def one(at, _):
            step(delta, logs, at)
            return 0

        lax.fori_loop(low, high, one, 0)

    if own:
        sweep(jnp.maximum(f - place, 0), f + 1)
        cosine, sine = cosines(cp, sp, fr, f)
        dq[0] = turn((dq_acc[...] + before_ref[0]) * 0.125, cosine, -sine).astype(BF16)
    else:
        count = jnp.maximum(place - f, 0)

        @pl.when(count > 0)
        def _():
            sweep(PREV - count, PREV)
            dq[0] = dq_acc[...]

        @pl.when(count == 0)
        def _():
            dq[0] = jnp.zeros_like(dq_acc)

        @pl.when(f == FPD - 1)
        def _():
            both_ref[0] = dk_acc[...].astype(BF16)
            both_ref[1] = dv_acc[...].astype(BF16)


def attend_back(own, places, q, k, v, grads, mixed, lse, tables=None, before=None):
    block = pl.BlockSpec((1, TOK, HC), lambda f, *_: (f, 0, 0))
    piece = pl.BlockSpec((1, PR, HC), lambda f, *_: (f, 0, 0))
    count = FPD if own else PREV
    wide = pltpu.VMEM((4 * TOK, HC), BF16)
    tall = pltpu.VMEM((TOK, 4 * TOK), BF16)
    scratch = [wide, wide, wide, tall, tall, wide, pltpu.VMEM((TOK, HC), F32)]
    specs = []
    extra = ()
    if own:
        specs = [whole((TOK, HC)), whole((TOK, HC)), whole((16, 2 * HC)), block]
        extra = tuple(tables) + (before,)
    else:
        scratch += [pltpu.VMEM((PREV, TOK, HC), F32)] * 2
    return pl.pallas_call(
        lambda *refs: attend_back_kernel(own, *refs),
        out_shape=[shape((FPD, TOK, HC), BF16 if own else F32)]
        + ([shape((FPD, TOK, HC), F32)] * 2 if own else [shape((2, PREV, TOK, HC))]),
        grid_spec=pltpu.PrefetchScalarGridSpec(
            num_scalar_prefetch=1,
            grid=(FPD,),
            in_specs=[block]
            + [whole((count, TOK, HC))] * 2
            + [piece] * 6
            + [pl.BlockSpec((2, 1, PR, HC), lambda f, *_: (0, f, 0, 0))]
            + [pl.BlockSpec((1, 8, TOK), lambda f, *_: (f, 0, 0))]
            + specs,
            out_specs=[block]
            + ([whole((FPD, TOK, HC))] * 2 if own else [whole((2, PREV, TOK, HC))]),
            scratch_shapes=scratch,
        ),
        compiler_params=params(58),
        cost_estimate=cost(1000 if own else 12 * 4 * 5 * 2 * TOK**3, 1000 if own else 12 * MB),
        name="attend_back_own" if own else "attend_back_prev",
    )(places, q, k, v, *grads, *mixed, lse, *extra)


HALF = 4
RAW = HALF * PR


def flat(ref):
    return ref[...].reshape(RAW, ref.shape[-1])


def frames_of(value):
    return value.reshape(HALF, PR, value.shape[-1])


def segment(table, s):
    both = table[:, s * D : (s + 1) * D]
    return jnp.where(pl.program_id(0) == 0, both[:HALF], both[HALF:])[:, None, :]


def fold(out, start, width, row):
    @pl.when(pl.program_id(0) == 0)
    def _():
        out[:, start : start + width] = jnp.zeros((8, width), F32)

    for i in range(8):
        at = (slice(i, i + 1), slice(start, start + width))
        out[at] = out[at] + row[:, i * width : (i + 1) * width]


def mid_kernel(o0, o1, o2, o3, w0, w1, w2, w3, table, x, cot, branch, middle, hidden, down, dsum):
    total = unfold(table, OB, 128)
    for o, w in zip((o0, o1, o2, o3), (w0, w1, w2, w3)):
        total = total + nn(flat(o), w[...])
    branched = frames_of(total)
    branch[...] = branched
    mid_value = x[...].astype(F32) + segment(table, 2) * branched
    middle[...] = mid_value
    normal, _ = norm(mid_value)
    hidden[...] = (normal * (1.0 + segment(table, 4)) + segment(table, 3)).astype(BF16)
    grad = (segment(table, 5) * cot[...].astype(F32)).astype(BF16)
    down[...] = grad
    fold(dsum, 0, 128, jnp.sum(grad.astype(F32).reshape(RAW, D), axis=0, keepdims=True))


def half_spec(width):
    return pl.BlockSpec((HALF, PR, width), lambda i, *_: (i, 0, 0))


def mid(pieces, weights, table, x, cot):
    return pl.pallas_call(
        mid_kernel,
        out_shape=[
            shape((FPD, PR, D), F32),
            shape((FPD, PR, D), F32),
            shape((FPD, PR, D)),
            shape((FPD, PR, D)),
            shape((8, 128), F32),
        ],
        grid=(FPD // HALF,),
        in_specs=[half_spec(HC)] * 4
        + [whole((HC, D))] * 4
        + [whole((FPD, WIDE)), half_spec(D), half_spec(D)],
        out_specs=[half_spec(D)] * 4 + [whole((8, 128))],
        compiler_params=params(26),
        cost_estimate=cost(2 * 512 * D * D, 12 * MB),
        name="mid",
    )(*pieces, *weights, table, x, cot)


def mid_back_kernel(hg, middle, branch, cot, table, w0, w1, w2, w3, mg, bg, a0, a1, a23, sums):
    grad = hg[...]
    normal, rate = norm(middle[...])
    put_half(sums, D, jnp.sum(grad, axis=1))
    put_half(sums, 2 * D, jnp.sum(grad * normal, axis=1))
    total = cot[...].astype(F32) + norm_back(normal, rate, grad * (1.0 + segment(table, 4)))
    mg[...] = total
    put_half(sums, 0, jnp.sum(total * branch[...], axis=1))
    low = (segment(table, 2) * total).astype(BF16)
    bg[...] = low
    low = low.reshape(RAW, D)
    fold(sums, 3 * D, 128, jnp.sum(low.astype(F32), axis=0, keepdims=True))
    for j, w in enumerate((w0, w1, w2, w3)):
        value = frames_of(nt(low, w[...]).astype(BF16))
        if j < 2:
            (a0, a1)[j][...] = value
        else:
            a23[j - 2] = value


def mid_back(hg, middle, branch, cot, table, weights):
    return pl.pallas_call(
        mid_back_kernel,
        out_shape=[shape((FPD, PR, D), F32), shape((FPD, PR, D))]
        + [shape((FPD, PR, HC))] * 2
        + [shape((2, FPD, PR, HC)), shape((8, 3 * D + 128), F32)],
        grid=(FPD // HALF,),
        in_specs=[half_spec(D)] * 4
        + [whole((FPD, WIDE))]
        + [whole((HC, D))] * 4,
        out_specs=[half_spec(D)] * 2
        + [half_spec(HC)] * 2
        + [pl.BlockSpec((2, HALF, PR, HC), lambda i: (0, i, 0, 0)), whole((8, 3 * D + 128))],
        compiler_params=params(26),
        cost_estimate=cost(2 * 512 * D * D, 12 * MB),
        name="mid_back",
    )(hg, middle, branch, cot, table, *weights)


NB = 512
STEPS = FF // NB
PER = D // NB
TOKENS = FPD * PR


def block_of(t):
    phase = t // PER
    return ((phase % 2) * 2) ^ (phase // 2)


def up_column(t, row):
    return (row ^ block_of(t)) * PER + t % PER


def down_row(t):
    return block_of(t) * PER + t % PER


def down_spec(j):
    phase = (0, 2, 1, 3)[j]
    return pl.BlockSpec((NB, D), lambda t, row: (jnp.clip(t - phase * PER, 0, PER - 1), 0))


def pick_down(d0, d1, d2, d3):
    phase = pl.program_id(0) // PER
    return jnp.where(
        phase < 2,
        jnp.where(phase == 0, d0[...], d2[...]),
        jnp.where(phase == 2, d1[...], d3[...]),
    )


def feed_kernel(row_ref, h2, dg, u0, u1, u2, u3, table, d0, d1, d2, d3, act, upg, hg, usum):
    row = row_ref[0]
    ups = (u0, u1, u2, u3)
    down = pick_down(d0, d1, d2, d3)
    at = pl.ds(up_column(pl.program_id(0), row), 1)
    u = table[at, UB : UB + NB]
    for j, w in enumerate(ups):
        u = u + nn(h2[:, columns(row, j)], w[...])
    rate = math.sqrt(2.0 / math.pi)
    square = u * u
    half = 0.5 + 0.5 * jnp.tanh(u * (rate + (rate * 0.044715) * square))
    active = u * half
    act[...] = active.astype(BF16)
    slope = half + active * (1.0 - half) * (2.0 * rate + (6.0 * rate * 0.044715) * square)
    grad = (nt(dg[...], down) * slope).astype(BF16)
    upg[...] = grad
    put(usum, 0, up_column(pl.program_id(0), row), jnp.sum(grad.astype(F32), axis=0, keepdims=True))

    @pl.when(pl.program_id(0) == 0)
    def _():
        hg[...] = jnp.zeros_like(hg)

    for j, w in enumerate(ups):
        hg[:, columns(row, j)] = hg[:, columns(row, j)] + nt(grad, w[...])


def feed(row, h2, dg, ups, table, downs):
    tok = whole((TOKENS, D))
    block = pl.BlockSpec((TOKENS, NB), lambda t, row: (0, t))
    return pl.pallas_call(
        feed_kernel,
        out_shape=[
            shape((TOKENS, FF)),
            shape((TOKENS, FF)),
            shape((TOKENS, D), F32),
            shape((8, NB), F32),
        ],
        grid_spec=pltpu.PrefetchScalarGridSpec(
            num_scalar_prefetch=1,
            grid=(STEPS,),
            in_specs=[tok, tok]
            + [pl.BlockSpec((HC, NB), lambda t, row: (0, up_column(t, row[0])))] * 4
            + [whole((FPD, WIDE))]
            + [down_spec(j) for j in range(4)],
            out_specs=[block, block, tok, whole((8, NB))],
        ),
        compiler_params=params(58),
        cost_estimate=cost(3 * 2 * TOKENS * D * FF, 30 * MB, TOKENS * FF),
        name="feed",
    )(row, h2, dg, *ups, table, *downs)


def down_weight_kernel(row_ref, dg, act, d0, d1, d2, d3, table, middle, cot, dk, ds, out, gate, dn):
    t = pl.program_id(0)
    down = pick_down(d0, d1, d2, d3)
    active = act[...]

    @pl.when(t == 0)
    def _():
        dn[...] = jnp.zeros_like(dn)

    dn[...] = dn[...] + nn(active, down)
    part = tn(active, dg[...]).astype(BF16)

    @pl.when(t < STEPS // 2)
    def _():
        dk[0] = part

    @pl.when(t >= STEPS // 2)
    def _():
        ds[0] = part

    @pl.when(t == STEPS - 1)
    def _():
        bias = unfold(table, DB, 128)
        for f in range(FPD):
            rows = slice(f * PR, (f + 1) * PR)
            value = dn[rows, :] + bias
            out[f] = (middle[f] + table[f : f + 1, 5 * D : 6 * D] * value).astype(BF16)
            gate[f : f + 1, :] = jnp.sum(cot[f].astype(F32) * value, axis=0, keepdims=True)


def down_weight_grad(row, dg, act, downs, table, middle, cot):
    tok = whole((TOKENS, D))
    full = whole((FPD, PR, D))
    block = pl.BlockSpec((TOKENS, NB), lambda t, row: (0, t))

    def down_out(first):
        def index(t, row):
            at = jnp.clip(t - first, 0, STEPS // 2 - 1)
            return (at // PER, at % PER, 0)

        return pl.BlockSpec((1, NB, D), index)

    return pl.pallas_call(
        down_weight_kernel,
        out_shape=[shape((2, D, D))] * 2 + [shape((FPD, PR, D)), shape((8, D), F32)],
        grid_spec=pltpu.PrefetchScalarGridSpec(
            num_scalar_prefetch=1,
            grid=(STEPS,),
            in_specs=[tok, block]
            + [down_spec(j) for j in range(4)]
            + [whole((FPD, WIDE)), full, full],
            out_specs=[down_out(0), down_out(STEPS // 2), full, whole((8, D))],
            scratch_shapes=[pltpu.VMEM((TOKENS, D), F32)],
        ),
        compiler_params=params(58),
        cost_estimate=cost(2 * 2 * TOKENS * D * FF, 24 * MB),
        name="down_weight_grad",
    )(row, dg, act, *downs, table, middle, cot)


def up_weight_kernel(row_ref, h2, upg, uk, us):
    row = row_ref[0]
    grad = upg[...]
    for j, ref in enumerate((uk, us, uk, us)):
        ref[j // 2, 0] = tn(h2[:, columns(row, j)], grad).astype(BF16)


def up_weight_grad(row, h2, upg):
    up_out = pl.BlockSpec(
        (2, 1, HC, NB),
        lambda t, row: (0, up_column(t, row[0]) // PER, 0, up_column(t, row[0]) % PER),
    )
    return pl.pallas_call(
        up_weight_kernel,
        out_shape=[shape((2, 4, HC, D))] * 2,
        grid_spec=pltpu.PrefetchScalarGridSpec(
            num_scalar_prefetch=1,
            grid=(STEPS,),
            in_specs=[whole((TOKENS, D)), pl.BlockSpec((TOKENS, NB), lambda t, row: (0, t))],
            out_specs=[up_out, up_out],
        ),
        compiler_params=params(58),
        cost_estimate=cost(2 * TOKENS * D * FF, 14 * MB),
        name="up_weight_grad",
    )(row, h2, upg)


def out_weight_kernel(t0, t1, t2, t3, bg, keep, send):
    grad = bg[...].reshape(TOKENS, D)
    for j, t in enumerate((t0, t1, t2, t3)):
        ref = (keep, send)[j % 2]
        ref[j // 2] = tn(t[...].reshape(TOKENS, HC), grad).astype(BF16)


def out_weight_grad(pieces, bg):
    return pl.pallas_call(
        out_weight_kernel,
        out_shape=[shape((2, HC, D))] * 2,
        grid=(1,),
        in_specs=[whole((FPD, PR, HC))] * 4 + [whole((FPD, PR, D))],
        out_specs=[whole((2, HC, D))] * 2,
        compiler_params=params(14),
        cost_estimate=cost(2 * TOKENS * D * D, 4 * MB),
        name="out_weight_grad",
    )(*pieces, bg)


CHUNKS = 16
UP_ROWS, OUT_ROWS, DOWN_ROWS = D // CHUNKS, HC // CHUNKS, D // CHUNKS
FIRST = UP_ROWS + OUT_ROWS
ROWS = FIRST + DOWN_ROWS


def core_sum_kernel(ua, ub, oa, ob, out):
    def both(a, b):
        return (a.astype(F32) + b.astype(F32)).astype(BF16)

    for c in range(4):
        at = c * FIRST
        low, high = c * OUT_ROWS, (c + 1) * OUT_ROWS
        for i in range(4):
            to = at + i * OUT_ROWS
            out[0, to : to + OUT_ROWS] = both(ua[0, i, low:high], ub[0, i, low:high])
        out[0, at + UP_ROWS : at + FIRST] = both(oa[0, low:high], ob[0, low:high])


def core_sum(up, out):
    ups = pl.BlockSpec((1, 4, 4 * OUT_ROWS, D), lambda j, c: (j, 0, c, 0))
    outs = pl.BlockSpec((1, 4 * OUT_ROWS, D), lambda j, c: (j, c, 0))
    return pl.pallas_call(
        core_sum_kernel,
        out_shape=shape((2, CHUNKS * FIRST, D)),
        grid=(2, CHUNKS // 4),
        in_specs=[ups, ups, outs, outs],
        out_specs=pl.BlockSpec((1, 4 * FIRST, D), lambda j, c: (j, c, 0)),
        compiler_params=params(58),
        cost_estimate=cost(1000, 1000),
        name="core_sum",
    )(*up, *out)


def spread_kernel(index_ref, *refs):
    pieces, (up, out) = refs[:4], refs[4:]
    for m, a in enumerate(pieces):

        @pl.when(pl.program_id(0) == m)
        def _():
            for k in range(4):
                at = index_ref[0] ^ k
                for i in range(4):
                    rows = slice(i * OUT_ROWS, (i + 1) * OUT_ROWS)
                    up[at, 0, :, i * D : (i + 1) * D] = a[k, rows].astype(F32)
                out[at, 0] = a[k, UP_ROWS:].astype(F32)


def spread(index, pieces):
    def at(i, index):
        return (0, index[1] ^ i, 0, 0)

    up, out = pl.pallas_call(
        spread_kernel,
        out_shape=[shape((4, 4, OUT_ROWS, FF), F32), shape((4, 4, OUT_ROWS, D), F32)],
        grid_spec=pltpu.PrefetchScalarGridSpec(
            num_scalar_prefetch=1,
            grid=(4,),
            in_specs=[whole((4, FIRST, D))] * 4,
            out_specs=[
                pl.BlockSpec((4, 1, OUT_ROWS, FF), at),
                pl.BlockSpec((4, 1, OUT_ROWS, D), at),
            ],
        ),
        compiler_params=params(24),
        cost_estimate=cost(0, 8 * MB),
        name="spread",
    )(index, *pieces)
    return up.reshape(HC, FF), out.reshape(HC, D)


LATE = 3 * D + 2 * HC
EARLY = 3 * D + NB + 256


def arrange_kernel(row_ref, a0, a1, a2, a3, late, far, out):
    row = row_ref[0]
    for j, a in enumerate((a0, a1, a2, a3)):
        for s in range(3):
            lanes = pl.ds(pl.multiple_of(s * D + (row ^ j) * HC, HC), HC)
            out[:, lanes] = a[:, s * HC : (s + 1) * HC]
    both = jnp.concatenate([late[...].astype(F32), far[...].astype(F32)], axis=0)
    out[:, 3 * D :] = both.astype(BF16)


def arrange(row, pieces, late, far):
    rows = pieces[0].shape[0]
    return pl.pallas_call(
        arrange_kernel,
        out_shape=shape((rows, 3 * D + LATE)),
        grid_spec=pltpu.PrefetchScalarGridSpec(
            num_scalar_prefetch=1,
            grid=(1,),
            in_specs=[whole((rows, 3 * HC))] * 4 + [whole((8, LATE))] * 2,
            out_specs=whole((rows, 3 * D + LATE)),
        ),
        compiler_params=params(16),
        cost_estimate=cost(0, 8 * rows * D),
        name="arrange",
    )(row, *pieces, late, far)


def stack_kernel(a0, a1, a2, a3, weights, sums):
    for k, a in enumerate((a0, a1, a2, a3)):
        weights[k] = a[:, : 3 * D]
        sums[k] = a[:, 3 * D :]


def stack(pieces):
    rows, width = pieces[0].shape
    return pl.pallas_call(
        stack_kernel,
        out_shape=[shape((4, rows, 3 * D)), shape((4, rows, LATE))],
        grid=(1,),
        in_specs=[whole((rows, width))] * 4,
        out_specs=[whole((4, rows, 3 * D)), whole((4, rows, LATE))],
        compiler_params=params(16),
        cost_estimate=cost(0, 2 * MB),
        name="stack",
    )(*pieces)


def place_kernel(index_ref, low, high, out):
    for m, a in enumerate((low.at[0], low.at[1], high.at[1], high.at[0])):

        @pl.when(pl.program_id(0) == m)
        def _():
            for k in range(4):
                out[0, index_ref[1] ^ k] = a[k].astype(F32)


def place(index, low, high):
    rows = low.shape[2]
    return pl.pallas_call(
        place_kernel,
        out_shape=shape((4, 4, rows, 3 * D), F32),
        grid_spec=pltpu.PrefetchScalarGridSpec(
            num_scalar_prefetch=1,
            grid=(4,),
            in_specs=[whole(low.shape)] * 2,
            out_specs=pl.BlockSpec((1, 4, rows, 3 * D), lambda i, index: (index[0] ^ i, 0, 0, 0)),
        ),
        compiler_params=params(24),
        cost_estimate=cost(0, 24 * rows * D),
        name="place",
    )(index, low, high).reshape(HC, 3 * D)


def project_back_kernel(row_ref, dq, dk, dv, rk, rv, w0, w1, w2, w3, cp, sp, fr, dp, h0, h2, hs, bsum):
    row = row_ref[0]
    f = pl.program_id(0)
    later = (f > 0).astype(F32)
    keys = dk[0] + later * rk[0, 0].astype(F32)
    values = dv[0] + later * rv[0, 0].astype(F32)
    cosine, sine = cosines(cp, sp, fr, f)
    dp[0, :, :HC] = dq[0]
    dp[0, :, HC : 2 * HC] = turn(keys, cosine, -sine).astype(BF16)
    dp[0, :, 2 * HC :] = values.astype(BF16)
    grad = dp[0]
    sums = jnp.sum(grad.astype(F32), axis=0, keepdims=True)

    @pl.when(f == 0)
    def _():
        bsum[...] = jnp.zeros_like(bsum)

    number = lax.broadcasted_iota(jnp.int32, (8, 2 * HC), 0)
    bsum[...] = bsum[...] + jnp.where(number == row, sums[:, : 2 * HC], 0.0)
    bsum[:, :HC] = bsum[:, :HC] + jnp.where(number[:, :HC] == row + 4, sums[:, 2 * HC :], 0.0)
    for j, w in enumerate((w0, w1, w2, w3)):
        part = nt(grad, w[...]).astype(BF16)
        at = (0, slice(None), columns(row, j))
        h0[at] = part[:PR]
        hs[(0,) + at] = part[PR : 2 * PR]
        h2[at] = part[2 * PR : 3 * PR]
        hs[(1,) + at] = part[3 * PR :]


def project_back(row, dq, dk, dv, returned, weights, tables):
    block = pl.BlockSpec((1, TOK, HC), lambda f, *_: (f, 0, 0))
    late = [
        pl.BlockSpec((1, 1, TOK, HC), lambda f, *_, i=i: (i, jnp.maximum(f - 1, 0), 0, 0))
        for i in range(2)
    ]
    piece = pl.BlockSpec((1, PR, D), lambda f, *_: (f, 0, 0))
    return pl.pallas_call(
        project_back_kernel,
        out_shape=[
            shape((FPD, TOK, 3 * HC)),
            shape((FPD, PR, D)),
            shape((FPD, PR, D)),
            shape((2, FPD, PR, D)),
            shape((8, 2 * HC), F32),
        ],
        grid_spec=pltpu.PrefetchScalarGridSpec(
            num_scalar_prefetch=1,
            grid=(FPD,),
            in_specs=[block] * 3
            + late
            + [whole((HC, 3 * HC))] * 4
            + [whole((TOK, HC)), whole((TOK, HC)), whole((16, 2 * HC))],
            out_specs=[
                pl.BlockSpec((1, TOK, 3 * HC), lambda f, *_: (f, 0, 0)),
                piece,
                piece,
                pl.BlockSpec((2, 1, PR, D), lambda f, *_: (0, f, 0, 0)),
                whole((8, 2 * HC)),
            ],
        ),
        compiler_params=params(20),
        cost_estimate=cost(2 * FPD * TOK * D * 3 * HC, 14 * MB),
        name="project_back",
    )(row, dq, dk, dv, returned, returned, *weights, *tables)


def weight_kernel(row_ref, h, dp, w):
    w[0] = tn(h[...], dp[...]).astype(BF16)


def project_weight(row, hidden, dproj):
    tokens = FPD * TOK
    return pl.pallas_call(
        weight_kernel,
        out_shape=shape((4, HC, 3 * HC)),
        grid_spec=pltpu.PrefetchScalarGridSpec(
            num_scalar_prefetch=1,
            grid=(4,),
            in_specs=[
                pl.BlockSpec((tokens, HC), lambda j, row: (0, row[0] ^ j)),
                whole((tokens, 3 * HC)),
            ],
            out_specs=pl.BlockSpec((1, HC, 3 * HC), lambda j, row: (j, 0, 0)),
        ),
        compiler_params=params(20),
        cost_estimate=cost(2 * tokens * D * 3 * HC, 9 * MB),
        name="project_weight",
    )(row, hidden.reshape(tokens, D), dproj.reshape(tokens, 3 * HC))


def input_back_kernel(x, h0, near, far, table, mg, bsum, gate, out, sums):
    grad = h0[...].astype(F32) + near[0].astype(F32) + far[...].astype(F32)
    normal, rate = norm(x[...].astype(F32))
    put_half(sums, 0, jnp.sum(grad, axis=1))
    put_half(sums, D, jnp.sum(grad * normal, axis=1))
    sums[:, 2 * D : 3 * D] = gate[...]
    sums[:, 3 * D :] = bsum[...]
    out[...] = mg[...] + norm_back(normal, rate, grad * (1.0 + segment(table, 1)))


def input_back(x, h0, near, far, table, mg, bsum, gate):
    return pl.pallas_call(
        input_back_kernel,
        out_shape=[shape((FPD, PR, D), F32), shape((8, LATE), F32)],
        grid=(FPD // HALF,),
        in_specs=[half_spec(D)] * 2
        + [pl.BlockSpec((1, HALF, PR, D), lambda i: (0, i, 0, 0))]
        + [half_spec(D), whole((FPD, WIDE)), half_spec(D), whole((8, 2 * HC)), whole((8, D))],
        out_specs=[half_spec(D), whole((8, LATE))],
        compiler_params=params(20),
        cost_estimate=cost(20 * 512 * D, 10 * MB),
        name="input_back",
    )(x, h0, near, far, table, mg, bsum, gate)


def early_kernel(m, u, d, out):
    out[:, : 3 * D] = m[:, : 3 * D]
    out[:, 3 * D : 3 * D + NB] = u[...]
    out[:, 3 * D + NB : 3 * D + NB + 128] = d[...]
    out[:, 3 * D + NB + 128 :] = m[:, 3 * D :]


def early_sums(sums, usum, dsum):
    return pl.pallas_call(
        early_kernel,
        out_shape=shape((8, EARLY), F32),
        grid=(1,),
        in_specs=[whole(a.shape) for a in (sums, usum, dsum)],
        out_specs=whole((8, EARLY)),
        cost_estimate=cost(0, MB),
        name="early_sums",
    )(sums, usum, dsum)


def final_kernel(row_ref, *refs):
    row = row_ref[0]
    low, high, *early = refs[:6]
    ada, ab, qb, ob, ub, db, asum = refs[6:]
    late = [low.at[0], low.at[1], high.at[0], high.at[1]]
    early = [early[0], early[3], early[1], early[2]]

    def rows(ref, cols):
        value = ref[:, :, cols].astype(F32)
        return value.reshape(64, value.shape[-1])

    left = [rows(s, slice(EARLY, EARLY + HC)).astype(BF16) for s in early]
    for segment in range(6):
        source, start = ((late, 0), (late, 1), (early, 0), (early, 1), (early, 2), (late, 2))[segment]
        cols = slice(start * D, (start + 1) * D)
        product, total = 0.0, 0.0
        for s, ref in zip(left, source):
            right = rows(ref, cols)
            total = total + jnp.sum(right, axis=0, keepdims=True)
            product = product + tn(s, right.astype(BF16))
        at = segment * D
        ada[:, at : at + D] = product
        asum[0:1, at : at + D] = total

    def fold8(value):
        value = jnp.sum(value, axis=0)
        return value if value.shape[0] == 8 else value[:8] + value[8:]

    def bias(source, start, stop):
        return sum(
            fold8(ref[:, :, start:stop].astype(F32)) for ref in source
        )

    ab[...] = asum[0:1, pl.ds(pl.multiple_of(row * 1536, 512), 1536)]
    folded = bias(late, 3 * D, LATE)
    for i in range(3):
        chunk = 3 * row + i
        at = jnp.where(chunk < 4, chunk, chunk - 4)
        second = (chunk >= 4) & (chunk < 8)
        value = jnp.where(second, folded[:, HC:], folded[:, :HC])
        qb[:, i * HC : (i + 1) * HC] = take(value, at)
    folded = bias(early, 3 * D, EARLY)
    for i in range(2):
        at = 2 * row + i
        ub[:, i * NB : (i + 1) * NB] = take(folded[:, :NB], at)
        db[:, i * 128 : (i + 1) * 128] = take(folded[:, NB : NB + 128], at)
        ob[:, i * 128 : (i + 1) * 128] = take(folded[:, NB + 128 :], at)


def final_sums(row, late, early):
    sizes = (1536, 768, 256, 1024, 256)
    return pl.pallas_call(
        final_kernel,
        out_shape=[shape((HC, 6 * D), F32)] + [shape((1, n), F32) for n in sizes],
        grid_spec=pltpu.PrefetchScalarGridSpec(
            num_scalar_prefetch=1,
            grid=(1,),
            in_specs=[whole((2, 4, 16, LATE))] * 2
            + [whole((8, 8, EARLY + HC))] * 4,
            out_specs=[whole((HC, 6 * D))] + [whole((1, n)) for n in sizes],
            scratch_shapes=[pltpu.VMEM((8, 6 * D), F32)],
        ),
        compiler_params=params(28),
        cost_estimate=cost(2 * 256 * HC * 6 * D, 10 * MB),
        name="final_sums",
    )(row, *late, *early)


def row_sum(value):
    value = value + swap(value, CORE)
    return value + swap(value, DIRECT)


def row_pieces(value):
    return [value, swap(value, CORE), swap(value, DIRECT), swap(value, DIRECT ^ CORE)]


def by_row(pieces, row):
    a, b, c, d = pieces
    odd, high = row % 2 == 1, row >= 2
    a, b = jnp.where(odd, b, a), jnp.where(odd, a, b)
    c, d = jnp.where(odd, d, c), jnp.where(odd, c, d)
    return jnp.stack(
        [
            jnp.where(high, c, a),
            jnp.where(high, d, b),
            jnp.where(high, a, c),
            jnp.where(high, b, d),
        ]
    )


def quarter_rows(value, bit, index, axis):
    rows = value.shape[1] // 4
    at = lambda m: lax.dynamic_slice_in_dim(value, (index[axis] ^ m) * rows, rows, 1)
    return [at(0)] + [swap(at(m), bit * m) for m in (1, 2, 3)]


def add_all(parts):
    return sum(part.astype(F32) for part in parts).astype(BF16)


def exchange_rows(value, bit, index, axis):
    return add_all(quarter_rows(value, bit, index, axis))


def turn_heads(own, beside, across, order=lambda piece: piece):
    across = swap(across, DIRECT)
    return [own, swap(beside, CORE), across[0], swap(order(across)[1], CORE)]


def per_device(
    activations,
    noise_embed,
    frame_position,
    cotangent,
    ada_weight,
    ada_bias,
    qkv_weight,
    qkv_bias,
    out_weight,
    out_bias,
    up_weight,
    up_bias,
    down_weight,
    down_bias,
):
    row = lax.axis_index(("xl", "c")).astype(jnp.int32)
    row_arg = row.reshape(1)
    index = [lax.axis_index("y").astype(jnp.int32), lax.axis_index("z").astype(jnp.int32)]
    index_arg = jnp.stack(index)

    x0 = activations
    x2 = swap(x0, DIRECT)
    x1 = swap(x0, CORE)
    p0 = shift(activations[1:], 1)
    biases = (ada_bias, qkv_bias, out_bias, up_bias, down_bias)
    heads = list(split_heads(row_arg, qkv_weight))
    noise, heads[1] = lax.optimization_barrier((noise_embed, heads[1]))
    part, silu_own, *tables = prepare(row_arg, frame_position, noise, ada_weight, biases)
    across = swap(heads[2], OTHER)
    qkv_pieces = [heads[0], swap(heads[1], CORE), across]
    part = part + swap(part, CORE)
    table = part + swap(part, DIRECT)
    x2, p0, table, *qkv_pieces = lax.optimization_barrier((x2, p0, table, *qkv_pieces))

    qkv_pieces = qkv_pieces[:2] + [qkv_pieces[2][0], swap(qkv_pieces[2][1], CORE)]
    x3 = swap(x2, CORE)
    p2 = swap(p0, DIRECT)
    p1 = swap(p0, CORE)
    before_mods = shift(table[:, : 2 * D], 1)

    out_own, up_own, _ = lax.optimization_barrier((out_weight, up_weight, table))
    outs2 = swap(out_own, OTHER)
    ups2 = swap(up_own, OTHER)

    hidden1, q, k, v = project(True, row_arg, (x0, x1, x2, x3), table, table, qkv_pieces, tables)
    p2, down_own, q, before_mods = lax.optimization_barrier((p2, down_weight, q, before_mods))
    p3 = swap(p2, CORE)
    downs2 = swap(down_own, DIRECT)
    kp, vp = project(
        False, row_arg, (p0, p1, p2, p3), table, before_mods, qkv_pieces, tables
    )
    *mixed, lse = attend(frame_position, q, k, v, kp, vp)
    outs2, ups2, downs2, lse = lax.optimization_barrier((outs2, ups2, downs2, lse))
    outs = [out_weight, swap(out_own, CORE), outs2, swap(outs2, CORE)]
    ups = [up_weight, swap(up_own, CORE), ups2, swap(ups2, CORE)]
    downs = [down_weight, swap(down_own, CORE), downs2, swap(downs2, CORE)]
    turned = turn_heads(*mixed)
    branch, middle, hidden2, down_grad, dsum = mid(turned, outs, table, x0, cotangent)
    h2 = hidden2.reshape(TOKENS, D)
    dg = down_grad.reshape(TOKENS, D)
    act, upg, hg, usum = feed(row_arg, h2, dg, ups, table, downs)
    mg, bg, *ag, sums = mid_back(hg.reshape(FPD, PR, D), middle, branch, cotangent, table, outs)
    late = []
    back = turn_heads(*ag[:2], ag[2], order=lambda piece: late.append(piece) or piece)[:2]

    early = early_sums(sums, usum, dsum)
    early = early + swap(early, CORE)
    early, dg_later = lax.optimization_barrier((early, dg))
    early_far = swap(early, DIRECT)
    dk_part, ds_part, layer_output, gate = down_weight_grad(
        row_arg, after(dg_later, bg), act, downs, table, middle, cotangent
    )
    ds_part = swap(ds_part, CORE)
    upg, early_far, gate, far_back, *back = lax.optimization_barrier(
        (upg, early_far, gate, *late, *back)
    )
    back += [far_back[0], swap(far_back[1], CORE)]
    early = jnp.concatenate([(early + early_far).astype(BF16), silu_own], axis=1)
    early_far = swap(early, FAR)
    uk, us = up_weight_grad(row_arg, h2, upg)
    us = swap(us, CORE)
    uk, early, early_far, ds_part = lax.optimization_barrier((uk, early, early_far, ds_part))
    early = jnp.stack([early, early_far])
    early_parts = [early] + [swap(early, m) for m in (16, 32, 48)]
    ok, os = out_weight_grad(turned, bg)
    packed_down = (dk_part.astype(F32) + ds_part.astype(F32)).astype(BF16)

    ok, packed_down, early_parts, back = lax.optimization_barrier(
        (ok, packed_down, early_parts, back)
    )
    scattered_down = lax.psum_scatter(packed_down, ("y", "z"), scatter_dimension=1, tiled=True)
    dq_before, both = attend_back(False, frame_position, q, kp, vp, back, mixed, lse)
    returned = shift(both, -1)
    uk, dq_before = lax.optimization_barrier((uk, dq_before))
    packed = core_sum((uk, us), (ok, swap(os, CORE)))
    dq_before, packed = lax.optimization_barrier((dq_before, packed))
    scattered = lax.psum_scatter(packed, ("y", "z"), scatter_dimension=1, tiled=True)
    dq, dk, dv = attend_back(
        True, frame_position, q, k, v, back, mixed, lse, tables, dq_before
    )
    early_parts, dq_before = lax.optimization_barrier((early_parts, dq))[0], None
    early = jnp.concatenate(early_parts)
    early_all = [early] + [swap(early, m) for m in (4, 8, 12)]
    early = early[0].astype(F32)

    dproj, h0, h2_part, send, bsum = project_back(row_arg, dq, dk, dv, returned, qkv_pieces, tables)
    near = swap(send, CORE)
    qkv_parts = project_weight(row_arg, hidden1, dproj)
    far = swap((h2_part.astype(F32) + near[1].astype(F32)).astype(BF16), DIRECT)
    qkv_parts, early_all, scattered_down = lax.optimization_barrier(
        (qkv_parts, early_all, scattered_down)
    )
    down_far = swap(scattered_down[1], DIRECT)
    qkv_parts = exchange_rows(qkv_parts, 4, index, 0)
    far, qkv_parts, down_far = lax.optimization_barrier((far, qkv_parts, down_far))
    down_share = scattered_down[0].astype(F32) + down_far.astype(F32)
    down_far = swap(down_share.astype(BF16), FAR)
    quarters = quarter_rows(qkv_parts, 16, index, 1)
    input_grad, late = input_back(x0, h0, near, far, table, mg, bsum, gate)
    late, *quarters = lax.optimization_barrier((late, *quarters))
    qkv_parts = add_all(quarters)
    late_near = swap(late, CORE)
    late, late_near, qkv_parts, down_far = lax.optimization_barrier(
        (late, late_near, qkv_parts, down_far)
    )
    down_share = (down_share + down_far.astype(F32)).astype(BF16)
    late = late + late_near
    late_far = swap(late, DIRECT)
    qkv_far = swap(qkv_parts, FAR)
    late, late_far, qkv_parts, qkv_far = lax.optimization_barrier(
        (late, late_far, qkv_parts, qkv_far)
    )
    late = late + late_far
    qkv_parts = add_all([qkv_parts, qkv_far])
    late_low = late.astype(BF16)
    late_far = swap(late_low, FAR)
    turned = turn_heads(qkv_parts[0], qkv_parts[1], qkv_parts[2:])
    last = arrange(row_arg, turned, late_low, late_far)

    down_total = lax.all_gather(down_share, ("y", "z"), axis=0, tiled=True).astype(F32)
    scattered, last = lax.optimization_barrier((scattered, last))
    last = [last] + [swap(last, m) for m in (16, 32, 48)]
    share = scattered[0].astype(F32) + swap(scattered[1], DIRECT).astype(F32)
    share, last = lax.optimization_barrier((share, last))
    share_far = swap(share.astype(BF16), FAR)
    weights, sums_late = stack(last)
    weights = jnp.stack([weights, swap(weights, 4)])
    sums_late = jnp.stack([sums_late, swap(sums_late, 12)])
    share_far, weights, sums_late = lax.optimization_barrier((share_far, weights, sums_late))
    share = (share + share_far.astype(F32)).astype(BF16)
    share = jnp.stack([share] + [swap(share, m) for m in (4, 8, 12)])
    weights_far, sums_far = swap(weights, 12), swap(sums_late, 4)
    share, sums_far = lax.optimization_barrier((share, sums_far))
    share_all = [share] + [swap(share, m) for m in (16, 32, 48)]
    up_total, out_total = spread(index_arg, share_all)
    qkv_total = place(index_arg, weights, weights_far)

    ada_total, *bias_sums = final_sums(row_arg, (sums_late, sums_far), early_all)
    ada_sum, qkv_sum, out_sum, up_sum, down_sum = [b[0] for b in bias_sums]
    mod_own = jnp.concatenate(
        [late[:, : 2 * D], early[:, : 3 * D], late[:, 2 * D : 3 * D]], axis=1
    ).astype(BF16)
    silu_grad = nt(mod_own, ada_weight)
    silu_grad = by_row(row_pieces(silu_grad), row).transpose(1, 0, 2).reshape(FPD, D)
    embed = noise_embed.astype(F32)
    sigma = jax.nn.sigmoid(embed)
    embed_grad = silu_grad * (sigma * (1.0 + embed * (1.0 - sigma)))

    return (
        layer_output,
        input_grad,
        embed_grad,
        ada_total,
        ada_sum,
        qkv_total,
        qkv_sum,
        out_total,
        out_sum,
        up_total,
        up_sum,
        down_total,
        down_sum,
    )


def solution(mesh):
    fine = Mesh(mesh.devices.reshape(2, 4, 4, 2, 2), AXES)
    seq, row = ("xh", "z", "y"), ("xl", "c")
    token, weight, vector = P(seq, row, None), P(row, None), P(row)
    in_specs = (token, P(seq, None), P(seq), token) + (weight, vector) * 5
    out_specs = (token, token, P(seq, None)) + (weight, vector) * 5
    return jax.shard_map(
        per_device, mesh=fine, in_specs=in_specs, out_specs=out_specs, check_vma=False
    )
```

```python
import math

import jax
import jax.numpy as jnp
from jax import lax
from jax.experimental import pallas as pl
from jax.experimental.pallas import tpu as pltpu
from jax.sharding import Mesh, PartitionSpec as P

F32 = jnp.float32
BF16 = jnp.bfloat16
HD = 64
GRID = 16
FPD = 8
PR = 64
D = 1024
FF = 4096
HC = 256
TOK = 256
PREV = 7
AXES = ("xh", "z", "y", "xl", "c")
CORE, DIRECT, OTHER, FAR = 1, 2, 66, 64
MB = 1024 * 1024


def swap(value, mask):
    return lax.ppermute(value, AXES, [(i, i ^ mask) for i in range(128)])


def shift(value, steps):
    return lax.ppermute(value, AXES, [(i, (i + 4 * steps) % 128) for i in range(128)])


def after(value, *others):
    return lax.optimization_barrier((value,) + others)[0]


def nt(left, right):
    return lax.dot_general(left, right, (((1,), (1,)), ((), ())), preferred_element_type=F32)


def tn(left, right):
    return lax.dot_general(left, right, (((0,), (0,)), ((), ())), preferred_element_type=F32)


def nn(left, right):
    return jnp.dot(left, right, preferred_element_type=F32)


def norm(values):
    center = values - jnp.mean(values, axis=-1, keepdims=True)
    spread = jnp.mean(center * center, axis=-1, keepdims=True)
    rate = lax.rsqrt(spread + 1e-06)
    return center * rate, rate


def norm_back(normal, rate, grad):
    mean_grad = jnp.mean(grad, axis=-1, keepdims=True)
    mean_both = jnp.mean(grad * normal, axis=-1, keepdims=True)
    return rate * (grad - mean_grad - normal * mean_both)


def turn(values, cosine, sine):
    lanes = lax.broadcasted_iota(jnp.int32, values.shape, 1)
    other = jnp.where(
        lanes % HD < HD // 2, pltpu.roll(values, HC - HD // 2, 1), pltpu.roll(values, HD // 2, 1)
    )
    return values * cosine + other * sine


def params(mib):
    return pltpu.CompilerParams(vmem_limit_bytes=mib * MB)


def cost(flops, moved, exps=0):
    return pl.CostEstimate(flops=int(flops), bytes_accessed=int(moved), transcendentals=int(exps))


def whole(shape):
    return pl.BlockSpec(shape, lambda i, *_: (0,) * len(shape))


def columns(row, j):
    return pl.ds(pl.multiple_of((row ^ j) * HC, HC), HC)


def shape(dims, kind=BF16):
    return jax.ShapeDtypeStruct(dims, kind)


UB, QB, OB, DB, WIDE = 6144, 6656, 7168, 7296, 7424


def put(ref, start, at, value):
    cols = slice(start, start + value.shape[1])
    number = lax.broadcasted_iota(jnp.int32, (8, value.shape[1]), 0)
    ref[:, cols] = jnp.where(number == at, value, ref[:, cols])


def take(value, at):
    number = lax.broadcasted_iota(jnp.int32, value.shape, 0)
    return jnp.sum(jnp.where(number == at, value, 0.0), axis=0, keepdims=True)


def put_half(ref, start, value):
    cols = slice(start, start + value.shape[1])
    number = lax.broadcasted_iota(jnp.int32, (8, value.shape[1]), 0)
    both = jnp.concatenate([value, value], axis=0)
    ref[:, cols] = jnp.where(number // 4 == pl.program_id(0), both, ref[:, cols])


def unfold(ref, start, width):
    return jnp.concatenate([ref[i : i + 1, start : start + width] for i in range(8)], axis=1)


def prepare_kernel(row_ref, pos_ref, noise, ada, ab, qb, ob, ub, db, pack, silu, cp, sp, frames):
    row = row_ref[0]
    embed = noise[...].astype(F32)
    value = (embed / (1.0 + jnp.exp(-embed))).astype(BF16)
    own = jnp.where(
        row < 2,
        jnp.where(row == 0, value[:, :HC], value[:, HC : 2 * HC]),
        jnp.where(row == 2, value[:, 2 * HC : 3 * HC], value[:, 3 * HC :]),
    )
    silu[...] = own
    pack[:, UB:] = jnp.zeros((FPD, WIDE - UB), F32)
    for segment in range(6):
        cols = slice(segment * D, (segment + 1) * D)
        pack[:, cols] = nn(own, ada[:, cols])
    bias = pl.ds(pl.multiple_of(row * 1536, 512), 1536)
    pack[:, bias] = pack[:, bias] + ab[...].astype(F32)
    for i in range(2):
        at = 2 * row + i
        put(pack, UB, at, ub[:, i * 512 : (i + 1) * 512].astype(F32))
        put(pack, OB, at, ob[:, i * 128 : (i + 1) * 128].astype(F32))
        put(pack, DB, at, db[:, i * 128 : (i + 1) * 128].astype(F32))
    for i in range(3):
        chunk = 3 * row + i
        at = jnp.where(chunk < 4, chunk, chunk - 4)
        second = (chunk >= 4) & (chunk < 8)
        value = qb[:, i * HC : (i + 1) * HC].astype(F32)
        put(pack, QB, jnp.where(second, -1, at), value)
        put(pack, QB + HC, jnp.where(second, at, -1), value)

    def parts(dims):
        lane = lax.broadcasted_iota(jnp.int32, dims, 1)
        index = lane % (HD // 2)
        quarter, eighth = HD // 4, HD // 8
        in_frame = index < quarter
        in_row = (index >= quarter) & (index < quarter + eighth)
        offset = jnp.where(
            in_frame, index, jnp.where(in_row, index - quarter, index - quarter - eighth)
        ).astype(F32)
        length = jnp.where(in_frame, 1.0 * quarter, 1.0 * eighth)
        frequency = jnp.exp(-math.log(10000.0) * offset / length)
        sign = jnp.where(lane % HD < HD // 2, -1.0, 1.0)
        return in_frame, in_row, frequency, sign

    in_frame, in_row, frequency, sign = parts((TOK, HC))
    slot = lax.broadcasted_iota(jnp.int32, (TOK, HC), 0)
    patch = ((slot // PR) ^ row) * PR + slot % PR
    angle = jnp.where(in_row, patch // GRID, patch % GRID).astype(F32) * frequency
    cp[...] = jnp.where(in_frame, 0.0, jnp.cos(angle))
    sp[...] = jnp.where(in_frame, 0.0, jnp.sin(angle) * sign)
    in_frame, _, frequency, sign = parts((16, HC))
    slot = lax.broadcasted_iota(jnp.int32, (16, HC), 0)
    place = pos_ref[0] - PREV + (slot - FPD)
    for f in range(FPD):
        place = jnp.where(slot == f, pos_ref[f], place)
    angle = place.astype(F32) * frequency
    frames[:, :HC] = jnp.where(in_frame, jnp.cos(angle), 0.0)
    frames[:, HC:] = jnp.where(in_frame, jnp.sin(angle) * sign, 0.0)


def prepare(row, places, noise, ada, biases):
    return pl.pallas_call(
        prepare_kernel,
        out_shape=[
            shape((FPD, WIDE), F32),
            shape((FPD, HC)),
            shape((TOK, HC), F32),
            shape((TOK, HC), F32),
            shape((16, 2 * HC), F32),
        ],
        grid_spec=pltpu.PrefetchScalarGridSpec(
            num_scalar_prefetch=2,
            grid=(1,),
            in_specs=[whole((FPD, D)), whole((HC, 6 * D))]
            + [whole((1, b.shape[0])) for b in biases],
            out_specs=[
                whole((FPD, WIDE)),
                whole((FPD, HC)),
                whole((TOK, HC)),
                whole((TOK, HC)),
                whole((16, 2 * HC)),
            ],
        ),
        compiler_params=params(24),
        cost_estimate=cost(2 * 8 * HC * 6 * D, 4 * MB, 4 * TOK * HC),
        name="prepare",
    )(row, places, noise, ada, *[b[None] for b in biases])


def split_heads_kernel(row_ref, q, k, v, p0, p1, p23):
    for j, p in enumerate((p0, p1, p23.at[0], p23.at[1])):

        @pl.when(pl.program_id(0) == j)
        def _():
            p[:, :HC] = q[...]
            p[:, HC : 2 * HC] = k[...]
            p[:, 2 * HC :] = v[...]


def split_heads(row, weight):
    piece = (HC, 3 * HC)
    return pl.pallas_call(
        split_heads_kernel,
        out_shape=[shape(piece), shape(piece), shape((2,) + piece)],
        grid_spec=pltpu.PrefetchScalarGridSpec(
            num_scalar_prefetch=1,
            grid=(4,),
            in_specs=[
                pl.BlockSpec((HC, HC), lambda j, row, s=s: (0, 4 * s + (row[0] ^ j)))
                for s in range(3)
            ],
            out_specs=[whole(piece), whole(piece), whole((2,) + piece)],
        ),
        compiler_params=params(12),
        cost_estimate=cost(0, 3 * MB),
        name="split_heads",
    )(row, weight, weight, weight)


def cosines(cp, sp, frames, at):
    both = frames[pl.ds(at, 1), :]
    return cp[...] + both[:, :HC], sp[...] + both[:, HC:]


def project_kernel(own, row_ref, x0, x1, x2, x3, table, mods, w0, w1, w2, w3, cp, sp, fr, *outs):
    row = row_ref[0]
    f = pl.program_id(0)
    if own:
        h_ref, q_ref, k_ref, v_ref = outs
        first, at, angle = 0, f, f
    else:
        k_ref, v_ref, h_ref = outs
        first, at, angle = HC, f + FPD - PREV, f + FPD
    x = jnp.concatenate([r[0] for r in (x0, x1, x2, x3)], axis=0).astype(F32)
    normal, _ = norm(x)
    shift_row = mods[pl.ds(at, 1), :D]
    scale_row = mods[pl.ds(at, 1), D : 2 * D]
    hidden = (normal * (1.0 + scale_row) + shift_row).astype(BF16)
    where = (0,) if own else ()
    h_ref[where + (slice(None), slice(None))] = hidden
    low, high = table[pl.ds(row, 1), QB : QB + 2 * HC], table[pl.ds(row + 4, 1), QB : QB + HC]
    total = jnp.concatenate([low, high], axis=1)[:, first:]
    for j, w in enumerate((w0, w1, w2, w3)):
        total = total + nn(h_ref[where + (slice(None), columns(row, j))], w[:, first:])
    cosine, sine = cosines(cp, sp, fr, angle)
    if own:
        q_ref[0] = (turn(total[:, :HC], cosine, sine).astype(BF16).astype(F32) * 0.125).astype(BF16)
        total = total[:, HC:]
    k_ref[0] = turn(total[:, :HC], cosine, sine).astype(BF16)
    v_ref[0] = total[:, HC:].astype(BF16)


def project(own, row, xs, table, mods, weights, tables):
    frames = xs[0].shape[0]
    x_spec = pl.BlockSpec((1, PR, D), lambda f, *_: (f, 0, 0))
    out_spec = pl.BlockSpec((1, TOK, HC), lambda f, *_: (f, 0, 0))
    out = shape((frames, TOK, HC))
    if own:
        out_specs = [pl.BlockSpec((1, TOK, D), lambda f, *_: (f, 0, 0)), out_spec, out_spec, out_spec]
        out_shape = [shape((frames, TOK, D)), out, out, out]
        scratch = []
    else:
        out_specs = [out_spec, out_spec]
        out_shape = [out, out]
        scratch = [pltpu.VMEM((TOK, D), BF16)]
    return pl.pallas_call(
        lambda *refs: project_kernel(own, *refs),
        out_shape=out_shape,
        grid_spec=pltpu.PrefetchScalarGridSpec(
            num_scalar_prefetch=1,
            grid=(frames,),
            in_specs=[x_spec] * 4
            + [whole((FPD, WIDE)), whole(mods.shape)]
            + [whole((HC, 3 * HC))] * 4
            + [whole((TOK, HC)), whole((TOK, HC)), whole((16, 2 * HC))],
            out_specs=out_specs,
            scratch_shapes=scratch,
        ),
        compiler_params=params(20),
        cost_estimate=cost(2 * frames * TOK * D * 3 * HC, frames * TOK * D * 4 + 4 * MB),
        name="project_own" if own else "project_prev",
    )(row, *xs, table, mods, *weights, *tables)


def head_lanes():
    return lax.broadcasted_iota(jnp.int32, (TOK, HC), 1) // HD


def attend_kernel(pos_ref, q, k, v, kp, vp, o0, o1, o23, lse, qs, scores, acc, top, low):
    f = pl.program_id(0)
    place = pos_ref[f]
    lanes = head_lanes()
    query = q[0]
    for h in range(4):
        qs[pl.ds(h * TOK, TOK), :] = jnp.where(lanes == h, query, jnp.zeros_like(query))
    top[...] = jnp.full_like(top, -1e30)
    low[...] = jnp.zeros_like(low)
    acc[...] = jnp.zeros_like(acc)
    before = jnp.maximum(place - f, 0)
    start = jnp.maximum(f - place, 0)

    def score(keys, slot):
        for h in range(4):
            rows = pl.ds(h * TOK, TOK)
            s = nt(qs[rows, :], keys)
            scores[slot, rows, :] = s
            top[rows, :] = jnp.maximum(top[rows, :], jnp.maximum(s[:, :128], s[:, 128:]))

    def mix(values, slot):
        for h in range(4):
            rows = pl.ds(h * TOK, TOK)
            p = jnp.exp(scores[slot, rows, :] - jnp.concatenate([top[rows, :]] * 2, axis=1))
            low[rows, :] = low[rows, :] + (p[:, :128] + p[:, 128:])
            acc[rows, :] = acc[rows, :] + nn(p.astype(BF16), values)

    def run(step):
        def prev(i, _):
            at = PREV - before + i
            step(kp[at] if step is score else vp[at], i)
            return 0

        def own(g, _):
            step(k[g] if step is score else v[g], g - f + place)
            return 0

        lax.fori_loop(0, before, prev, 0)
        lax.fori_loop(start, f + 1, own, 0)

    run(score)
    for h in range(4):
        rows = pl.ds(h * TOK, TOK)
        top[rows, :] = jnp.broadcast_to(jnp.max(top[rows, :], axis=1, keepdims=True), (TOK, 128))
    run(mix)
    result = jnp.zeros((TOK, HC), F32)
    logs = jnp.zeros((TOK, 128), F32)
    narrow = lax.broadcasted_iota(jnp.int32, (TOK, 128), 1)
    for h in range(4):
        rows = pl.ds(h * TOK, TOK)
        total = jnp.sum(low[rows, :], axis=1, keepdims=True)
        result = jnp.where(lanes == h, acc[rows, :] / total, result)
        logs = jnp.where(narrow == h, top[rows, :] + jnp.log(total), logs)
    lse[0] = logs.T[:8]
    result = result.astype(BF16)
    o0[0] = result[:PR]
    o1[0] = result[PR : 2 * PR]
    o23[0, 0] = result[2 * PR : 3 * PR]
    o23[1, 0] = result[3 * PR :]


def attend(places, q, k, v, kp, vp):
    block = pl.BlockSpec((1, TOK, HC), lambda f, *_: (f, 0, 0))
    piece = pl.BlockSpec((1, PR, HC), lambda f, *_: (f, 0, 0))
    return pl.pallas_call(
        attend_kernel,
        out_shape=[shape((FPD, PR, HC))] * 2
        + [shape((2, FPD, PR, HC)), shape((FPD, 8, TOK), F32)],
        grid_spec=pltpu.PrefetchScalarGridSpec(
            num_scalar_prefetch=1,
            grid=(FPD,),
            in_specs=[block]
            + [whole((FPD, TOK, HC))] * 2
            + [whole((PREV, TOK, HC))] * 2,
            out_specs=[piece] * 2
            + [
                pl.BlockSpec((2, 1, PR, HC), lambda f, *_: (0, f, 0, 0)),
                pl.BlockSpec((1, 8, TOK), lambda f, *_: (f, 0, 0)),
            ],
            scratch_shapes=[
                pltpu.VMEM((4 * TOK, HC), BF16),
                pltpu.VMEM((8, 4 * TOK, TOK), F32),
                pltpu.VMEM((4 * TOK, HC), F32),
                pltpu.VMEM((4 * TOK, 128), F32),
                pltpu.VMEM((4 * TOK, 128), F32),
            ],
        ),
        compiler_params=params(58),
        cost_estimate=cost(36 * 4 * 2 * 2 * TOK**3, 6 * MB, 36 * 4 * TOK * TOK),
        name="attend",
    )(places, q, k, v, kp, vp)


def attend_back_kernel(own, pos_ref, q, k, v, g0, g1, g2, g3, o0, o1, o23, lse, *rest):
    if own:
        cp, sp, fr, before_ref, dq, dk, dv, qs, gs, ks, pl_scr, dl_scr, ds_scr, dq_acc = rest
        dk_acc, dv_acc = dk, dv
    else:
        dq, both_ref, qs, gs, ks, pl_scr, dl_scr, ds_scr, dq_acc, dk_acc, dv_acc = rest
    f = pl.program_id(0)
    place = pos_ref[f]
    lanes = head_lanes()

    @pl.when(f == 0)
    def _():
        for ref in (dk_acc, dv_acc):
            ref[...] = jnp.zeros_like(ref)

    def prelude():
        query = q[0]
        grad = jnp.concatenate([r[0] for r in (g0, g1, g2, g3)], axis=0)
        mixed = jnp.concatenate([o0[0], o1[0], o23[0, 0], o23[1, 0]], axis=0)
        for h in range(4):
            rows = pl.ds(h * TOK, TOK)
            qs[rows, :] = jnp.where(lanes == h, query, jnp.zeros_like(query))
            gs[rows, :] = jnp.where(lanes == h, grad, jnp.zeros_like(grad))
        both = grad.astype(F32) * mixed.astype(F32)
        pick = (
            lax.broadcasted_iota(jnp.int32, (8, HC), 1) // HD
            == lax.broadcasted_iota(jnp.int32, (8, HC), 0)
        ).astype(F32)
        return lax.dot_general(
            pick, both, (((1,), (1,)), ((), ())),
            preferred_element_type=F32, precision=lax.Precision.HIGHEST,
        )

    def step(delta, logs, at):
        keys, values = k[at], v[at]
        for h in range(4):
            rows = pl.ds(h * TOK, TOK)
            ks[rows, :] = jnp.where(lanes == h, keys, jnp.zeros_like(keys))
            p = jnp.exp(nt(keys, qs[rows, :]) - logs[h : h + 1])
            ds = (p * (nt(values, gs[rows, :]) - delta[h : h + 1])).astype(BF16)
            pl_scr[:, rows] = p.astype(BF16)
            dl_scr[:, rows] = ds
            ds_scr[rows, :] = ds
        dv_acc[at] = dv_acc[at] + nn(pl_scr[...], gs[...])
        dk_acc[at] = dk_acc[at] + nn(dl_scr[...], qs[...])
        dq_acc[...] = dq_acc[...] + tn(ds_scr[...], ks[...])

    def sweep(low, high):
        delta = prelude()
        logs = lse[0]
        dq_acc[...] = jnp.zeros_like(dq_acc)

        def one(at, _):
            step(delta, logs, at)
            return 0

        lax.fori_loop(low, high, one, 0)

    if own:
        sweep(jnp.maximum(f - place, 0), f + 1)
        cosine, sine = cosines(cp, sp, fr, f)
        dq[0] = turn((dq_acc[...] + before_ref[0]) * 0.125, cosine, -sine).astype(BF16)
    else:
        count = jnp.maximum(place - f, 0)

        @pl.when(count > 0)
        def _():
            sweep(PREV - count, PREV)
            dq[0] = dq_acc[...]

        @pl.when(count == 0)
        def _():
            dq[0] = jnp.zeros_like(dq_acc)

        @pl.when(f == FPD - 1)
        def _():
            both_ref[0] = dk_acc[...].astype(BF16)
            both_ref[1] = dv_acc[...].astype(BF16)


def attend_back(own, places, q, k, v, grads, mixed, lse, tables=None, before=None):
    block = pl.BlockSpec((1, TOK, HC), lambda f, *_: (f, 0, 0))
    piece = pl.BlockSpec((1, PR, HC), lambda f, *_: (f, 0, 0))
    count = FPD if own else PREV
    wide = pltpu.VMEM((4 * TOK, HC), BF16)
    tall = pltpu.VMEM((TOK, 4 * TOK), BF16)
    scratch = [wide, wide, wide, tall, tall, wide, pltpu.VMEM((TOK, HC), F32)]
    specs = []
    extra = ()
    if own:
        specs = [whole((TOK, HC)), whole((TOK, HC)), whole((16, 2 * HC)), block]
        extra = tuple(tables) + (before,)
    else:
        scratch += [pltpu.VMEM((PREV, TOK, HC), F32)] * 2
    return pl.pallas_call(
        lambda *refs: attend_back_kernel(own, *refs),
        out_shape=[shape((FPD, TOK, HC), BF16 if own else F32)]
        + ([shape((FPD, TOK, HC), F32)] * 2 if own else [shape((2, PREV, TOK, HC))]),
        grid_spec=pltpu.PrefetchScalarGridSpec(
            num_scalar_prefetch=1,
            grid=(FPD,),
            in_specs=[block]
            + [whole((count, TOK, HC))] * 2
            + [piece] * 6
            + [pl.BlockSpec((2, 1, PR, HC), lambda f, *_: (0, f, 0, 0))]
            + [pl.BlockSpec((1, 8, TOK), lambda f, *_: (f, 0, 0))]
            + specs,
            out_specs=[block]
            + ([whole((FPD, TOK, HC))] * 2 if own else [whole((2, PREV, TOK, HC))]),
            scratch_shapes=scratch,
        ),
        compiler_params=params(58),
        cost_estimate=cost(1000 if own else 12 * 4 * 5 * 2 * TOK**3, 1000 if own else 12 * MB),
        name="attend_back_own" if own else "attend_back_prev",
    )(places, q, k, v, *grads, *mixed, lse, *extra)


HALF = 4
RAW = HALF * PR


def flat(ref):
    return ref[...].reshape(RAW, ref.shape[-1])


def frames_of(value):
    return value.reshape(HALF, PR, value.shape[-1])


def segment(table, s):
    both = table[:, s * D : (s + 1) * D]
    return jnp.where(pl.program_id(0) == 0, both[:HALF], both[HALF:])[:, None, :]


def fold(out, start, width, row):
    @pl.when(pl.program_id(0) == 0)
    def _():
        out[:, start : start + width] = jnp.zeros((8, width), F32)

    for i in range(8):
        at = (slice(i, i + 1), slice(start, start + width))
        out[at] = out[at] + row[:, i * width : (i + 1) * width]


def mid_kernel(o0, o1, o2, o3, w0, w1, w2, w3, table, x, cot, branch, middle, hidden, down, dsum):
    total = unfold(table, OB, 128)
    for o, w in zip((o0, o1, o2, o3), (w0, w1, w2, w3)):
        total = total + nn(flat(o), w[...])
    branched = frames_of(total)
    branch[...] = branched
    mid_value = x[...].astype(F32) + segment(table, 2) * branched
    middle[...] = mid_value
    normal, _ = norm(mid_value)
    hidden[...] = (normal * (1.0 + segment(table, 4)) + segment(table, 3)).astype(BF16)
    grad = (segment(table, 5) * cot[...].astype(F32)).astype(BF16)
    down[...] = grad
    fold(dsum, 0, 128, jnp.sum(grad.astype(F32).reshape(RAW, D), axis=0, keepdims=True))


def half_spec(width):
    return pl.BlockSpec((HALF, PR, width), lambda i, *_: (i, 0, 0))


def mid(pieces, weights, table, x, cot):
    return pl.pallas_call(
        mid_kernel,
        out_shape=[
            shape((FPD, PR, D), F32),
            shape((FPD, PR, D), F32),
            shape((FPD, PR, D)),
            shape((FPD, PR, D)),
            shape((8, 128), F32),
        ],
        grid=(FPD // HALF,),
        in_specs=[half_spec(HC)] * 4
        + [whole((HC, D))] * 4
        + [whole((FPD, WIDE)), half_spec(D), half_spec(D)],
        out_specs=[half_spec(D)] * 4 + [whole((8, 128))],
        compiler_params=params(26),
        cost_estimate=cost(2 * 512 * D * D, 12 * MB),
        name="mid",
    )(*pieces, *weights, table, x, cot)


def mid_back_kernel(hg, middle, branch, cot, table, w0, w1, w2, w3, mg, bg, a0, a1, a23, sums):
    grad = hg[...]
    normal, rate = norm(middle[...])
    put_half(sums, D, jnp.sum(grad, axis=1))
    put_half(sums, 2 * D, jnp.sum(grad * normal, axis=1))
    total = cot[...].astype(F32) + norm_back(normal, rate, grad * (1.0 + segment(table, 4)))
    mg[...] = total
    put_half(sums, 0, jnp.sum(total * branch[...], axis=1))
    low = (segment(table, 2) * total).astype(BF16)
    bg[...] = low
    low = low.reshape(RAW, D)
    fold(sums, 3 * D, 128, jnp.sum(low.astype(F32), axis=0, keepdims=True))
    for j, w in enumerate((w0, w1, w2, w3)):
        value = frames_of(nt(low, w[...]).astype(BF16))
        if j < 2:
            (a0, a1)[j][...] = value
        else:
            a23[j - 2] = value


def mid_back(hg, middle, branch, cot, table, weights):
    return pl.pallas_call(
        mid_back_kernel,
        out_shape=[shape((FPD, PR, D), F32), shape((FPD, PR, D))]
        + [shape((FPD, PR, HC))] * 2
        + [shape((2, FPD, PR, HC)), shape((8, 3 * D + 128), F32)],
        grid=(FPD // HALF,),
        in_specs=[half_spec(D)] * 4
        + [whole((FPD, WIDE))]
        + [whole((HC, D))] * 4,
        out_specs=[half_spec(D)] * 2
        + [half_spec(HC)] * 2
        + [pl.BlockSpec((2, HALF, PR, HC), lambda i: (0, i, 0, 0)), whole((8, 3 * D + 128))],
        compiler_params=params(26),
        cost_estimate=cost(2 * 512 * D * D, 12 * MB),
        name="mid_back",
    )(hg, middle, branch, cot, table, *weights)


NB = 512
STEPS = FF // NB
PER = D // NB
TOKENS = FPD * PR


def block_of(t):
    phase = t // PER
    return ((phase % 2) * 2) ^ (phase // 2)


def up_column(t, row):
    return (row ^ block_of(t)) * PER + t % PER


def down_row(t):
    return block_of(t) * PER + t % PER


def down_spec(j):
    phase = (0, 2, 1, 3)[j]
    return pl.BlockSpec((NB, D), lambda t, row: (jnp.clip(t - phase * PER, 0, PER - 1), 0))


def pick_down(d0, d1, d2, d3):
    phase = pl.program_id(0) // PER
    return jnp.where(
        phase < 2,
        jnp.where(phase == 0, d0[...], d2[...]),
        jnp.where(phase == 2, d1[...], d3[...]),
    )


def feed_kernel(row_ref, h2, dg, u0, u1, u2, u3, table, d0, d1, d2, d3, act, upg, hg, usum):
    row = row_ref[0]
    ups = (u0, u1, u2, u3)
    down = pick_down(d0, d1, d2, d3)
    at = pl.ds(up_column(pl.program_id(0), row), 1)
    u = table[at, UB : UB + NB]
    for j, w in enumerate(ups):
        u = u + nn(h2[:, columns(row, j)], w[...])
    rate = math.sqrt(2.0 / math.pi)
    square = u * u
    half = 0.5 + 0.5 * jnp.tanh(u * (rate + (rate * 0.044715) * square))
    active = u * half
    act[...] = active.astype(BF16)
    slope = half + active * (1.0 - half) * (2.0 * rate + (6.0 * rate * 0.044715) * square)
    grad = (nt(dg[...], down) * slope).astype(BF16)
    upg[...] = grad
    put(usum, 0, up_column(pl.program_id(0), row), jnp.sum(grad.astype(F32), axis=0, keepdims=True))

    @pl.when(pl.program_id(0) == 0)
    def _():
        hg[...] = jnp.zeros_like(hg)

    for j, w in enumerate(ups):
        hg[:, columns(row, j)] = hg[:, columns(row, j)] + nt(grad, w[...])


def feed(row, h2, dg, ups, table, downs):
    tok = whole((TOKENS, D))
    block = pl.BlockSpec((TOKENS, NB), lambda t, row: (0, t))
    return pl.pallas_call(
        feed_kernel,
        out_shape=[
            shape((TOKENS, FF)),
            shape((TOKENS, FF)),
            shape((TOKENS, D), F32),
            shape((8, NB), F32),
        ],
        grid_spec=pltpu.PrefetchScalarGridSpec(
            num_scalar_prefetch=1,
            grid=(STEPS,),
            in_specs=[tok, tok]
            + [pl.BlockSpec((HC, NB), lambda t, row: (0, up_column(t, row[0])))] * 4
            + [whole((FPD, WIDE))]
            + [down_spec(j) for j in range(4)],
            out_specs=[block, block, tok, whole((8, NB))],
        ),
        compiler_params=params(58),
        cost_estimate=cost(3 * 2 * TOKENS * D * FF, 30 * MB, TOKENS * FF),
        name="feed",
    )(row, h2, dg, *ups, table, *downs)


def down_weight_kernel(row_ref, dg, act, d0, d1, d2, d3, table, middle, cot, dk, ds, out, gate, dn):
    t = pl.program_id(0)
    down = pick_down(d0, d1, d2, d3)
    active = act[...]

    @pl.when(t == 0)
    def _():
        dn[...] = jnp.zeros_like(dn)

    dn[...] = dn[...] + nn(active, down)
    part = tn(active, dg[...]).astype(BF16)

    @pl.when(t < STEPS // 2)
    def _():
        dk[0] = part

    @pl.when(t >= STEPS // 2)
    def _():
        ds[0] = part

    @pl.when(t == STEPS - 1)
    def _():
        bias = unfold(table, DB, 128)
        for f in range(FPD):
            rows = slice(f * PR, (f + 1) * PR)
            value = dn[rows, :] + bias
            out[f] = (middle[f] + table[f : f + 1, 5 * D : 6 * D] * value).astype(BF16)
            gate[f : f + 1, :] = jnp.sum(cot[f].astype(F32) * value, axis=0, keepdims=True)


def down_weight_grad(row, dg, act, downs, table, middle, cot):
    tok = whole((TOKENS, D))
    full = whole((FPD, PR, D))
    block = pl.BlockSpec((TOKENS, NB), lambda t, row: (0, t))

    def down_out(first):
        def index(t, row):
            at = jnp.clip(t - first, 0, STEPS // 2 - 1)
            return (at // PER, at % PER, 0)

        return pl.BlockSpec((1, NB, D), index)

    return pl.pallas_call(
        down_weight_kernel,
        out_shape=[shape((2, D, D))] * 2 + [shape((FPD, PR, D)), shape((8, D), F32)],
        grid_spec=pltpu.PrefetchScalarGridSpec(
            num_scalar_prefetch=1,
            grid=(STEPS,),
            in_specs=[tok, block]
            + [down_spec(j) for j in range(4)]
            + [whole((FPD, WIDE)), full, full],
            out_specs=[down_out(0), down_out(STEPS // 2), full, whole((8, D))],
            scratch_shapes=[pltpu.VMEM((TOKENS, D), F32)],
        ),
        compiler_params=params(58),
        cost_estimate=cost(2 * 2 * TOKENS * D * FF, 24 * MB),
        name="down_weight_grad",
    )(row, dg, act, *downs, table, middle, cot)


def up_weight_kernel(row_ref, h2, upg, uk, us):
    row = row_ref[0]
    grad = upg[...]
    for j, ref in enumerate((uk, us, uk, us)):
        ref[j // 2, 0] = tn(h2[:, columns(row, j)], grad).astype(BF16)


def up_weight_grad(row, h2, upg):
    up_out = pl.BlockSpec(
        (2, 1, HC, NB),
        lambda t, row: (0, up_column(t, row[0]) // PER, 0, up_column(t, row[0]) % PER),
    )
    return pl.pallas_call(
        up_weight_kernel,
        out_shape=[shape((2, 4, HC, D))] * 2,
        grid_spec=pltpu.PrefetchScalarGridSpec(
            num_scalar_prefetch=1,
            grid=(STEPS,),
            in_specs=[whole((TOKENS, D)), pl.BlockSpec((TOKENS, NB), lambda t, row: (0, t))],
            out_specs=[up_out, up_out],
        ),
        compiler_params=params(58),
        cost_estimate=cost(2 * TOKENS * D * FF, 14 * MB),
        name="up_weight_grad",
    )(row, h2, upg)


def out_weight_kernel(t0, t1, t2, t3, bg, keep, send):
    grad = bg[...].reshape(TOKENS, D)
    for j, t in enumerate((t0, t1, t2, t3)):
        ref = (keep, send)[j % 2]
        ref[j // 2] = tn(t[...].reshape(TOKENS, HC), grad).astype(BF16)


def out_weight_grad(pieces, bg):
    return pl.pallas_call(
        out_weight_kernel,
        out_shape=[shape((2, HC, D))] * 2,
        grid=(1,),
        in_specs=[whole((FPD, PR, HC))] * 4 + [whole((FPD, PR, D))],
        out_specs=[whole((2, HC, D))] * 2,
        compiler_params=params(14),
        cost_estimate=cost(2 * TOKENS * D * D, 4 * MB),
        name="out_weight_grad",
    )(*pieces, bg)


CHUNKS = 16
UP_ROWS, OUT_ROWS, DOWN_ROWS = D // CHUNKS, HC // CHUNKS, D // CHUNKS
FIRST = UP_ROWS + OUT_ROWS
ROWS = FIRST + DOWN_ROWS


def core_sum_kernel(ua, ub, da, db, oa, ob, out):
    def both(a, b):
        return (a.astype(F32) + b.astype(F32)).astype(BF16)

    for c in range(4):
        at = c * ROWS
        low, high = c * OUT_ROWS, (c + 1) * OUT_ROWS
        for i in range(4):
            to = at + i * OUT_ROWS
            out[0, to : to + OUT_ROWS] = both(ua[0, i, low:high], ub[0, i, low:high])
        out[0, at + UP_ROWS : at + FIRST] = both(oa[0, low:high], ob[0, low:high])
        low, high = c * DOWN_ROWS, (c + 1) * DOWN_ROWS
        out[0, at + FIRST : at + ROWS] = both(da[0, low:high], db[0, low:high])


def core_sum(up, down, out):
    ups = pl.BlockSpec((1, 4, 4 * OUT_ROWS, D), lambda j, c: (j, 0, c, 0))
    outs = pl.BlockSpec((1, 4 * OUT_ROWS, D), lambda j, c: (j, c, 0))
    downs = pl.BlockSpec((1, 4 * DOWN_ROWS, D), lambda j, c: (j, c, 0))
    return pl.pallas_call(
        core_sum_kernel,
        out_shape=shape((2, CHUNKS * ROWS, D)),
        grid=(2, CHUNKS // 4),
        in_specs=[ups, ups, downs, downs, outs, outs],
        out_specs=pl.BlockSpec((1, 4 * ROWS, D), lambda j, c: (j, c, 0)),
        compiler_params=params(58),
        cost_estimate=cost(1000, 1000),
        name="core_sum",
    )(*up, *down, *out)


def unpack_kernel(total, up, out, down):
    for k in range(4):
        at = k * ROWS
        for i in range(4):
            rows = slice(at + i * OUT_ROWS, at + (i + 1) * OUT_ROWS)
            up[k * OUT_ROWS : (k + 1) * OUT_ROWS, i * D : (i + 1) * D] = total[rows].astype(F32)
        out[k * OUT_ROWS : (k + 1) * OUT_ROWS] = total[at + UP_ROWS : at + FIRST].astype(F32)
        down[k * DOWN_ROWS : (k + 1) * DOWN_ROWS] = total[at + FIRST : at + ROWS].astype(F32)


def unpack(total):
    block = lambda i: (i, 0)
    return pl.pallas_call(
        unpack_kernel,
        out_shape=[shape((HC, FF), F32), shape((HC, D), F32), shape((D, D), F32)],
        grid=(4,),
        in_specs=[pl.BlockSpec((4 * ROWS, D), block)],
        out_specs=[
            pl.BlockSpec((4 * OUT_ROWS, FF), block),
            pl.BlockSpec((4 * OUT_ROWS, D), block),
            pl.BlockSpec((4 * DOWN_ROWS, D), block),
        ],
        compiler_params=params(24),
        cost_estimate=cost(0, 14 * MB),
        name="unpack",
    )(total)


LATE = 3 * D + 2 * HC
EARLY = 3 * D + NB + 256


def arrange_kernel(row_ref, a0, a1, a2, a3, late, far, out):
    row = row_ref[0]
    for j, a in enumerate((a0, a1, a2, a3)):
        for s in range(3):
            lanes = pl.ds(pl.multiple_of(s * D + (row ^ j) * HC, HC), HC)
            out[:, lanes] = a[:, s * HC : (s + 1) * HC]
    both = jnp.concatenate([late[...].astype(F32), far[...].astype(F32)], axis=0)
    out[:, 3 * D :] = both.astype(BF16)


def arrange(row, pieces, late, far):
    rows = pieces[0].shape[0]
    return pl.pallas_call(
        arrange_kernel,
        out_shape=shape((rows, 3 * D + LATE)),
        grid_spec=pltpu.PrefetchScalarGridSpec(
            num_scalar_prefetch=1,
            grid=(1,),
            in_specs=[whole((rows, 3 * HC))] * 4 + [whole((8, LATE))] * 2,
            out_specs=whole((rows, 3 * D + LATE)),
        ),
        compiler_params=params(16),
        cost_estimate=cost(0, 8 * rows * D),
        name="arrange",
    )(row, *pieces, late, far)


def stack_kernel(a0, a1, a2, a3, weights, sums):
    for k, a in enumerate((a0, a1, a2, a3)):
        weights[k] = a[:, : 3 * D]
        sums[k] = a[:, 3 * D :]


def stack(pieces):
    rows, width = pieces[0].shape
    return pl.pallas_call(
        stack_kernel,
        out_shape=[shape((4, rows, 3 * D)), shape((4, rows, LATE))],
        grid=(1,),
        in_specs=[whole((rows, width))] * 4,
        out_specs=[whole((4, rows, 3 * D)), whole((4, rows, LATE))],
        compiler_params=params(16),
        cost_estimate=cost(0, 2 * MB),
        name="stack",
    )(*pieces)


def place_kernel(index_ref, low, high, out):
    for m, a in enumerate((low.at[0], low.at[1], high.at[1], high.at[0])):

        @pl.when(pl.program_id(0) == m)
        def _():
            for k in range(4):
                out[0, index_ref[1] ^ k] = a[k].astype(F32)


def place(index, low, high):
    rows = low.shape[2]
    return pl.pallas_call(
        place_kernel,
        out_shape=shape((4, 4, rows, 3 * D), F32),
        grid_spec=pltpu.PrefetchScalarGridSpec(
            num_scalar_prefetch=1,
            grid=(4,),
            in_specs=[whole(low.shape)] * 2,
            out_specs=pl.BlockSpec((1, 4, rows, 3 * D), lambda i, index: (index[0] ^ i, 0, 0, 0)),
        ),
        compiler_params=params(24),
        cost_estimate=cost(0, 24 * rows * D),
        name="place",
    )(index, low, high).reshape(HC, 3 * D)


def project_back_kernel(row_ref, dq, dk, dv, rk, rv, w0, w1, w2, w3, cp, sp, fr, dp, h0, h2, hs, bsum):
    row = row_ref[0]
    f = pl.program_id(0)
    later = (f > 0).astype(F32)
    keys = dk[0] + later * rk[0, 0].astype(F32)
    values = dv[0] + later * rv[0, 0].astype(F32)
    cosine, sine = cosines(cp, sp, fr, f)
    dp[0, :, :HC] = dq[0]
    dp[0, :, HC : 2 * HC] = turn(keys, cosine, -sine).astype(BF16)
    dp[0, :, 2 * HC :] = values.astype(BF16)
    grad = dp[0]
    sums = jnp.sum(grad.astype(F32), axis=0, keepdims=True)

    @pl.when(f == 0)
    def _():
        bsum[...] = jnp.zeros_like(bsum)

    number = lax.broadcasted_iota(jnp.int32, (8, 2 * HC), 0)
    bsum[...] = bsum[...] + jnp.where(number == row, sums[:, : 2 * HC], 0.0)
    bsum[:, :HC] = bsum[:, :HC] + jnp.where(number[:, :HC] == row + 4, sums[:, 2 * HC :], 0.0)
    for j, w in enumerate((w0, w1, w2, w3)):
        part = nt(grad, w[...]).astype(BF16)
        at = (0, slice(None), columns(row, j))
        h0[at] = part[:PR]
        hs[(0,) + at] = part[PR : 2 * PR]
        h2[at] = part[2 * PR : 3 * PR]
        hs[(1,) + at] = part[3 * PR :]


def project_back(row, dq, dk, dv, returned, weights, tables):
    block = pl.BlockSpec((1, TOK, HC), lambda f, *_: (f, 0, 0))
    late = [
        pl.BlockSpec((1, 1, TOK, HC), lambda f, *_, i=i: (i, jnp.maximum(f - 1, 0), 0, 0))
        for i in range(2)
    ]
    piece = pl.BlockSpec((1, PR, D), lambda f, *_: (f, 0, 0))
    return pl.pallas_call(
        project_back_kernel,
        out_shape=[
            shape((FPD, TOK, 3 * HC)),
            shape((FPD, PR, D)),
            shape((FPD, PR, D)),
            shape((2, FPD, PR, D)),
            shape((8, 2 * HC), F32),
        ],
        grid_spec=pltpu.PrefetchScalarGridSpec(
            num_scalar_prefetch=1,
            grid=(FPD,),
            in_specs=[block] * 3
            + late
            + [whole((HC, 3 * HC))] * 4
            + [whole((TOK, HC)), whole((TOK, HC)), whole((16, 2 * HC))],
            out_specs=[
                pl.BlockSpec((1, TOK, 3 * HC), lambda f, *_: (f, 0, 0)),
                piece,
                piece,
                pl.BlockSpec((2, 1, PR, D), lambda f, *_: (0, f, 0, 0)),
                whole((8, 2 * HC)),
            ],
        ),
        compiler_params=params(20),
        cost_estimate=cost(2 * FPD * TOK * D * 3 * HC, 14 * MB),
        name="project_back",
    )(row, dq, dk, dv, returned, returned, *weights, *tables)


def weight_kernel(row_ref, h, dp, w):
    w[0] = tn(h[...], dp[...]).astype(BF16)


def project_weight(row, hidden, dproj):
    tokens = FPD * TOK
    return pl.pallas_call(
        weight_kernel,
        out_shape=shape((4, HC, 3 * HC)),
        grid_spec=pltpu.PrefetchScalarGridSpec(
            num_scalar_prefetch=1,
            grid=(4,),
            in_specs=[
                pl.BlockSpec((tokens, HC), lambda j, row: (0, row[0] ^ j)),
                whole((tokens, 3 * HC)),
            ],
            out_specs=pl.BlockSpec((1, HC, 3 * HC), lambda j, row: (j, 0, 0)),
        ),
        compiler_params=params(20),
        cost_estimate=cost(2 * tokens * D * 3 * HC, 9 * MB),
        name="project_weight",
    )(row, hidden.reshape(tokens, D), dproj.reshape(tokens, 3 * HC))


def input_back_kernel(x, h0, near, far, table, mg, bsum, gate, out, sums):
    grad = h0[...].astype(F32) + near[0].astype(F32) + far[...].astype(F32)
    normal, rate = norm(x[...].astype(F32))
    put_half(sums, 0, jnp.sum(grad, axis=1))
    put_half(sums, D, jnp.sum(grad * normal, axis=1))
    sums[:, 2 * D : 3 * D] = gate[...]
    sums[:, 3 * D :] = bsum[...]
    out[...] = mg[...] + norm_back(normal, rate, grad * (1.0 + segment(table, 1)))


def input_back(x, h0, near, far, table, mg, bsum, gate):
    return pl.pallas_call(
        input_back_kernel,
        out_shape=[shape((FPD, PR, D), F32), shape((8, LATE), F32)],
        grid=(FPD // HALF,),
        in_specs=[half_spec(D)] * 2
        + [pl.BlockSpec((1, HALF, PR, D), lambda i: (0, i, 0, 0))]
        + [half_spec(D), whole((FPD, WIDE)), half_spec(D), whole((8, 2 * HC)), whole((8, D))],
        out_specs=[half_spec(D), whole((8, LATE))],
        compiler_params=params(20),
        cost_estimate=cost(20 * 512 * D, 10 * MB),
        name="input_back",
    )(x, h0, near, far, table, mg, bsum, gate)


def early_kernel(m, u, d, out):
    out[:, : 3 * D] = m[:, : 3 * D]
    out[:, 3 * D : 3 * D + NB] = u[...]
    out[:, 3 * D + NB : 3 * D + NB + 128] = d[...]
    out[:, 3 * D + NB + 128 :] = m[:, 3 * D :]


def early_sums(sums, usum, dsum):
    return pl.pallas_call(
        early_kernel,
        out_shape=shape((8, EARLY), F32),
        grid=(1,),
        in_specs=[whole(a.shape) for a in (sums, usum, dsum)],
        out_specs=whole((8, EARLY)),
        cost_estimate=cost(0, MB),
        name="early_sums",
    )(sums, usum, dsum)


def final_kernel(row_ref, *refs):
    row = row_ref[0]
    low, high, *early = refs[:6]
    ada, ab, qb, ob, ub, db, asum = refs[6:]
    late = [low.at[0], low.at[1], high.at[0], high.at[1]]
    early = [early[0], early[3], early[1], early[2]]

    def rows(ref, cols):
        value = ref[:, :, cols].astype(F32)
        return value.reshape(64, value.shape[-1])

    left = [rows(s, slice(EARLY, EARLY + HC)).astype(BF16) for s in early]
    for segment in range(6):
        source, start = ((late, 0), (late, 1), (early, 0), (early, 1), (early, 2), (late, 2))[segment]
        cols = slice(start * D, (start + 1) * D)
        product, total = 0.0, 0.0
        for s, ref in zip(left, source):
            right = rows(ref, cols)
            total = total + jnp.sum(right, axis=0, keepdims=True)
            product = product + tn(s, right.astype(BF16))
        at = segment * D
        ada[:, at : at + D] = product
        asum[0:1, at : at + D] = total

    def fold8(value):
        value = jnp.sum(value, axis=0)
        return value if value.shape[0] == 8 else value[:8] + value[8:]

    def bias(source, start, stop):
        return sum(
            fold8(ref[:, :, start:stop].astype(F32)) for ref in source
        )

    ab[...] = asum[0:1, pl.ds(pl.multiple_of(row * 1536, 512), 1536)]
    folded = bias(late, 3 * D, LATE)
    for i in range(3):
        chunk = 3 * row + i
        at = jnp.where(chunk < 4, chunk, chunk - 4)
        second = (chunk >= 4) & (chunk < 8)
        value = jnp.where(second, folded[:, HC:], folded[:, :HC])
        qb[:, i * HC : (i + 1) * HC] = take(value, at)
    folded = bias(early, 3 * D, EARLY)
    for i in range(2):
        at = 2 * row + i
        ub[:, i * NB : (i + 1) * NB] = take(folded[:, :NB], at)
        db[:, i * 128 : (i + 1) * 128] = take(folded[:, NB : NB + 128], at)
        ob[:, i * 128 : (i + 1) * 128] = take(folded[:, NB + 128 :], at)


def final_sums(row, late, early):
    sizes = (1536, 768, 256, 1024, 256)
    return pl.pallas_call(
        final_kernel,
        out_shape=[shape((HC, 6 * D), F32)] + [shape((1, n), F32) for n in sizes],
        grid_spec=pltpu.PrefetchScalarGridSpec(
            num_scalar_prefetch=1,
            grid=(1,),
            in_specs=[whole((2, 4, 16, LATE))] * 2
            + [whole((8, 8, EARLY + HC))] * 4,
            out_specs=[whole((HC, 6 * D))] + [whole((1, n)) for n in sizes],
            scratch_shapes=[pltpu.VMEM((8, 6 * D), F32)],
        ),
        compiler_params=params(28),
        cost_estimate=cost(2 * 256 * HC * 6 * D, 10 * MB),
        name="final_sums",
    )(row, *late, *early)


def row_sum(value):
    value = value + swap(value, CORE)
    return value + swap(value, DIRECT)


def row_pieces(value):
    return [value, swap(value, CORE), swap(value, DIRECT), swap(value, DIRECT ^ CORE)]


def by_row(pieces, row):
    a, b, c, d = pieces
    odd, high = row % 2 == 1, row >= 2
    a, b = jnp.where(odd, b, a), jnp.where(odd, a, b)
    c, d = jnp.where(odd, d, c), jnp.where(odd, c, d)
    return jnp.stack(
        [
            jnp.where(high, c, a),
            jnp.where(high, d, b),
            jnp.where(high, a, c),
            jnp.where(high, b, d),
        ]
    )


def quarter_rows(value, bit, index, axis):
    rows = value.shape[1] // 4
    at = lambda m: lax.dynamic_slice_in_dim(value, (index[axis] ^ m) * rows, rows, 1)
    return [at(0)] + [swap(at(m), bit * m) for m in (1, 2, 3)]


def add_all(parts):
    return sum(part.astype(F32) for part in parts).astype(BF16)


def exchange_rows(value, bit, index, axis):
    return add_all(quarter_rows(value, bit, index, axis))


def turn_heads(own, beside, across, order=lambda piece: piece):
    across = swap(across, DIRECT)
    return [own, swap(beside, CORE), across[0], swap(order(across)[1], CORE)]


def per_device(
    activations,
    noise_embed,
    frame_position,
    cotangent,
    ada_weight,
    ada_bias,
    qkv_weight,
    qkv_bias,
    out_weight,
    out_bias,
    up_weight,
    up_bias,
    down_weight,
    down_bias,
):
    row = lax.axis_index(("xl", "c")).astype(jnp.int32)
    row_arg = row.reshape(1)
    index = [lax.axis_index("y").astype(jnp.int32), lax.axis_index("z").astype(jnp.int32)]
    index_arg = jnp.stack(index)

    x0 = activations
    x2 = swap(x0, DIRECT)
    x1 = swap(x0, CORE)
    p0 = shift(activations[1:], 1)
    biases = (ada_bias, qkv_bias, out_bias, up_bias, down_bias)
    heads = list(split_heads(row_arg, qkv_weight))
    noise, heads[1] = lax.optimization_barrier((noise_embed, heads[1]))
    part, silu_own, *tables = prepare(row_arg, frame_position, noise, ada_weight, biases)
    across = swap(heads[2], OTHER)
    qkv_pieces = [heads[0], swap(heads[1], CORE), across]
    part = part + swap(part, CORE)
    table = part + swap(part, DIRECT)
    x2, p0, table, *qkv_pieces = lax.optimization_barrier((x2, p0, table, *qkv_pieces))

    qkv_pieces = qkv_pieces[:2] + [qkv_pieces[2][0], swap(qkv_pieces[2][1], CORE)]
    x3 = swap(x2, CORE)
    p2 = swap(p0, DIRECT)
    p1 = swap(p0, CORE)
    before_mods = shift(table[:, : 2 * D], 1)

    out_own, up_own, _ = lax.optimization_barrier((out_weight, up_weight, table))
    outs2 = swap(out_own, OTHER)
    ups2 = swap(up_own, OTHER)

    hidden1, q, k, v = project(True, row_arg, (x0, x1, x2, x3), table, table, qkv_pieces, tables)
    p2, down_own, q, before_mods = lax.optimization_barrier((p2, down_weight, q, before_mods))
    p3 = swap(p2, CORE)
    downs2 = swap(down_own, DIRECT)
    kp, vp = project(
        False, row_arg, (p0, p1, p2, p3), table, before_mods, qkv_pieces, tables
    )
    *mixed, lse = attend(frame_position, q, k, v, kp, vp)
    outs2, ups2, downs2, lse = lax.optimization_barrier((outs2, ups2, downs2, lse))
    outs = [out_weight, swap(out_own, CORE), outs2, swap(outs2, CORE)]
    ups = [up_weight, swap(up_own, CORE), ups2, swap(ups2, CORE)]
    downs = [down_weight, swap(down_own, CORE), downs2, swap(downs2, CORE)]
    turned = turn_heads(*mixed)
    branch, middle, hidden2, down_grad, dsum = mid(turned, outs, table, x0, cotangent)
    h2 = hidden2.reshape(TOKENS, D)
    dg = down_grad.reshape(TOKENS, D)
    act, upg, hg, usum = feed(row_arg, h2, dg, ups, table, downs)
    mg, bg, *ag, sums = mid_back(hg.reshape(FPD, PR, D), middle, branch, cotangent, table, outs)
    late = []
    back = turn_heads(*ag[:2], ag[2], order=lambda piece: late.append(piece) or piece)[:2]

    early = early_sums(sums, usum, dsum)
    early = early + swap(early, CORE)
    upg, early, _ = lax.optimization_barrier((upg, early, bg))
    early_far = swap(early, DIRECT)
    uk, us = up_weight_grad(row_arg, h2, upg)
    us = swap(us, CORE)
    dg_later, early_far, far_back, uk, *back = lax.optimization_barrier(
        (dg, early_far, *late, uk, *back)
    )
    back += [far_back[0], swap(far_back[1], CORE)]
    early = jnp.concatenate([(early + early_far).astype(BF16), silu_own], axis=1)
    early_far = swap(early, FAR)
    dk_part, ds_part, layer_output, gate = down_weight_grad(
        row_arg, dg_later, act, downs, table, middle, cotangent
    )
    ds_part = swap(ds_part, CORE)
    dk_part, early, early_far, bg_later, us, *back = lax.optimization_barrier(
        (dk_part, early, early_far, bg, us, *back)
    )
    early = jnp.stack([early, early_far])
    early_parts = [early] + [swap(early, m) for m in (16, 32, 48)]
    ok, os = out_weight_grad(turned, bg_later)
    packed = core_sum((uk, us), (dk_part, ds_part), (ok, swap(os, CORE)))
    packed, early_parts, back = lax.optimization_barrier((packed, early_parts, back))
    scattered = lax.psum_scatter(packed, ("y", "z"), scatter_dimension=1, tiled=True)

    dq_before, both = attend_back(False, frame_position, q, kp, vp, back, mixed, lse)
    returned = shift(both, -1)
    dq, dk, dv = attend_back(
        True, frame_position, q, k, v, back, mixed, lse, tables, dq_before
    )
    early_parts = lax.optimization_barrier((early_parts, dq))[0]
    early = jnp.concatenate(early_parts)
    early_all = [early] + [swap(early, m) for m in (4, 8, 12)]
    early = early[0].astype(F32)

    dproj, h0, h2_part, send, bsum = project_back(row_arg, dq, dk, dv, returned, qkv_pieces, tables)
    near = swap(send, CORE)
    qkv_parts = project_weight(row_arg, hidden1, dproj)
    far = swap((h2_part.astype(F32) + near[1].astype(F32)).astype(BF16), DIRECT)
    qkv_parts, early_all = lax.optimization_barrier((qkv_parts, early_all))
    qkv_parts = exchange_rows(qkv_parts, 4, index, 0)
    far, qkv_parts = lax.optimization_barrier((far, qkv_parts))
    quarters = quarter_rows(qkv_parts, 16, index, 1)
    input_grad, late = input_back(x0, h0, near, far, table, mg, bsum, gate)
    late, *quarters = lax.optimization_barrier((late, *quarters))
    qkv_parts = add_all(quarters)
    late_near = swap(late, CORE)
    late, late_near, qkv_parts = lax.optimization_barrier((late, late_near, qkv_parts))
    late = late + late_near
    late_far = swap(late, DIRECT)
    qkv_far = swap(qkv_parts, FAR)
    late, late_far, qkv_parts, qkv_far = lax.optimization_barrier(
        (late, late_far, qkv_parts, qkv_far)
    )
    late = late + late_far
    qkv_parts = add_all([qkv_parts, qkv_far])
    late_low = late.astype(BF16)
    late_far = swap(late_low, FAR)
    turned = turn_heads(qkv_parts[0], qkv_parts[1], qkv_parts[2:])
    last = arrange(row_arg, turned, late_low, late_far)

    scattered, last = lax.optimization_barrier((scattered, last))
    last = [last] + [swap(last, m) for m in (16, 32, 48)]
    share = scattered[0].astype(F32) + swap(scattered[1], DIRECT).astype(F32)
    share, last = lax.optimization_barrier((share, last))
    share_far = swap(share.astype(BF16), FAR)
    weights, sums_late = stack(last)
    weights_far, sums_far = swap(weights, 4), swap(sums_late, 12)
    share, share_far = lax.optimization_barrier((share, share_far))
    share = (share + share_far.astype(F32)).astype(BF16)
    totals = lax.all_gather(share, ("y", "z"), axis=0, tiled=True)
    weights = jnp.stack([weights, weights_far])
    sums_late = jnp.stack([sums_late, sums_far])
    weights_far, sums_far = swap(weights, 12), swap(sums_late, 4)
    up_total, out_total, down_total = unpack(totals)
    qkv_total = place(index_arg, weights, weights_far)

    ada_total, *bias_sums = final_sums(row_arg, (sums_late, sums_far), early_all)
    ada_sum, qkv_sum, out_sum, up_sum, down_sum = [b[0] for b in bias_sums]
    mod_own = jnp.concatenate(
        [late[:, : 2 * D], early[:, : 3 * D], late[:, 2 * D : 3 * D]], axis=1
    ).astype(BF16)
    silu_grad = nt(mod_own, ada_weight)
    silu_grad = by_row(row_pieces(silu_grad), row).transpose(1, 0, 2).reshape(FPD, D)
    embed = noise_embed.astype(F32)
    sigma = jax.nn.sigmoid(embed)
    embed_grad = silu_grad * (sigma * (1.0 + embed * (1.0 - sigma)))

    return (
        layer_output,
        input_grad,
        embed_grad,
        ada_total,
        ada_sum,
        qkv_total,
        qkv_sum,
        out_total,
        out_sum,
        up_total,
        up_sum,
        down_total,
        down_sum,
    )


def solution(mesh):
    fine = Mesh(mesh.devices.reshape(2, 4, 4, 2, 2), AXES)
    seq, row = ("xh", "z", "y"), ("xl", "c")
    token, weight, vector = P(seq, row, None), P(row, None), P(row)
    in_specs = (token, P(seq, None), P(seq), token) + (weight, vector) * 5
    out_specs = (token, token, P(seq, None)) + (weight, vector) * 5
    return jax.shard_map(
        per_device, mesh=fine, in_specs=in_specs, out_specs=out_specs, check_vma=False
    )
```

```python
import math

import jax
import jax.numpy as jnp
from jax import lax
from jax.experimental import pallas as pl
from jax.experimental.pallas import tpu as pltpu
from jax.sharding import Mesh, PartitionSpec as P

F32 = jnp.float32
BF16 = jnp.bfloat16
HD = 64
GRID = 16
FPD = 8
PR = 64
D = 1024
FF = 4096
HC = 256
TOK = 256
PREV = 7
AXES = ("xh", "z", "y", "xl", "c")
CORE, DIRECT, OTHER, FAR = 1, 2, 66, 64
MB = 1024 * 1024


def swap(value, mask):
    return lax.ppermute(value, AXES, [(i, i ^ mask) for i in range(128)])


def shift(value, steps):
    return lax.ppermute(value, AXES, [(i, (i + 4 * steps) % 128) for i in range(128)])


def after(value, *others):
    return lax.optimization_barrier((value,) + others)[0]


def nt(left, right):
    return lax.dot_general(left, right, (((1,), (1,)), ((), ())), preferred_element_type=F32)


def tn(left, right):
    return lax.dot_general(left, right, (((0,), (0,)), ((), ())), preferred_element_type=F32)


def nn(left, right):
    return jnp.dot(left, right, preferred_element_type=F32)


def norm(values):
    center = values - jnp.mean(values, axis=-1, keepdims=True)
    spread = jnp.mean(center * center, axis=-1, keepdims=True)
    rate = lax.rsqrt(spread + 1e-06)
    return center * rate, rate


def norm_back(normal, rate, grad):
    mean_grad = jnp.mean(grad, axis=-1, keepdims=True)
    mean_both = jnp.mean(grad * normal, axis=-1, keepdims=True)
    return rate * (grad - mean_grad - normal * mean_both)


def turn(values, cosine, sine):
    lanes = lax.broadcasted_iota(jnp.int32, values.shape, 1)
    other = jnp.where(
        lanes % HD < HD // 2, pltpu.roll(values, HC - HD // 2, 1), pltpu.roll(values, HD // 2, 1)
    )
    return values * cosine + other * sine


def params(mib):
    return pltpu.CompilerParams(vmem_limit_bytes=mib * MB)


def cost(flops, moved, exps=0):
    return pl.CostEstimate(flops=int(flops), bytes_accessed=int(moved), transcendentals=int(exps))


def whole(shape):
    return pl.BlockSpec(shape, lambda i, *_: (0,) * len(shape))


def columns(row, j):
    return pl.ds(pl.multiple_of((row ^ j) * HC, HC), HC)


def shape(dims, kind=BF16):
    return jax.ShapeDtypeStruct(dims, kind)


UB, QB, OB, DB, WIDE = 6144, 6656, 7168, 7296, 7424


def put(ref, start, at, value):
    cols = slice(start, start + value.shape[1])
    number = lax.broadcasted_iota(jnp.int32, (8, value.shape[1]), 0)
    ref[:, cols] = jnp.where(number == at, value, ref[:, cols])


def take(value, at):
    number = lax.broadcasted_iota(jnp.int32, value.shape, 0)
    return jnp.sum(jnp.where(number == at, value, 0.0), axis=0, keepdims=True)


def put_half(ref, start, value):
    cols = slice(start, start + value.shape[1])
    number = lax.broadcasted_iota(jnp.int32, (8, value.shape[1]), 0)
    both = jnp.concatenate([value, value], axis=0)
    ref[:, cols] = jnp.where(number // 4 == pl.program_id(0), both, ref[:, cols])


def unfold(ref, start, width):
    return jnp.concatenate([ref[i : i + 1, start : start + width] for i in range(8)], axis=1)


def prepare_kernel(row_ref, pos_ref, noise, ada, ab, qb, ob, ub, db, pack, silu, cp, sp, frames):
    row = row_ref[0]
    embed = noise[...].astype(F32)
    value = (embed / (1.0 + jnp.exp(-embed))).astype(BF16)
    own = jnp.where(
        row < 2,
        jnp.where(row == 0, value[:, :HC], value[:, HC : 2 * HC]),
        jnp.where(row == 2, value[:, 2 * HC : 3 * HC], value[:, 3 * HC :]),
    )
    silu[...] = own
    pack[:, UB:] = jnp.zeros((FPD, WIDE - UB), F32)
    for segment in range(6):
        cols = slice(segment * D, (segment + 1) * D)
        pack[:, cols] = nn(own, ada[:, cols])
    bias = pl.ds(pl.multiple_of(row * 1536, 512), 1536)
    pack[:, bias] = pack[:, bias] + ab[...].astype(F32)
    for i in range(2):
        at = 2 * row + i
        put(pack, UB, at, ub[:, i * 512 : (i + 1) * 512].astype(F32))
        put(pack, OB, at, ob[:, i * 128 : (i + 1) * 128].astype(F32))
        put(pack, DB, at, db[:, i * 128 : (i + 1) * 128].astype(F32))
    for i in range(3):
        chunk = 3 * row + i
        at = jnp.where(chunk < 4, chunk, chunk - 4)
        second = (chunk >= 4) & (chunk < 8)
        value = qb[:, i * HC : (i + 1) * HC].astype(F32)
        put(pack, QB, jnp.where(second, -1, at), value)
        put(pack, QB + HC, jnp.where(second, at, -1), value)

    def parts(dims):
        lane = lax.broadcasted_iota(jnp.int32, dims, 1)
        index = lane % (HD // 2)
        quarter, eighth = HD // 4, HD // 8
        in_frame = index < quarter
        in_row = (index >= quarter) & (index < quarter + eighth)
        offset = jnp.where(
            in_frame, index, jnp.where(in_row, index - quarter, index - quarter - eighth)
        ).astype(F32)
        length = jnp.where(in_frame, 1.0 * quarter, 1.0 * eighth)
        frequency = jnp.exp(-math.log(10000.0) * offset / length)
        sign = jnp.where(lane % HD < HD // 2, -1.0, 1.0)
        return in_frame, in_row, frequency, sign

    in_frame, in_row, frequency, sign = parts((TOK, HC))
    slot = lax.broadcasted_iota(jnp.int32, (TOK, HC), 0)
    patch = ((slot // PR) ^ row) * PR + slot % PR
    angle = jnp.where(in_row, patch // GRID, patch % GRID).astype(F32) * frequency
    cp[...] = jnp.where(in_frame, 0.0, jnp.cos(angle))
    sp[...] = jnp.where(in_frame, 0.0, jnp.sin(angle) * sign)
    in_frame, _, frequency, sign = parts((16, HC))
    slot = lax.broadcasted_iota(jnp.int32, (16, HC), 0)
    place = pos_ref[0] - PREV + (slot - FPD)
    for f in range(FPD):
        place = jnp.where(slot == f, pos_ref[f], place)
    angle = place.astype(F32) * frequency
    frames[:, :HC] = jnp.where(in_frame, jnp.cos(angle), 0.0)
    frames[:, HC:] = jnp.where(in_frame, jnp.sin(angle) * sign, 0.0)


def prepare(row, places, noise, ada, biases):
    return pl.pallas_call(
        prepare_kernel,
        out_shape=[
            shape((FPD, WIDE), F32),
            shape((FPD, HC)),
            shape((TOK, HC), F32),
            shape((TOK, HC), F32),
            shape((16, 2 * HC), F32),
        ],
        grid_spec=pltpu.PrefetchScalarGridSpec(
            num_scalar_prefetch=2,
            grid=(1,),
            in_specs=[whole((FPD, D)), whole((HC, 6 * D))]
            + [whole((1, b.shape[0])) for b in biases],
            out_specs=[
                whole((FPD, WIDE)),
                whole((FPD, HC)),
                whole((TOK, HC)),
                whole((TOK, HC)),
                whole((16, 2 * HC)),
            ],
        ),
        compiler_params=params(24),
        cost_estimate=cost(2 * 8 * HC * 6 * D, 4 * MB, 4 * TOK * HC),
        name="prepare",
    )(row, places, noise, ada, *[b[None] for b in biases])


def split_heads_kernel(row_ref, q, k, v, p0, p1, p23):
    for j, p in enumerate((p0, p1, p23.at[0], p23.at[1])):

        @pl.when(pl.program_id(0) == j)
        def _():
            p[:, :HC] = q[...]
            p[:, HC : 2 * HC] = k[...]
            p[:, 2 * HC :] = v[...]


def split_heads(row, weight):
    piece = (HC, 3 * HC)
    return pl.pallas_call(
        split_heads_kernel,
        out_shape=[shape(piece), shape(piece), shape((2,) + piece)],
        grid_spec=pltpu.PrefetchScalarGridSpec(
            num_scalar_prefetch=1,
            grid=(4,),
            in_specs=[
                pl.BlockSpec((HC, HC), lambda j, row, s=s: (0, 4 * s + (row[0] ^ j)))
                for s in range(3)
            ],
            out_specs=[whole(piece), whole(piece), whole((2,) + piece)],
        ),
        compiler_params=params(12),
        cost_estimate=cost(0, 3 * MB),
        name="split_heads",
    )(row, weight, weight, weight)


def cosines(cp, sp, frames, at):
    both = frames[pl.ds(at, 1), :]
    return cp[...] + both[:, :HC], sp[...] + both[:, HC:]


def project_kernel(own, row_ref, x0, x1, x2, x3, table, mods, w0, w1, w2, w3, cp, sp, fr, *outs):
    row = row_ref[0]
    f = pl.program_id(0)
    if own:
        h_ref, q_ref, k_ref, v_ref = outs
        first, at, angle = 0, f, f
    else:
        k_ref, v_ref, h_ref = outs
        first, at, angle = HC, f + FPD - PREV, f + FPD
    x = jnp.concatenate([r[0] for r in (x0, x1, x2, x3)], axis=0).astype(F32)
    normal, _ = norm(x)
    shift_row = mods[pl.ds(at, 1), :D]
    scale_row = mods[pl.ds(at, 1), D : 2 * D]
    hidden = (normal * (1.0 + scale_row) + shift_row).astype(BF16)
    where = (0,) if own else ()
    h_ref[where + (slice(None), slice(None))] = hidden
    low, high = table[pl.ds(row, 1), QB : QB + 2 * HC], table[pl.ds(row + 4, 1), QB : QB + HC]
    total = jnp.concatenate([low, high], axis=1)[:, first:]
    for j, w in enumerate((w0, w1, w2, w3)):
        total = total + nn(h_ref[where + (slice(None), columns(row, j))], w[:, first:])
    cosine, sine = cosines(cp, sp, fr, angle)
    if own:
        q_ref[0] = (turn(total[:, :HC], cosine, sine).astype(BF16).astype(F32) * 0.125).astype(BF16)
        total = total[:, HC:]
    k_ref[0] = turn(total[:, :HC], cosine, sine).astype(BF16)
    v_ref[0] = total[:, HC:].astype(BF16)


def project(own, row, xs, table, mods, weights, tables):
    frames = xs[0].shape[0]
    x_spec = pl.BlockSpec((1, PR, D), lambda f, *_: (f, 0, 0))
    out_spec = pl.BlockSpec((1, TOK, HC), lambda f, *_: (f, 0, 0))
    out = shape((frames, TOK, HC))
    if own:
        out_specs = [pl.BlockSpec((1, TOK, D), lambda f, *_: (f, 0, 0)), out_spec, out_spec, out_spec]
        out_shape = [shape((frames, TOK, D)), out, out, out]
        scratch = []
    else:
        out_specs = [out_spec, out_spec]
        out_shape = [out, out]
        scratch = [pltpu.VMEM((TOK, D), BF16)]
    return pl.pallas_call(
        lambda *refs: project_kernel(own, *refs),
        out_shape=out_shape,
        grid_spec=pltpu.PrefetchScalarGridSpec(
            num_scalar_prefetch=1,
            grid=(frames,),
            in_specs=[x_spec] * 4
            + [whole((FPD, WIDE)), whole(mods.shape)]
            + [whole((HC, 3 * HC))] * 4
            + [whole((TOK, HC)), whole((TOK, HC)), whole((16, 2 * HC))],
            out_specs=out_specs,
            scratch_shapes=scratch,
        ),
        compiler_params=params(20),
        cost_estimate=cost(2 * frames * TOK * D * 3 * HC, frames * TOK * D * 4 + 4 * MB),
        name="project_own" if own else "project_prev",
    )(row, *xs, table, mods, *weights, *tables)


def head_lanes():
    return lax.broadcasted_iota(jnp.int32, (TOK, HC), 1) // HD


def attend_kernel(pos_ref, q, k, v, kp, vp, o0, o1, o23, lse, qs, scores, acc, top, low):
    f = pl.program_id(0)
    place = pos_ref[f]
    lanes = head_lanes()
    query = q[0]
    for h in range(4):
        qs[pl.ds(h * TOK, TOK), :] = jnp.where(lanes == h, query, jnp.zeros_like(query))
    top[...] = jnp.full_like(top, -1e30)
    low[...] = jnp.zeros_like(low)
    acc[...] = jnp.zeros_like(acc)
    before = jnp.maximum(place - f, 0)
    start = jnp.maximum(f - place, 0)

    def score(keys, slot):
        for h in range(4):
            rows = pl.ds(h * TOK, TOK)
            s = nt(qs[rows, :], keys)
            scores[slot, rows, :] = s
            top[rows, :] = jnp.maximum(top[rows, :], jnp.maximum(s[:, :128], s[:, 128:]))

    def mix(values, slot):
        for h in range(4):
            rows = pl.ds(h * TOK, TOK)
            p = jnp.exp(scores[slot, rows, :] - jnp.concatenate([top[rows, :]] * 2, axis=1))
            low[rows, :] = low[rows, :] + (p[:, :128] + p[:, 128:])
            acc[rows, :] = acc[rows, :] + nn(p.astype(BF16), values)

    def run(step):
        def prev(i, _):
            at = PREV - before + i
            step(kp[at] if step is score else vp[at], i)
            return 0

        def own(g, _):
            step(k[g] if step is score else v[g], g - f + place)
            return 0

        lax.fori_loop(0, before, prev, 0)
        lax.fori_loop(start, f + 1, own, 0)

    run(score)
    for h in range(4):
        rows = pl.ds(h * TOK, TOK)
        top[rows, :] = jnp.broadcast_to(jnp.max(top[rows, :], axis=1, keepdims=True), (TOK, 128))
    run(mix)
    result = jnp.zeros((TOK, HC), F32)
    logs = jnp.zeros((TOK, 128), F32)
    narrow = lax.broadcasted_iota(jnp.int32, (TOK, 128), 1)
    for h in range(4):
        rows = pl.ds(h * TOK, TOK)
        total = jnp.sum(low[rows, :], axis=1, keepdims=True)
        result = jnp.where(lanes == h, acc[rows, :] / total, result)
        logs = jnp.where(narrow == h, top[rows, :] + jnp.log(total), logs)
    lse[0] = logs.T[:8]
    result = result.astype(BF16)
    o0[0] = result[:PR]
    o1[0] = result[PR : 2 * PR]
    o23[0, 0] = result[2 * PR : 3 * PR]
    o23[1, 0] = result[3 * PR :]


def attend(places, q, k, v, kp, vp):
    block = pl.BlockSpec((1, TOK, HC), lambda f, *_: (f, 0, 0))
    piece = pl.BlockSpec((1, PR, HC), lambda f, *_: (f, 0, 0))
    return pl.pallas_call(
        attend_kernel,
        out_shape=[shape((FPD, PR, HC))] * 2
        + [shape((2, FPD, PR, HC)), shape((FPD, 8, TOK), F32)],
        grid_spec=pltpu.PrefetchScalarGridSpec(
            num_scalar_prefetch=1,
            grid=(FPD,),
            in_specs=[block]
            + [whole((FPD, TOK, HC))] * 2
            + [whole((PREV, TOK, HC))] * 2,
            out_specs=[piece] * 2
            + [
                pl.BlockSpec((2, 1, PR, HC), lambda f, *_: (0, f, 0, 0)),
                pl.BlockSpec((1, 8, TOK), lambda f, *_: (f, 0, 0)),
            ],
            scratch_shapes=[
                pltpu.VMEM((4 * TOK, HC), BF16),
                pltpu.VMEM((8, 4 * TOK, TOK), F32),
                pltpu.VMEM((4 * TOK, HC), F32),
                pltpu.VMEM((4 * TOK, 128), F32),
                pltpu.VMEM((4 * TOK, 128), F32),
            ],
        ),
        compiler_params=params(58),
        cost_estimate=cost(36 * 4 * 2 * 2 * TOK**3, 6 * MB, 36 * 4 * TOK * TOK),
        name="attend",
    )(places, q, k, v, kp, vp)


def attend_back_kernel(own, pos_ref, q, k, v, g0, g1, g2, g3, o0, o1, o23, lse, *rest):
    if own:
        cp, sp, fr, before_ref, dq, dk, dv, qs, gs, ks, pl_scr, dl_scr, ds_scr, dq_acc = rest
        dk_acc, dv_acc = dk, dv
    else:
        dq, both_ref, qs, gs, ks, pl_scr, dl_scr, ds_scr, dq_acc, dk_acc, dv_acc = rest
    f = pl.program_id(0)
    place = pos_ref[f]
    lanes = head_lanes()

    @pl.when(f == 0)
    def _():
        for ref in (dk_acc, dv_acc):
            ref[...] = jnp.zeros_like(ref)

    def prelude():
        query = q[0]
        grad = jnp.concatenate([r[0] for r in (g0, g1, g2, g3)], axis=0)
        mixed = jnp.concatenate([o0[0], o1[0], o23[0, 0], o23[1, 0]], axis=0)
        for h in range(4):
            rows = pl.ds(h * TOK, TOK)
            qs[rows, :] = jnp.where(lanes == h, query, jnp.zeros_like(query))
            gs[rows, :] = jnp.where(lanes == h, grad, jnp.zeros_like(grad))
        both = grad.astype(F32) * mixed.astype(F32)
        pick = (
            lax.broadcasted_iota(jnp.int32, (8, HC), 1) // HD
            == lax.broadcasted_iota(jnp.int32, (8, HC), 0)
        ).astype(F32)
        return lax.dot_general(
            pick, both, (((1,), (1,)), ((), ())),
            preferred_element_type=F32, precision=lax.Precision.HIGHEST,
        )

    def step(delta, logs, at):
        keys, values = k[at], v[at]
        for h in range(4):
            rows = pl.ds(h * TOK, TOK)
            ks[rows, :] = jnp.where(lanes == h, keys, jnp.zeros_like(keys))
            p = jnp.exp(nt(keys, qs[rows, :]) - logs[h : h + 1])
            ds = (p * (nt(values, gs[rows, :]) - delta[h : h + 1])).astype(BF16)
            pl_scr[:, rows] = p.astype(BF16)
            dl_scr[:, rows] = ds
            ds_scr[rows, :] = ds
        dv_acc[at] = dv_acc[at] + nn(pl_scr[...], gs[...])
        dk_acc[at] = dk_acc[at] + nn(dl_scr[...], qs[...])
        dq_acc[...] = dq_acc[...] + tn(ds_scr[...], ks[...])

    def sweep(low, high):
        delta = prelude()
        logs = lse[0]
        dq_acc[...] = jnp.zeros_like(dq_acc)

        def one(at, _):
            step(delta, logs, at)
            return 0

        lax.fori_loop(low, high, one, 0)

    if own:
        sweep(jnp.maximum(f - place, 0), f + 1)
        cosine, sine = cosines(cp, sp, fr, f)
        dq[0] = turn((dq_acc[...] + before_ref[0]) * 0.125, cosine, -sine).astype(BF16)
    else:
        count = jnp.maximum(place - f, 0)

        @pl.when(count > 0)
        def _():
            sweep(PREV - count, PREV)
            dq[0] = dq_acc[...]

        @pl.when(count == 0)
        def _():
            dq[0] = jnp.zeros_like(dq_acc)

        @pl.when(f == FPD - 1)
        def _():
            both_ref[0] = dk_acc[...].astype(BF16)
            both_ref[1] = dv_acc[...].astype(BF16)


def attend_back(own, places, q, k, v, grads, mixed, lse, tables=None, before=None):
    block = pl.BlockSpec((1, TOK, HC), lambda f, *_: (f, 0, 0))
    piece = pl.BlockSpec((1, PR, HC), lambda f, *_: (f, 0, 0))
    count = FPD if own else PREV
    wide = pltpu.VMEM((4 * TOK, HC), BF16)
    tall = pltpu.VMEM((TOK, 4 * TOK), BF16)
    scratch = [wide, wide, wide, tall, tall, wide, pltpu.VMEM((TOK, HC), F32)]
    specs = []
    extra = ()
    if own:
        specs = [whole((TOK, HC)), whole((TOK, HC)), whole((16, 2 * HC)), block]
        extra = tuple(tables) + (before,)
    else:
        scratch += [pltpu.VMEM((PREV, TOK, HC), F32)] * 2
    return pl.pallas_call(
        lambda *refs: attend_back_kernel(own, *refs),
        out_shape=[shape((FPD, TOK, HC), BF16 if own else F32)]
        + ([shape((FPD, TOK, HC), F32)] * 2 if own else [shape((2, PREV, TOK, HC))]),
        grid_spec=pltpu.PrefetchScalarGridSpec(
            num_scalar_prefetch=1,
            grid=(FPD,),
            in_specs=[block]
            + [whole((count, TOK, HC))] * 2
            + [piece] * 6
            + [pl.BlockSpec((2, 1, PR, HC), lambda f, *_: (0, f, 0, 0))]
            + [pl.BlockSpec((1, 8, TOK), lambda f, *_: (f, 0, 0))]
            + specs,
            out_specs=[block]
            + ([whole((FPD, TOK, HC))] * 2 if own else [whole((2, PREV, TOK, HC))]),
            scratch_shapes=scratch,
        ),
        compiler_params=params(58),
        cost_estimate=cost(1000 if own else 12 * 4 * 5 * 2 * TOK**3, 1000 if own else 12 * MB),
        name="attend_back_own" if own else "attend_back_prev",
    )(places, q, k, v, *grads, *mixed, lse, *extra)


HALF = 4
RAW = HALF * PR


def flat(ref):
    return ref[...].reshape(RAW, ref.shape[-1])


def frames_of(value):
    return value.reshape(HALF, PR, value.shape[-1])


def segment(table, s):
    both = table[:, s * D : (s + 1) * D]
    return jnp.where(pl.program_id(0) == 0, both[:HALF], both[HALF:])[:, None, :]


def fold(out, start, width, row):
    @pl.when(pl.program_id(0) == 0)
    def _():
        out[:, start : start + width] = jnp.zeros((8, width), F32)

    for i in range(8):
        at = (slice(i, i + 1), slice(start, start + width))
        out[at] = out[at] + row[:, i * width : (i + 1) * width]


def mid_kernel(o0, o1, o2, o3, w0, w1, w2, w3, table, x, cot, branch, middle, hidden, down, dsum):
    total = unfold(table, OB, 128)
    for o, w in zip((o0, o1, o2, o3), (w0, w1, w2, w3)):
        total = total + nn(flat(o), w[...])
    branched = frames_of(total)
    branch[...] = branched
    mid_value = x[...].astype(F32) + segment(table, 2) * branched
    middle[...] = mid_value
    normal, _ = norm(mid_value)
    hidden[...] = (normal * (1.0 + segment(table, 4)) + segment(table, 3)).astype(BF16)
    grad = (segment(table, 5) * cot[...].astype(F32)).astype(BF16)
    down[...] = grad
    fold(dsum, 0, 128, jnp.sum(grad.astype(F32).reshape(RAW, D), axis=0, keepdims=True))


def half_spec(width):
    return pl.BlockSpec((HALF, PR, width), lambda i, *_: (i, 0, 0))


def mid(pieces, weights, table, x, cot):
    return pl.pallas_call(
        mid_kernel,
        out_shape=[
            shape((FPD, PR, D), F32),
            shape((FPD, PR, D), F32),
            shape((FPD, PR, D)),
            shape((FPD, PR, D)),
            shape((8, 128), F32),
        ],
        grid=(FPD // HALF,),
        in_specs=[half_spec(HC)] * 4
        + [whole((HC, D))] * 4
        + [whole((FPD, WIDE)), half_spec(D), half_spec(D)],
        out_specs=[half_spec(D)] * 4 + [whole((8, 128))],
        compiler_params=params(26),
        cost_estimate=cost(2 * 512 * D * D, 12 * MB),
        name="mid",
    )(*pieces, *weights, table, x, cot)


def mid_back_kernel(
    hg, middle, branch, cot, table, w0, w1, w2, w3, usum, dsum, mg, bg, a0, a1, a23, sums
):
    grad = hg[...]
    normal, rate = norm(middle[...])
    put_half(sums, D, jnp.sum(grad, axis=1))
    put_half(sums, 2 * D, jnp.sum(grad * normal, axis=1))
    total = cot[...].astype(F32) + norm_back(normal, rate, grad * (1.0 + segment(table, 4)))
    mg[...] = total
    put_half(sums, 0, jnp.sum(total * branch[...], axis=1))
    low = (segment(table, 2) * total).astype(BF16)
    bg[...] = low
    low = low.reshape(RAW, D)
    sums[:, 3 * D : 3 * D + NB] = usum[...]
    sums[:, 3 * D + NB : 3 * D + NB + 128] = dsum[...]
    fold(sums, 3 * D + NB + 128, 128, jnp.sum(low.astype(F32), axis=0, keepdims=True))
    for j, w in enumerate((w0, w1, w2, w3)):
        value = frames_of(nt(low, w[...]).astype(BF16))
        if j < 2:
            (a0, a1)[j][...] = value
        else:
            a23[j - 2] = value


def mid_back(hg, middle, branch, cot, table, weights, usum, dsum):
    return pl.pallas_call(
        mid_back_kernel,
        out_shape=[shape((FPD, PR, D), F32), shape((FPD, PR, D))]
        + [shape((FPD, PR, HC))] * 2
        + [shape((2, FPD, PR, HC)), shape((8, EARLY), F32)],
        grid=(FPD // HALF,),
        in_specs=[half_spec(D)] * 4
        + [whole((FPD, WIDE))]
        + [whole((HC, D))] * 4
        + [whole((8, NB)), whole((8, 128))],
        out_specs=[half_spec(D)] * 2
        + [half_spec(HC)] * 2
        + [pl.BlockSpec((2, HALF, PR, HC), lambda i: (0, i, 0, 0)), whole((8, EARLY))],
        compiler_params=params(26),
        cost_estimate=cost(2 * 512 * D * D, 12 * MB),
        name="mid_back",
    )(hg, middle, branch, cot, table, *weights, usum, dsum)


NB = 512
STEPS = FF // NB
PER = D // NB
TOKENS = FPD * PR


def block_of(t):
    phase = t // PER
    return ((phase % 2) * 2) ^ (phase // 2)


def up_column(t, row):
    return (row ^ block_of(t)) * PER + t % PER


def down_row(t):
    return block_of(t) * PER + t % PER


def down_spec(j):
    phase = (0, 2, 1, 3)[j]
    return pl.BlockSpec((NB, D), lambda t, row: (jnp.clip(t - phase * PER, 0, PER - 1), 0))


def pick_down(d0, d1, d2, d3):
    phase = pl.program_id(0) // PER
    return jnp.where(
        phase < 2,
        jnp.where(phase == 0, d0[...], d2[...]),
        jnp.where(phase == 2, d1[...], d3[...]),
    )


def feed_kernel(row_ref, h2, dg, u0, u1, u2, u3, table, d0, d1, d2, d3, act, upg, hg, usum):
    row = row_ref[0]
    ups = (u0, u1, u2, u3)
    down = pick_down(d0, d1, d2, d3)
    at = pl.ds(up_column(pl.program_id(0), row), 1)
    u = table[at, UB : UB + NB]
    for j, w in enumerate(ups):
        u = u + nn(h2[:, columns(row, j)], w[...])
    rate = math.sqrt(2.0 / math.pi)
    square = u * u
    half = 0.5 + 0.5 * jnp.tanh(u * (rate + (rate * 0.044715) * square))
    active = u * half
    act[...] = active.astype(BF16)
    slope = half + active * (1.0 - half) * (2.0 * rate + (6.0 * rate * 0.044715) * square)
    grad = (nt(dg[...], down) * slope).astype(BF16)
    upg[...] = grad
    put(usum, 0, up_column(pl.program_id(0), row), jnp.sum(grad.astype(F32), axis=0, keepdims=True))

    @pl.when(pl.program_id(0) == 0)
    def _():
        hg[...] = jnp.zeros_like(hg)

    for j, w in enumerate(ups):
        hg[:, columns(row, j)] = hg[:, columns(row, j)] + nt(grad, w[...])


def feed(row, h2, dg, ups, table, downs):
    tok = whole((TOKENS, D))
    block = pl.BlockSpec((TOKENS, NB), lambda t, row: (0, t))
    return pl.pallas_call(
        feed_kernel,
        out_shape=[
            shape((TOKENS, FF)),
            shape((TOKENS, FF)),
            shape((TOKENS, D), F32),
            shape((8, NB), F32),
        ],
        grid_spec=pltpu.PrefetchScalarGridSpec(
            num_scalar_prefetch=1,
            grid=(STEPS,),
            in_specs=[tok, tok]
            + [pl.BlockSpec((HC, NB), lambda t, row: (0, up_column(t, row[0])))] * 4
            + [whole((FPD, WIDE))]
            + [down_spec(j) for j in range(4)],
            out_specs=[block, block, tok, whole((8, NB))],
        ),
        compiler_params=params(58),
        cost_estimate=cost(3 * 2 * TOKENS * D * FF, 30 * MB, TOKENS * FF),
        name="feed",
    )(row, h2, dg, *ups, table, *downs)


def down_weight_kernel(row_ref, dg, act, d0, d1, d2, d3, table, middle, cot, dk, ds, out, gate, dn):
    t = pl.program_id(0)
    down = pick_down(d0, d1, d2, d3)
    active = act[...]

    @pl.when(t == 0)
    def _():
        dn[...] = jnp.zeros_like(dn)

    dn[...] = dn[...] + nn(active, down)
    part = tn(active, dg[...]).astype(BF16)

    @pl.when(t < STEPS // 2)
    def _():
        dk[0] = part

    @pl.when(t >= STEPS // 2)
    def _():
        ds[0] = part

    @pl.when(t == STEPS - 1)
    def _():
        bias = unfold(table, DB, 128)
        for f in range(FPD):
            rows = slice(f * PR, (f + 1) * PR)
            value = dn[rows, :] + bias
            out[f] = (middle[f] + table[f : f + 1, 5 * D : 6 * D] * value).astype(BF16)
            gate[f : f + 1, :] = jnp.sum(cot[f].astype(F32) * value, axis=0, keepdims=True)


def down_weight_grad(row, dg, act, downs, table, middle, cot):
    tok = whole((TOKENS, D))
    full = whole((FPD, PR, D))
    block = pl.BlockSpec((TOKENS, NB), lambda t, row: (0, t))

    def down_out(first):
        def index(t, row):
            at = jnp.clip(t - first, 0, STEPS // 2 - 1)
            return (at // PER, at % PER, 0)

        return pl.BlockSpec((1, NB, D), index)

    return pl.pallas_call(
        down_weight_kernel,
        out_shape=[shape((2, D, D))] * 2 + [shape((FPD, PR, D)), shape((8, D), F32)],
        grid_spec=pltpu.PrefetchScalarGridSpec(
            num_scalar_prefetch=1,
            grid=(STEPS,),
            in_specs=[tok, block]
            + [down_spec(j) for j in range(4)]
            + [whole((FPD, WIDE)), full, full],
            out_specs=[down_out(0), down_out(STEPS // 2), full, whole((8, D))],
            scratch_shapes=[pltpu.VMEM((TOKENS, D), F32)],
        ),
        compiler_params=params(58),
        cost_estimate=cost(2 * 2 * TOKENS * D * FF, 24 * MB),
        name="down_weight_grad",
    )(row, dg, act, *downs, table, middle, cot)


def up_weight_kernel(row_ref, h2, upg, uk, us):
    row = row_ref[0]
    grad = upg[...]
    for j, ref in enumerate((uk, us, uk, us)):
        ref[j // 2, 0] = tn(h2[:, columns(row, j)], grad).astype(BF16)


def up_weight_grad(row, h2, upg):
    up_out = pl.BlockSpec(
        (2, 1, HC, NB),
        lambda t, row: (0, up_column(t, row[0]) // PER, 0, up_column(t, row[0]) % PER),
    )
    return pl.pallas_call(
        up_weight_kernel,
        out_shape=[shape((2, 4, HC, D))] * 2,
        grid_spec=pltpu.PrefetchScalarGridSpec(
            num_scalar_prefetch=1,
            grid=(STEPS,),
            in_specs=[whole((TOKENS, D)), pl.BlockSpec((TOKENS, NB), lambda t, row: (0, t))],
            out_specs=[up_out, up_out],
        ),
        compiler_params=params(58),
        cost_estimate=cost(2 * TOKENS * D * FF, 14 * MB),
        name="up_weight_grad",
    )(row, h2, upg)


def out_weight_kernel(t0, t1, t2, t3, bg, keep, send):
    grad = bg[...].reshape(TOKENS, D)
    for j, t in enumerate((t0, t1, t2, t3)):
        ref = (keep, send)[j % 2]
        ref[j // 2] = tn(t[...].reshape(TOKENS, HC), grad).astype(BF16)


def out_weight_grad(pieces, bg):
    return pl.pallas_call(
        out_weight_kernel,
        out_shape=[shape((2, HC, D))] * 2,
        grid=(1,),
        in_specs=[whole((FPD, PR, HC))] * 4 + [whole((FPD, PR, D))],
        out_specs=[whole((2, HC, D))] * 2,
        compiler_params=params(14),
        cost_estimate=cost(2 * TOKENS * D * D, 4 * MB),
        name="out_weight_grad",
    )(*pieces, bg)


CHUNKS = 16
UP_ROWS, OUT_ROWS, DOWN_ROWS = D // CHUNKS, HC // CHUNKS, D // CHUNKS
FIRST = UP_ROWS + OUT_ROWS
ROWS = FIRST + DOWN_ROWS


def core_sum_kernel(ua, ub, da, db, oa, ob, out):
    def both(a, b):
        return (a.astype(F32) + b.astype(F32)).astype(BF16)

    for c in range(4):
        at = c * ROWS
        low, high = c * OUT_ROWS, (c + 1) * OUT_ROWS
        for i in range(4):
            to = at + i * OUT_ROWS
            out[0, to : to + OUT_ROWS] = both(ua[0, i, low:high], ub[0, i, low:high])
        out[0, at + UP_ROWS : at + FIRST] = both(oa[0, low:high], ob[0, low:high])
        low, high = c * DOWN_ROWS, (c + 1) * DOWN_ROWS
        out[0, at + FIRST : at + ROWS] = both(da[0, low:high], db[0, low:high])


def core_sum(up, down, out):
    ups = pl.BlockSpec((1, 4, 4 * OUT_ROWS, D), lambda j, c: (j, 0, c, 0))
    outs = pl.BlockSpec((1, 4 * OUT_ROWS, D), lambda j, c: (j, c, 0))
    downs = pl.BlockSpec((1, 4 * DOWN_ROWS, D), lambda j, c: (j, c, 0))
    return pl.pallas_call(
        core_sum_kernel,
        out_shape=shape((2, CHUNKS * ROWS, D)),
        grid=(2, CHUNKS // 4),
        in_specs=[ups, ups, downs, downs, outs, outs],
        out_specs=pl.BlockSpec((1, 4 * ROWS, D), lambda j, c: (j, c, 0)),
        compiler_params=params(58),
        cost_estimate=cost(1000, 1000),
        name="core_sum",
    )(*up, *down, *out)


def unpack_kernel(total, up, out, down):
    for k in range(4):
        at = k * ROWS
        for i in range(4):
            rows = slice(at + i * OUT_ROWS, at + (i + 1) * OUT_ROWS)
            up[k * OUT_ROWS : (k + 1) * OUT_ROWS, i * D : (i + 1) * D] = total[rows].astype(F32)
        out[k * OUT_ROWS : (k + 1) * OUT_ROWS] = total[at + UP_ROWS : at + FIRST].astype(F32)
        down[k * DOWN_ROWS : (k + 1) * DOWN_ROWS] = total[at + FIRST : at + ROWS].astype(F32)


def unpack(total):
    block = lambda i: (i, 0)
    return pl.pallas_call(
        unpack_kernel,
        out_shape=[shape((HC, FF), F32), shape((HC, D), F32), shape((D, D), F32)],
        grid=(4,),
        in_specs=[pl.BlockSpec((4 * ROWS, D), block)],
        out_specs=[
            pl.BlockSpec((4 * OUT_ROWS, FF), block),
            pl.BlockSpec((4 * OUT_ROWS, D), block),
            pl.BlockSpec((4 * DOWN_ROWS, D), block),
        ],
        compiler_params=params(24),
        cost_estimate=cost(0, 14 * MB),
        name="unpack",
    )(total)


LATE = 3 * D + 2 * HC
EARLY = 3 * D + NB + 256


def arrange_kernel(row_ref, a0, a1, a2, a3, late, far, out):
    row = row_ref[0]
    for j, a in enumerate((a0, a1, a2, a3)):
        for s in range(3):
            lanes = pl.ds(pl.multiple_of(s * D + (row ^ j) * HC, HC), HC)
            out[:, lanes] = a[:, s * HC : (s + 1) * HC]
    both = jnp.concatenate([late[...].astype(F32), far[...].astype(F32)], axis=0)
    out[:, 3 * D :] = both.astype(BF16)


def arrange(row, pieces, late, far):
    rows = pieces[0].shape[0]
    return pl.pallas_call(
        arrange_kernel,
        out_shape=shape((rows, 3 * D + LATE)),
        grid_spec=pltpu.PrefetchScalarGridSpec(
            num_scalar_prefetch=1,
            grid=(1,),
            in_specs=[whole((rows, 3 * HC))] * 4 + [whole((8, LATE))] * 2,
            out_specs=whole((rows, 3 * D + LATE)),
        ),
        compiler_params=params(16),
        cost_estimate=cost(0, 8 * rows * D),
        name="arrange",
    )(row, *pieces, late, far)


def stack_kernel(a0, a1, a2, a3, weights, sums):
    for k, a in enumerate((a0, a1, a2, a3)):
        weights[k] = a[:, : 3 * D]
        sums[k] = a[:, 3 * D :]


def stack(pieces):
    rows, width = pieces[0].shape
    return pl.pallas_call(
        stack_kernel,
        out_shape=[shape((4, rows, 3 * D)), shape((4, rows, LATE))],
        grid=(1,),
        in_specs=[whole((rows, width))] * 4,
        out_specs=[whole((4, rows, 3 * D)), whole((4, rows, LATE))],
        compiler_params=params(16),
        cost_estimate=cost(0, 2 * MB),
        name="stack",
    )(*pieces)


def place_kernel(index_ref, low, high, out):
    for m, a in enumerate((low.at[0], low.at[1], high.at[1], high.at[0])):

        @pl.when(pl.program_id(0) == m)
        def _():
            for k in range(4):
                out[0, index_ref[1] ^ k] = a[k].astype(F32)


def place(index, low, high):
    rows = low.shape[2]
    return pl.pallas_call(
        place_kernel,
        out_shape=shape((4, 4, rows, 3 * D), F32),
        grid_spec=pltpu.PrefetchScalarGridSpec(
            num_scalar_prefetch=1,
            grid=(4,),
            in_specs=[whole(low.shape)] * 2,
            out_specs=pl.BlockSpec((1, 4, rows, 3 * D), lambda i, index: (index[0] ^ i, 0, 0, 0)),
        ),
        compiler_params=params(24),
        cost_estimate=cost(0, 24 * rows * D),
        name="place",
    )(index, low, high).reshape(HC, 3 * D)


def project_back_kernel(row_ref, dq, dk, dv, rk, rv, w0, w1, w2, w3, cp, sp, fr, dp, h0, h2, hs, bsum):
    row = row_ref[0]
    f = pl.program_id(0)
    later = (f > 0).astype(F32)
    keys = dk[0] + later * rk[0, 0].astype(F32)
    values = dv[0] + later * rv[0, 0].astype(F32)
    cosine, sine = cosines(cp, sp, fr, f)
    dp[0, :, :HC] = dq[0]
    dp[0, :, HC : 2 * HC] = turn(keys, cosine, -sine).astype(BF16)
    dp[0, :, 2 * HC :] = values.astype(BF16)
    grad = dp[0]
    sums = jnp.sum(grad.astype(F32), axis=0, keepdims=True)

    @pl.when(f == 0)
    def _():
        bsum[...] = jnp.zeros_like(bsum)

    number = lax.broadcasted_iota(jnp.int32, (8, 2 * HC), 0)
    bsum[...] = bsum[...] + jnp.where(number == row, sums[:, : 2 * HC], 0.0)
    bsum[:, :HC] = bsum[:, :HC] + jnp.where(number[:, :HC] == row + 4, sums[:, 2 * HC :], 0.0)
    for j, w in enumerate((w0, w1, w2, w3)):
        part = nt(grad, w[...]).astype(BF16)
        at = (0, slice(None), columns(row, j))
        h0[at] = part[:PR]
        hs[(0,) + at] = part[PR : 2 * PR]
        h2[at] = part[2 * PR : 3 * PR]
        hs[(1,) + at] = part[3 * PR :]


def project_back(row, dq, dk, dv, returned, weights, tables):
    block = pl.BlockSpec((1, TOK, HC), lambda f, *_: (f, 0, 0))
    late = [
        pl.BlockSpec((1, 1, TOK, HC), lambda f, *_, i=i: (i, jnp.maximum(f - 1, 0), 0, 0))
        for i in range(2)
    ]
    piece = pl.BlockSpec((1, PR, D), lambda f, *_: (f, 0, 0))
    return pl.pallas_call(
        project_back_kernel,
        out_shape=[
            shape((FPD, TOK, 3 * HC)),
            shape((FPD, PR, D)),
            shape((FPD, PR, D)),
            shape((2, FPD, PR, D)),
            shape((8, 2 * HC), F32),
        ],
        grid_spec=pltpu.PrefetchScalarGridSpec(
            num_scalar_prefetch=1,
            grid=(FPD,),
            in_specs=[block] * 3
            + late
            + [whole((HC, 3 * HC))] * 4
            + [whole((TOK, HC)), whole((TOK, HC)), whole((16, 2 * HC))],
            out_specs=[
                pl.BlockSpec((1, TOK, 3 * HC), lambda f, *_: (f, 0, 0)),
                piece,
                piece,
                pl.BlockSpec((2, 1, PR, D), lambda f, *_: (0, f, 0, 0)),
                whole((8, 2 * HC)),
            ],
        ),
        compiler_params=params(20),
        cost_estimate=cost(2 * FPD * TOK * D * 3 * HC, 14 * MB),
        name="project_back",
    )(row, dq, dk, dv, returned, returned, *weights, *tables)


def weight_kernel(row_ref, h, dp, w):
    w[0] = tn(h[...], dp[...]).astype(BF16)


def project_weight(row, hidden, dproj):
    tokens = FPD * TOK
    return pl.pallas_call(
        weight_kernel,
        out_shape=shape((4, HC, 3 * HC)),
        grid_spec=pltpu.PrefetchScalarGridSpec(
            num_scalar_prefetch=1,
            grid=(4,),
            in_specs=[
                pl.BlockSpec((tokens, HC), lambda j, row: (0, row[0] ^ j)),
                whole((tokens, 3 * HC)),
            ],
            out_specs=pl.BlockSpec((1, HC, 3 * HC), lambda j, row: (j, 0, 0)),
        ),
        compiler_params=params(20),
        cost_estimate=cost(2 * tokens * D * 3 * HC, 9 * MB),
        name="project_weight",
    )(row, hidden.reshape(tokens, D), dproj.reshape(tokens, 3 * HC))


def input_back_kernel(x, h0, near, far, table, mg, bsum, gate, out, sums):
    grad = h0[...].astype(F32) + near[0].astype(F32) + far[...].astype(F32)
    normal, rate = norm(x[...].astype(F32))
    put_half(sums, 0, jnp.sum(grad, axis=1))
    put_half(sums, D, jnp.sum(grad * normal, axis=1))
    sums[:, 2 * D : 3 * D] = gate[...]
    sums[:, 3 * D :] = bsum[...]
    out[...] = mg[...] + norm_back(normal, rate, grad * (1.0 + segment(table, 1)))


def input_back(x, h0, near, far, table, mg, bsum, gate):
    return pl.pallas_call(
        input_back_kernel,
        out_shape=[shape((FPD, PR, D), F32), shape((8, LATE), F32)],
        grid=(FPD // HALF,),
        in_specs=[half_spec(D)] * 2
        + [pl.BlockSpec((1, HALF, PR, D), lambda i: (0, i, 0, 0))]
        + [half_spec(D), whole((FPD, WIDE)), half_spec(D), whole((8, 2 * HC)), whole((8, D))],
        out_specs=[half_spec(D), whole((8, LATE))],
        compiler_params=params(20),
        cost_estimate=cost(20 * 512 * D, 10 * MB),
        name="input_back",
    )(x, h0, near, far, table, mg, bsum, gate)


def join_kernel(a0, a1, a2, a3, out):
    for k, a in enumerate((a0, a1, a2, a3)):
        out[2 * k : 2 * k + 2] = a[...]


def join(pieces):
    width = pieces[0].shape[-1]
    return pl.pallas_call(
        join_kernel,
        out_shape=shape((8, 8, width)),
        grid=(1,),
        in_specs=[whole((2, 8, width))] * 4,
        out_specs=whole((8, 8, width)),
        compiler_params=params(16),
        cost_estimate=cost(0, 2 * MB),
        name="join",
    )(*pieces)


def final_kernel(row_ref, *refs):
    row = row_ref[0]
    low, high, *early = refs[:6]
    ada, ab, qb, ob, ub, db, asum = refs[6:]
    late = [low.at[0], low.at[1], high.at[0], high.at[1]]
    early = [early[0], early[3], early[1], early[2]]

    def rows(ref, cols):
        value = ref[:, :, cols].astype(F32)
        return value.reshape(64, value.shape[-1])

    left = [rows(s, slice(EARLY, EARLY + HC)).astype(BF16) for s in early]
    for segment in range(6):
        source, start = ((late, 0), (late, 1), (early, 0), (early, 1), (early, 2), (late, 2))[segment]
        cols = slice(start * D, (start + 1) * D)
        product, total = 0.0, 0.0
        for s, ref in zip(left, source):
            right = rows(ref, cols)
            total = total + jnp.sum(right, axis=0, keepdims=True)
            product = product + tn(s, right.astype(BF16))
        at = segment * D
        ada[:, at : at + D] = product
        asum[0:1, at : at + D] = total

    def fold8(value):
        value = jnp.sum(value, axis=0)
        return value if value.shape[0] == 8 else value[:8] + value[8:]

    def bias(source, start, stop):
        return sum(
            fold8(ref[:, :, start:stop].astype(F32)) for ref in source
        )

    ab[...] = asum[0:1, pl.ds(pl.multiple_of(row * 1536, 512), 1536)]
    folded = bias(late, 3 * D, LATE)
    for i in range(3):
        chunk = 3 * row + i
        at = jnp.where(chunk < 4, chunk, chunk - 4)
        second = (chunk >= 4) & (chunk < 8)
        value = jnp.where(second, folded[:, HC:], folded[:, :HC])
        qb[:, i * HC : (i + 1) * HC] = take(value, at)
    folded = bias(early, 3 * D, EARLY)
    for i in range(2):
        at = 2 * row + i
        ub[:, i * NB : (i + 1) * NB] = take(folded[:, :NB], at)
        db[:, i * 128 : (i + 1) * 128] = take(folded[:, NB : NB + 128], at)
        ob[:, i * 128 : (i + 1) * 128] = take(folded[:, NB + 128 :], at)


def final_sums(row, late, early):
    sizes = (1536, 768, 256, 1024, 256)
    return pl.pallas_call(
        final_kernel,
        out_shape=[shape((HC, 6 * D), F32)] + [shape((1, n), F32) for n in sizes],
        grid_spec=pltpu.PrefetchScalarGridSpec(
            num_scalar_prefetch=1,
            grid=(1,),
            in_specs=[whole((2, 4, 16, LATE))] * 2
            + [whole((8, 8, EARLY + HC))] * 4,
            out_specs=[whole((HC, 6 * D))] + [whole((1, n)) for n in sizes],
            scratch_shapes=[pltpu.VMEM((8, 6 * D), F32)],
        ),
        compiler_params=params(28),
        cost_estimate=cost(2 * 256 * HC * 6 * D, 10 * MB),
        name="final_sums",
    )(row, *late, *early)


def row_sum(value):
    value = value + swap(value, CORE)
    return value + swap(value, DIRECT)


def row_pieces(value):
    return [value, swap(value, CORE), swap(value, DIRECT), swap(value, DIRECT ^ CORE)]


def by_row(pieces, row):
    a, b, c, d = pieces
    odd, high = row % 2 == 1, row >= 2
    a, b = jnp.where(odd, b, a), jnp.where(odd, a, b)
    c, d = jnp.where(odd, d, c), jnp.where(odd, c, d)
    return jnp.stack(
        [
            jnp.where(high, c, a),
            jnp.where(high, d, b),
            jnp.where(high, a, c),
            jnp.where(high, b, d),
        ]
    )


def quarter_rows(value, bit, index, axis):
    rows = value.shape[1] // 4
    at = lambda m: lax.dynamic_slice_in_dim(value, (index[axis] ^ m) * rows, rows, 1)
    return [at(0)] + [swap(at(m), bit * m) for m in (1, 2, 3)]


def add_all(parts):
    return sum(part.astype(F32) for part in parts).astype(BF16)


def exchange_rows(value, bit, index, axis):
    return add_all(quarter_rows(value, bit, index, axis))


def turn_heads(own, beside, across, order=lambda piece: piece):
    across = swap(across, DIRECT)
    return [own, swap(beside, CORE), across[0], swap(order(across)[1], CORE)]


def per_device(
    activations,
    noise_embed,
    frame_position,
    cotangent,
    ada_weight,
    ada_bias,
    qkv_weight,
    qkv_bias,
    out_weight,
    out_bias,
    up_weight,
    up_bias,
    down_weight,
    down_bias,
):
    row = lax.axis_index(("xl", "c")).astype(jnp.int32)
    row_arg = row.reshape(1)
    index = [lax.axis_index("y").astype(jnp.int32), lax.axis_index("z").astype(jnp.int32)]
    index_arg = jnp.stack(index)

    x0 = activations
    x2 = swap(x0, DIRECT)
    x1 = swap(x0, CORE)
    p0 = shift(activations[1:], 1)
    biases = (ada_bias, qkv_bias, out_bias, up_bias, down_bias)
    heads = list(split_heads(row_arg, qkv_weight))
    noise, heads[1] = lax.optimization_barrier((noise_embed, heads[1]))
    part, silu_own, *tables = prepare(row_arg, frame_position, noise, ada_weight, biases)
    across = swap(heads[2], OTHER)
    qkv_pieces = [heads[0], swap(heads[1], CORE), across]
    part = part + swap(part, CORE)
    table = part + swap(part, DIRECT)
    x2, table, *qkv_pieces = lax.optimization_barrier((x2, table, *qkv_pieces))

    qkv_pieces = qkv_pieces[:2] + [qkv_pieces[2][0], swap(qkv_pieces[2][1], CORE)]
    x3 = swap(x2, CORE)
    before_mods = shift(table[:, : 2 * D], 1)

    out_own, up_own, _ = lax.optimization_barrier((out_weight, up_weight, table))
    outs2 = swap(out_own, OTHER)
    ups2 = swap(up_own, OTHER)

    hidden1, q, k, v = project(True, row_arg, (x0, x1, x2, x3), table, table, qkv_pieces, tables)
    p0, q, before_mods = lax.optimization_barrier((p0, q, before_mods))
    p2 = swap(p0, DIRECT)
    p1 = swap(p0, CORE)
    p2, down_own = lax.optimization_barrier((p2, down_weight))
    p3 = swap(p2, CORE)
    downs2 = swap(down_own, DIRECT)
    kp, vp = project(
        False, row_arg, (p0, p1, p2, p3), table, before_mods, qkv_pieces, tables
    )
    *mixed, lse = attend(frame_position, q, k, v, kp, vp)
    outs2, ups2, downs2, lse = lax.optimization_barrier((outs2, ups2, downs2, lse))
    outs = [out_weight, swap(out_own, CORE), outs2, swap(outs2, CORE)]
    ups = [up_weight, swap(up_own, CORE), ups2, swap(ups2, CORE)]
    downs = [down_weight, swap(down_own, CORE), downs2, swap(downs2, CORE)]
    turned = turn_heads(*mixed)
    branch, middle, hidden2, down_grad, dsum = mid(turned, outs, table, x0, cotangent)
    h2 = hidden2.reshape(TOKENS, D)
    dg = down_grad.reshape(TOKENS, D)
    act, upg, hg, usum = feed(row_arg, h2, dg, ups, table, downs)
    mg, bg, *ag, early = mid_back(
        hg.reshape(FPD, PR, D), middle, branch, cotangent, table, outs, usum, dsum
    )
    late = []
    back = turn_heads(*ag[:2], ag[2], order=lambda piece: late.append(piece) or piece)[:2]

    early = early + swap(early, CORE)
    upg, early, _ = lax.optimization_barrier((upg, early, bg))
    early_far = swap(early, DIRECT)
    uk, us = up_weight_grad(row_arg, h2, upg)
    us = swap(us, CORE)
    dg_later, early_far, far_back, uk, *back = lax.optimization_barrier(
        (dg, early_far, *late, uk, *back)
    )
    back += [far_back[0], swap(far_back[1], CORE)]
    early = jnp.concatenate([(early + early_far).astype(BF16), silu_own], axis=1)
    early_far = swap(early, FAR)
    dk_part, ds_part, layer_output, gate = down_weight_grad(
        row_arg, dg_later, act, downs, table, middle, cotangent
    )
    ds_part = swap(ds_part, CORE)
    dk_part, early, early_far, bg_later, us, *back = lax.optimization_barrier(
        (dk_part, early, early_far, bg, us, *back)
    )
    early = jnp.stack([early, early_far])
    early_parts = [early] + [swap(early, m) for m in (16, 32, 48)]
    ok, os = out_weight_grad(turned, bg_later)
    packed = core_sum((uk, us), (dk_part, ds_part), (ok, swap(os, CORE)))
    packed, early_parts = lax.optimization_barrier((packed, early_parts))
    early = join(early_parts)
    early_all = [early] + [swap(early, m) for m in (4, 8, 12)]
    packed, early, back = lax.optimization_barrier((packed, early, back))
    scattered = lax.psum_scatter(packed, ("y", "z"), scatter_dimension=1, tiled=True)

    dq_before, both = attend_back(False, frame_position, q, kp, vp, back, mixed, lse)
    returned = shift(both, -1)
    dq, dk, dv = attend_back(
        True, frame_position, q, k, v, back, mixed, lse, tables, dq_before
    )
    dq, *early_all = lax.optimization_barrier((dq, *early_all))
    early = early[0].astype(F32)

    dproj, h0, h2_part, send, bsum = project_back(row_arg, dq, dk, dv, returned, qkv_pieces, tables)
    near = swap(send, CORE)
    qkv_parts = project_weight(row_arg, hidden1, dproj)
    far_part = (h2_part.astype(F32) + near[1].astype(F32)).astype(BF16)
    far = swap(far_part, DIRECT)
    far_part, qkv_parts = lax.optimization_barrier((far_part, qkv_parts))
    quarters = quarter_rows(qkv_parts, 4, index, 0)
    input_grad, late = input_back(x0, h0, near, far, table, mg, bsum, gate)
    late_near = swap(late, CORE)
    late, *quarters = lax.optimization_barrier((late, *quarters))
    quarters = quarter_rows(add_all(quarters), 16, index, 1)
    late = late + late_near
    late_far = swap(late, DIRECT)
    late, *quarters = lax.optimization_barrier((late, *quarters))
    qkv_parts = add_all(quarters)
    qkv_far = swap(qkv_parts, FAR)
    scattered, late, late_far, qkv_parts = lax.optimization_barrier(
        (scattered, late, late_far, qkv_parts)
    )
    late = late + late_far
    late_low = late.astype(BF16)
    late_far = swap(late_low, FAR)
    share_far = swap(scattered[1], DIRECT)
    late_low, qkv_far = lax.optimization_barrier((late_low, qkv_far))
    qkv_parts = add_all([qkv_parts, qkv_far])
    turned = turn_heads(qkv_parts[0], qkv_parts[1], qkv_parts[2:])
    turned, share_far = lax.optimization_barrier((turned, share_far))
    share = scattered[0].astype(F32) + share_far.astype(F32)
    share_far = swap(share.astype(BF16), FAR)
    last = arrange(row_arg, turned, late_low, late_far)

    share, share_far, last = lax.optimization_barrier((share, share_far, last))
    share = (share + share_far.astype(F32)).astype(BF16)
    totals = lax.all_gather(share, ("y", "z"), axis=0, tiled=True)
    weights, sums_late = stack([last] + [swap(last, m) for m in (16, 32, 48)])
    weights = jnp.stack([weights, swap(weights, 4)])
    sums_late = jnp.stack([sums_late, swap(sums_late, 12)])
    weights_far, sums_far = swap(weights, 12), swap(sums_late, 4)
    up_total, out_total, down_total = unpack(totals)
    qkv_total = place(index_arg, weights, weights_far)

    ada_total, *bias_sums = final_sums(row_arg, (sums_late, sums_far), early_all)
    ada_sum, qkv_sum, out_sum, up_sum, down_sum = [b[0] for b in bias_sums]
    mod_own = jnp.concatenate(
        [late[:, : 2 * D], early[:, : 3 * D], late[:, 2 * D : 3 * D]], axis=1
    ).astype(BF16)
    silu_grad = nt(mod_own, ada_weight)
    silu_grad = by_row(row_pieces(silu_grad), row).transpose(1, 0, 2).reshape(FPD, D)
    embed = noise_embed.astype(F32)
    sigma = jax.nn.sigmoid(embed)
    embed_grad = silu_grad * (sigma * (1.0 + embed * (1.0 - sigma)))

    return (
        layer_output,
        input_grad,
        embed_grad,
        ada_total,
        ada_sum,
        qkv_total,
        qkv_sum,
        out_total,
        out_sum,
        up_total,
        up_sum,
        down_total,
        down_sum,
    )


def solution(mesh):
    fine = Mesh(mesh.devices.reshape(2, 4, 4, 2, 2), AXES)
    seq, row = ("xh", "z", "y"), ("xl", "c")
    token, weight, vector = P(seq, row, None), P(row, None), P(row)
    in_specs = (token, P(seq, None), P(seq), token) + (weight, vector) * 5
    out_specs = (token, token, P(seq, None)) + (weight, vector) * 5
    return jax.shard_map(
        per_device, mesh=fine, in_specs=in_specs, out_specs=out_specs, check_vma=False
    )
```

```python
import math

import jax
import jax.numpy as jnp
from jax import lax
from jax.experimental import pallas as pl
from jax.experimental.pallas import tpu as pltpu
from jax.sharding import Mesh, PartitionSpec as P

F32 = jnp.float32
BF16 = jnp.bfloat16
HD = 64
GRID = 16
FPD = 8
PR = 64
D = 1024
FF = 4096
HC = 256
TOK = 256
PREV = 7
AXES = ("xh", "z", "y", "xl", "c")
CORE, DIRECT, OTHER, FAR = 1, 2, 66, 64
MB = 1024 * 1024


def swap(value, mask):
    return lax.ppermute(value, AXES, [(i, i ^ mask) for i in range(128)])


def shift(value, steps):
    return lax.ppermute(value, AXES, [(i, (i + 4 * steps) % 128) for i in range(128)])


def after(value, *others):
    return lax.optimization_barrier((value,) + others)[0]


def nt(left, right):
    return lax.dot_general(left, right, (((1,), (1,)), ((), ())), preferred_element_type=F32)


def tn(left, right):
    return lax.dot_general(left, right, (((0,), (0,)), ((), ())), preferred_element_type=F32)


def nn(left, right):
    return jnp.dot(left, right, preferred_element_type=F32)


def norm(values):
    center = values - jnp.mean(values, axis=-1, keepdims=True)
    spread = jnp.mean(center * center, axis=-1, keepdims=True)
    rate = lax.rsqrt(spread + 1e-06)
    return center * rate, rate


def norm_back(normal, rate, grad):
    mean_grad = jnp.mean(grad, axis=-1, keepdims=True)
    mean_both = jnp.mean(grad * normal, axis=-1, keepdims=True)
    return rate * (grad - mean_grad - normal * mean_both)


def turn(values, cosine, sine):
    lanes = lax.broadcasted_iota(jnp.int32, values.shape, 1)
    other = jnp.where(
        lanes % HD < HD // 2, pltpu.roll(values, HC - HD // 2, 1), pltpu.roll(values, HD // 2, 1)
    )
    return values * cosine + other * sine


def params(mib):
    return pltpu.CompilerParams(vmem_limit_bytes=mib * MB)


def cost(flops, moved, exps=0):
    return pl.CostEstimate(flops=int(flops), bytes_accessed=int(moved), transcendentals=int(exps))


def whole(shape):
    return pl.BlockSpec(shape, lambda i, *_: (0,) * len(shape))


def columns(row, j):
    return pl.ds(pl.multiple_of((row ^ j) * HC, HC), HC)


def shape(dims, kind=BF16):
    return jax.ShapeDtypeStruct(dims, kind)


UB, QB, OB, DB, WIDE = 6144, 6656, 7168, 7296, 7424


def put(ref, start, at, value):
    cols = slice(start, start + value.shape[1])
    number = lax.broadcasted_iota(jnp.int32, (8, value.shape[1]), 0)
    ref[:, cols] = jnp.where(number == at, value, ref[:, cols])


def take(value, at):
    number = lax.broadcasted_iota(jnp.int32, value.shape, 0)
    return jnp.sum(jnp.where(number == at, value, 0.0), axis=0, keepdims=True)


def put_half(ref, start, value):
    cols = slice(start, start + value.shape[1])
    number = lax.broadcasted_iota(jnp.int32, (8, value.shape[1]), 0)
    both = jnp.concatenate([value, value], axis=0)
    ref[:, cols] = jnp.where(number // 4 == pl.program_id(0), both, ref[:, cols])


def unfold(ref, start, width):
    return jnp.concatenate([ref[i : i + 1, start : start + width] for i in range(8)], axis=1)


def prepare_kernel(row_ref, pos_ref, noise, ada, ab, qb, ob, ub, db, pack, silu, cp, sp, frames):
    row = row_ref[0]
    embed = noise[...].astype(F32)
    value = (embed / (1.0 + jnp.exp(-embed))).astype(BF16)
    own = jnp.where(
        row < 2,
        jnp.where(row == 0, value[:, :HC], value[:, HC : 2 * HC]),
        jnp.where(row == 2, value[:, 2 * HC : 3 * HC], value[:, 3 * HC :]),
    )
    silu[...] = own
    pack[:, UB:] = jnp.zeros((FPD, WIDE - UB), F32)
    for segment in range(6):
        cols = slice(segment * D, (segment + 1) * D)
        pack[:, cols] = nn(own, ada[:, cols])
    bias = pl.ds(pl.multiple_of(row * 1536, 512), 1536)
    pack[:, bias] = pack[:, bias] + ab[...].astype(F32)
    for i in range(2):
        at = 2 * row + i
        put(pack, UB, at, ub[:, i * 512 : (i + 1) * 512].astype(F32))
        put(pack, OB, at, ob[:, i * 128 : (i + 1) * 128].astype(F32))
        put(pack, DB, at, db[:, i * 128 : (i + 1) * 128].astype(F32))
    for i in range(3):
        chunk = 3 * row + i
        at = jnp.where(chunk < 4, chunk, chunk - 4)
        second = (chunk >= 4) & (chunk < 8)
        value = qb[:, i * HC : (i + 1) * HC].astype(F32)
        put(pack, QB, jnp.where(second, -1, at), value)
        put(pack, QB + HC, jnp.where(second, at, -1), value)

    def parts(dims):
        lane = lax.broadcasted_iota(jnp.int32, dims, 1)
        index = lane % (HD // 2)
        quarter, eighth = HD // 4, HD // 8
        in_frame = index < quarter
        in_row = (index >= quarter) & (index < quarter + eighth)
        offset = jnp.where(
            in_frame, index, jnp.where(in_row, index - quarter, index - quarter - eighth)
        ).astype(F32)
        length = jnp.where(in_frame, 1.0 * quarter, 1.0 * eighth)
        frequency = jnp.exp(-math.log(10000.0) * offset / length)
        sign = jnp.where(lane % HD < HD // 2, -1.0, 1.0)
        return in_frame, in_row, frequency, sign

    in_frame, in_row, frequency, sign = parts((TOK, HC))
    slot = lax.broadcasted_iota(jnp.int32, (TOK, HC), 0)
    patch = ((slot // PR) ^ row) * PR + slot % PR
    angle = jnp.where(in_row, patch // GRID, patch % GRID).astype(F32) * frequency
    cp[...] = jnp.where(in_frame, 0.0, jnp.cos(angle))
    sp[...] = jnp.where(in_frame, 0.0, jnp.sin(angle) * sign)
    in_frame, _, frequency, sign = parts((16, HC))
    slot = lax.broadcasted_iota(jnp.int32, (16, HC), 0)
    place = pos_ref[0] - PREV + (slot - FPD)
    for f in range(FPD):
        place = jnp.where(slot == f, pos_ref[f], place)
    angle = place.astype(F32) * frequency
    frames[:, :HC] = jnp.where(in_frame, jnp.cos(angle), 0.0)
    frames[:, HC:] = jnp.where(in_frame, jnp.sin(angle) * sign, 0.0)


def prepare(row, places, noise, ada, biases):
    return pl.pallas_call(
        prepare_kernel,
        out_shape=[
            shape((FPD, WIDE), F32),
            shape((FPD, HC)),
            shape((TOK, HC), F32),
            shape((TOK, HC), F32),
            shape((16, 2 * HC), F32),
        ],
        grid_spec=pltpu.PrefetchScalarGridSpec(
            num_scalar_prefetch=2,
            grid=(1,),
            in_specs=[whole((FPD, D)), whole((HC, 6 * D))]
            + [whole((1, b.shape[0])) for b in biases],
            out_specs=[
                whole((FPD, WIDE)),
                whole((FPD, HC)),
                whole((TOK, HC)),
                whole((TOK, HC)),
                whole((16, 2 * HC)),
            ],
        ),
        compiler_params=params(24),
        cost_estimate=cost(2 * 8 * HC * 6 * D, 4 * MB, 4 * TOK * HC),
        name="prepare",
    )(row, places, noise, ada, *[b[None] for b in biases])


def split_heads_kernel(row_ref, q, k, v, p0, p1, p23):
    for j, p in enumerate((p0, p1, p23.at[0], p23.at[1])):

        @pl.when(pl.program_id(0) == j)
        def _():
            p[:, :HC] = q[...]
            p[:, HC : 2 * HC] = k[...]
            p[:, 2 * HC :] = v[...]


def split_heads(row, weight):
    piece = (HC, 3 * HC)
    return pl.pallas_call(
        split_heads_kernel,
        out_shape=[shape(piece), shape(piece), shape((2,) + piece)],
        grid_spec=pltpu.PrefetchScalarGridSpec(
            num_scalar_prefetch=1,
            grid=(4,),
            in_specs=[
                pl.BlockSpec((HC, HC), lambda j, row, s=s: (0, 4 * s + (row[0] ^ j)))
                for s in range(3)
            ],
            out_specs=[whole(piece), whole(piece), whole((2,) + piece)],
        ),
        compiler_params=params(12),
        cost_estimate=cost(0, 3 * MB),
        name="split_heads",
    )(row, weight, weight, weight)


def cosines(cp, sp, frames, at):
    both = frames[pl.ds(at, 1), :]
    return cp[...] + both[:, :HC], sp[...] + both[:, HC:]


def project_kernel(own, row_ref, x0, x1, x2, x3, table, mods, w0, w1, w2, w3, cp, sp, fr, *outs):
    row = row_ref[0]
    f = pl.program_id(0)
    if own:
        h_ref, q_ref, k_ref, v_ref = outs
        first, at, angle = 0, f, f
    else:
        k_ref, v_ref, h_ref = outs
        first, at, angle = HC, f + FPD - PREV, f + FPD
    x = jnp.concatenate([r[0] for r in (x0, x1, x2, x3)], axis=0).astype(F32)
    normal, _ = norm(x)
    shift_row = mods[pl.ds(at, 1), :D]
    scale_row = mods[pl.ds(at, 1), D : 2 * D]
    hidden = (normal * (1.0 + scale_row) + shift_row).astype(BF16)
    where = (0,) if own else ()
    h_ref[where + (slice(None), slice(None))] = hidden
    low, high = table[pl.ds(row, 1), QB : QB + 2 * HC], table[pl.ds(row + 4, 1), QB : QB + HC]
    total = jnp.concatenate([low, high], axis=1)[:, first:]
    for j, w in enumerate((w0, w1, w2, w3)):
        total = total + nn(h_ref[where + (slice(None), columns(row, j))], w[:, first:])
    cosine, sine = cosines(cp, sp, fr, angle)
    if own:
        q_ref[0] = (turn(total[:, :HC], cosine, sine).astype(BF16).astype(F32) * 0.125).astype(BF16)
        total = total[:, HC:]
    k_ref[0] = turn(total[:, :HC], cosine, sine).astype(BF16)
    v_ref[0] = total[:, HC:].astype(BF16)


def project(own, row, xs, table, mods, weights, tables):
    frames = xs[0].shape[0]
    x_spec = pl.BlockSpec((1, PR, D), lambda f, *_: (f, 0, 0))
    out_spec = pl.BlockSpec((1, TOK, HC), lambda f, *_: (f, 0, 0))
    out = shape((frames, TOK, HC))
    if own:
        out_specs = [pl.BlockSpec((1, TOK, D), lambda f, *_: (f, 0, 0)), out_spec, out_spec, out_spec]
        out_shape = [shape((frames, TOK, D)), out, out, out]
        scratch = []
    else:
        out_specs = [out_spec, out_spec]
        out_shape = [out, out]
        scratch = [pltpu.VMEM((TOK, D), BF16)]
    return pl.pallas_call(
        lambda *refs: project_kernel(own, *refs),
        out_shape=out_shape,
        grid_spec=pltpu.PrefetchScalarGridSpec(
            num_scalar_prefetch=1,
            grid=(frames,),
            in_specs=[x_spec] * 4
            + [whole((FPD, WIDE)), whole(mods.shape)]
            + [whole((HC, 3 * HC))] * 4
            + [whole((TOK, HC)), whole((TOK, HC)), whole((16, 2 * HC))],
            out_specs=out_specs,
            scratch_shapes=scratch,
        ),
        compiler_params=params(20),
        cost_estimate=cost(2 * frames * TOK * D * 3 * HC, frames * TOK * D * 4 + 4 * MB),
        name="project_own" if own else "project_prev",
    )(row, *xs, table, mods, *weights, *tables)


def head_lanes():
    return lax.broadcasted_iota(jnp.int32, (TOK, HC), 1) // HD


def attend_kernel(pos_ref, q, k, v, kp, vp, o0, o1, o23, lse, qs, scores, acc, top, low):
    f = pl.program_id(0)
    place = pos_ref[f]
    lanes = head_lanes()
    query = q[0]
    for h in range(4):
        qs[pl.ds(h * TOK, TOK), :] = jnp.where(lanes == h, query, jnp.zeros_like(query))
    top[...] = jnp.full_like(top, -1e30)
    low[...] = jnp.zeros_like(low)
    acc[...] = jnp.zeros_like(acc)
    before = jnp.maximum(place - f, 0)
    start = jnp.maximum(f - place, 0)

    def score(keys, slot):
        for h in range(4):
            rows = pl.ds(h * TOK, TOK)
            s = nt(qs[rows, :], keys)
            scores[slot, rows, :] = s
            top[rows, :] = jnp.maximum(top[rows, :], jnp.maximum(s[:, :128], s[:, 128:]))

    def mix(values, slot):
        for h in range(4):
            rows = pl.ds(h * TOK, TOK)
            p = jnp.exp(scores[slot, rows, :] - jnp.concatenate([top[rows, :]] * 2, axis=1))
            low[rows, :] = low[rows, :] + (p[:, :128] + p[:, 128:])
            acc[rows, :] = acc[rows, :] + nn(p.astype(BF16), values)

    def run(step):
        def prev(i, _):
            at = PREV - before + i
            step(kp[at] if step is score else vp[at], i)
            return 0

        def own(g, _):
            step(k[g] if step is score else v[g], g - f + place)
            return 0

        lax.fori_loop(0, before, prev, 0)
        lax.fori_loop(start, f + 1, own, 0)

    run(score)
    for h in range(4):
        rows = pl.ds(h * TOK, TOK)
        top[rows, :] = jnp.broadcast_to(jnp.max(top[rows, :], axis=1, keepdims=True), (TOK, 128))
    run(mix)
    result = jnp.zeros((TOK, HC), F32)
    logs = jnp.zeros((TOK, 128), F32)
    narrow = lax.broadcasted_iota(jnp.int32, (TOK, 128), 1)
    for h in range(4):
        rows = pl.ds(h * TOK, TOK)
        total = jnp.sum(low[rows, :], axis=1, keepdims=True)
        result = jnp.where(lanes == h, acc[rows, :] / total, result)
        logs = jnp.where(narrow == h, top[rows, :] + jnp.log(total), logs)
    lse[0] = logs.T[:8]
    result = result.astype(BF16)
    o0[0] = result[:PR]
    o1[0] = result[PR : 2 * PR]
    o23[0, 0] = result[2 * PR : 3 * PR]
    o23[1, 0] = result[3 * PR :]


def attend(places, q, k, v, kp, vp):
    block = pl.BlockSpec((1, TOK, HC), lambda f, *_: (f, 0, 0))
    piece = pl.BlockSpec((1, PR, HC), lambda f, *_: (f, 0, 0))
    return pl.pallas_call(
        attend_kernel,
        out_shape=[shape((FPD, PR, HC))] * 2
        + [shape((2, FPD, PR, HC)), shape((FPD, 8, TOK), F32)],
        grid_spec=pltpu.PrefetchScalarGridSpec(
            num_scalar_prefetch=1,
            grid=(FPD,),
            in_specs=[block]
            + [whole((FPD, TOK, HC))] * 2
            + [whole((PREV, TOK, HC))] * 2,
            out_specs=[piece] * 2
            + [
                pl.BlockSpec((2, 1, PR, HC), lambda f, *_: (0, f, 0, 0)),
                pl.BlockSpec((1, 8, TOK), lambda f, *_: (f, 0, 0)),
            ],
            scratch_shapes=[
                pltpu.VMEM((4 * TOK, HC), BF16),
                pltpu.VMEM((8, 4 * TOK, TOK), F32),
                pltpu.VMEM((4 * TOK, HC), F32),
                pltpu.VMEM((4 * TOK, 128), F32),
                pltpu.VMEM((4 * TOK, 128), F32),
            ],
        ),
        compiler_params=params(58),
        cost_estimate=cost(36 * 4 * 2 * 2 * TOK**3, 6 * MB, 36 * 4 * TOK * TOK),
        name="attend",
    )(places, q, k, v, kp, vp)


def attend_back_kernel(own, pos_ref, q, k, v, g0, g1, g2, g3, o0, o1, o23, lse, *rest):
    if own:
        cp, sp, fr, before_ref, dq, dk, dv, qs, gs, ks, pl_scr, dl_scr, ds_scr, dq_acc = rest
        dk_acc, dv_acc = dk, dv
    else:
        dq, both_ref, qs, gs, ks, pl_scr, dl_scr, ds_scr, dq_acc, dk_acc, dv_acc = rest
    f = pl.program_id(0)
    place = pos_ref[f]
    lanes = head_lanes()

    @pl.when(f == 0)
    def _():
        for ref in (dk_acc, dv_acc):
            ref[...] = jnp.zeros_like(ref)

    def prelude():
        query = q[0]
        grad = jnp.concatenate([r[0] for r in (g0, g1, g2, g3)], axis=0)
        mixed = jnp.concatenate([o0[0], o1[0], o23[0, 0], o23[1, 0]], axis=0)
        for h in range(4):
            rows = pl.ds(h * TOK, TOK)
            qs[rows, :] = jnp.where(lanes == h, query, jnp.zeros_like(query))
            gs[rows, :] = jnp.where(lanes == h, grad, jnp.zeros_like(grad))
        both = grad.astype(F32) * mixed.astype(F32)
        pick = (
            lax.broadcasted_iota(jnp.int32, (8, HC), 1) // HD
            == lax.broadcasted_iota(jnp.int32, (8, HC), 0)
        ).astype(F32)
        return lax.dot_general(
            pick, both, (((1,), (1,)), ((), ())),
            preferred_element_type=F32, precision=lax.Precision.HIGHEST,
        )

    def step(delta, logs, at):
        keys, values = k[at], v[at]
        for h in range(4):
            rows = pl.ds(h * TOK, TOK)
            ks[rows, :] = jnp.where(lanes == h, keys, jnp.zeros_like(keys))
            p = jnp.exp(nt(keys, qs[rows, :]) - logs[h : h + 1])
            ds = (p * (nt(values, gs[rows, :]) - delta[h : h + 1])).astype(BF16)
            pl_scr[:, rows] = p.astype(BF16)
            dl_scr[:, rows] = ds
            ds_scr[rows, :] = ds
        dv_acc[at] = dv_acc[at] + nn(pl_scr[...], gs[...])
        dk_acc[at] = dk_acc[at] + nn(dl_scr[...], qs[...])
        dq_acc[...] = dq_acc[...] + tn(ds_scr[...], ks[...])

    def sweep(low, high):
        delta = prelude()
        logs = lse[0]
        dq_acc[...] = jnp.zeros_like(dq_acc)

        def one(at, _):
            step(delta, logs, at)
            return 0

        lax.fori_loop(low, high, one, 0)

    if own:
        sweep(jnp.maximum(f - place, 0), f + 1)
        cosine, sine = cosines(cp, sp, fr, f)
        dq[0] = turn((dq_acc[...] + before_ref[0]) * 0.125, cosine, -sine).astype(BF16)
    else:
        count = jnp.maximum(place - f, 0)

        @pl.when(count > 0)
        def _():
            sweep(PREV - count, PREV)
            dq[0] = dq_acc[...]

        @pl.when(count == 0)
        def _():
            dq[0] = jnp.zeros_like(dq_acc)

        @pl.when(f == FPD - 1)
        def _():
            both_ref[0] = dk_acc[...].astype(BF16)
            both_ref[1] = dv_acc[...].astype(BF16)


def attend_back(own, places, q, k, v, grads, mixed, lse, tables=None, before=None):
    block = pl.BlockSpec((1, TOK, HC), lambda f, *_: (f, 0, 0))
    piece = pl.BlockSpec((1, PR, HC), lambda f, *_: (f, 0, 0))
    count = FPD if own else PREV
    wide = pltpu.VMEM((4 * TOK, HC), BF16)
    tall = pltpu.VMEM((TOK, 4 * TOK), BF16)
    scratch = [wide, wide, wide, tall, tall, wide, pltpu.VMEM((TOK, HC), F32)]
    specs = []
    extra = ()
    if own:
        specs = [whole((TOK, HC)), whole((TOK, HC)), whole((16, 2 * HC)), block]
        extra = tuple(tables) + (before,)
    else:
        scratch += [pltpu.VMEM((PREV, TOK, HC), F32)] * 2
    return pl.pallas_call(
        lambda *refs: attend_back_kernel(own, *refs),
        out_shape=[shape((FPD, TOK, HC), BF16 if own else F32)]
        + ([shape((FPD, TOK, HC), F32)] * 2 if own else [shape((2, PREV, TOK, HC))]),
        grid_spec=pltpu.PrefetchScalarGridSpec(
            num_scalar_prefetch=1,
            grid=(FPD,),
            in_specs=[block]
            + [whole((count, TOK, HC))] * 2
            + [piece] * 6
            + [pl.BlockSpec((2, 1, PR, HC), lambda f, *_: (0, f, 0, 0))]
            + [pl.BlockSpec((1, 8, TOK), lambda f, *_: (f, 0, 0))]
            + specs,
            out_specs=[block]
            + ([whole((FPD, TOK, HC))] * 2 if own else [whole((2, PREV, TOK, HC))]),
            scratch_shapes=scratch,
        ),
        compiler_params=params(58),
        cost_estimate=cost(1000 if own else 12 * 4 * 5 * 2 * TOK**3, 1000 if own else 12 * MB),
        name="attend_back_own" if own else "attend_back_prev",
    )(places, q, k, v, *grads, *mixed, lse, *extra)


HALF = 4
RAW = HALF * PR


def flat(ref):
    return ref[...].reshape(RAW, ref.shape[-1])


def frames_of(value):
    return value.reshape(HALF, PR, value.shape[-1])


def segment(table, s):
    both = table[:, s * D : (s + 1) * D]
    return jnp.where(pl.program_id(0) == 0, both[:HALF], both[HALF:])[:, None, :]


def fold(out, start, width, row):
    @pl.when(pl.program_id(0) == 0)
    def _():
        out[:, start : start + width] = jnp.zeros((8, width), F32)

    for i in range(8):
        at = (slice(i, i + 1), slice(start, start + width))
        out[at] = out[at] + row[:, i * width : (i + 1) * width]


def mid_kernel(o0, o1, o2, o3, w0, w1, w2, w3, table, x, cot, branch, middle, hidden, down, dsum):
    total = unfold(table, OB, 128)
    for o, w in zip((o0, o1, o2, o3), (w0, w1, w2, w3)):
        total = total + nn(flat(o), w[...])
    branched = frames_of(total)
    branch[...] = branched
    mid_value = x[...].astype(F32) + segment(table, 2) * branched
    middle[...] = mid_value
    normal, _ = norm(mid_value)
    hidden[...] = (normal * (1.0 + segment(table, 4)) + segment(table, 3)).astype(BF16)
    grad = (segment(table, 5) * cot[...].astype(F32)).astype(BF16)
    down[...] = grad
    fold(dsum, 0, 128, jnp.sum(grad.astype(F32).reshape(RAW, D), axis=0, keepdims=True))


def half_spec(width):
    return pl.BlockSpec((HALF, PR, width), lambda i, *_: (i, 0, 0))


def mid(pieces, weights, table, x, cot):
    return pl.pallas_call(
        mid_kernel,
        out_shape=[
            shape((FPD, PR, D), F32),
            shape((FPD, PR, D), F32),
            shape((FPD, PR, D)),
            shape((FPD, PR, D)),
            shape((8, 128), F32),
        ],
        grid=(FPD // HALF,),
        in_specs=[half_spec(HC)] * 4
        + [whole((HC, D))] * 4
        + [whole((FPD, WIDE)), half_spec(D), half_spec(D)],
        out_specs=[half_spec(D)] * 4 + [whole((8, 128))],
        compiler_params=params(26),
        cost_estimate=cost(2 * 512 * D * D, 12 * MB),
        name="mid",
    )(*pieces, *weights, table, x, cot)


def mid_back_kernel(
    hg, middle, branch, cot, table, w0, w1, w2, w3, usum, dsum, mg, bg, a0, a1, a23, sums
):
    grad = hg[...]
    normal, rate = norm(middle[...])
    put_half(sums, D, jnp.sum(grad, axis=1))
    put_half(sums, 2 * D, jnp.sum(grad * normal, axis=1))
    total = cot[...].astype(F32) + norm_back(normal, rate, grad * (1.0 + segment(table, 4)))
    mg[...] = total
    put_half(sums, 0, jnp.sum(total * branch[...], axis=1))
    low = (segment(table, 2) * total).astype(BF16)
    bg[...] = low
    low = low.reshape(RAW, D)
    sums[:, 3 * D : 3 * D + NB] = usum[...]
    sums[:, 3 * D + NB : 3 * D + NB + 128] = dsum[...]
    fold(sums, 3 * D + NB + 128, 128, jnp.sum(low.astype(F32), axis=0, keepdims=True))
    for j, w in enumerate((w0, w1, w2, w3)):
        value = frames_of(nt(low, w[...]).astype(BF16))
        if j < 2:
            (a0, a1)[j][...] = value
        else:
            a23[j - 2] = value


def mid_back(hg, middle, branch, cot, table, weights, usum, dsum):
    return pl.pallas_call(
        mid_back_kernel,
        out_shape=[shape((FPD, PR, D), F32), shape((FPD, PR, D))]
        + [shape((FPD, PR, HC))] * 2
        + [shape((2, FPD, PR, HC)), shape((8, EARLY), F32)],
        grid=(FPD // HALF,),
        in_specs=[half_spec(D)] * 4
        + [whole((FPD, WIDE))]
        + [whole((HC, D))] * 4
        + [whole((8, NB)), whole((8, 128))],
        out_specs=[half_spec(D)] * 2
        + [half_spec(HC)] * 2
        + [pl.BlockSpec((2, HALF, PR, HC), lambda i: (0, i, 0, 0)), whole((8, EARLY))],
        compiler_params=params(26),
        cost_estimate=cost(2 * 512 * D * D, 12 * MB),
        name="mid_back",
    )(hg, middle, branch, cot, table, *weights, usum, dsum)


NB = 512
STEPS = FF // NB
PER = D // NB
TOKENS = FPD * PR


def block_of(t):
    phase = t // PER
    return ((phase % 2) * 2) ^ (phase // 2)


def up_column(t, row):
    return (row ^ block_of(t)) * PER + t % PER


def down_row(t):
    return block_of(t) * PER + t % PER


def down_spec(j):
    phase = (0, 2, 1, 3)[j]
    return pl.BlockSpec((NB, D), lambda t, row: (jnp.clip(t - phase * PER, 0, PER - 1), 0))


def pick_down(d0, d1, d2, d3):
    phase = pl.program_id(0) // PER
    return jnp.where(
        phase < 2,
        jnp.where(phase == 0, d0[...], d2[...]),
        jnp.where(phase == 2, d1[...], d3[...]),
    )


def feed_kernel(row_ref, h2, dg, u0, u1, u2, u3, table, d0, d1, d2, d3, act, upg, hg, usum):
    row = row_ref[0]
    ups = (u0, u1, u2, u3)
    down = pick_down(d0, d1, d2, d3)
    at = pl.ds(up_column(pl.program_id(0), row), 1)
    u = table[at, UB : UB + NB]
    for j, w in enumerate(ups):
        u = u + nn(h2[:, columns(row, j)], w[...])
    rate = math.sqrt(2.0 / math.pi)
    square = u * u
    half = 0.5 + 0.5 * jnp.tanh(u * (rate + (rate * 0.044715) * square))
    active = u * half
    act[...] = active.astype(BF16)
    slope = half + active * (1.0 - half) * (2.0 * rate + (6.0 * rate * 0.044715) * square)
    grad = (nt(dg[...], down) * slope).astype(BF16)
    upg[...] = grad
    put(usum, 0, up_column(pl.program_id(0), row), jnp.sum(grad.astype(F32), axis=0, keepdims=True))

    @pl.when(pl.program_id(0) == 0)
    def _():
        hg[...] = jnp.zeros_like(hg)

    for j, w in enumerate(ups):
        hg[:, columns(row, j)] = hg[:, columns(row, j)] + nt(grad, w[...])


def feed(row, h2, dg, ups, table, downs):
    tok = whole((TOKENS, D))
    block = pl.BlockSpec((TOKENS, NB), lambda t, row: (0, t))
    return pl.pallas_call(
        feed_kernel,
        out_shape=[
            shape((TOKENS, FF)),
            shape((TOKENS, FF)),
            shape((TOKENS, D), F32),
            shape((8, NB), F32),
        ],
        grid_spec=pltpu.PrefetchScalarGridSpec(
            num_scalar_prefetch=1,
            grid=(STEPS,),
            in_specs=[tok, tok]
            + [pl.BlockSpec((HC, NB), lambda t, row: (0, up_column(t, row[0])))] * 4
            + [whole((FPD, WIDE))]
            + [down_spec(j) for j in range(4)],
            out_specs=[block, block, tok, whole((8, NB))],
        ),
        compiler_params=params(58),
        cost_estimate=cost(3 * 2 * TOKENS * D * FF, 30 * MB, TOKENS * FF),
        name="feed",
    )(row, h2, dg, *ups, table, *downs)


def down_step(da, db, dg, act, part, dn):
    g = pl.program_id(0)
    down = jnp.where(g < PER, da[...], db[...])
    active = act[...]
    dn[...] = dn[...] + nn(active, down)
    part[0] = tn(active, dg[...]).astype(BF16)


def down_send_kernel(dg, act, da, db, part, dn):
    @pl.when(pl.program_id(0) == 0)
    def _():
        dn[...] = jnp.zeros_like(dn)

    down_step(da, db, dg, act, part, dn)


def down_keep_kernel(dg, act, da, db, before, table, middle, cot, part, out, gate, dn):
    @pl.when(pl.program_id(0) == 0)
    def _():
        dn[...] = before[...]

    down_step(da, db, dg, act, part, dn)

    @pl.when(pl.program_id(0) == STEPS // 2 - 1)
    def _():
        bias = unfold(table, DB, 128)
        for f in range(FPD):
            rows = slice(f * PR, (f + 1) * PR)
            value = dn[rows, :] + bias
            out[f] = (middle[f] + table[f : f + 1, 5 * D : 6 * D] * value).astype(BF16)
            gate[f : f + 1, :] = jnp.sum(cot[f].astype(F32) * value, axis=0, keepdims=True)


def down_half(first, dg, act, downs, extra=()):
    tok = whole((TOKENS, D))
    full = whole((FPD, PR, D))
    half = STEPS // 2
    weight = lambda k: pl.BlockSpec((NB, D), lambda g: (jnp.clip(g - k * PER, 0, PER - 1), 0))
    start = half if first else 0
    part = pl.BlockSpec((1, NB, D), lambda g: (g // PER, g % PER, 0))
    out_specs, out_shape, scratch, specs = [part], [shape((2, D, D))], [], []
    if first:
        out_specs += [tok]
        out_shape += [shape((TOKENS, D), F32)]
    else:
        specs = [tok, whole((FPD, WIDE)), full, full]
        out_specs += [full, whole((8, D))]
        out_shape += [shape((FPD, PR, D)), shape((8, D), F32)]
        scratch = [pltpu.VMEM((TOKENS, D), F32)]
    return pl.pallas_call(
        down_send_kernel if first else down_keep_kernel,
        out_shape=out_shape,
        grid=(half,),
        in_specs=[tok, pl.BlockSpec((TOKENS, NB), lambda g: (0, g + start)), weight(0), weight(1)]
        + specs,
        out_specs=out_specs,
        scratch_shapes=scratch,
        compiler_params=params(40),
        cost_estimate=cost(2 * TOKENS * D * FF, 14 * MB),
        name="down_weight_send" if first else "down_weight_keep",
    )(dg, act, *downs, *extra)


def up_weight_kernel(row_ref, h2, upg, uk, us):
    row = row_ref[0]
    grad = upg[...]
    for j, ref in enumerate((uk, us, uk, us)):
        ref[j // 2, 0] = tn(h2[:, columns(row, j)], grad).astype(BF16)


def up_weight_grad(row, h2, upg):
    up_out = pl.BlockSpec(
        (2, 1, HC, NB),
        lambda t, row: (0, up_column(t, row[0]) // PER, 0, up_column(t, row[0]) % PER),
    )
    return pl.pallas_call(
        up_weight_kernel,
        out_shape=[shape((2, 4, HC, D))] * 2,
        grid_spec=pltpu.PrefetchScalarGridSpec(
            num_scalar_prefetch=1,
            grid=(STEPS,),
            in_specs=[whole((TOKENS, D)), pl.BlockSpec((TOKENS, NB), lambda t, row: (0, t))],
            out_specs=[up_out, up_out],
        ),
        compiler_params=params(58),
        cost_estimate=cost(2 * TOKENS * D * FF, 14 * MB),
        name="up_weight_grad",
    )(row, h2, upg)


def out_weight_kernel(t0, t1, t2, t3, bg, keep, send):
    grad = bg[...].reshape(TOKENS, D)
    for j, t in enumerate((t0, t1, t2, t3)):
        ref = (keep, send)[j % 2]
        ref[j // 2] = tn(t[...].reshape(TOKENS, HC), grad).astype(BF16)


def out_weight_grad(pieces, bg):
    return pl.pallas_call(
        out_weight_kernel,
        out_shape=[shape((2, HC, D))] * 2,
        grid=(1,),
        in_specs=[whole((FPD, PR, HC))] * 4 + [whole((FPD, PR, D))],
        out_specs=[whole((2, HC, D))] * 2,
        compiler_params=params(14),
        cost_estimate=cost(2 * TOKENS * D * D, 4 * MB),
        name="out_weight_grad",
    )(*pieces, bg)


CHUNKS = 16
UP_ROWS, OUT_ROWS, DOWN_ROWS = D // CHUNKS, HC // CHUNKS, D // CHUNKS
FIRST = UP_ROWS + OUT_ROWS
ROWS = FIRST + DOWN_ROWS


def core_sum_kernel(ua, ub, da, db, oa, ob, out):
    def both(a, b):
        return (a.astype(F32) + b.astype(F32)).astype(BF16)

    for c in range(4):
        at = c * ROWS
        low, high = c * OUT_ROWS, (c + 1) * OUT_ROWS
        for i in range(4):
            to = at + i * OUT_ROWS
            out[0, to : to + OUT_ROWS] = both(ua[0, i, low:high], ub[0, i, low:high])
        out[0, at + UP_ROWS : at + FIRST] = both(oa[0, low:high], ob[0, low:high])
        low, high = c * DOWN_ROWS, (c + 1) * DOWN_ROWS
        out[0, at + FIRST : at + ROWS] = both(da[0, low:high], db[0, low:high])


def core_sum(up, down, out):
    ups = pl.BlockSpec((1, 4, 4 * OUT_ROWS, D), lambda j, c: (j, 0, c, 0))
    outs = pl.BlockSpec((1, 4 * OUT_ROWS, D), lambda j, c: (j, c, 0))
    downs = pl.BlockSpec((1, 4 * DOWN_ROWS, D), lambda j, c: (j, c, 0))
    return pl.pallas_call(
        core_sum_kernel,
        out_shape=shape((2, CHUNKS * ROWS, D)),
        grid=(2, CHUNKS // 4),
        in_specs=[ups, ups, downs, downs, outs, outs],
        out_specs=pl.BlockSpec((1, 4 * ROWS, D), lambda j, c: (j, c, 0)),
        compiler_params=params(58),
        cost_estimate=cost(1000, 1000),
        name="core_sum",
    )(*up, *down, *out)


def unpack_kernel(total, up, out, down):
    for k in range(4):
        at = k * ROWS
        for i in range(4):
            rows = slice(at + i * OUT_ROWS, at + (i + 1) * OUT_ROWS)
            up[k * OUT_ROWS : (k + 1) * OUT_ROWS, i * D : (i + 1) * D] = total[rows].astype(F32)
        out[k * OUT_ROWS : (k + 1) * OUT_ROWS] = total[at + UP_ROWS : at + FIRST].astype(F32)
        down[k * DOWN_ROWS : (k + 1) * DOWN_ROWS] = total[at + FIRST : at + ROWS].astype(F32)


def unpack(total):
    block = lambda i: (i, 0)
    return pl.pallas_call(
        unpack_kernel,
        out_shape=[shape((HC, FF), F32), shape((HC, D), F32), shape((D, D), F32)],
        grid=(4,),
        in_specs=[pl.BlockSpec((4 * ROWS, D), block)],
        out_specs=[
            pl.BlockSpec((4 * OUT_ROWS, FF), block),
            pl.BlockSpec((4 * OUT_ROWS, D), block),
            pl.BlockSpec((4 * DOWN_ROWS, D), block),
        ],
        compiler_params=params(24),
        cost_estimate=cost(0, 14 * MB),
        name="unpack",
    )(total)


LATE = 3 * D + 2 * HC
EARLY = 3 * D + NB + 256


def arrange_kernel(row_ref, a0, a1, a2, a3, late, far, out):
    row = row_ref[0]
    for j, a in enumerate((a0, a1, a2, a3)):
        for s in range(3):
            lanes = pl.ds(pl.multiple_of(s * D + (row ^ j) * HC, HC), HC)
            out[:, lanes] = a[:, s * HC : (s + 1) * HC]
    both = jnp.concatenate([late[...].astype(F32), far[...].astype(F32)], axis=0)
    out[:, 3 * D :] = both.astype(BF16)


def arrange(row, pieces, late, far):
    rows = pieces[0].shape[0]
    return pl.pallas_call(
        arrange_kernel,
        out_shape=shape((rows, 3 * D + LATE)),
        grid_spec=pltpu.PrefetchScalarGridSpec(
            num_scalar_prefetch=1,
            grid=(1,),
            in_specs=[whole((rows, 3 * HC))] * 4 + [whole((8, LATE))] * 2,
            out_specs=whole((rows, 3 * D + LATE)),
        ),
        compiler_params=params(16),
        cost_estimate=cost(0, 8 * rows * D),
        name="arrange",
    )(row, *pieces, late, far)


def stack_kernel(a0, a1, a2, a3, weights, sums):
    for k, a in enumerate((a0, a1, a2, a3)):
        weights[k] = a[:, : 3 * D]
        sums[k] = a[:, 3 * D :]


def stack(pieces):
    rows, width = pieces[0].shape
    return pl.pallas_call(
        stack_kernel,
        out_shape=[shape((4, rows, 3 * D)), shape((4, rows, LATE))],
        grid=(1,),
        in_specs=[whole((rows, width))] * 4,
        out_specs=[whole((4, rows, 3 * D)), whole((4, rows, LATE))],
        compiler_params=params(16),
        cost_estimate=cost(0, 2 * MB),
        name="stack",
    )(*pieces)


def place_kernel(index_ref, low, high, out):
    for m, a in enumerate((low.at[0], low.at[1], high.at[1], high.at[0])):

        @pl.when(pl.program_id(0) == m)
        def _():
            for k in range(4):
                out[0, index_ref[1] ^ k] = a[k].astype(F32)


def place(index, low, high):
    rows = low.shape[2]
    return pl.pallas_call(
        place_kernel,
        out_shape=shape((4, 4, rows, 3 * D), F32),
        grid_spec=pltpu.PrefetchScalarGridSpec(
            num_scalar_prefetch=1,
            grid=(4,),
            in_specs=[whole(low.shape)] * 2,
            out_specs=pl.BlockSpec((1, 4, rows, 3 * D), lambda i, index: (index[0] ^ i, 0, 0, 0)),
        ),
        compiler_params=params(24),
        cost_estimate=cost(0, 24 * rows * D),
        name="place",
    )(index, low, high).reshape(HC, 3 * D)


def project_back_kernel(row_ref, dq, dk, dv, rk, rv, w0, w1, w2, w3, cp, sp, fr, dp, h0, h2, hs, bsum):
    row = row_ref[0]
    f = pl.program_id(0)
    later = (f > 0).astype(F32)
    keys = dk[0] + later * rk[0, 0].astype(F32)
    values = dv[0] + later * rv[0, 0].astype(F32)
    cosine, sine = cosines(cp, sp, fr, f)
    dp[0, :, :HC] = dq[0]
    dp[0, :, HC : 2 * HC] = turn(keys, cosine, -sine).astype(BF16)
    dp[0, :, 2 * HC :] = values.astype(BF16)
    grad = dp[0]
    sums = jnp.sum(grad.astype(F32), axis=0, keepdims=True)

    @pl.when(f == 0)
    def _():
        bsum[...] = jnp.zeros_like(bsum)

    number = lax.broadcasted_iota(jnp.int32, (8, 2 * HC), 0)
    bsum[...] = bsum[...] + jnp.where(number == row, sums[:, : 2 * HC], 0.0)
    bsum[:, :HC] = bsum[:, :HC] + jnp.where(number[:, :HC] == row + 4, sums[:, 2 * HC :], 0.0)
    for j, w in enumerate((w0, w1, w2, w3)):
        part = nt(grad, w[...]).astype(BF16)
        at = (0, slice(None), columns(row, j))
        h0[at] = part[:PR]
        hs[(0,) + at] = part[PR : 2 * PR]
        h2[at] = part[2 * PR : 3 * PR]
        hs[(1,) + at] = part[3 * PR :]


def project_back(row, dq, dk, dv, returned, weights, tables):
    block = pl.BlockSpec((1, TOK, HC), lambda f, *_: (f, 0, 0))
    late = [
        pl.BlockSpec((1, 1, TOK, HC), lambda f, *_, i=i: (i, jnp.maximum(f - 1, 0), 0, 0))
        for i in range(2)
    ]
    piece = pl.BlockSpec((1, PR, D), lambda f, *_: (f, 0, 0))
    return pl.pallas_call(
        project_back_kernel,
        out_shape=[
            shape((FPD, TOK, 3 * HC)),
            shape((FPD, PR, D)),
            shape((FPD, PR, D)),
            shape((2, FPD, PR, D)),
            shape((8, 2 * HC), F32),
        ],
        grid_spec=pltpu.PrefetchScalarGridSpec(
            num_scalar_prefetch=1,
            grid=(FPD,),
            in_specs=[block] * 3
            + late
            + [whole((HC, 3 * HC))] * 4
            + [whole((TOK, HC)), whole((TOK, HC)), whole((16, 2 * HC))],
            out_specs=[
                pl.BlockSpec((1, TOK, 3 * HC), lambda f, *_: (f, 0, 0)),
                piece,
                piece,
                pl.BlockSpec((2, 1, PR, D), lambda f, *_: (0, f, 0, 0)),
                whole((8, 2 * HC)),
            ],
        ),
        compiler_params=params(20),
        cost_estimate=cost(2 * FPD * TOK * D * 3 * HC, 14 * MB),
        name="project_back",
    )(row, dq, dk, dv, returned, returned, *weights, *tables)


def weight_kernel(row_ref, h, dp, w):
    w[0] = tn(h[...], dp[...]).astype(BF16)


def project_weight(row, hidden, dproj):
    tokens = FPD * TOK
    return pl.pallas_call(
        weight_kernel,
        out_shape=shape((4, HC, 3 * HC)),
        grid_spec=pltpu.PrefetchScalarGridSpec(
            num_scalar_prefetch=1,
            grid=(4,),
            in_specs=[
                pl.BlockSpec((tokens, HC), lambda j, row: (0, row[0] ^ j)),
                whole((tokens, 3 * HC)),
            ],
            out_specs=pl.BlockSpec((1, HC, 3 * HC), lambda j, row: (j, 0, 0)),
        ),
        compiler_params=params(20),
        cost_estimate=cost(2 * tokens * D * 3 * HC, 9 * MB),
        name="project_weight",
    )(row, hidden.reshape(tokens, D), dproj.reshape(tokens, 3 * HC))


def input_back_kernel(x, h0, near, far, table, mg, bsum, gate, out, sums):
    grad = h0[...].astype(F32) + near[0].astype(F32) + far[...].astype(F32)
    normal, rate = norm(x[...].astype(F32))
    put_half(sums, 0, jnp.sum(grad, axis=1))
    put_half(sums, D, jnp.sum(grad * normal, axis=1))
    sums[:, 2 * D : 3 * D] = gate[...]
    sums[:, 3 * D :] = bsum[...]
    out[...] = mg[...] + norm_back(normal, rate, grad * (1.0 + segment(table, 1)))


def input_back(x, h0, near, far, table, mg, bsum, gate):
    return pl.pallas_call(
        input_back_kernel,
        out_shape=[shape((FPD, PR, D), F32), shape((8, LATE), F32)],
        grid=(FPD // HALF,),
        in_specs=[half_spec(D)] * 2
        + [pl.BlockSpec((1, HALF, PR, D), lambda i: (0, i, 0, 0))]
        + [half_spec(D), whole((FPD, WIDE)), half_spec(D), whole((8, 2 * HC)), whole((8, D))],
        out_specs=[half_spec(D), whole((8, LATE))],
        compiler_params=params(20),
        cost_estimate=cost(20 * 512 * D, 10 * MB),
        name="input_back",
    )(x, h0, near, far, table, mg, bsum, gate)


def join_kernel(a0, a1, a2, a3, out):
    for k, a in enumerate((a0, a1, a2, a3)):
        out[2 * k : 2 * k + 2] = a[...]


def join(pieces):
    width = pieces[0].shape[-1]
    return pl.pallas_call(
        join_kernel,
        out_shape=shape((8, 8, width)),
        grid=(1,),
        in_specs=[whole((2, 8, width))] * 4,
        out_specs=whole((8, 8, width)),
        compiler_params=params(16),
        cost_estimate=cost(0, 2 * MB),
        name="join",
    )(*pieces)


def final_kernel(row_ref, *refs):
    row = row_ref[0]
    low, high, *early = refs[:6]
    ada, ab, qb, ob, ub, db, asum = refs[6:]
    late = [low.at[0], low.at[1], high.at[0], high.at[1]]
    early = [early[0], early[3], early[1], early[2]]

    def rows(ref, cols):
        value = ref[:, :, cols].astype(F32)
        return value.reshape(64, value.shape[-1])

    left = [rows(s, slice(EARLY, EARLY + HC)).astype(BF16) for s in early]
    for segment in range(6):
        source, start = ((late, 0), (late, 1), (early, 0), (early, 1), (early, 2), (late, 2))[segment]
        cols = slice(start * D, (start + 1) * D)
        product, total = 0.0, 0.0
        for s, ref in zip(left, source):
            right = rows(ref, cols)
            total = total + jnp.sum(right, axis=0, keepdims=True)
            product = product + tn(s, right.astype(BF16))
        at = segment * D
        ada[:, at : at + D] = product
        asum[0:1, at : at + D] = total

    def fold8(value):
        value = jnp.sum(value, axis=0)
        return value if value.shape[0] == 8 else value[:8] + value[8:]

    def bias(source, start, stop):
        return sum(
            fold8(ref[:, :, start:stop].astype(F32)) for ref in source
        )

    ab[...] = asum[0:1, pl.ds(pl.multiple_of(row * 1536, 512), 1536)]
    folded = bias(late, 3 * D, LATE)
    for i in range(3):
        chunk = 3 * row + i
        at = jnp.where(chunk < 4, chunk, chunk - 4)
        second = (chunk >= 4) & (chunk < 8)
        value = jnp.where(second, folded[:, HC:], folded[:, :HC])
        qb[:, i * HC : (i + 1) * HC] = take(value, at)
    folded = bias(early, 3 * D, EARLY)
    for i in range(2):
        at = 2 * row + i
        ub[:, i * NB : (i + 1) * NB] = take(folded[:, :NB], at)
        db[:, i * 128 : (i + 1) * 128] = take(folded[:, NB : NB + 128], at)
        ob[:, i * 128 : (i + 1) * 128] = take(folded[:, NB + 128 :], at)


def final_sums(row, late, early):
    sizes = (1536, 768, 256, 1024, 256)
    return pl.pallas_call(
        final_kernel,
        out_shape=[shape((HC, 6 * D), F32)] + [shape((1, n), F32) for n in sizes],
        grid_spec=pltpu.PrefetchScalarGridSpec(
            num_scalar_prefetch=1,
            grid=(1,),
            in_specs=[whole((2, 4, 16, LATE))] * 2
            + [whole((8, 8, EARLY + HC))] * 4,
            out_specs=[whole((HC, 6 * D))] + [whole((1, n)) for n in sizes],
            scratch_shapes=[pltpu.VMEM((8, 6 * D), F32)],
        ),
        compiler_params=params(28),
        cost_estimate=cost(2 * 256 * HC * 6 * D, 10 * MB),
        name="final_sums",
    )(row, *late, *early)


def row_sum(value):
    value = value + swap(value, CORE)
    return value + swap(value, DIRECT)


def row_pieces(value):
    return [value, swap(value, CORE), swap(value, DIRECT), swap(value, DIRECT ^ CORE)]


def by_row(pieces, row):
    a, b, c, d = pieces
    odd, high = row % 2 == 1, row >= 2
    a, b = jnp.where(odd, b, a), jnp.where(odd, a, b)
    c, d = jnp.where(odd, d, c), jnp.where(odd, c, d)
    return jnp.stack(
        [
            jnp.where(high, c, a),
            jnp.where(high, d, b),
            jnp.where(high, a, c),
            jnp.where(high, b, d),
        ]
    )


def quarter_rows(value, bit, index, axis):
    rows = value.shape[1] // 4
    at = lambda m: lax.dynamic_slice_in_dim(value, (index[axis] ^ m) * rows, rows, 1)
    return [at(0)] + [swap(at(m), bit * m) for m in (1, 2, 3)]


def add_all(parts):
    return sum(part.astype(F32) for part in parts).astype(BF16)


def exchange_rows(value, bit, index, axis):
    return add_all(quarter_rows(value, bit, index, axis))


def turn_heads(own, beside, across, order=lambda piece: piece):
    across = swap(across, DIRECT)
    return [own, swap(beside, CORE), across[0], swap(order(across)[1], CORE)]


def per_device(
    activations,
    noise_embed,
    frame_position,
    cotangent,
    ada_weight,
    ada_bias,
    qkv_weight,
    qkv_bias,
    out_weight,
    out_bias,
    up_weight,
    up_bias,
    down_weight,
    down_bias,
):
    row = lax.axis_index(("xl", "c")).astype(jnp.int32)
    row_arg = row.reshape(1)
    index = [lax.axis_index("y").astype(jnp.int32), lax.axis_index("z").astype(jnp.int32)]
    index_arg = jnp.stack(index)

    x0 = activations
    x2 = swap(x0, DIRECT)
    x1 = swap(x0, CORE)
    p0 = shift(activations[1:], 1)
    biases = (ada_bias, qkv_bias, out_bias, up_bias, down_bias)
    heads = list(split_heads(row_arg, qkv_weight))
    noise, heads[1] = lax.optimization_barrier((noise_embed, heads[1]))
    part, silu_own, *tables = prepare(row_arg, frame_position, noise, ada_weight, biases)
    across = swap(heads[2], OTHER)
    qkv_pieces = [heads[0], swap(heads[1], CORE), across]
    part = part + swap(part, CORE)
    table = part + swap(part, DIRECT)
    x2, p0, table, *qkv_pieces = lax.optimization_barrier((x2, p0, table, *qkv_pieces))

    qkv_pieces = qkv_pieces[:2] + [qkv_pieces[2][0], swap(qkv_pieces[2][1], CORE)]
    x3 = swap(x2, CORE)
    p2 = swap(p0, DIRECT)
    p1 = swap(p0, CORE)
    before_mods = shift(table[:, : 2 * D], 1)

    out_own, up_own, _ = lax.optimization_barrier((out_weight, up_weight, table))
    outs2 = swap(out_own, OTHER)
    ups2 = swap(up_own, OTHER)

    hidden1, q, k, v = project(True, row_arg, (x0, x1, x2, x3), table, table, qkv_pieces, tables)
    p2, down_own, q, before_mods = lax.optimization_barrier((p2, down_weight, q, before_mods))
    p3 = swap(p2, CORE)
    downs2 = swap(down_own, DIRECT)
    kp, vp = project(
        False, row_arg, (p0, p1, p2, p3), table, before_mods, qkv_pieces, tables
    )
    *mixed, lse = attend(frame_position, q, k, v, kp, vp)
    outs2, ups2, downs2, lse = lax.optimization_barrier((outs2, ups2, downs2, lse))
    outs = [out_weight, swap(out_own, CORE), outs2, swap(outs2, CORE)]
    ups = [up_weight, swap(up_own, CORE), ups2, swap(ups2, CORE)]
    downs = [down_weight, swap(down_own, CORE), downs2, swap(downs2, CORE)]
    turned = turn_heads(*mixed)
    branch, middle, hidden2, down_grad, dsum = mid(turned, outs, table, x0, cotangent)
    h2 = hidden2.reshape(TOKENS, D)
    dg = down_grad.reshape(TOKENS, D)
    act, upg, hg, usum = feed(row_arg, h2, dg, ups, table, downs)
    mg, bg, *ag, early = mid_back(
        hg.reshape(FPD, PR, D), middle, branch, cotangent, table, outs, usum, dsum
    )
    late = []
    back = turn_heads(*ag[:2], ag[2], order=lambda piece: late.append(piece) or piece)[:2]

    early = early + swap(early, CORE)
    upg, early, _ = lax.optimization_barrier((upg, early, bg))
    early_far = swap(early, DIRECT)
    uk, us = up_weight_grad(row_arg, h2, upg)
    us = swap(us, CORE)
    dg_later, early_far, uk = lax.optimization_barrier((dg, early_far, uk))
    early = jnp.concatenate([(early + early_far).astype(BF16), silu_own], axis=1)
    early_far = swap(early, FAR)
    ds_part, dn = down_half(True, dg_later, act, (downs[1], downs[3]))
    ds_part_far = swap(ds_part, CORE)
    dn, early, early_far, bg_later, us, far_back, *back = lax.optimization_barrier(
        (dn, early, early_far, bg, us, *late, *back)
    )
    early = jnp.stack([early, early_far])
    early_parts = [early] + [swap(early, m) for m in (16, 32, 48)]
    ok, os = out_weight_grad(turned, bg_later)
    os = swap(os, CORE)
    dk_part, layer_output, gate = down_half(
        False, dg_later, act, (downs[0], downs[2]), (dn, table, middle, cotangent)
    )
    dk_part, early_parts, ds_part_far, os, far_back = lax.optimization_barrier(
        (dk_part, early_parts, ds_part_far, os, far_back)
    )
    back += [far_back[0], swap(far_back[1], CORE)]
    packed = core_sum((uk, us), (dk_part, ds_part_far), (ok, os))
    packed, back = lax.optimization_barrier((packed, back))
    scattered = lax.psum_scatter(packed, ("y", "z"), scatter_dimension=1, tiled=True)

    dq_before, both = attend_back(False, frame_position, q, kp, vp, back, mixed, lse)
    returned = shift(both, -1)
    dq, dk, dv = attend_back(
        True, frame_position, q, k, v, back, mixed, lse, tables, dq_before
    )
    early_parts, dq = lax.optimization_barrier((early_parts, dq))
    early = join(early_parts)
    early_all = [early] + [swap(early, m) for m in (4, 8, 12)]
    dq, early = lax.optimization_barrier((dq, early))
    early = early[0].astype(F32)

    dproj, h0, h2_part, send, bsum = project_back(row_arg, dq, dk, dv, returned, qkv_pieces, tables)
    near = swap(send, CORE)
    qkv_parts = project_weight(row_arg, hidden1, dproj)
    far_part = (h2_part.astype(F32) + near[1].astype(F32)).astype(BF16)
    far = swap(far_part, DIRECT)
    far_part, qkv_parts, *early_all = lax.optimization_barrier((far_part, qkv_parts, *early_all))
    quarters = quarter_rows(qkv_parts, 4, index, 0)
    input_grad, late = input_back(x0, h0, near, far, table, mg, bsum, gate)
    late_near = swap(late, CORE)
    late, *quarters = lax.optimization_barrier((late, *quarters))
    quarters = quarter_rows(add_all(quarters), 16, index, 1)
    late = late + late_near
    late_far = swap(late, DIRECT)
    late, *quarters = lax.optimization_barrier((late, *quarters))
    qkv_parts = add_all(quarters)
    qkv_far = swap(qkv_parts, FAR)
    scattered, late, late_far, qkv_parts = lax.optimization_barrier(
        (scattered, late, late_far, qkv_parts)
    )
    late = late + late_far
    late_low = late.astype(BF16)
    late_far = swap(late_low, FAR)
    share_far = swap(scattered[1], DIRECT)
    late_low, qkv_far = lax.optimization_barrier((late_low, qkv_far))
    qkv_parts = add_all([qkv_parts, qkv_far])
    turned = turn_heads(qkv_parts[0], qkv_parts[1], qkv_parts[2:])
    turned, share_far = lax.optimization_barrier((turned, share_far))
    share = scattered[0].astype(F32) + share_far.astype(F32)
    share_far = swap(share.astype(BF16), FAR)
    last = arrange(row_arg, turned, late_low, late_far)

    share, share_far, last = lax.optimization_barrier((share, share_far, last))
    share = (share + share_far.astype(F32)).astype(BF16)
    totals = lax.all_gather(share, ("y", "z"), axis=0, tiled=True)
    weights, sums_late = stack([last] + [swap(last, m) for m in (16, 32, 48)])
    weights = jnp.stack([weights, swap(weights, 4)])
    sums_late = jnp.stack([sums_late, swap(sums_late, 12)])
    weights_far, sums_far = swap(weights, 12), swap(sums_late, 4)
    up_total, out_total, down_total = unpack(totals)
    qkv_total = place(index_arg, weights, weights_far)

    ada_total, *bias_sums = final_sums(row_arg, (sums_late, sums_far), early_all)
    ada_sum, qkv_sum, out_sum, up_sum, down_sum = [b[0] for b in bias_sums]
    mod_own = jnp.concatenate(
        [late[:, : 2 * D], early[:, : 3 * D], late[:, 2 * D : 3 * D]], axis=1
    ).astype(BF16)
    silu_grad = nt(mod_own, ada_weight)
    silu_grad = by_row(row_pieces(silu_grad), row).transpose(1, 0, 2).reshape(FPD, D)
    embed = noise_embed.astype(F32)
    sigma = jax.nn.sigmoid(embed)
    embed_grad = silu_grad * (sigma * (1.0 + embed * (1.0 - sigma)))

    return (
        layer_output,
        input_grad,
        embed_grad,
        ada_total,
        ada_sum,
        qkv_total,
        qkv_sum,
        out_total,
        out_sum,
        up_total,
        up_sum,
        down_total,
        down_sum,
    )


def solution(mesh):
    fine = Mesh(mesh.devices.reshape(2, 4, 4, 2, 2), AXES)
    seq, row = ("xh", "z", "y"), ("xl", "c")
    token, weight, vector = P(seq, row, None), P(row, None), P(row)
    in_specs = (token, P(seq, None), P(seq), token) + (weight, vector) * 5
    out_specs = (token, token, P(seq, None)) + (weight, vector) * 5
    return jax.shard_map(
        per_device, mesh=fine, in_specs=in_specs, out_specs=out_specs, check_vma=False
    )
```

```python
import math

import jax
import jax.numpy as jnp
from jax import lax
from jax.experimental import pallas as pl
from jax.experimental.pallas import tpu as pltpu
from jax.sharding import Mesh, PartitionSpec as P

F32 = jnp.float32
BF16 = jnp.bfloat16
HD = 64
GRID = 16
FPD = 8
PR = 64
D = 1024
FF = 4096
HC = 256
TOK = 256
PREV = 7
AXES = ("xh", "z", "y", "xl", "c")
CORE, DIRECT, OTHER, FAR = 1, 2, 66, 64
MB = 1024 * 1024


def swap(value, mask):
    return lax.ppermute(value, AXES, [(i, i ^ mask) for i in range(128)])


def shift(value, steps):
    return lax.ppermute(value, AXES, [(i, (i + 4 * steps) % 128) for i in range(128)])


def after(value, *others):
    return lax.optimization_barrier((value,) + others)[0]


def nt(left, right):
    return lax.dot_general(left, right, (((1,), (1,)), ((), ())), preferred_element_type=F32)


def tn(left, right):
    return lax.dot_general(left, right, (((0,), (0,)), ((), ())), preferred_element_type=F32)


def nn(left, right):
    return jnp.dot(left, right, preferred_element_type=F32)


def norm(values):
    center = values - jnp.mean(values, axis=-1, keepdims=True)
    spread = jnp.mean(center * center, axis=-1, keepdims=True)
    rate = lax.rsqrt(spread + 1e-06)
    return center * rate, rate


def norm_back(normal, rate, grad):
    mean_grad = jnp.mean(grad, axis=-1, keepdims=True)
    mean_both = jnp.mean(grad * normal, axis=-1, keepdims=True)
    return rate * (grad - mean_grad - normal * mean_both)


def turn(values, cosine, sine):
    lanes = lax.broadcasted_iota(jnp.int32, values.shape, 1)
    other = jnp.where(
        lanes % HD < HD // 2, pltpu.roll(values, HC - HD // 2, 1), pltpu.roll(values, HD // 2, 1)
    )
    return values * cosine + other * sine


def params(mib):
    return pltpu.CompilerParams(vmem_limit_bytes=mib * MB)


def cost(flops, moved, exps=0):
    return pl.CostEstimate(flops=int(flops), bytes_accessed=int(moved), transcendentals=int(exps))


def whole(shape):
    return pl.BlockSpec(shape, lambda i, *_: (0,) * len(shape))


def columns(row, j):
    return pl.ds(pl.multiple_of((row ^ j) * HC, HC), HC)


def shape(dims, kind=BF16):
    return jax.ShapeDtypeStruct(dims, kind)


UB, QB, OB, DB, WIDE = 6144, 6656, 7168, 7296, 7424


def put(ref, start, at, value):
    cols = slice(start, start + value.shape[1])
    number = lax.broadcasted_iota(jnp.int32, (8, value.shape[1]), 0)
    ref[:, cols] = jnp.where(number == at, value, ref[:, cols])


def take(value, at):
    number = lax.broadcasted_iota(jnp.int32, value.shape, 0)
    return jnp.sum(jnp.where(number == at, value, 0.0), axis=0, keepdims=True)


def put_half(ref, start, value):
    cols = slice(start, start + value.shape[1])
    number = lax.broadcasted_iota(jnp.int32, (8, value.shape[1]), 0)
    both = jnp.concatenate([value, value], axis=0)
    ref[:, cols] = jnp.where(number // 4 == pl.program_id(0), both, ref[:, cols])


def unfold(ref, start, width):
    return jnp.concatenate([ref[i : i + 1, start : start + width] for i in range(8)], axis=1)


def prepare_kernel(row_ref, pos_ref, noise, ada, ab, qb, ob, ub, db, pack, silu, cp, sp, frames):
    row = row_ref[0]
    embed = noise[...].astype(F32)
    value = (embed / (1.0 + jnp.exp(-embed))).astype(BF16)
    own = jnp.where(
        row < 2,
        jnp.where(row == 0, value[:, :HC], value[:, HC : 2 * HC]),
        jnp.where(row == 2, value[:, 2 * HC : 3 * HC], value[:, 3 * HC :]),
    )
    silu[...] = own
    pack[:, UB:] = jnp.zeros((FPD, WIDE - UB), F32)
    for segment in range(6):
        cols = slice(segment * D, (segment + 1) * D)
        pack[:, cols] = nn(own, ada[:, cols])
    bias = pl.ds(pl.multiple_of(row * 1536, 512), 1536)
    pack[:, bias] = pack[:, bias] + ab[...].astype(F32)
    for i in range(2):
        at = 2 * row + i
        put(pack, UB, at, ub[:, i * 512 : (i + 1) * 512].astype(F32))
        put(pack, OB, at, ob[:, i * 128 : (i + 1) * 128].astype(F32))
        put(pack, DB, at, db[:, i * 128 : (i + 1) * 128].astype(F32))
    for i in range(3):
        chunk = 3 * row + i
        at = jnp.where(chunk < 4, chunk, chunk - 4)
        second = (chunk >= 4) & (chunk < 8)
        value = qb[:, i * HC : (i + 1) * HC].astype(F32)
        put(pack, QB, jnp.where(second, -1, at), value)
        put(pack, QB + HC, jnp.where(second, at, -1), value)

    def parts(dims):
        lane = lax.broadcasted_iota(jnp.int32, dims, 1)
        index = lane % (HD // 2)
        quarter, eighth = HD // 4, HD // 8
        in_frame = index < quarter
        in_row = (index >= quarter) & (index < quarter + eighth)
        offset = jnp.where(
            in_frame, index, jnp.where(in_row, index - quarter, index - quarter - eighth)
        ).astype(F32)
        length = jnp.where(in_frame, 1.0 * quarter, 1.0 * eighth)
        frequency = jnp.exp(-math.log(10000.0) * offset / length)
        sign = jnp.where(lane % HD < HD // 2, -1.0, 1.0)
        return in_frame, in_row, frequency, sign

    in_frame, in_row, frequency, sign = parts((TOK, HC))
    slot = lax.broadcasted_iota(jnp.int32, (TOK, HC), 0)
    patch = ((slot // PR) ^ row) * PR + slot % PR
    angle = jnp.where(in_row, patch // GRID, patch % GRID).astype(F32) * frequency
    cp[...] = jnp.where(in_frame, 0.0, jnp.cos(angle))
    sp[...] = jnp.where(in_frame, 0.0, jnp.sin(angle) * sign)
    in_frame, _, frequency, sign = parts((16, HC))
    slot = lax.broadcasted_iota(jnp.int32, (16, HC), 0)
    place = pos_ref[0] - PREV + (slot - FPD)
    for f in range(FPD):
        place = jnp.where(slot == f, pos_ref[f], place)
    angle = place.astype(F32) * frequency
    frames[:, :HC] = jnp.where(in_frame, jnp.cos(angle), 0.0)
    frames[:, HC:] = jnp.where(in_frame, jnp.sin(angle) * sign, 0.0)


def prepare(row, places, noise, ada, biases):
    return pl.pallas_call(
        prepare_kernel,
        out_shape=[
            shape((FPD, WIDE), F32),
            shape((FPD, HC)),
            shape((TOK, HC), F32),
            shape((TOK, HC), F32),
            shape((16, 2 * HC), F32),
        ],
        grid_spec=pltpu.PrefetchScalarGridSpec(
            num_scalar_prefetch=2,
            grid=(1,),
            in_specs=[whole((FPD, D)), whole((HC, 6 * D))]
            + [whole((1, b.shape[0])) for b in biases],
            out_specs=[
                whole((FPD, WIDE)),
                whole((FPD, HC)),
                whole((TOK, HC)),
                whole((TOK, HC)),
                whole((16, 2 * HC)),
            ],
        ),
        compiler_params=params(24),
        cost_estimate=cost(2 * 8 * HC * 6 * D, 4 * MB, 4 * TOK * HC),
        name="prepare",
    )(row, places, noise, ada, *[b[None] for b in biases])


def split_heads_kernel(row_ref, q, k, v, p0, p1, p23):
    for j, p in enumerate((p0, p1, p23.at[0], p23.at[1])):

        @pl.when(pl.program_id(0) == j)
        def _():
            p[:, :HC] = q[...]
            p[:, HC : 2 * HC] = k[...]
            p[:, 2 * HC :] = v[...]


def split_heads(row, weight):
    piece = (HC, 3 * HC)
    return pl.pallas_call(
        split_heads_kernel,
        out_shape=[shape(piece), shape(piece), shape((2,) + piece)],
        grid_spec=pltpu.PrefetchScalarGridSpec(
            num_scalar_prefetch=1,
            grid=(4,),
            in_specs=[
                pl.BlockSpec((HC, HC), lambda j, row, s=s: (0, 4 * s + (row[0] ^ j)))
                for s in range(3)
            ],
            out_specs=[whole(piece), whole(piece), whole((2,) + piece)],
        ),
        compiler_params=params(12),
        cost_estimate=cost(0, 3 * MB),
        name="split_heads",
    )(row, weight, weight, weight)


def cosines(cp, sp, frames, at):
    both = frames[pl.ds(at, 1), :]
    return cp[...] + both[:, :HC], sp[...] + both[:, HC:]


def project_kernel(own, row_ref, x0, x1, x2, x3, table, mods, w0, w1, w2, w3, cp, sp, fr, *outs):
    row = row_ref[0]
    f = pl.program_id(0)
    if own:
        h_ref, q_ref, k_ref, v_ref = outs
        first, at, angle = 0, f, f
    else:
        k_ref, v_ref, h_ref = outs
        first, at, angle = HC, f + FPD - PREV, f + FPD
    x = jnp.concatenate([r[0] for r in (x0, x1, x2, x3)], axis=0).astype(F32)
    normal, _ = norm(x)
    shift_row = mods[pl.ds(at, 1), :D]
    scale_row = mods[pl.ds(at, 1), D : 2 * D]
    hidden = (normal * (1.0 + scale_row) + shift_row).astype(BF16)
    where = (0,) if own else ()
    h_ref[where + (slice(None), slice(None))] = hidden
    low, high = table[pl.ds(row, 1), QB : QB + 2 * HC], table[pl.ds(row + 4, 1), QB : QB + HC]
    total = jnp.concatenate([low, high], axis=1)[:, first:]
    for j, w in enumerate((w0, w1, w2, w3)):
        total = total + nn(h_ref[where + (slice(None), columns(row, j))], w[:, first:])
    cosine, sine = cosines(cp, sp, fr, angle)
    if own:
        q_ref[0] = (turn(total[:, :HC], cosine, sine).astype(BF16).astype(F32) * 0.125).astype(BF16)
        total = total[:, HC:]
    k_ref[0] = turn(total[:, :HC], cosine, sine).astype(BF16)
    v_ref[0] = total[:, HC:].astype(BF16)


def project(own, row, xs, table, mods, weights, tables):
    frames = xs[0].shape[0]
    x_spec = pl.BlockSpec((1, PR, D), lambda f, *_: (f, 0, 0))
    out_spec = pl.BlockSpec((1, TOK, HC), lambda f, *_: (f, 0, 0))
    out = shape((frames, TOK, HC))
    if own:
        out_specs = [pl.BlockSpec((1, TOK, D), lambda f, *_: (f, 0, 0)), out_spec, out_spec, out_spec]
        out_shape = [shape((frames, TOK, D)), out, out, out]
        scratch = []
    else:
        out_specs = [out_spec, out_spec]
        out_shape = [out, out]
        scratch = [pltpu.VMEM((TOK, D), BF16)]
    return pl.pallas_call(
        lambda *refs: project_kernel(own, *refs),
        out_shape=out_shape,
        grid_spec=pltpu.PrefetchScalarGridSpec(
            num_scalar_prefetch=1,
            grid=(frames,),
            in_specs=[x_spec] * 4
            + [whole((FPD, WIDE)), whole(mods.shape)]
            + [whole((HC, 3 * HC))] * 4
            + [whole((TOK, HC)), whole((TOK, HC)), whole((16, 2 * HC))],
            out_specs=out_specs,
            scratch_shapes=scratch,
        ),
        compiler_params=params(20),
        cost_estimate=cost(2 * frames * TOK * D * 3 * HC, frames * TOK * D * 4 + 4 * MB),
        name="project_own" if own else "project_prev",
    )(row, *xs, table, mods, *weights, *tables)


def head_lanes():
    return lax.broadcasted_iota(jnp.int32, (TOK, HC), 1) // HD


def spread_queries(q, qs):
    lanes = head_lanes()
    query = q[0]
    for h in range(4):
        qs[pl.ds(h * TOK, TOK), :] = jnp.where(lanes == h, query, jnp.zeros_like(query))


def sweep_scores(low_at, high_at, k, qs, scores, top):
    def one(at, _):
        keys = k[at]
        for h in range(4):
            rows = pl.ds(h * TOK, TOK)
            s = nt(qs[rows, :], keys)
            scores[at - low_at, rows, :] = s
            top[rows, :] = jnp.maximum(top[rows, :], jnp.maximum(s[:, :128], s[:, 128:]))
        return 0

    lax.fori_loop(low_at, high_at, one, 0)
    for h in range(4):
        rows = pl.ds(h * TOK, TOK)
        top[rows, :] = jnp.broadcast_to(jnp.max(top[rows, :], axis=1, keepdims=True), (TOK, 128))


def sweep_values(low_at, high_at, v, scores, top, low, acc):
    low[...] = jnp.zeros_like(low)
    acc[...] = jnp.zeros_like(acc)

    def one(at, _):
        values = v[at]
        for h in range(4):
            rows = pl.ds(h * TOK, TOK)
            p = jnp.exp(scores[at - low_at, rows, :] - jnp.concatenate([top[rows, :]] * 2, axis=1))
            low[rows, :] = low[rows, :] + (p[:, :128] + p[:, 128:])
            acc[rows, :] = acc[rows, :] + nn(p.astype(BF16), values)
        return 0

    lax.fori_loop(low_at, high_at, one, 0)


def attend_own_kernel(pos_ref, q, k, v, mixed, stats, qs, scores, acc, top, low):
    f = pl.program_id(0)
    start = jnp.maximum(f - pos_ref[f], 0)
    spread_queries(q, qs)
    top[...] = jnp.full_like(top, -1e30)
    sweep_scores(start, f + 1, k, qs, scores, top)
    sweep_values(start, f + 1, v, scores, top, low, acc)
    lanes = head_lanes()
    narrow = lax.broadcasted_iota(jnp.int32, (TOK, 128), 1)
    result = jnp.zeros((TOK, HC), F32)
    state = jnp.zeros((TOK, 128), F32)
    for h in range(4):
        rows = pl.ds(h * TOK, TOK)
        result = jnp.where(lanes == h, acc[rows, :], result)
        state = jnp.where(narrow == h, top[rows, :], state)
        state = jnp.where(narrow == 4 + h, jnp.sum(low[rows, :], axis=1, keepdims=True), state)
    mixed[0] = result
    stats[0] = state


def attend_prev_kernel(
    pos_ref, q, k, v, mixed, stats, o0, o1, o23, lse, qs, scores, acc, top, low, result, logs
):
    f = pl.program_id(0)
    count = jnp.maximum(pos_ref[f] - f, 0)
    lanes = head_lanes()
    narrow = lax.broadcasted_iota(jnp.int32, (TOK, 128), 1)
    state = stats[0]

    def finish(part):
        total_mixed = jnp.zeros((TOK, HC), F32)
        total_logs = jnp.zeros((TOK, 128), F32)
        for h in range(4):
            largest, total, value = part(h, state[:, h : h + 1], state[:, 4 + h : 5 + h])
            total_mixed = jnp.where(lanes == h, value / total, total_mixed)
            total_logs = jnp.where(narrow == h, largest + jnp.log(total), total_logs)
        result[...] = total_mixed.astype(BF16)
        logs[...] = total_logs

    @pl.when(count == 0)
    def _():
        finish(lambda h, largest, total: (largest, total, mixed[0]))

    @pl.when(count > 0)
    def _():
        spread_queries(q, qs)
        for h in range(4):
            top[pl.ds(h * TOK, TOK), :] = jnp.broadcast_to(state[:, h : h + 1], (TOK, 128))
        sweep_scores(PREV - count, PREV, k, qs, scores, top)
        sweep_values(PREV - count, PREV, v, scores, top, low, acc)

        def part(h, largest, total):
            rows = pl.ds(h * TOK, TOK)
            most = top[rows, :1]
            fade = jnp.exp(largest - most)
            total = total * fade + jnp.sum(low[rows, :], axis=1, keepdims=True)
            return most, total, mixed[0] * fade + acc[rows, :]

        finish(part)

    lse[0] = logs[...].T[:8]
    o0[0] = result[:PR, :]
    o1[0] = result[PR : 2 * PR, :]
    o23[0, 0] = result[2 * PR : 3 * PR, :]
    o23[1, 0] = result[3 * PR :, :]


def attend(own, places, q, k, v, state=()):
    block = pl.BlockSpec((1, TOK, HC), lambda f, *_: (f, 0, 0))
    narrow = pl.BlockSpec((1, TOK, 128), lambda f, *_: (f, 0, 0))
    piece = pl.BlockSpec((1, PR, HC), lambda f, *_: (f, 0, 0))
    count = FPD if own else PREV
    scratch = [
        pltpu.VMEM((4 * TOK, HC), BF16),
        pltpu.VMEM((8, 4 * TOK, TOK), F32),
        pltpu.VMEM((4 * TOK, HC), F32),
        pltpu.VMEM((4 * TOK, 128), F32),
        pltpu.VMEM((4 * TOK, 128), F32),
    ]
    specs = [block] + [whole((count, TOK, HC))] * 2
    if own:
        out_shape = [shape((FPD, TOK, HC), F32), shape((FPD, TOK, 128), F32)]
        out_specs = [block, narrow]
    else:
        specs += [block, narrow]
        out_shape = [shape((FPD, PR, HC))] * 2 + [
            shape((2, FPD, PR, HC)),
            shape((FPD, 8, TOK), F32),
        ]
        out_specs = [piece] * 2 + [
            pl.BlockSpec((2, 1, PR, HC), lambda f, *_: (0, f, 0, 0)),
            pl.BlockSpec((1, 8, TOK), lambda f, *_: (f, 0, 0)),
        ]
        scratch += [pltpu.VMEM((TOK, HC), BF16), pltpu.VMEM((TOK, 128), F32)]
    return pl.pallas_call(
        attend_own_kernel if own else attend_prev_kernel,
        out_shape=out_shape,
        grid_spec=pltpu.PrefetchScalarGridSpec(
            num_scalar_prefetch=1,
            grid=(FPD,),
            in_specs=specs,
            out_specs=out_specs,
            scratch_shapes=scratch,
        ),
        compiler_params=params(40),
        cost_estimate=cost(
            (30 if own else 12) * 4 * 2 * 2 * TOK**3, 6 * MB, 30 * 4 * TOK * TOK
        ),
        name="attend_own" if own else "attend_prev",
    )(places, q, k, v, *state)


def attend_back_kernel(own, pos_ref, q, k, v, g0, g1, g2, g3, o0, o1, o23, lse, *rest):
    if own:
        cp, sp, fr, before_ref, dq, dk, dv, qs, gs, ks, pl_scr, dl_scr, ds_scr, dq_acc = rest
        dk_acc, dv_acc = dk, dv
    else:
        dq, both_ref, qs, gs, ks, pl_scr, dl_scr, ds_scr, dq_acc, dk_acc, dv_acc = rest
    f = pl.program_id(0)
    place = pos_ref[f]
    lanes = head_lanes()

    @pl.when(f == 0)
    def _():
        for ref in (dk_acc, dv_acc):
            ref[...] = jnp.zeros_like(ref)

    def prelude():
        query = q[0]
        grad = jnp.concatenate([r[0] for r in (g0, g1, g2, g3)], axis=0)
        mixed = jnp.concatenate([o0[0], o1[0], o23[0, 0], o23[1, 0]], axis=0)
        for h in range(4):
            rows = pl.ds(h * TOK, TOK)
            qs[rows, :] = jnp.where(lanes == h, query, jnp.zeros_like(query))
            gs[rows, :] = jnp.where(lanes == h, grad, jnp.zeros_like(grad))
        both = grad.astype(F32) * mixed.astype(F32)
        pick = (
            lax.broadcasted_iota(jnp.int32, (8, HC), 1) // HD
            == lax.broadcasted_iota(jnp.int32, (8, HC), 0)
        ).astype(F32)
        return lax.dot_general(
            pick, both, (((1,), (1,)), ((), ())),
            preferred_element_type=F32, precision=lax.Precision.HIGHEST,
        )

    def step(delta, logs, at):
        keys, values = k[at], v[at]
        for h in range(4):
            rows = pl.ds(h * TOK, TOK)
            ks[rows, :] = jnp.where(lanes == h, keys, jnp.zeros_like(keys))
            p = jnp.exp(nt(keys, qs[rows, :]) - logs[h : h + 1])
            ds = (p * (nt(values, gs[rows, :]) - delta[h : h + 1])).astype(BF16)
            pl_scr[:, rows] = p.astype(BF16)
            dl_scr[:, rows] = ds
            ds_scr[rows, :] = ds
        dv_acc[at] = dv_acc[at] + nn(pl_scr[...], gs[...])
        dk_acc[at] = dk_acc[at] + nn(dl_scr[...], qs[...])
        dq_acc[...] = dq_acc[...] + tn(ds_scr[...], ks[...])

    def sweep(low, high):
        delta = prelude()
        logs = lse[0]
        dq_acc[...] = jnp.zeros_like(dq_acc)

        def one(at, _):
            step(delta, logs, at)
            return 0

        lax.fori_loop(low, high, one, 0)

    if own:
        sweep(jnp.maximum(f - place, 0), f + 1)
        cosine, sine = cosines(cp, sp, fr, f)
        dq[0] = turn((dq_acc[...] + before_ref[0]) * 0.125, cosine, -sine).astype(BF16)
    else:
        count = jnp.maximum(place - f, 0)

        @pl.when(count > 0)
        def _():
            sweep(PREV - count, PREV)
            dq[0] = dq_acc[...]

        @pl.when(count == 0)
        def _():
            dq[0] = jnp.zeros_like(dq_acc)

        @pl.when(f == FPD - 1)
        def _():
            both_ref[0] = dk_acc[...].astype(BF16)
            both_ref[1] = dv_acc[...].astype(BF16)


def attend_back(own, places, q, k, v, grads, mixed, lse, tables=None, before=None):
    block = pl.BlockSpec((1, TOK, HC), lambda f, *_: (f, 0, 0))
    piece = pl.BlockSpec((1, PR, HC), lambda f, *_: (f, 0, 0))
    count = FPD if own else PREV
    wide = pltpu.VMEM((4 * TOK, HC), BF16)
    tall = pltpu.VMEM((TOK, 4 * TOK), BF16)
    scratch = [wide, wide, wide, tall, tall, wide, pltpu.VMEM((TOK, HC), F32)]
    specs = []
    extra = ()
    if own:
        specs = [whole((TOK, HC)), whole((TOK, HC)), whole((16, 2 * HC)), block]
        extra = tuple(tables) + (before,)
    else:
        scratch += [pltpu.VMEM((PREV, TOK, HC), F32)] * 2
    return pl.pallas_call(
        lambda *refs: attend_back_kernel(own, *refs),
        out_shape=[shape((FPD, TOK, HC), BF16 if own else F32)]
        + ([shape((FPD, TOK, HC), F32)] * 2 if own else [shape((2, PREV, TOK, HC))]),
        grid_spec=pltpu.PrefetchScalarGridSpec(
            num_scalar_prefetch=1,
            grid=(FPD,),
            in_specs=[block]
            + [whole((count, TOK, HC))] * 2
            + [piece] * 6
            + [pl.BlockSpec((2, 1, PR, HC), lambda f, *_: (0, f, 0, 0))]
            + [pl.BlockSpec((1, 8, TOK), lambda f, *_: (f, 0, 0))]
            + specs,
            out_specs=[block]
            + ([whole((FPD, TOK, HC))] * 2 if own else [whole((2, PREV, TOK, HC))]),
            scratch_shapes=scratch,
        ),
        compiler_params=params(58),
        cost_estimate=cost(1000 if own else 12 * 4 * 5 * 2 * TOK**3, 1000 if own else 12 * MB),
        name="attend_back_own" if own else "attend_back_prev",
    )(places, q, k, v, *grads, *mixed, lse, *extra)


HALF = 4
RAW = HALF * PR


def flat(ref):
    return ref[...].reshape(RAW, ref.shape[-1])


def frames_of(value):
    return value.reshape(HALF, PR, value.shape[-1])


def segment(table, s):
    both = table[:, s * D : (s + 1) * D]
    return jnp.where(pl.program_id(0) == 0, both[:HALF], both[HALF:])[:, None, :]


def fold(out, start, width, row):
    @pl.when(pl.program_id(0) == 0)
    def _():
        out[:, start : start + width] = jnp.zeros((8, width), F32)

    for i in range(8):
        at = (slice(i, i + 1), slice(start, start + width))
        out[at] = out[at] + row[:, i * width : (i + 1) * width]


def mid_kernel(o0, o1, o2, o3, w0, w1, w2, w3, table, x, cot, branch, middle, hidden, down, dsum):
    total = unfold(table, OB, 128)
    for o, w in zip((o0, o1, o2, o3), (w0, w1, w2, w3)):
        total = total + nn(flat(o), w[...])
    branched = frames_of(total)
    branch[...] = branched
    mid_value = x[...].astype(F32) + segment(table, 2) * branched
    middle[...] = mid_value
    normal, _ = norm(mid_value)
    hidden[...] = (normal * (1.0 + segment(table, 4)) + segment(table, 3)).astype(BF16)
    grad = (segment(table, 5) * cot[...].astype(F32)).astype(BF16)
    down[...] = grad
    fold(dsum, 0, 128, jnp.sum(grad.astype(F32).reshape(RAW, D), axis=0, keepdims=True))


def half_spec(width):
    return pl.BlockSpec((HALF, PR, width), lambda i, *_: (i, 0, 0))


def mid(pieces, weights, table, x, cot):
    return pl.pallas_call(
        mid_kernel,
        out_shape=[
            shape((FPD, PR, D), F32),
            shape((FPD, PR, D), F32),
            shape((FPD, PR, D)),
            shape((FPD, PR, D)),
            shape((8, 128), F32),
        ],
        grid=(FPD // HALF,),
        in_specs=[half_spec(HC)] * 4
        + [whole((HC, D))] * 4
        + [whole((FPD, WIDE)), half_spec(D), half_spec(D)],
        out_specs=[half_spec(D)] * 4 + [whole((8, 128))],
        compiler_params=params(26),
        cost_estimate=cost(2 * 512 * D * D, 12 * MB),
        name="mid",
    )(*pieces, *weights, table, x, cot)


def mid_back_kernel(
    hg, middle, branch, cot, table, w0, w1, w2, w3, usum, dsum, mg, bg, a0, a1, a23, sums
):
    grad = hg[...]
    normal, rate = norm(middle[...])
    put_half(sums, D, jnp.sum(grad, axis=1))
    put_half(sums, 2 * D, jnp.sum(grad * normal, axis=1))
    total = cot[...].astype(F32) + norm_back(normal, rate, grad * (1.0 + segment(table, 4)))
    mg[...] = total
    put_half(sums, 0, jnp.sum(total * branch[...], axis=1))
    low = (segment(table, 2) * total).astype(BF16)
    bg[...] = low
    low = low.reshape(RAW, D)
    sums[:, 3 * D : 3 * D + NB] = usum[...]
    sums[:, 3 * D + NB : 3 * D + NB + 128] = dsum[...]
    fold(sums, 3 * D + NB + 128, 128, jnp.sum(low.astype(F32), axis=0, keepdims=True))
    for j, w in enumerate((w0, w1, w2, w3)):
        value = frames_of(nt(low, w[...]).astype(BF16))
        if j < 2:
            (a0, a1)[j][...] = value
        else:
            a23[j - 2] = value


def mid_back(hg, middle, branch, cot, table, weights, usum, dsum):
    return pl.pallas_call(
        mid_back_kernel,
        out_shape=[shape((FPD, PR, D), F32), shape((FPD, PR, D))]
        + [shape((FPD, PR, HC))] * 2
        + [shape((2, FPD, PR, HC)), shape((8, EARLY), F32)],
        grid=(FPD // HALF,),
        in_specs=[half_spec(D)] * 4
        + [whole((FPD, WIDE))]
        + [whole((HC, D))] * 4
        + [whole((8, NB)), whole((8, 128))],
        out_specs=[half_spec(D)] * 2
        + [half_spec(HC)] * 2
        + [pl.BlockSpec((2, HALF, PR, HC), lambda i: (0, i, 0, 0)), whole((8, EARLY))],
        compiler_params=params(26),
        cost_estimate=cost(2 * 512 * D * D, 12 * MB),
        name="mid_back",
    )(hg, middle, branch, cot, table, *weights, usum, dsum)


NB = 512
STEPS = FF // NB
PER = D // NB
TOKENS = FPD * PR


def block_of(t):
    phase = t // PER
    return ((phase % 2) * 2) ^ (phase // 2)


def up_column(t, row):
    return (row ^ block_of(t)) * PER + t % PER


def down_row(t):
    return block_of(t) * PER + t % PER


def down_spec(j):
    phase = (0, 2, 1, 3)[j]
    return pl.BlockSpec((NB, D), lambda t, row: (jnp.clip(t - phase * PER, 0, PER - 1), 0))


def pick_down(d0, d1, d2, d3):
    phase = pl.program_id(0) // PER
    return jnp.where(
        phase < 2,
        jnp.where(phase == 0, d0[...], d2[...]),
        jnp.where(phase == 2, d1[...], d3[...]),
    )


def feed_kernel(row_ref, h2, dg, u0, u1, u2, u3, table, d0, d1, d2, d3, act, upg, hg, usum):
    row = row_ref[0]
    ups = (u0, u1, u2, u3)
    down = pick_down(d0, d1, d2, d3)
    at = pl.ds(up_column(pl.program_id(0), row), 1)
    u = table[at, UB : UB + NB]
    for j, w in enumerate(ups):
        u = u + nn(h2[:, columns(row, j)], w[...])
    rate = math.sqrt(2.0 / math.pi)
    square = u * u
    half = 0.5 + 0.5 * jnp.tanh(u * (rate + (rate * 0.044715) * square))
    active = u * half
    act[...] = active.astype(BF16)
    slope = half + active * (1.0 - half) * (2.0 * rate + (6.0 * rate * 0.044715) * square)
    grad = (nt(dg[...], down) * slope).astype(BF16)
    upg[...] = grad
    put(usum, 0, up_column(pl.program_id(0), row), jnp.sum(grad.astype(F32), axis=0, keepdims=True))

    @pl.when(pl.program_id(0) == 0)
    def _():
        hg[...] = jnp.zeros_like(hg)

    for j, w in enumerate(ups):
        hg[:, columns(row, j)] = hg[:, columns(row, j)] + nt(grad, w[...])


def feed(row, h2, dg, ups, table, downs):
    tok = whole((TOKENS, D))
    block = pl.BlockSpec((TOKENS, NB), lambda t, row: (0, t))
    return pl.pallas_call(
        feed_kernel,
        out_shape=[
            shape((TOKENS, FF)),
            shape((TOKENS, FF)),
            shape((TOKENS, D), F32),
            shape((8, NB), F32),
        ],
        grid_spec=pltpu.PrefetchScalarGridSpec(
            num_scalar_prefetch=1,
            grid=(STEPS,),
            in_specs=[tok, tok]
            + [pl.BlockSpec((HC, NB), lambda t, row: (0, up_column(t, row[0])))] * 4
            + [whole((FPD, WIDE))]
            + [down_spec(j) for j in range(4)],
            out_specs=[block, block, tok, whole((8, NB))],
        ),
        compiler_params=params(58),
        cost_estimate=cost(3 * 2 * TOKENS * D * FF, 30 * MB, TOKENS * FF),
        name="feed",
    )(row, h2, dg, *ups, table, *downs)


def down_step(da, db, dg, act, part, dn):
    g = pl.program_id(0)
    down = jnp.where(g < PER, da[...], db[...])
    active = act[...]
    dn[...] = dn[...] + nn(active, down)
    part[0] = tn(active, dg[...]).astype(BF16)


def down_send_kernel(dg, act, da, db, part, dn):
    @pl.when(pl.program_id(0) == 0)
    def _():
        dn[...] = jnp.zeros_like(dn)

    down_step(da, db, dg, act, part, dn)


def down_keep_kernel(dg, act, da, db, before, table, middle, cot, part, out, gate, dn):
    @pl.when(pl.program_id(0) == 0)
    def _():
        dn[...] = before[...]

    down_step(da, db, dg, act, part, dn)

    @pl.when(pl.program_id(0) == STEPS // 2 - 1)
    def _():
        bias = unfold(table, DB, 128)
        for f in range(FPD):
            rows = slice(f * PR, (f + 1) * PR)
            value = dn[rows, :] + bias
            out[f] = (middle[f] + table[f : f + 1, 5 * D : 6 * D] * value).astype(BF16)
            gate[f : f + 1, :] = jnp.sum(cot[f].astype(F32) * value, axis=0, keepdims=True)


def down_half(first, dg, act, downs, extra=()):
    tok = whole((TOKENS, D))
    full = whole((FPD, PR, D))
    half = STEPS // 2
    weight = lambda k: pl.BlockSpec((NB, D), lambda g: (jnp.clip(g - k * PER, 0, PER - 1), 0))
    start = half if first else 0
    part = pl.BlockSpec((1, NB, D), lambda g: (g // PER, g % PER, 0))
    out_specs, out_shape, scratch, specs = [part], [shape((2, D, D))], [], []
    if first:
        out_specs += [tok]
        out_shape += [shape((TOKENS, D), F32)]
    else:
        specs = [tok, whole((FPD, WIDE)), full, full]
        out_specs += [full, whole((8, D))]
        out_shape += [shape((FPD, PR, D)), shape((8, D), F32)]
        scratch = [pltpu.VMEM((TOKENS, D), F32)]
    return pl.pallas_call(
        down_send_kernel if first else down_keep_kernel,
        out_shape=out_shape,
        grid=(half,),
        in_specs=[tok, pl.BlockSpec((TOKENS, NB), lambda g: (0, g + start)), weight(0), weight(1)]
        + specs,
        out_specs=out_specs,
        scratch_shapes=scratch,
        compiler_params=params(40),
        cost_estimate=cost(2 * TOKENS * D * FF, 14 * MB),
        name="down_weight_send" if first else "down_weight_keep",
    )(dg, act, *downs, *extra)


def up_weight_kernel(row_ref, h2, upg, uk, us):
    row = row_ref[0]
    grad = upg[...]
    for j, ref in enumerate((uk, us, uk, us)):
        ref[j // 2, 0] = tn(h2[:, columns(row, j)], grad).astype(BF16)


def up_weight_grad(row, h2, upg):
    up_out = pl.BlockSpec(
        (2, 1, HC, NB),
        lambda t, row: (0, up_column(t, row[0]) // PER, 0, up_column(t, row[0]) % PER),
    )
    return pl.pallas_call(
        up_weight_kernel,
        out_shape=[shape((2, 4, HC, D))] * 2,
        grid_spec=pltpu.PrefetchScalarGridSpec(
            num_scalar_prefetch=1,
            grid=(STEPS,),
            in_specs=[whole((TOKENS, D)), pl.BlockSpec((TOKENS, NB), lambda t, row: (0, t))],
            out_specs=[up_out, up_out],
        ),
        compiler_params=params(58),
        cost_estimate=cost(2 * TOKENS * D * FF, 14 * MB),
        name="up_weight_grad",
    )(row, h2, upg)


def out_weight_kernel(t0, t1, t2, t3, bg, keep, send):
    grad = bg[...].reshape(TOKENS, D)
    for j, t in enumerate((t0, t1, t2, t3)):
        ref = (keep, send)[j % 2]
        ref[j // 2] = tn(t[...].reshape(TOKENS, HC), grad).astype(BF16)


def out_weight_grad(pieces, bg):
    return pl.pallas_call(
        out_weight_kernel,
        out_shape=[shape((2, HC, D))] * 2,
        grid=(1,),
        in_specs=[whole((FPD, PR, HC))] * 4 + [whole((FPD, PR, D))],
        out_specs=[whole((2, HC, D))] * 2,
        compiler_params=params(14),
        cost_estimate=cost(2 * TOKENS * D * D, 4 * MB),
        name="out_weight_grad",
    )(*pieces, bg)


CHUNKS = 16
UP_ROWS, OUT_ROWS, DOWN_ROWS = D // CHUNKS, HC // CHUNKS, D // CHUNKS
FIRST = UP_ROWS + OUT_ROWS
ROWS = FIRST + DOWN_ROWS


def core_sum_kernel(ua, ub, da, db, oa, ob, out):
    def both(a, b):
        return (a.astype(F32) + b.astype(F32)).astype(BF16)

    for c in range(4):
        at = c * ROWS
        low, high = c * OUT_ROWS, (c + 1) * OUT_ROWS
        for i in range(4):
            to = at + i * OUT_ROWS
            out[0, to : to + OUT_ROWS] = both(ua[0, i, low:high], ub[0, i, low:high])
        out[0, at + UP_ROWS : at + FIRST] = both(oa[0, low:high], ob[0, low:high])
        low, high = c * DOWN_ROWS, (c + 1) * DOWN_ROWS
        out[0, at + FIRST : at + ROWS] = both(da[0, low:high], db[0, low:high])


def core_sum(up, down, out):
    ups = pl.BlockSpec((1, 4, 4 * OUT_ROWS, D), lambda j, c: (j, 0, c, 0))
    outs = pl.BlockSpec((1, 4 * OUT_ROWS, D), lambda j, c: (j, c, 0))
    downs = pl.BlockSpec((1, 4 * DOWN_ROWS, D), lambda j, c: (j, c, 0))
    return pl.pallas_call(
        core_sum_kernel,
        out_shape=shape((2, CHUNKS * ROWS, D)),
        grid=(2, CHUNKS // 4),
        in_specs=[ups, ups, downs, downs, outs, outs],
        out_specs=pl.BlockSpec((1, 4 * ROWS, D), lambda j, c: (j, c, 0)),
        compiler_params=params(58),
        cost_estimate=cost(1000, 1000),
        name="core_sum",
    )(*up, *down, *out)


def unpack_kernel(total, up, out, down):
    for k in range(4):
        at = k * ROWS
        for i in range(4):
            rows = slice(at + i * OUT_ROWS, at + (i + 1) * OUT_ROWS)
            up[k * OUT_ROWS : (k + 1) * OUT_ROWS, i * D : (i + 1) * D] = total[rows].astype(F32)
        out[k * OUT_ROWS : (k + 1) * OUT_ROWS] = total[at + UP_ROWS : at + FIRST].astype(F32)
        down[k * DOWN_ROWS : (k + 1) * DOWN_ROWS] = total[at + FIRST : at + ROWS].astype(F32)


def unpack(total):
    block = lambda i: (i, 0)
    return pl.pallas_call(
        unpack_kernel,
        out_shape=[shape((HC, FF), F32), shape((HC, D), F32), shape((D, D), F32)],
        grid=(4,),
        in_specs=[pl.BlockSpec((4 * ROWS, D), block)],
        out_specs=[
            pl.BlockSpec((4 * OUT_ROWS, FF), block),
            pl.BlockSpec((4 * OUT_ROWS, D), block),
            pl.BlockSpec((4 * DOWN_ROWS, D), block),
        ],
        compiler_params=params(24),
        cost_estimate=cost(0, 14 * MB),
        name="unpack",
    )(total)


LATE = 3 * D + 2 * HC
EARLY = 3 * D + NB + 256


def arrange_kernel(row_ref, a0, a1, a2, a3, late, far, out):
    row = row_ref[0]
    for j, a in enumerate((a0, a1, a2, a3)):
        for s in range(3):
            lanes = pl.ds(pl.multiple_of(s * D + (row ^ j) * HC, HC), HC)
            out[:, lanes] = a[:, s * HC : (s + 1) * HC]
    both = jnp.concatenate([late[...].astype(F32), far[...].astype(F32)], axis=0)
    out[:, 3 * D :] = both.astype(BF16)


def arrange(row, pieces, late, far):
    rows = pieces[0].shape[0]
    return pl.pallas_call(
        arrange_kernel,
        out_shape=shape((rows, 3 * D + LATE)),
        grid_spec=pltpu.PrefetchScalarGridSpec(
            num_scalar_prefetch=1,
            grid=(1,),
            in_specs=[whole((rows, 3 * HC))] * 4 + [whole((8, LATE))] * 2,
            out_specs=whole((rows, 3 * D + LATE)),
        ),
        compiler_params=params(16),
        cost_estimate=cost(0, 8 * rows * D),
        name="arrange",
    )(row, *pieces, late, far)


def stack_kernel(a0, a1, a2, a3, weights, sums):
    for k, a in enumerate((a0, a1, a2, a3)):
        weights[k] = a[:, : 3 * D]
        sums[k] = a[:, 3 * D :]


def stack(pieces):
    rows, width = pieces[0].shape
    return pl.pallas_call(
        stack_kernel,
        out_shape=[shape((4, rows, 3 * D)), shape((4, rows, LATE))],
        grid=(1,),
        in_specs=[whole((rows, width))] * 4,
        out_specs=[whole((4, rows, 3 * D)), whole((4, rows, LATE))],
        compiler_params=params(16),
        cost_estimate=cost(0, 2 * MB),
        name="stack",
    )(*pieces)


def place_kernel(index_ref, low, high, out):
    for m, a in enumerate((low.at[0], low.at[1], high.at[1], high.at[0])):

        @pl.when(pl.program_id(0) == m)
        def _():
            for k in range(4):
                out[0, index_ref[1] ^ k] = a[k].astype(F32)


def place(index, low, high):
    rows = low.shape[2]
    return pl.pallas_call(
        place_kernel,
        out_shape=shape((4, 4, rows, 3 * D), F32),
        grid_spec=pltpu.PrefetchScalarGridSpec(
            num_scalar_prefetch=1,
            grid=(4,),
            in_specs=[whole(low.shape)] * 2,
            out_specs=pl.BlockSpec((1, 4, rows, 3 * D), lambda i, index: (index[0] ^ i, 0, 0, 0)),
        ),
        compiler_params=params(24),
        cost_estimate=cost(0, 24 * rows * D),
        name="place",
    )(index, low, high).reshape(HC, 3 * D)


def project_back_kernel(row_ref, dq, dk, dv, rk, rv, w0, w1, w2, w3, cp, sp, fr, dp, h0, h2, hs, bsum):
    row = row_ref[0]
    f = pl.program_id(0)
    later = (f > 0).astype(F32)
    keys = dk[0] + later * rk[0, 0].astype(F32)
    values = dv[0] + later * rv[0, 0].astype(F32)
    cosine, sine = cosines(cp, sp, fr, f)
    dp[0, :, :HC] = dq[0]
    dp[0, :, HC : 2 * HC] = turn(keys, cosine, -sine).astype(BF16)
    dp[0, :, 2 * HC :] = values.astype(BF16)
    grad = dp[0]
    sums = jnp.sum(grad.astype(F32), axis=0, keepdims=True)

    @pl.when(f == 0)
    def _():
        bsum[...] = jnp.zeros_like(bsum)

    number = lax.broadcasted_iota(jnp.int32, (8, 2 * HC), 0)
    bsum[...] = bsum[...] + jnp.where(number == row, sums[:, : 2 * HC], 0.0)
    bsum[:, :HC] = bsum[:, :HC] + jnp.where(number[:, :HC] == row + 4, sums[:, 2 * HC :], 0.0)
    for j, w in enumerate((w0, w1, w2, w3)):
        part = nt(grad, w[...]).astype(BF16)
        at = (0, slice(None), columns(row, j))
        h0[at] = part[:PR]
        hs[(0,) + at] = part[PR : 2 * PR]
        h2[at] = part[2 * PR : 3 * PR]
        hs[(1,) + at] = part[3 * PR :]


def project_back(row, dq, dk, dv, returned, weights, tables):
    block = pl.BlockSpec((1, TOK, HC), lambda f, *_: (f, 0, 0))
    late = [
        pl.BlockSpec((1, 1, TOK, HC), lambda f, *_, i=i: (i, jnp.maximum(f - 1, 0), 0, 0))
        for i in range(2)
    ]
    piece = pl.BlockSpec((1, PR, D), lambda f, *_: (f, 0, 0))
    return pl.pallas_call(
        project_back_kernel,
        out_shape=[
            shape((FPD, TOK, 3 * HC)),
            shape((FPD, PR, D)),
            shape((FPD, PR, D)),
            shape((2, FPD, PR, D)),
            shape((8, 2 * HC), F32),
        ],
        grid_spec=pltpu.PrefetchScalarGridSpec(
            num_scalar_prefetch=1,
            grid=(FPD,),
            in_specs=[block] * 3
            + late
            + [whole((HC, 3 * HC))] * 4
            + [whole((TOK, HC)), whole((TOK, HC)), whole((16, 2 * HC))],
            out_specs=[
                pl.BlockSpec((1, TOK, 3 * HC), lambda f, *_: (f, 0, 0)),
                piece,
                piece,
                pl.BlockSpec((2, 1, PR, D), lambda f, *_: (0, f, 0, 0)),
                whole((8, 2 * HC)),
            ],
        ),
        compiler_params=params(20),
        cost_estimate=cost(2 * FPD * TOK * D * 3 * HC, 14 * MB),
        name="project_back",
    )(row, dq, dk, dv, returned, returned, *weights, *tables)


def weight_kernel(row_ref, h, dp, w):
    w[0] = tn(h[...], dp[...]).astype(BF16)


def project_weight(row, hidden, dproj):
    tokens = FPD * TOK
    return pl.pallas_call(
        weight_kernel,
        out_shape=shape((4, HC, 3 * HC)),
        grid_spec=pltpu.PrefetchScalarGridSpec(
            num_scalar_prefetch=1,
            grid=(4,),
            in_specs=[
                pl.BlockSpec((tokens, HC), lambda j, row: (0, row[0] ^ j)),
                whole((tokens, 3 * HC)),
            ],
            out_specs=pl.BlockSpec((1, HC, 3 * HC), lambda j, row: (j, 0, 0)),
        ),
        compiler_params=params(20),
        cost_estimate=cost(2 * tokens * D * 3 * HC, 9 * MB),
        name="project_weight",
    )(row, hidden.reshape(tokens, D), dproj.reshape(tokens, 3 * HC))


def input_back_kernel(x, h0, near, far, table, mg, bsum, gate, out, sums):
    grad = h0[...].astype(F32) + near[0].astype(F32) + far[...].astype(F32)
    normal, rate = norm(x[...].astype(F32))
    put_half(sums, 0, jnp.sum(grad, axis=1))
    put_half(sums, D, jnp.sum(grad * normal, axis=1))
    sums[:, 2 * D : 3 * D] = gate[...]
    sums[:, 3 * D :] = bsum[...]
    out[...] = mg[...] + norm_back(normal, rate, grad * (1.0 + segment(table, 1)))


def input_back(x, h0, near, far, table, mg, bsum, gate):
    return pl.pallas_call(
        input_back_kernel,
        out_shape=[shape((FPD, PR, D), F32), shape((8, LATE), F32)],
        grid=(FPD // HALF,),
        in_specs=[half_spec(D)] * 2
        + [pl.BlockSpec((1, HALF, PR, D), lambda i: (0, i, 0, 0))]
        + [half_spec(D), whole((FPD, WIDE)), half_spec(D), whole((8, 2 * HC)), whole((8, D))],
        out_specs=[half_spec(D), whole((8, LATE))],
        compiler_params=params(20),
        cost_estimate=cost(20 * 512 * D, 10 * MB),
        name="input_back",
    )(x, h0, near, far, table, mg, bsum, gate)


def join_kernel(a0, a1, a2, a3, out):
    for k, a in enumerate((a0, a1, a2, a3)):
        out[2 * k : 2 * k + 2] = a[...]


def join(pieces):
    width = pieces[0].shape[-1]
    return pl.pallas_call(
        join_kernel,
        out_shape=shape((8, 8, width)),
        grid=(1,),
        in_specs=[whole((2, 8, width))] * 4,
        out_specs=whole((8, 8, width)),
        compiler_params=params(16),
        cost_estimate=cost(0, 2 * MB),
        name="join",
    )(*pieces)


def final_kernel(row_ref, *refs):
    row = row_ref[0]
    low, high, *early = refs[:6]
    ada, ab, qb, ob, ub, db, asum = refs[6:]
    late = [low.at[0], low.at[1], high.at[0], high.at[1]]
    early = [early[0], early[3], early[1], early[2]]

    def rows(ref, cols):
        value = ref[:, :, cols].astype(F32)
        return value.reshape(64, value.shape[-1])

    left = [rows(s, slice(EARLY, EARLY + HC)).astype(BF16) for s in early]
    for segment in range(6):
        source, start = ((late, 0), (late, 1), (early, 0), (early, 1), (early, 2), (late, 2))[segment]
        cols = slice(start * D, (start + 1) * D)
        product, total = 0.0, 0.0
        for s, ref in zip(left, source):
            right = rows(ref, cols)
            total = total + jnp.sum(right, axis=0, keepdims=True)
            product = product + tn(s, right.astype(BF16))
        at = segment * D
        ada[:, at : at + D] = product
        asum[0:1, at : at + D] = total

    def fold8(value):
        value = jnp.sum(value, axis=0)
        return value if value.shape[0] == 8 else value[:8] + value[8:]

    def bias(source, start, stop):
        return sum(
            fold8(ref[:, :, start:stop].astype(F32)) for ref in source
        )

    ab[...] = asum[0:1, pl.ds(pl.multiple_of(row * 1536, 512), 1536)]
    folded = bias(late, 3 * D, LATE)
    for i in range(3):
        chunk = 3 * row + i
        at = jnp.where(chunk < 4, chunk, chunk - 4)
        second = (chunk >= 4) & (chunk < 8)
        value = jnp.where(second, folded[:, HC:], folded[:, :HC])
        qb[:, i * HC : (i + 1) * HC] = take(value, at)
    folded = bias(early, 3 * D, EARLY)
    for i in range(2):
        at = 2 * row + i
        ub[:, i * NB : (i + 1) * NB] = take(folded[:, :NB], at)
        db[:, i * 128 : (i + 1) * 128] = take(folded[:, NB : NB + 128], at)
        ob[:, i * 128 : (i + 1) * 128] = take(folded[:, NB + 128 :], at)


def final_sums(row, late, early):
    sizes = (1536, 768, 256, 1024, 256)
    return pl.pallas_call(
        final_kernel,
        out_shape=[shape((HC, 6 * D), F32)] + [shape((1, n), F32) for n in sizes],
        grid_spec=pltpu.PrefetchScalarGridSpec(
            num_scalar_prefetch=1,
            grid=(1,),
            in_specs=[whole((2, 4, 16, LATE))] * 2
            + [whole((8, 8, EARLY + HC))] * 4,
            out_specs=[whole((HC, 6 * D))] + [whole((1, n)) for n in sizes],
            scratch_shapes=[pltpu.VMEM((8, 6 * D), F32)],
        ),
        compiler_params=params(28),
        cost_estimate=cost(2 * 256 * HC * 6 * D, 10 * MB),
        name="final_sums",
    )(row, *late, *early)


def row_sum(value):
    value = value + swap(value, CORE)
    return value + swap(value, DIRECT)


def row_pieces(value):
    return [value, swap(value, CORE), swap(value, DIRECT), swap(value, DIRECT ^ CORE)]


def by_row(pieces, row):
    a, b, c, d = pieces
    odd, high = row % 2 == 1, row >= 2
    a, b = jnp.where(odd, b, a), jnp.where(odd, a, b)
    c, d = jnp.where(odd, d, c), jnp.where(odd, c, d)
    return jnp.stack(
        [
            jnp.where(high, c, a),
            jnp.where(high, d, b),
            jnp.where(high, a, c),
            jnp.where(high, b, d),
        ]
    )


def quarter_rows(value, bit, index, axis):
    rows = value.shape[1] // 4
    at = lambda m: lax.dynamic_slice_in_dim(value, (index[axis] ^ m) * rows, rows, 1)
    return [at(0)] + [swap(at(m), bit * m) for m in (1, 2, 3)]


def add_all(parts):
    return sum(part.astype(F32) for part in parts).astype(BF16)


def exchange_rows(value, bit, index, axis):
    return add_all(quarter_rows(value, bit, index, axis))


def turn_heads(own, beside, across, order=lambda piece: piece):
    across = swap(across, DIRECT)
    return [own, swap(beside, CORE), across[0], swap(order(across)[1], CORE)]


def per_device(
    activations,
    noise_embed,
    frame_position,
    cotangent,
    ada_weight,
    ada_bias,
    qkv_weight,
    qkv_bias,
    out_weight,
    out_bias,
    up_weight,
    up_bias,
    down_weight,
    down_bias,
):
    row = lax.axis_index(("xl", "c")).astype(jnp.int32)
    row_arg = row.reshape(1)
    index = [lax.axis_index("y").astype(jnp.int32), lax.axis_index("z").astype(jnp.int32)]
    index_arg = jnp.stack(index)

    x0 = activations
    x2 = swap(x0, DIRECT)
    x1 = swap(x0, CORE)
    p0 = shift(activations[1:], 1)
    biases = (ada_bias, qkv_bias, out_bias, up_bias, down_bias)
    heads = list(split_heads(row_arg, qkv_weight))
    noise, heads[1] = lax.optimization_barrier((noise_embed, heads[1]))
    part, silu_own, *tables = prepare(row_arg, frame_position, noise, ada_weight, biases)
    across = swap(heads[2], OTHER)
    qkv_pieces = [heads[0], swap(heads[1], CORE), across]
    part = part + swap(part, CORE)
    table = part + swap(part, DIRECT)
    x2, p0, table, *qkv_pieces = lax.optimization_barrier((x2, p0, table, *qkv_pieces))

    qkv_pieces = qkv_pieces[:2] + [qkv_pieces[2][0], swap(qkv_pieces[2][1], CORE)]
    x3 = swap(x2, CORE)
    p2 = swap(p0, DIRECT)
    p1 = swap(p0, CORE)
    before_mods = shift(table[:, : 2 * D], 1)

    out_own, up_own, _ = lax.optimization_barrier((out_weight, up_weight, table))
    outs2 = swap(out_own, OTHER)
    ups2 = swap(up_own, OTHER)

    hidden1, q, k, v = project(True, row_arg, (x0, x1, x2, x3), table, table, qkv_pieces, tables)
    down_own, q, before_mods = lax.optimization_barrier((down_weight, q, before_mods))
    downs2 = swap(down_own, DIRECT)
    state = attend(True, frame_position, q, k, v)
    p2, *state = lax.optimization_barrier((p2, *state))
    p3 = swap(p2, CORE)
    kp, vp = project(
        False, row_arg, (p0, p1, p2, p3), table, before_mods, qkv_pieces, tables
    )
    *mixed, lse = attend(False, frame_position, q, kp, vp, state)
    outs2, ups2, downs2, lse = lax.optimization_barrier((outs2, ups2, downs2, lse))
    outs = [out_weight, swap(out_own, CORE), outs2, swap(outs2, CORE)]
    ups = [up_weight, swap(up_own, CORE), ups2, swap(ups2, CORE)]
    downs = [down_weight, swap(down_own, CORE), downs2, swap(downs2, CORE)]
    turned = turn_heads(*mixed)
    branch, middle, hidden2, down_grad, dsum = mid(turned, outs, table, x0, cotangent)
    h2 = hidden2.reshape(TOKENS, D)
    dg = down_grad.reshape(TOKENS, D)
    act, upg, hg, usum = feed(row_arg, h2, dg, ups, table, downs)
    mg, bg, *ag, early = mid_back(
        hg.reshape(FPD, PR, D), middle, branch, cotangent, table, outs, usum, dsum
    )
    late = []
    back = turn_heads(*ag[:2], ag[2], order=lambda piece: late.append(piece) or piece)[:2]

    early = early + swap(early, CORE)
    upg, early, _ = lax.optimization_barrier((upg, early, bg))
    early_far = swap(early, DIRECT)
    uk, us = up_weight_grad(row_arg, h2, upg)
    us = swap(us, CORE)
    dg_later, early_far, uk = lax.optimization_barrier((dg, early_far, uk))
    early = jnp.concatenate([(early + early_far).astype(BF16), silu_own], axis=1)
    early_far = swap(early, FAR)
    ds_part, dn = down_half(True, dg_later, act, (downs[1], downs[3]))
    ds_part_far = swap(ds_part, CORE)
    dn, early, early_far, bg_later, us, far_back, *back = lax.optimization_barrier(
        (dn, early, early_far, bg, us, *late, *back)
    )
    early = jnp.stack([early, early_far])
    early_parts = [early] + [swap(early, m) for m in (16, 32, 48)]
    ok, os = out_weight_grad(turned, bg_later)
    os = swap(os, CORE)
    dk_part, layer_output, gate = down_half(
        False, dg_later, act, (downs[0], downs[2]), (dn, table, middle, cotangent)
    )
    dk_part, early_parts, ds_part_far, os, far_back = lax.optimization_barrier(
        (dk_part, early_parts, ds_part_far, os, far_back)
    )
    back += [far_back[0], swap(far_back[1], CORE)]
    packed = core_sum((uk, us), (dk_part, ds_part_far), (ok, os))
    packed, back = lax.optimization_barrier((packed, back))
    scattered = lax.psum_scatter(packed, ("y", "z"), scatter_dimension=1, tiled=True)

    dq_before, both = attend_back(False, frame_position, q, kp, vp, back, mixed, lse)
    returned = shift(both, -1)
    dq, dk, dv = attend_back(
        True, frame_position, q, k, v, back, mixed, lse, tables, dq_before
    )
    early_parts, dq = lax.optimization_barrier((early_parts, dq))
    early = join(early_parts)
    early_all = [early] + [swap(early, m) for m in (4, 8, 12)]
    dq, early = lax.optimization_barrier((dq, early))
    early = early[0].astype(F32)

    dproj, h0, h2_part, send, bsum = project_back(row_arg, dq, dk, dv, returned, qkv_pieces, tables)
    near = swap(send, CORE)
    qkv_parts = project_weight(row_arg, hidden1, dproj)
    far_part = (h2_part.astype(F32) + near[1].astype(F32)).astype(BF16)
    far = swap(far_part, DIRECT)
    far_part, qkv_parts, *early_all = lax.optimization_barrier((far_part, qkv_parts, *early_all))
    quarters = quarter_rows(qkv_parts, 4, index, 0)
    input_grad, late = input_back(x0, h0, near, far, table, mg, bsum, gate)
    late_near = swap(late, CORE)
    late, *quarters = lax.optimization_barrier((late, *quarters))
    quarters = quarter_rows(add_all(quarters), 16, index, 1)
    late = late + late_near
    late_far = swap(late, DIRECT)
    late, *quarters = lax.optimization_barrier((late, *quarters))
    qkv_parts = add_all(quarters)
    qkv_far = swap(qkv_parts, FAR)
    scattered, late, late_far, qkv_parts = lax.optimization_barrier(
        (scattered, late, late_far, qkv_parts)
    )
    late = late + late_far
    late_low = late.astype(BF16)
    late_far = swap(late_low, FAR)
    share_far = swap(scattered[1], DIRECT)
    late_low, qkv_far = lax.optimization_barrier((late_low, qkv_far))
    qkv_parts = add_all([qkv_parts, qkv_far])
    turned = turn_heads(qkv_parts[0], qkv_parts[1], qkv_parts[2:])
    turned, share_far = lax.optimization_barrier((turned, share_far))
    share = scattered[0].astype(F32) + share_far.astype(F32)
    share_far = swap(share.astype(BF16), FAR)
    last = arrange(row_arg, turned, late_low, late_far)

    share, share_far, last = lax.optimization_barrier((share, share_far, last))
    share = (share + share_far.astype(F32)).astype(BF16)
    totals = lax.all_gather(share, ("y", "z"), axis=0, tiled=True)
    weights, sums_late = stack([last] + [swap(last, m) for m in (16, 32, 48)])
    weights = jnp.stack([weights, swap(weights, 4)])
    sums_late = jnp.stack([sums_late, swap(sums_late, 12)])
    weights_far, sums_far = swap(weights, 12), swap(sums_late, 4)
    up_total, out_total, down_total = unpack(totals)
    qkv_total = place(index_arg, weights, weights_far)

    ada_total, *bias_sums = final_sums(row_arg, (sums_late, sums_far), early_all)
    ada_sum, qkv_sum, out_sum, up_sum, down_sum = [b[0] for b in bias_sums]
    mod_own = jnp.concatenate(
        [late[:, : 2 * D], early[:, : 3 * D], late[:, 2 * D : 3 * D]], axis=1
    ).astype(BF16)
    silu_grad = nt(mod_own, ada_weight)
    silu_grad = by_row(row_pieces(silu_grad), row).transpose(1, 0, 2).reshape(FPD, D)
    embed = noise_embed.astype(F32)
    sigma = jax.nn.sigmoid(embed)
    embed_grad = silu_grad * (sigma * (1.0 + embed * (1.0 - sigma)))

    return (
        layer_output,
        input_grad,
        embed_grad,
        ada_total,
        ada_sum,
        qkv_total,
        qkv_sum,
        out_total,
        out_sum,
        up_total,
        up_sum,
        down_total,
        down_sum,
    )


def solution(mesh):
    fine = Mesh(mesh.devices.reshape(2, 4, 4, 2, 2), AXES)
    seq, row = ("xh", "z", "y"), ("xl", "c")
    token, weight, vector = P(seq, row, None), P(row, None), P(row)
    in_specs = (token, P(seq, None), P(seq), token) + (weight, vector) * 5
    out_specs = (token, token, P(seq, None)) + (weight, vector) * 5
    return jax.shard_map(
        per_device, mesh=fine, in_specs=in_specs, out_specs=out_specs, check_vma=False
    )
```

```python
import math

import jax
import jax.numpy as jnp
from jax import lax
from jax.experimental import pallas as pl
from jax.experimental.pallas import tpu as pltpu
from jax.sharding import Mesh, PartitionSpec as P

F32 = jnp.float32
BF16 = jnp.bfloat16
HD = 64
GRID = 16
FPD = 8
PR = 64
D = 1024
FF = 4096
HC = 256
TOK = 256
PREV = 7
AXES = ("xh", "z", "y", "xl", "c")
CORE, DIRECT, OTHER, FAR = 1, 2, 66, 64
MB = 1024 * 1024


def swap(value, mask):
    return lax.ppermute(value, AXES, [(i, i ^ mask) for i in range(128)])


def shift(value, steps):
    return lax.ppermute(value, AXES, [(i, (i + 4 * steps) % 128) for i in range(128)])


def after(value, *others):
    return lax.optimization_barrier((value,) + others)[0]


def nt(left, right):
    return lax.dot_general(left, right, (((1,), (1,)), ((), ())), preferred_element_type=F32)


def tn(left, right):
    return lax.dot_general(left, right, (((0,), (0,)), ((), ())), preferred_element_type=F32)


def nn(left, right):
    return jnp.dot(left, right, preferred_element_type=F32)


def norm(values):
    center = values - jnp.mean(values, axis=-1, keepdims=True)
    spread = jnp.mean(center * center, axis=-1, keepdims=True)
    rate = lax.rsqrt(spread + 1e-06)
    return center * rate, rate


def norm_back(normal, rate, grad):
    mean_grad = jnp.mean(grad, axis=-1, keepdims=True)
    mean_both = jnp.mean(grad * normal, axis=-1, keepdims=True)
    return rate * (grad - mean_grad - normal * mean_both)


def turn(values, cosine, sine):
    lanes = lax.broadcasted_iota(jnp.int32, values.shape, 1)
    other = jnp.where(
        lanes % HD < HD // 2, pltpu.roll(values, HC - HD // 2, 1), pltpu.roll(values, HD // 2, 1)
    )
    return values * cosine + other * sine


def params(mib):
    return pltpu.CompilerParams(vmem_limit_bytes=mib * MB)


def cost(flops, moved, exps=0):
    return pl.CostEstimate(flops=int(flops), bytes_accessed=int(moved), transcendentals=int(exps))


def whole(shape):
    return pl.BlockSpec(shape, lambda i, *_: (0,) * len(shape))


def columns(row, j):
    return pl.ds(pl.multiple_of((row ^ j) * HC, HC), HC)


def shape(dims, kind=BF16):
    return jax.ShapeDtypeStruct(dims, kind)


UB, QB, OB, DB, WIDE = 6144, 6656, 7168, 7296, 7424


def put(ref, start, at, value):
    cols = slice(start, start + value.shape[1])
    number = lax.broadcasted_iota(jnp.int32, (8, value.shape[1]), 0)
    ref[:, cols] = jnp.where(number == at, value, ref[:, cols])


def take(value, at):
    number = lax.broadcasted_iota(jnp.int32, value.shape, 0)
    return jnp.sum(jnp.where(number == at, value, 0.0), axis=0, keepdims=True)


def put_half(ref, start, value):
    cols = slice(start, start + value.shape[1])
    number = lax.broadcasted_iota(jnp.int32, (8, value.shape[1]), 0)
    both = jnp.concatenate([value, value], axis=0)
    ref[:, cols] = jnp.where(number // 4 == pl.program_id(0), both, ref[:, cols])


def unfold(ref, start, width):
    return jnp.concatenate([ref[i : i + 1, start : start + width] for i in range(8)], axis=1)


def prepare_kernel(row_ref, pos_ref, noise, ada, ab, qb, ob, ub, db, pack, silu, cp, sp, frames):
    row = row_ref[0]
    embed = noise[...].astype(F32)
    value = (embed / (1.0 + jnp.exp(-embed))).astype(BF16)
    own = jnp.where(
        row < 2,
        jnp.where(row == 0, value[:, :HC], value[:, HC : 2 * HC]),
        jnp.where(row == 2, value[:, 2 * HC : 3 * HC], value[:, 3 * HC :]),
    )
    silu[...] = own
    pack[:, UB:] = jnp.zeros((FPD, WIDE - UB), F32)
    for segment in range(6):
        cols = slice(segment * D, (segment + 1) * D)
        pack[:, cols] = nn(own, ada[:, cols])
    bias = pl.ds(pl.multiple_of(row * 1536, 512), 1536)
    pack[:, bias] = pack[:, bias] + ab[...].astype(F32)
    for i in range(2):
        at = 2 * row + i
        put(pack, UB, at, ub[:, i * 512 : (i + 1) * 512].astype(F32))
        put(pack, OB, at, ob[:, i * 128 : (i + 1) * 128].astype(F32))
        put(pack, DB, at, db[:, i * 128 : (i + 1) * 128].astype(F32))
    for i in range(3):
        chunk = 3 * row + i
        at = jnp.where(chunk < 4, chunk, chunk - 4)
        second = (chunk >= 4) & (chunk < 8)
        value = qb[:, i * HC : (i + 1) * HC].astype(F32)
        put(pack, QB, jnp.where(second, -1, at), value)
        put(pack, QB + HC, jnp.where(second, at, -1), value)

    def parts(dims):
        lane = lax.broadcasted_iota(jnp.int32, dims, 1)
        index = lane % (HD // 2)
        quarter, eighth = HD // 4, HD // 8
        in_frame = index < quarter
        in_row = (index >= quarter) & (index < quarter + eighth)
        offset = jnp.where(
            in_frame, index, jnp.where(in_row, index - quarter, index - quarter - eighth)
        ).astype(F32)
        length = jnp.where(in_frame, 1.0 * quarter, 1.0 * eighth)
        frequency = jnp.exp(-math.log(10000.0) * offset / length)
        sign = jnp.where(lane % HD < HD // 2, -1.0, 1.0)
        return in_frame, in_row, frequency, sign

    in_frame, in_row, frequency, sign = parts((TOK, HC))
    slot = lax.broadcasted_iota(jnp.int32, (TOK, HC), 0)
    patch = ((slot // PR) ^ row) * PR + slot % PR
    angle = jnp.where(in_row, patch // GRID, patch % GRID).astype(F32) * frequency
    cp[...] = jnp.where(in_frame, 0.0, jnp.cos(angle))
    sp[...] = jnp.where(in_frame, 0.0, jnp.sin(angle) * sign)
    in_frame, _, frequency, sign = parts((16, HC))
    slot = lax.broadcasted_iota(jnp.int32, (16, HC), 0)
    place = pos_ref[0] - PREV + (slot - FPD)
    for f in range(FPD):
        place = jnp.where(slot == f, pos_ref[f], place)
    angle = place.astype(F32) * frequency
    frames[:, :HC] = jnp.where(in_frame, jnp.cos(angle), 0.0)
    frames[:, HC:] = jnp.where(in_frame, jnp.sin(angle) * sign, 0.0)


def prepare(row, places, noise, ada, biases):
    return pl.pallas_call(
        prepare_kernel,
        out_shape=[
            shape((FPD, WIDE), F32),
            shape((FPD, HC)),
            shape((TOK, HC), F32),
            shape((TOK, HC), F32),
            shape((16, 2 * HC), F32),
        ],
        grid_spec=pltpu.PrefetchScalarGridSpec(
            num_scalar_prefetch=2,
            grid=(1,),
            in_specs=[whole((FPD, D)), whole((HC, 6 * D))]
            + [whole((1, b.shape[0])) for b in biases],
            out_specs=[
                whole((FPD, WIDE)),
                whole((FPD, HC)),
                whole((TOK, HC)),
                whole((TOK, HC)),
                whole((16, 2 * HC)),
            ],
        ),
        compiler_params=params(24),
        cost_estimate=cost(2 * 8 * HC * 6 * D, 4 * MB, 4 * TOK * HC),
        name="prepare",
    )(row, places, noise, ada, *[b[None] for b in biases])


def split_heads_kernel(row_ref, q, k, v, p0, p1, p23):
    for j, p in enumerate((p0, p1, p23.at[0], p23.at[1])):

        @pl.when(pl.program_id(0) == j)
        def _():
            p[:, :HC] = q[...]
            p[:, HC : 2 * HC] = k[...]
            p[:, 2 * HC :] = v[...]


def split_heads(row, weight):
    piece = (HC, 3 * HC)
    return pl.pallas_call(
        split_heads_kernel,
        out_shape=[shape(piece), shape(piece), shape((2,) + piece)],
        grid_spec=pltpu.PrefetchScalarGridSpec(
            num_scalar_prefetch=1,
            grid=(4,),
            in_specs=[
                pl.BlockSpec((HC, HC), lambda j, row, s=s: (0, 4 * s + (row[0] ^ j)))
                for s in range(3)
            ],
            out_specs=[whole(piece), whole(piece), whole((2,) + piece)],
        ),
        compiler_params=params(12),
        cost_estimate=cost(0, 3 * MB),
        name="split_heads",
    )(row, weight, weight, weight)


def cosines(cp, sp, frames, at):
    both = frames[pl.ds(at, 1), :]
    return cp[...] + both[:, :HC], sp[...] + both[:, HC:]


def project_kernel(own, row_ref, x0, x1, x2, x3, table, mods, w0, w1, w2, w3, cp, sp, fr, *outs):
    row = row_ref[0]
    f = pl.program_id(0)
    if own:
        h_ref, q_ref, k_ref, v_ref = outs
        first, at, angle = 0, f, f
    else:
        k_ref, v_ref, h_ref = outs
        first, at, angle = HC, f + FPD - PREV, f + FPD
    x = jnp.concatenate([r[0] for r in (x0, x1, x2, x3)], axis=0).astype(F32)
    normal, _ = norm(x)
    shift_row = mods[pl.ds(at, 1), :D]
    scale_row = mods[pl.ds(at, 1), D : 2 * D]
    hidden = (normal * (1.0 + scale_row) + shift_row).astype(BF16)
    where = (0,) if own else ()
    h_ref[where + (slice(None), slice(None))] = hidden
    low, high = table[pl.ds(row, 1), QB : QB + 2 * HC], table[pl.ds(row + 4, 1), QB : QB + HC]
    total = jnp.concatenate([low, high], axis=1)[:, first:]
    for j, w in enumerate((w0, w1, w2, w3)):
        total = total + nn(h_ref[where + (slice(None), columns(row, j))], w[:, first:])
    cosine, sine = cosines(cp, sp, fr, angle)
    if own:
        q_ref[0] = (turn(total[:, :HC], cosine, sine).astype(BF16).astype(F32) * 0.125).astype(BF16)
        total = total[:, HC:]
    k_ref[0] = turn(total[:, :HC], cosine, sine).astype(BF16)
    v_ref[0] = total[:, HC:].astype(BF16)


def project(own, row, xs, table, mods, weights, tables):
    frames = xs[0].shape[0]
    x_spec = pl.BlockSpec((1, PR, D), lambda f, *_: (f, 0, 0))
    out_spec = pl.BlockSpec((1, TOK, HC), lambda f, *_: (f, 0, 0))
    out = shape((frames, TOK, HC))
    if own:
        out_specs = [pl.BlockSpec((1, TOK, D), lambda f, *_: (f, 0, 0)), out_spec, out_spec, out_spec]
        out_shape = [shape((frames, TOK, D)), out, out, out]
        scratch = []
    else:
        out_specs = [out_spec, out_spec]
        out_shape = [out, out]
        scratch = [pltpu.VMEM((TOK, D), BF16)]
    return pl.pallas_call(
        lambda *refs: project_kernel(own, *refs),
        out_shape=out_shape,
        grid_spec=pltpu.PrefetchScalarGridSpec(
            num_scalar_prefetch=1,
            grid=(frames,),
            in_specs=[x_spec] * 4
            + [whole((FPD, WIDE)), whole(mods.shape)]
            + [whole((HC, 3 * HC))] * 4
            + [whole((TOK, HC)), whole((TOK, HC)), whole((16, 2 * HC))],
            out_specs=out_specs,
            scratch_shapes=scratch,
        ),
        compiler_params=params(20),
        cost_estimate=cost(2 * frames * TOK * D * 3 * HC, frames * TOK * D * 4 + 4 * MB),
        name="project_own" if own else "project_prev",
    )(row, *xs, table, mods, *weights, *tables)


def head_lanes():
    return lax.broadcasted_iota(jnp.int32, (TOK, HC), 1) // HD


def spread_queries(q, qs):
    lanes = head_lanes()
    query = q[0]
    for h in range(4):
        qs[pl.ds(h * TOK, TOK), :] = jnp.where(lanes == h, query, jnp.zeros_like(query))


def sweep_scores(low_at, high_at, k, qs, scores, top):
    def one(at, _):
        keys = k[at]
        for h in range(4):
            rows = pl.ds(h * TOK, TOK)
            s = nt(qs[rows, :], keys)
            scores[at - low_at, rows, :] = s
            top[rows, :] = jnp.maximum(top[rows, :], jnp.maximum(s[:, :128], s[:, 128:]))
        return 0

    lax.fori_loop(low_at, high_at, one, 0)
    for h in range(4):
        rows = pl.ds(h * TOK, TOK)
        top[rows, :] = jnp.broadcast_to(jnp.max(top[rows, :], axis=1, keepdims=True), (TOK, 128))


def sweep_values(low_at, high_at, v, scores, top, low, acc):
    low[...] = jnp.zeros_like(low)
    acc[...] = jnp.zeros_like(acc)

    def one(at, _):
        values = v[at]
        for h in range(4):
            rows = pl.ds(h * TOK, TOK)
            p = jnp.exp(scores[at - low_at, rows, :] - jnp.concatenate([top[rows, :]] * 2, axis=1))
            low[rows, :] = low[rows, :] + (p[:, :128] + p[:, 128:])
            acc[rows, :] = acc[rows, :] + nn(p.astype(BF16), values)
        return 0

    lax.fori_loop(low_at, high_at, one, 0)


def attend_own_kernel(pos_ref, q, k, v, mixed, stats, qs, scores, acc, top, low):
    f = pl.program_id(0)
    start = jnp.maximum(f - pos_ref[f], 0)
    spread_queries(q, qs)
    top[...] = jnp.full_like(top, -1e30)
    sweep_scores(start, f + 1, k, qs, scores, top)
    sweep_values(start, f + 1, v, scores, top, low, acc)
    lanes = head_lanes()
    narrow = lax.broadcasted_iota(jnp.int32, (TOK, 128), 1)
    result = jnp.zeros((TOK, HC), F32)
    state = jnp.zeros((TOK, 128), F32)
    for h in range(4):
        rows = pl.ds(h * TOK, TOK)
        result = jnp.where(lanes == h, acc[rows, :], result)
        state = jnp.where(narrow == h, top[rows, :], state)
        state = jnp.where(narrow == 4 + h, jnp.sum(low[rows, :], axis=1, keepdims=True), state)
    mixed[0] = result
    stats[0] = state


def attend_prev_kernel(
    pos_ref, q, k, v, mixed, stats, o0, o1, o23, lse, qs, scores, acc, top, low, result, logs
):
    f = pl.program_id(0)
    count = jnp.maximum(pos_ref[f] - f, 0)
    lanes = head_lanes()
    narrow = lax.broadcasted_iota(jnp.int32, (TOK, 128), 1)
    state = stats[0]

    def finish(part):
        total_mixed = jnp.zeros((TOK, HC), F32)
        total_logs = jnp.zeros((TOK, 128), F32)
        for h in range(4):
            largest, total, value = part(h, state[:, h : h + 1], state[:, 4 + h : 5 + h])
            total_mixed = jnp.where(lanes == h, value / total, total_mixed)
            total_logs = jnp.where(narrow == h, largest + jnp.log(total), total_logs)
        result[...] = total_mixed.astype(BF16)
        logs[...] = total_logs

    @pl.when(count == 0)
    def _():
        finish(lambda h, largest, total: (largest, total, mixed[0]))

    @pl.when(count > 0)
    def _():
        spread_queries(q, qs)
        for h in range(4):
            top[pl.ds(h * TOK, TOK), :] = jnp.broadcast_to(state[:, h : h + 1], (TOK, 128))
        sweep_scores(PREV - count, PREV, k, qs, scores, top)
        sweep_values(PREV - count, PREV, v, scores, top, low, acc)

        def part(h, largest, total):
            rows = pl.ds(h * TOK, TOK)
            most = top[rows, :1]
            fade = jnp.exp(largest - most)
            total = total * fade + jnp.sum(low[rows, :], axis=1, keepdims=True)
            return most, total, mixed[0] * fade + acc[rows, :]

        finish(part)

    lse[0] = logs[...].T[:8]
    o0[0] = result[:PR, :]
    o1[0] = result[PR : 2 * PR, :]
    o23[0, 0] = result[2 * PR : 3 * PR, :]
    o23[1, 0] = result[3 * PR :, :]


def attend(own, places, q, k, v, state=()):
    block = pl.BlockSpec((1, TOK, HC), lambda f, *_: (f, 0, 0))
    narrow = pl.BlockSpec((1, TOK, 128), lambda f, *_: (f, 0, 0))
    piece = pl.BlockSpec((1, PR, HC), lambda f, *_: (f, 0, 0))
    count = FPD if own else PREV
    scratch = [
        pltpu.VMEM((4 * TOK, HC), BF16),
        pltpu.VMEM((8, 4 * TOK, TOK), F32),
        pltpu.VMEM((4 * TOK, HC), F32),
        pltpu.VMEM((4 * TOK, 128), F32),
        pltpu.VMEM((4 * TOK, 128), F32),
    ]
    specs = [block] + [whole((count, TOK, HC))] * 2
    if own:
        out_shape = [shape((FPD, TOK, HC), F32), shape((FPD, TOK, 128), F32)]
        out_specs = [block, narrow]
    else:
        specs += [block, narrow]
        out_shape = [shape((FPD, PR, HC))] * 2 + [
            shape((2, FPD, PR, HC)),
            shape((FPD, 8, TOK), F32),
        ]
        out_specs = [piece] * 2 + [
            pl.BlockSpec((2, 1, PR, HC), lambda f, *_: (0, f, 0, 0)),
            pl.BlockSpec((1, 8, TOK), lambda f, *_: (f, 0, 0)),
        ]
        scratch += [pltpu.VMEM((TOK, HC), BF16), pltpu.VMEM((TOK, 128), F32)]
    return pl.pallas_call(
        attend_own_kernel if own else attend_prev_kernel,
        out_shape=out_shape,
        grid_spec=pltpu.PrefetchScalarGridSpec(
            num_scalar_prefetch=1,
            grid=(FPD,),
            in_specs=specs,
            out_specs=out_specs,
            scratch_shapes=scratch,
        ),
        compiler_params=params(40),
        cost_estimate=cost(
            (30 if own else 12) * 4 * 2 * 2 * TOK**3, 6 * MB, 30 * 4 * TOK * TOK
        ),
        name="attend_own" if own else "attend_prev",
    )(places, q, k, v, *state)


def attend_back_kernel(own, pos_ref, q, k, v, g0, g1, g2, g3, o0, o1, o23, lse, *rest):
    if own:
        cp, sp, fr, before_ref, dq, dk, dv, qs, gs, ks, pl_scr, dl_scr, ds_scr, dq_acc = rest
        dk_acc, dv_acc = dk, dv
    else:
        dq, both_ref, qs, gs, ks, pl_scr, dl_scr, ds_scr, dq_acc, dk_acc, dv_acc = rest
    f = pl.program_id(0)
    place = pos_ref[f]
    lanes = head_lanes()

    @pl.when(f == 0)
    def _():
        for ref in (dk_acc, dv_acc):
            ref[...] = jnp.zeros_like(ref)

    def prelude():
        query = q[0]
        grad = jnp.concatenate([r[0] for r in (g0, g1, g2, g3)], axis=0)
        mixed = jnp.concatenate([o0[0], o1[0], o23[0, 0], o23[1, 0]], axis=0)
        for h in range(4):
            rows = pl.ds(h * TOK, TOK)
            qs[rows, :] = jnp.where(lanes == h, query, jnp.zeros_like(query))
            gs[rows, :] = jnp.where(lanes == h, grad, jnp.zeros_like(grad))
        both = grad.astype(F32) * mixed.astype(F32)
        pick = (
            lax.broadcasted_iota(jnp.int32, (8, HC), 1) // HD
            == lax.broadcasted_iota(jnp.int32, (8, HC), 0)
        ).astype(F32)
        return lax.dot_general(
            pick, both, (((1,), (1,)), ((), ())),
            preferred_element_type=F32, precision=lax.Precision.HIGHEST,
        )

    def step(delta, logs, at):
        keys, values = k[at], v[at]
        for h in range(4):
            rows = pl.ds(h * TOK, TOK)
            ks[rows, :] = jnp.where(lanes == h, keys, jnp.zeros_like(keys))
            p = jnp.exp(nt(keys, qs[rows, :]) - logs[h : h + 1])
            ds = (p * (nt(values, gs[rows, :]) - delta[h : h + 1])).astype(BF16)
            pl_scr[:, rows] = p.astype(BF16)
            dl_scr[:, rows] = ds
            ds_scr[rows, :] = ds
        dv_acc[at] = dv_acc[at] + nn(pl_scr[...], gs[...])
        dk_acc[at] = dk_acc[at] + nn(dl_scr[...], qs[...])
        dq_acc[...] = dq_acc[...] + tn(ds_scr[...], ks[...])

    def sweep(low, high):
        delta = prelude()
        logs = lse[0]
        dq_acc[...] = jnp.zeros_like(dq_acc)

        def one(at, _):
            step(delta, logs, at)
            return 0

        lax.fori_loop(low, high, one, 0)

    if own:
        sweep(jnp.maximum(f - place, 0), f + 1)
        cosine, sine = cosines(cp, sp, fr, f)
        dq[0] = turn((dq_acc[...] + before_ref[0]) * 0.125, cosine, -sine).astype(BF16)
    else:
        count = jnp.maximum(place - f, 0)

        @pl.when(count > 0)
        def _():
            sweep(PREV - count, PREV)
            dq[0] = dq_acc[...]

        @pl.when(count == 0)
        def _():
            dq[0] = jnp.zeros_like(dq_acc)

        @pl.when(f == FPD - 1)
        def _():
            both_ref[0] = dk_acc[...].astype(BF16)
            both_ref[1] = dv_acc[...].astype(BF16)


def attend_back(own, places, q, k, v, grads, mixed, lse, tables=None, before=None):
    block = pl.BlockSpec((1, TOK, HC), lambda f, *_: (f, 0, 0))
    piece = pl.BlockSpec((1, PR, HC), lambda f, *_: (f, 0, 0))
    count = FPD if own else PREV
    wide = pltpu.VMEM((4 * TOK, HC), BF16)
    tall = pltpu.VMEM((TOK, 4 * TOK), BF16)
    scratch = [wide, wide, wide, tall, tall, wide, pltpu.VMEM((TOK, HC), F32)]
    specs = []
    extra = ()
    if own:
        specs = [whole((TOK, HC)), whole((TOK, HC)), whole((16, 2 * HC)), block]
        extra = tuple(tables) + (before,)
    else:
        scratch += [pltpu.VMEM((PREV, TOK, HC), F32)] * 2
    return pl.pallas_call(
        lambda *refs: attend_back_kernel(own, *refs),
        out_shape=[shape((FPD, TOK, HC), BF16 if own else F32)]
        + ([shape((FPD, TOK, HC), F32)] * 2 if own else [shape((2, PREV, TOK, HC))]),
        grid_spec=pltpu.PrefetchScalarGridSpec(
            num_scalar_prefetch=1,
            grid=(FPD,),
            in_specs=[block]
            + [whole((count, TOK, HC))] * 2
            + [piece] * 6
            + [pl.BlockSpec((2, 1, PR, HC), lambda f, *_: (0, f, 0, 0))]
            + [pl.BlockSpec((1, 8, TOK), lambda f, *_: (f, 0, 0))]
            + specs,
            out_specs=[block]
            + ([whole((FPD, TOK, HC))] * 2 if own else [whole((2, PREV, TOK, HC))]),
            scratch_shapes=scratch,
        ),
        compiler_params=params(58),
        cost_estimate=cost(1000 if own else 12 * 4 * 5 * 2 * TOK**3, 1000 if own else 12 * MB),
        name="attend_back_own" if own else "attend_back_prev",
    )(places, q, k, v, *grads, *mixed, lse, *extra)


HALF = 4
RAW = HALF * PR


def flat(ref):
    return ref[...].reshape(RAW, ref.shape[-1])


def frames_of(value):
    return value.reshape(HALF, PR, value.shape[-1])


def segment(table, s):
    both = table[:, s * D : (s + 1) * D]
    return jnp.where(pl.program_id(0) == 0, both[:HALF], both[HALF:])[:, None, :]


def fold(out, start, width, row):
    @pl.when(pl.program_id(0) == 0)
    def _():
        out[:, start : start + width] = jnp.zeros((8, width), F32)

    for i in range(8):
        at = (slice(i, i + 1), slice(start, start + width))
        out[at] = out[at] + row[:, i * width : (i + 1) * width]


def mid_kernel(o0, o1, o2, o3, w0, w1, w2, w3, table, x, cot, branch, middle, hidden, down, dsum):
    total = unfold(table, OB, 128)
    for o, w in zip((o0, o1, o2, o3), (w0, w1, w2, w3)):
        total = total + nn(flat(o), w[...])
    branched = frames_of(total)
    branch[...] = branched
    mid_value = x[...].astype(F32) + segment(table, 2) * branched
    middle[...] = mid_value
    normal, _ = norm(mid_value)
    hidden[...] = (normal * (1.0 + segment(table, 4)) + segment(table, 3)).astype(BF16)
    grad = (segment(table, 5) * cot[...].astype(F32)).astype(BF16)
    down[...] = grad
    fold(dsum, 0, 128, jnp.sum(grad.astype(F32).reshape(RAW, D), axis=0, keepdims=True))


def half_spec(width):
    return pl.BlockSpec((HALF, PR, width), lambda i, *_: (i, 0, 0))


def mid(pieces, weights, table, x, cot):
    return pl.pallas_call(
        mid_kernel,
        out_shape=[
            shape((FPD, PR, D), F32),
            shape((FPD, PR, D), F32),
            shape((FPD, PR, D)),
            shape((FPD, PR, D)),
            shape((8, 128), F32),
        ],
        grid=(FPD // HALF,),
        in_specs=[half_spec(HC)] * 4
        + [whole((HC, D))] * 4
        + [whole((FPD, WIDE)), half_spec(D), half_spec(D)],
        out_specs=[half_spec(D)] * 4 + [whole((8, 128))],
        compiler_params=params(26),
        cost_estimate=cost(2 * 512 * D * D, 12 * MB),
        name="mid",
    )(*pieces, *weights, table, x, cot)


def mid_back_kernel(
    hg, middle, branch, cot, table, w0, w1, w2, w3, usum, dsum, mg, bg, a0, a1, a23, sums
):
    grad = hg[...]
    normal, rate = norm(middle[...])
    put_half(sums, D, jnp.sum(grad, axis=1))
    put_half(sums, 2 * D, jnp.sum(grad * normal, axis=1))
    total = cot[...].astype(F32) + norm_back(normal, rate, grad * (1.0 + segment(table, 4)))
    mg[...] = total
    put_half(sums, 0, jnp.sum(total * branch[...], axis=1))
    low = (segment(table, 2) * total).astype(BF16)
    bg[...] = low
    low = low.reshape(RAW, D)
    sums[:, 3 * D : 3 * D + NB] = usum[...]
    sums[:, 3 * D + NB : 3 * D + NB + 128] = dsum[...]
    fold(sums, 3 * D + NB + 128, 128, jnp.sum(low.astype(F32), axis=0, keepdims=True))
    for j, w in enumerate((w0, w1, w2, w3)):
        value = frames_of(nt(low, w[...]).astype(BF16))
        if j < 2:
            (a0, a1)[j][...] = value
        else:
            a23[j - 2] = value


def mid_back(hg, middle, branch, cot, table, weights, usum, dsum):
    return pl.pallas_call(
        mid_back_kernel,
        out_shape=[shape((FPD, PR, D), F32), shape((FPD, PR, D))]
        + [shape((FPD, PR, HC))] * 2
        + [shape((2, FPD, PR, HC)), shape((8, EARLY), F32)],
        grid=(FPD // HALF,),
        in_specs=[half_spec(D)] * 4
        + [whole((FPD, WIDE))]
        + [whole((HC, D))] * 4
        + [whole((8, NB)), whole((8, 128))],
        out_specs=[half_spec(D)] * 2
        + [half_spec(HC)] * 2
        + [pl.BlockSpec((2, HALF, PR, HC), lambda i: (0, i, 0, 0)), whole((8, EARLY))],
        compiler_params=params(26),
        cost_estimate=cost(2 * 512 * D * D, 12 * MB),
        name="mid_back",
    )(hg, middle, branch, cot, table, *weights, usum, dsum)


NB = 512
STEPS = FF // NB
PER = D // NB
TOKENS = FPD * PR


def block_of(t):
    phase = t // PER
    return ((phase % 2) * 2) ^ (phase // 2)


def up_column(t, row):
    return (row ^ block_of(t)) * PER + t % PER


def down_row(t):
    return block_of(t) * PER + t % PER


def down_spec(j):
    phase = (0, 2, 1, 3)[j]
    return pl.BlockSpec((NB, D), lambda t, row: (jnp.clip(t - phase * PER, 0, PER - 1), 0))


def pick_down(d0, d1, d2, d3):
    phase = pl.program_id(0) // PER
    return jnp.where(
        phase < 2,
        jnp.where(phase == 0, d0[...], d2[...]),
        jnp.where(phase == 2, d1[...], d3[...]),
    )


def feed_kernel(row_ref, h2, dg, u0, u1, u2, u3, table, d0, d1, d2, d3, act, upg, hg, usum):
    row = row_ref[0]
    ups = (u0, u1, u2, u3)
    down = pick_down(d0, d1, d2, d3)
    at = pl.ds(up_column(pl.program_id(0), row), 1)
    u = table[at, UB : UB + NB]
    for j, w in enumerate(ups):
        u = u + nn(h2[:, columns(row, j)], w[...])
    rate = math.sqrt(2.0 / math.pi)
    square = u * u
    half = 0.5 + 0.5 * jnp.tanh(u * (rate + (rate * 0.044715) * square))
    active = u * half
    act[...] = active.astype(BF16)
    slope = half + active * (1.0 - half) * (2.0 * rate + (6.0 * rate * 0.044715) * square)
    grad = (nt(dg[...], down) * slope).astype(BF16)
    upg[...] = grad
    put(usum, 0, up_column(pl.program_id(0), row), jnp.sum(grad.astype(F32), axis=0, keepdims=True))

    @pl.when(pl.program_id(0) == 0)
    def _():
        hg[...] = jnp.zeros_like(hg)

    for j, w in enumerate(ups):
        hg[:, columns(row, j)] = hg[:, columns(row, j)] + nt(grad, w[...])


def feed(row, h2, dg, ups, table, downs):
    tok = whole((TOKENS, D))
    block = pl.BlockSpec((TOKENS, NB), lambda t, row: (0, t))
    return pl.pallas_call(
        feed_kernel,
        out_shape=[
            shape((TOKENS, FF)),
            shape((TOKENS, FF)),
            shape((TOKENS, D), F32),
            shape((8, NB), F32),
        ],
        grid_spec=pltpu.PrefetchScalarGridSpec(
            num_scalar_prefetch=1,
            grid=(STEPS,),
            in_specs=[tok, tok]
            + [pl.BlockSpec((HC, NB), lambda t, row: (0, up_column(t, row[0])))] * 4
            + [whole((FPD, WIDE))]
            + [down_spec(j) for j in range(4)],
            out_specs=[block, block, tok, whole((8, NB))],
        ),
        compiler_params=params(58),
        cost_estimate=cost(3 * 2 * TOKENS * D * FF, 30 * MB, TOKENS * FF),
        name="feed",
    )(row, h2, dg, *ups, table, *downs)


def down_step(da, db, dg, act, part, dn):
    g = pl.program_id(0)
    down = jnp.where(g < PER, da[...], db[...])
    active = act[...]
    dn[...] = dn[...] + nn(active, down)
    part[0] = tn(active, dg[...]).astype(BF16)


def down_send_kernel(dg, act, da, db, part, dn):
    @pl.when(pl.program_id(0) == 0)
    def _():
        dn[...] = jnp.zeros_like(dn)

    down_step(da, db, dg, act, part, dn)


def down_keep_kernel(dg, act, da, db, before, table, middle, cot, part, out, gate, dn):
    @pl.when(pl.program_id(0) == 0)
    def _():
        dn[...] = before[...]

    down_step(da, db, dg, act, part, dn)

    @pl.when(pl.program_id(0) == STEPS // 2 - 1)
    def _():
        bias = unfold(table, DB, 128)
        for f in range(FPD):
            rows = slice(f * PR, (f + 1) * PR)
            value = dn[rows, :] + bias
            out[f] = (middle[f] + table[f : f + 1, 5 * D : 6 * D] * value).astype(BF16)
            gate[f : f + 1, :] = jnp.sum(cot[f].astype(F32) * value, axis=0, keepdims=True)


def down_half(first, dg, act, downs, extra=()):
    tok = whole((TOKENS, D))
    full = whole((FPD, PR, D))
    half = STEPS // 2
    weight = lambda k: pl.BlockSpec((NB, D), lambda g: (jnp.clip(g - k * PER, 0, PER - 1), 0))
    start = half if first else 0
    part = pl.BlockSpec((1, NB, D), lambda g: (g // PER, g % PER, 0))
    out_specs, out_shape, scratch, specs = [part], [shape((2, D, D))], [], []
    if first:
        out_specs += [tok]
        out_shape += [shape((TOKENS, D), F32)]
    else:
        specs = [tok, whole((FPD, WIDE)), full, full]
        out_specs += [full, whole((8, D))]
        out_shape += [shape((FPD, PR, D)), shape((8, D), F32)]
        scratch = [pltpu.VMEM((TOKENS, D), F32)]
    return pl.pallas_call(
        down_send_kernel if first else down_keep_kernel,
        out_shape=out_shape,
        grid=(half,),
        in_specs=[tok, pl.BlockSpec((TOKENS, NB), lambda g: (0, g + start)), weight(0), weight(1)]
        + specs,
        out_specs=out_specs,
        scratch_shapes=scratch,
        compiler_params=params(40),
        cost_estimate=cost(2 * TOKENS * D * FF, 14 * MB),
        name="down_weight_send" if first else "down_weight_keep",
    )(dg, act, *downs, *extra)


def up_weight_kernel(row_ref, h2, upg, uk, us):
    row = row_ref[0]
    grad = upg[...]
    for j, ref in enumerate((uk, us, uk, us)):
        ref[j // 2, 0] = tn(h2[:, columns(row, j)], grad).astype(BF16)


def up_weight_grad(row, h2, upg):
    up_out = pl.BlockSpec(
        (2, 1, HC, NB),
        lambda t, row: (0, up_column(t, row[0]) // PER, 0, up_column(t, row[0]) % PER),
    )
    return pl.pallas_call(
        up_weight_kernel,
        out_shape=[shape((2, 4, HC, D))] * 2,
        grid_spec=pltpu.PrefetchScalarGridSpec(
            num_scalar_prefetch=1,
            grid=(STEPS,),
            in_specs=[whole((TOKENS, D)), pl.BlockSpec((TOKENS, NB), lambda t, row: (0, t))],
            out_specs=[up_out, up_out],
        ),
        compiler_params=params(58),
        cost_estimate=cost(2 * TOKENS * D * FF, 14 * MB),
        name="up_weight_grad",
    )(row, h2, upg)


def out_weight_kernel(t0, t1, t2, t3, bg, keep, send):
    grad = bg[...].reshape(TOKENS, D)
    for j, t in enumerate((t0, t1, t2, t3)):
        ref = (keep, send)[j % 2]
        ref[j // 2] = tn(t[...].reshape(TOKENS, HC), grad).astype(BF16)


def out_weight_grad(pieces, bg):
    return pl.pallas_call(
        out_weight_kernel,
        out_shape=[shape((2, HC, D))] * 2,
        grid=(1,),
        in_specs=[whole((FPD, PR, HC))] * 4 + [whole((FPD, PR, D))],
        out_specs=[whole((2, HC, D))] * 2,
        compiler_params=params(14),
        cost_estimate=cost(2 * TOKENS * D * D, 4 * MB),
        name="out_weight_grad",
    )(*pieces, bg)


CHUNKS = 16
UP_ROWS, OUT_ROWS, DOWN_ROWS = D // CHUNKS, HC // CHUNKS, D // CHUNKS
FIRST = UP_ROWS + OUT_ROWS
ROWS = FIRST + DOWN_ROWS


def core_sum_kernel(ua, ub, da, db, oa, ob, out):
    def both(a, b):
        return (a.astype(F32) + b.astype(F32)).astype(BF16)

    for c in range(4):
        at = c * ROWS
        low, high = c * OUT_ROWS, (c + 1) * OUT_ROWS
        for i in range(4):
            to = at + i * OUT_ROWS
            out[0, to : to + OUT_ROWS] = both(ua[0, i, low:high], ub[0, i, low:high])
        out[0, at + UP_ROWS : at + FIRST] = both(oa[0, low:high], ob[0, low:high])
        low, high = c * DOWN_ROWS, (c + 1) * DOWN_ROWS
        out[0, at + FIRST : at + ROWS] = both(da[0, low:high], db[0, low:high])


def core_sum(up, down, out):
    ups = pl.BlockSpec((1, 4, 4 * OUT_ROWS, D), lambda j, c: (j, 0, c, 0))
    outs = pl.BlockSpec((1, 4 * OUT_ROWS, D), lambda j, c: (j, c, 0))
    downs = pl.BlockSpec((1, 4 * DOWN_ROWS, D), lambda j, c: (j, c, 0))
    return pl.pallas_call(
        core_sum_kernel,
        out_shape=shape((2, CHUNKS * ROWS, D)),
        grid=(2, CHUNKS // 4),
        in_specs=[ups, ups, downs, downs, outs, outs],
        out_specs=pl.BlockSpec((1, 4 * ROWS, D), lambda j, c: (j, c, 0)),
        compiler_params=params(58),
        cost_estimate=cost(1000, 1000),
        name="core_sum",
    )(*up, *down, *out)


def unpack_kernel(total, up, out, down):
    for k in range(4):
        at = k * ROWS
        for i in range(4):
            rows = slice(at + i * OUT_ROWS, at + (i + 1) * OUT_ROWS)
            up[k * OUT_ROWS : (k + 1) * OUT_ROWS, i * D : (i + 1) * D] = total[rows].astype(F32)
        out[k * OUT_ROWS : (k + 1) * OUT_ROWS] = total[at + UP_ROWS : at + FIRST].astype(F32)
        down[k * DOWN_ROWS : (k + 1) * DOWN_ROWS] = total[at + FIRST : at + ROWS].astype(F32)


def unpack(total):
    block = lambda i: (i, 0)
    return pl.pallas_call(
        unpack_kernel,
        out_shape=[shape((HC, FF), F32), shape((HC, D), F32), shape((D, D), F32)],
        grid=(4,),
        in_specs=[pl.BlockSpec((4 * ROWS, D), block)],
        out_specs=[
            pl.BlockSpec((4 * OUT_ROWS, FF), block),
            pl.BlockSpec((4 * OUT_ROWS, D), block),
            pl.BlockSpec((4 * DOWN_ROWS, D), block),
        ],
        compiler_params=params(24),
        cost_estimate=cost(0, 14 * MB),
        name="unpack",
    )(total)


LATE = 3 * D + 2 * HC
EARLY = 3 * D + NB + 256


def arrange_kernel(row_ref, a0, a1, a2, a3, late, far, out):
    row = row_ref[0]
    for j, a in enumerate((a0, a1, a2, a3)):
        for s in range(3):
            lanes = pl.ds(pl.multiple_of(s * D + (row ^ j) * HC, HC), HC)
            out[:, lanes] = a[:, s * HC : (s + 1) * HC]
    both = jnp.concatenate([late[...].astype(F32), far[...].astype(F32)], axis=0)
    out[:, 3 * D :] = both.astype(BF16)


def arrange(row, pieces, late, far):
    rows = pieces[0].shape[0]
    return pl.pallas_call(
        arrange_kernel,
        out_shape=shape((rows, 3 * D + LATE)),
        grid_spec=pltpu.PrefetchScalarGridSpec(
            num_scalar_prefetch=1,
            grid=(1,),
            in_specs=[whole((rows, 3 * HC))] * 4 + [whole((8, LATE))] * 2,
            out_specs=whole((rows, 3 * D + LATE)),
        ),
        compiler_params=params(16),
        cost_estimate=cost(0, 8 * rows * D),
        name="arrange",
    )(row, *pieces, late, far)


def stack_kernel(a0, a1, a2, a3, weights, sums):
    for k, a in enumerate((a0, a1, a2, a3)):
        weights[k] = a[:, : 3 * D]
        sums[k] = a[:, 3 * D :]


def stack(pieces):
    rows, width = pieces[0].shape
    return pl.pallas_call(
        stack_kernel,
        out_shape=[shape((4, rows, 3 * D)), shape((4, rows, LATE))],
        grid=(1,),
        in_specs=[whole((rows, width))] * 4,
        out_specs=[whole((4, rows, 3 * D)), whole((4, rows, LATE))],
        compiler_params=params(16),
        cost_estimate=cost(0, 2 * MB),
        name="stack",
    )(*pieces)


def place_kernel(index_ref, low, high, out):
    for m, a in enumerate((low.at[0], low.at[1], high.at[1], high.at[0])):

        @pl.when(pl.program_id(0) == m)
        def _():
            for k in range(4):
                out[0, index_ref[1] ^ k] = a[k].astype(F32)


def place(index, low, high):
    rows = low.shape[2]
    return pl.pallas_call(
        place_kernel,
        out_shape=shape((4, 4, rows, 3 * D), F32),
        grid_spec=pltpu.PrefetchScalarGridSpec(
            num_scalar_prefetch=1,
            grid=(4,),
            in_specs=[whole(low.shape)] * 2,
            out_specs=pl.BlockSpec((1, 4, rows, 3 * D), lambda i, index: (index[0] ^ i, 0, 0, 0)),
        ),
        compiler_params=params(24),
        cost_estimate=cost(0, 24 * rows * D),
        name="place",
    )(index, low, high).reshape(HC, 3 * D)


def project_back_kernel(row_ref, dq, dk, dv, rk, rv, w0, w1, w2, w3, cp, sp, fr, dp, h0, h2, hs, bsum):
    row = row_ref[0]
    f = pl.program_id(0)
    later = (f > 0).astype(F32)
    keys = dk[0] + later * rk[0, 0].astype(F32)
    values = dv[0] + later * rv[0, 0].astype(F32)
    cosine, sine = cosines(cp, sp, fr, f)
    dp[0, :, :HC] = dq[0]
    dp[0, :, HC : 2 * HC] = turn(keys, cosine, -sine).astype(BF16)
    dp[0, :, 2 * HC :] = values.astype(BF16)
    grad = dp[0]
    sums = jnp.sum(grad.astype(F32), axis=0, keepdims=True)

    @pl.when(f == 0)
    def _():
        bsum[...] = jnp.zeros_like(bsum)

    number = lax.broadcasted_iota(jnp.int32, (8, 2 * HC), 0)
    bsum[...] = bsum[...] + jnp.where(number == row, sums[:, : 2 * HC], 0.0)
    bsum[:, :HC] = bsum[:, :HC] + jnp.where(number[:, :HC] == row + 4, sums[:, 2 * HC :], 0.0)
    for j, w in enumerate((w0, w1, w2, w3)):
        part = nt(grad, w[...]).astype(BF16)
        at = (0, slice(None), columns(row, j))
        h0[at] = part[:PR]
        hs[(0,) + at] = part[PR : 2 * PR]
        h2[at] = part[2 * PR : 3 * PR]
        hs[(1,) + at] = part[3 * PR :]


def project_back(row, dq, dk, dv, returned, weights, tables):
    block = pl.BlockSpec((1, TOK, HC), lambda f, *_: (f, 0, 0))
    late = [
        pl.BlockSpec((1, 1, TOK, HC), lambda f, *_, i=i: (i, jnp.maximum(f - 1, 0), 0, 0))
        for i in range(2)
    ]
    piece = pl.BlockSpec((1, PR, D), lambda f, *_: (f, 0, 0))
    return pl.pallas_call(
        project_back_kernel,
        out_shape=[
            shape((FPD, TOK, 3 * HC)),
            shape((FPD, PR, D)),
            shape((FPD, PR, D)),
            shape((2, FPD, PR, D)),
            shape((8, 2 * HC), F32),
        ],
        grid_spec=pltpu.PrefetchScalarGridSpec(
            num_scalar_prefetch=1,
            grid=(FPD,),
            in_specs=[block] * 3
            + late
            + [whole((HC, 3 * HC))] * 4
            + [whole((TOK, HC)), whole((TOK, HC)), whole((16, 2 * HC))],
            out_specs=[
                pl.BlockSpec((1, TOK, 3 * HC), lambda f, *_: (f, 0, 0)),
                piece,
                piece,
                pl.BlockSpec((2, 1, PR, D), lambda f, *_: (0, f, 0, 0)),
                whole((8, 2 * HC)),
            ],
        ),
        compiler_params=params(20),
        cost_estimate=cost(2 * FPD * TOK * D * 3 * HC, 14 * MB),
        name="project_back",
    )(row, dq, dk, dv, returned, returned, *weights, *tables)


def weight_kernel(row_ref, h, dp, w):
    w[0] = tn(h[...], dp[...]).astype(BF16)


def project_weight(row, hidden, dproj):
    tokens = FPD * TOK
    return pl.pallas_call(
        weight_kernel,
        out_shape=shape((4, HC, 3 * HC)),
        grid_spec=pltpu.PrefetchScalarGridSpec(
            num_scalar_prefetch=1,
            grid=(4,),
            in_specs=[
                pl.BlockSpec((tokens, HC), lambda j, row: (0, row[0] ^ j)),
                whole((tokens, 3 * HC)),
            ],
            out_specs=pl.BlockSpec((1, HC, 3 * HC), lambda j, row: (j, 0, 0)),
        ),
        compiler_params=params(20),
        cost_estimate=cost(2 * tokens * D * 3 * HC, 9 * MB),
        name="project_weight",
    )(row, hidden.reshape(tokens, D), dproj.reshape(tokens, 3 * HC))


def input_back_kernel(x, h0, near, far, table, mg, bsum, gate, out, sums):
    grad = h0[...].astype(F32) + near[0].astype(F32) + far[...].astype(F32)
    normal, rate = norm(x[...].astype(F32))
    put_half(sums, 0, jnp.sum(grad, axis=1))
    put_half(sums, D, jnp.sum(grad * normal, axis=1))
    sums[:, 2 * D : 3 * D] = gate[...]
    sums[:, 3 * D :] = bsum[...]
    out[...] = mg[...] + norm_back(normal, rate, grad * (1.0 + segment(table, 1)))


def input_back(x, h0, near, far, table, mg, bsum, gate):
    return pl.pallas_call(
        input_back_kernel,
        out_shape=[shape((FPD, PR, D), F32), shape((8, LATE), F32)],
        grid=(FPD // HALF,),
        in_specs=[half_spec(D)] * 2
        + [pl.BlockSpec((1, HALF, PR, D), lambda i: (0, i, 0, 0))]
        + [half_spec(D), whole((FPD, WIDE)), half_spec(D), whole((8, 2 * HC)), whole((8, D))],
        out_specs=[half_spec(D), whole((8, LATE))],
        compiler_params=params(20),
        cost_estimate=cost(20 * 512 * D, 10 * MB),
        name="input_back",
    )(x, h0, near, far, table, mg, bsum, gate)


def join_kernel(a0, a1, a2, a3, out):
    for k, a in enumerate((a0, a1, a2, a3)):
        out[2 * k : 2 * k + 2] = a[...]


def join(pieces):
    width = pieces[0].shape[-1]
    return pl.pallas_call(
        join_kernel,
        out_shape=shape((8, 8, width)),
        grid=(1,),
        in_specs=[whole((2, 8, width))] * 4,
        out_specs=whole((8, 8, width)),
        compiler_params=params(16),
        cost_estimate=cost(0, 2 * MB),
        name="join",
    )(*pieces)


def final_kernel(row_ref, *refs):
    row = row_ref[0]
    low, high, *early = refs[:6]
    ada, ab, qb, ob, ub, db, asum = refs[6:]
    late = [low.at[0], low.at[1], high.at[0], high.at[1]]
    early = [early[0], early[3], early[1], early[2]]

    def rows(ref, cols):
        value = ref[:, :, cols].astype(F32)
        return value.reshape(64, value.shape[-1])

    left = [rows(s, slice(EARLY, EARLY + HC)).astype(BF16) for s in early]
    for segment in range(6):
        source, start = ((late, 0), (late, 1), (early, 0), (early, 1), (early, 2), (late, 2))[segment]
        cols = slice(start * D, (start + 1) * D)
        product, total = 0.0, 0.0
        for s, ref in zip(left, source):
            right = rows(ref, cols)
            total = total + jnp.sum(right, axis=0, keepdims=True)
            product = product + tn(s, right.astype(BF16))
        at = segment * D
        ada[:, at : at + D] = product
        asum[0:1, at : at + D] = total

    def fold8(value):
        value = jnp.sum(value, axis=0)
        return value if value.shape[0] == 8 else value[:8] + value[8:]

    def bias(source, start, stop):
        return sum(
            fold8(ref[:, :, start:stop].astype(F32)) for ref in source
        )

    ab[...] = asum[0:1, pl.ds(pl.multiple_of(row * 1536, 512), 1536)]
    folded = bias(late, 3 * D, LATE)
    for i in range(3):
        chunk = 3 * row + i
        at = jnp.where(chunk < 4, chunk, chunk - 4)
        second = (chunk >= 4) & (chunk < 8)
        value = jnp.where(second, folded[:, HC:], folded[:, :HC])
        qb[:, i * HC : (i + 1) * HC] = take(value, at)
    folded = bias(early, 3 * D, EARLY)
    for i in range(2):
        at = 2 * row + i
        ub[:, i * NB : (i + 1) * NB] = take(folded[:, :NB], at)
        db[:, i * 128 : (i + 1) * 128] = take(folded[:, NB : NB + 128], at)
        ob[:, i * 128 : (i + 1) * 128] = take(folded[:, NB + 128 :], at)


def final_sums(row, late, early):
    sizes = (1536, 768, 256, 1024, 256)
    return pl.pallas_call(
        final_kernel,
        out_shape=[shape((HC, 6 * D), F32)] + [shape((1, n), F32) for n in sizes],
        grid_spec=pltpu.PrefetchScalarGridSpec(
            num_scalar_prefetch=1,
            grid=(1,),
            in_specs=[whole((2, 4, 16, LATE))] * 2
            + [whole((8, 8, EARLY + HC))] * 4,
            out_specs=[whole((HC, 6 * D))] + [whole((1, n)) for n in sizes],
            scratch_shapes=[pltpu.VMEM((8, 6 * D), F32)],
        ),
        compiler_params=params(28),
        cost_estimate=cost(2 * 256 * HC * 6 * D, 10 * MB),
        name="final_sums",
    )(row, *late, *early)


def row_sum(value):
    value = value + swap(value, CORE)
    return value + swap(value, DIRECT)


def row_pieces(value):
    return [value, swap(value, CORE), swap(value, DIRECT), swap(value, DIRECT ^ CORE)]


def by_row(pieces, row):
    a, b, c, d = pieces
    odd, high = row % 2 == 1, row >= 2
    a, b = jnp.where(odd, b, a), jnp.where(odd, a, b)
    c, d = jnp.where(odd, d, c), jnp.where(odd, c, d)
    return jnp.stack(
        [
            jnp.where(high, c, a),
            jnp.where(high, d, b),
            jnp.where(high, a, c),
            jnp.where(high, b, d),
        ]
    )


def quarter_rows(value, bit, index, axis):
    rows = value.shape[1] // 4
    at = lambda m: lax.dynamic_slice_in_dim(value, (index[axis] ^ m) * rows, rows, 1)
    return [at(0)] + [swap(at(m), bit * m) for m in (1, 2, 3)]


def add_all(parts):
    return sum(part.astype(F32) for part in parts).astype(BF16)


def exchange_rows(value, bit, index, axis):
    return add_all(quarter_rows(value, bit, index, axis))


def turn_heads(own, beside, across, order=lambda piece: piece):
    across = swap(across, DIRECT)
    return [own, swap(beside, CORE), across[0], swap(order(across)[1], CORE)]


def per_device(
    activations,
    noise_embed,
    frame_position,
    cotangent,
    ada_weight,
    ada_bias,
    qkv_weight,
    qkv_bias,
    out_weight,
    out_bias,
    up_weight,
    up_bias,
    down_weight,
    down_bias,
):
    row = lax.axis_index(("xl", "c")).astype(jnp.int32)
    row_arg = row.reshape(1)
    index = [lax.axis_index("y").astype(jnp.int32), lax.axis_index("z").astype(jnp.int32)]
    index_arg = jnp.stack(index)

    x0 = activations
    x2 = swap(x0, DIRECT)
    x1 = swap(x0, CORE)
    p0 = shift(activations[1:], 1)
    biases = (ada_bias, qkv_bias, out_bias, up_bias, down_bias)
    heads = list(split_heads(row_arg, qkv_weight))
    noise, heads[1] = lax.optimization_barrier((noise_embed, heads[1]))
    part, silu_own, *tables = prepare(row_arg, frame_position, noise, ada_weight, biases)
    across = swap(heads[2], OTHER)
    qkv_pieces = [heads[0], swap(heads[1], CORE), across]
    part = part + swap(part, CORE)
    table = part + swap(part, DIRECT)
    x2, p0, table, *qkv_pieces = lax.optimization_barrier((x2, p0, table, *qkv_pieces))

    qkv_pieces = qkv_pieces[:2] + [qkv_pieces[2][0], swap(qkv_pieces[2][1], CORE)]
    x3 = swap(x2, CORE)
    p2 = swap(p0, DIRECT)
    p1 = swap(p0, CORE)
    before_mods = shift(table[:, : 2 * D], 1)

    out_own = after(out_weight, table)
    outs2 = swap(out_own, OTHER)

    hidden1, q, k, v = project(True, row_arg, (x0, x1, x2, x3), table, table, qkv_pieces, tables)
    outs2, up_own, down_own, q = lax.optimization_barrier((outs2, up_weight, down_weight, q))
    ups2 = swap(up_own, OTHER)
    downs2 = swap(down_own, DIRECT)
    state = attend(True, frame_position, q, k, v)
    p2, before_mods, *state = lax.optimization_barrier((p2, before_mods, *state))
    p3 = swap(p2, CORE)
    kp, vp = project(
        False, row_arg, (p0, p1, p2, p3), table, before_mods, qkv_pieces, tables
    )
    *mixed, lse = attend(False, frame_position, q, kp, vp, state)
    outs2, ups2, downs2, lse = lax.optimization_barrier((outs2, ups2, downs2, lse))
    outs = [out_weight, swap(out_own, CORE), outs2, swap(outs2, CORE)]
    ups = [up_weight, swap(up_own, CORE), ups2, swap(ups2, CORE)]
    downs = [down_weight, swap(down_own, CORE), downs2, swap(downs2, CORE)]
    turned = turn_heads(*mixed)
    branch, middle, hidden2, down_grad, dsum = mid(turned, outs, table, x0, cotangent)
    h2 = hidden2.reshape(TOKENS, D)
    dg = down_grad.reshape(TOKENS, D)
    act, upg, hg, usum = feed(row_arg, h2, dg, ups, table, downs)
    mg, bg, *ag, early = mid_back(
        hg.reshape(FPD, PR, D), middle, branch, cotangent, table, outs, usum, dsum
    )
    late = []
    back = turn_heads(*ag[:2], ag[2], order=lambda piece: late.append(piece) or piece)[:2]

    early = early + swap(early, CORE)
    upg, early, _ = lax.optimization_barrier((upg, early, bg))
    early_far = swap(early, DIRECT)
    uk, us = up_weight_grad(row_arg, h2, upg)
    us = swap(us, CORE)
    dg_later, early_far, uk = lax.optimization_barrier((dg, early_far, uk))
    early = jnp.concatenate([(early + early_far).astype(BF16), silu_own], axis=1)
    early_far = swap(early, FAR)
    ds_part, dn = down_half(True, dg_later, act, (downs[1], downs[3]))
    ds_part_far = swap(ds_part, CORE)
    dn, early, early_far, bg_later, us, far_back, *back = lax.optimization_barrier(
        (dn, early, early_far, bg, us, *late, *back)
    )
    early = jnp.stack([early, early_far])
    early_parts = [early] + [swap(early, m) for m in (16, 32, 48)]
    ok, os = out_weight_grad(turned, bg_later)
    os = swap(os, CORE)
    dk_part, layer_output, gate = down_half(
        False, dg_later, act, (downs[0], downs[2]), (dn, table, middle, cotangent)
    )
    dk_part, early_parts, ds_part_far, os, far_back = lax.optimization_barrier(
        (dk_part, early_parts, ds_part_far, os, far_back)
    )
    back += [far_back[0], swap(far_back[1], CORE)]
    packed = core_sum((uk, us), (dk_part, ds_part_far), (ok, os))
    packed, back = lax.optimization_barrier((packed, back))
    scattered = lax.psum_scatter(packed, ("y", "z"), scatter_dimension=1, tiled=True)

    dq_before, both = attend_back(False, frame_position, q, kp, vp, back, mixed, lse)
    returned = shift(both, -1)
    dq, dk, dv = attend_back(
        True, frame_position, q, k, v, back, mixed, lse, tables, dq_before
    )
    early_parts, dq = lax.optimization_barrier((early_parts, dq))
    early = join(early_parts)
    early_all = [early] + [swap(early, m) for m in (4, 8, 12)]
    dq, early = lax.optimization_barrier((dq, early))
    early = early[0].astype(F32)

    dproj, h0, h2_part, send, bsum = project_back(row_arg, dq, dk, dv, returned, qkv_pieces, tables)
    near = swap(send, CORE)
    qkv_parts = project_weight(row_arg, hidden1, dproj)
    far_part = (h2_part.astype(F32) + near[1].astype(F32)).astype(BF16)
    far = swap(far_part, DIRECT)
    far_part, qkv_parts, *early_all = lax.optimization_barrier((far_part, qkv_parts, *early_all))
    quarters = quarter_rows(qkv_parts, 4, index, 0)
    input_grad, late = input_back(x0, h0, near, far, table, mg, bsum, gate)
    late_near = swap(late, CORE)
    late, *quarters = lax.optimization_barrier((late, *quarters))
    quarters = quarter_rows(add_all(quarters), 16, index, 1)
    late = late + late_near
    late_far = swap(late, DIRECT)
    late, *quarters = lax.optimization_barrier((late, *quarters))
    qkv_parts = add_all(quarters)
    qkv_far = swap(qkv_parts, FAR)
    scattered, late, late_far, qkv_parts = lax.optimization_barrier(
        (scattered, late, late_far, qkv_parts)
    )
    late = late + late_far
    late_low = late.astype(BF16)
    late_far = swap(late_low, FAR)
    share_far = swap(scattered[1], DIRECT)
    late_low, qkv_far = lax.optimization_barrier((late_low, qkv_far))
    qkv_parts = add_all([qkv_parts, qkv_far])
    turned = turn_heads(qkv_parts[0], qkv_parts[1], qkv_parts[2:])
    turned, share_far = lax.optimization_barrier((turned, share_far))
    share = scattered[0].astype(F32) + share_far.astype(F32)
    share_far = swap(share.astype(BF16), FAR)
    last = arrange(row_arg, turned, late_low, late_far)

    share, share_far, last = lax.optimization_barrier((share, share_far, last))
    share = (share + share_far.astype(F32)).astype(BF16)
    totals = lax.all_gather(share, ("y", "z"), axis=0, tiled=True)
    weights, sums_late = stack([last] + [swap(last, m) for m in (16, 32, 48)])
    weights = jnp.stack([weights, swap(weights, 4)])
    sums_late = jnp.stack([sums_late, swap(sums_late, 12)])
    weights_far, sums_far = swap(weights, 12), swap(sums_late, 4)
    up_total, out_total, down_total = unpack(totals)
    qkv_total = place(index_arg, weights, weights_far)

    ada_total, *bias_sums = final_sums(row_arg, (sums_late, sums_far), early_all)
    ada_sum, qkv_sum, out_sum, up_sum, down_sum = [b[0] for b in bias_sums]
    mod_own = jnp.concatenate(
        [late[:, : 2 * D], early[:, : 3 * D], late[:, 2 * D : 3 * D]], axis=1
    ).astype(BF16)
    silu_grad = nt(mod_own, ada_weight)
    silu_grad = by_row(row_pieces(silu_grad), row).transpose(1, 0, 2).reshape(FPD, D)
    embed = noise_embed.astype(F32)
    sigma = jax.nn.sigmoid(embed)
    embed_grad = silu_grad * (sigma * (1.0 + embed * (1.0 - sigma)))

    return (
        layer_output,
        input_grad,
        embed_grad,
        ada_total,
        ada_sum,
        qkv_total,
        qkv_sum,
        out_total,
        out_sum,
        up_total,
        up_sum,
        down_total,
        down_sum,
    )


def solution(mesh):
    fine = Mesh(mesh.devices.reshape(2, 4, 4, 2, 2), AXES)
    seq, row = ("xh", "z", "y"), ("xl", "c")
    token, weight, vector = P(seq, row, None), P(row, None), P(row)
    in_specs = (token, P(seq, None), P(seq), token) + (weight, vector) * 5
    out_specs = (token, token, P(seq, None)) + (weight, vector) * 5
    return jax.shard_map(
        per_device, mesh=fine, in_specs=in_specs, out_specs=out_specs, check_vma=False
    )
```

```python
import math

import jax
import jax.numpy as jnp
from jax import lax
from jax.experimental import pallas as pl
from jax.experimental.pallas import tpu as pltpu
from jax.sharding import Mesh, PartitionSpec as P

F32 = jnp.float32
BF16 = jnp.bfloat16
HD = 64
GRID = 16
FPD = 8
PR = 64
D = 1024
FF = 4096
HC = 256
TOK = 256
PREV = 7
AXES = ("xh", "z", "y", "xl", "c")
CORE, DIRECT, OTHER, FAR = 1, 2, 66, 64
MB = 1024 * 1024


def swap(value, mask):
    return lax.ppermute(value, AXES, [(i, i ^ mask) for i in range(128)])


def shift(value, steps):
    return lax.ppermute(value, AXES, [(i, (i + 4 * steps) % 128) for i in range(128)])


def after(value, *others):
    return lax.optimization_barrier((value,) + others)[0]


def nt(left, right):
    return lax.dot_general(left, right, (((1,), (1,)), ((), ())), preferred_element_type=F32)


def tn(left, right):
    return lax.dot_general(left, right, (((0,), (0,)), ((), ())), preferred_element_type=F32)


def nn(left, right):
    return jnp.dot(left, right, preferred_element_type=F32)


def norm(values):
    center = values - jnp.mean(values, axis=-1, keepdims=True)
    spread = jnp.mean(center * center, axis=-1, keepdims=True)
    rate = lax.rsqrt(spread + 1e-06)
    return center * rate, rate


def norm_back(normal, rate, grad):
    mean_grad = jnp.mean(grad, axis=-1, keepdims=True)
    mean_both = jnp.mean(grad * normal, axis=-1, keepdims=True)
    return rate * (grad - mean_grad - normal * mean_both)


def turn(values, cosine, sine):
    lanes = lax.broadcasted_iota(jnp.int32, values.shape, 1)
    other = jnp.where(
        lanes % HD < HD // 2, pltpu.roll(values, HC - HD // 2, 1), pltpu.roll(values, HD // 2, 1)
    )
    return values * cosine + other * sine


def params(mib):
    return pltpu.CompilerParams(vmem_limit_bytes=mib * MB)


def cost(flops, moved, exps=0):
    return pl.CostEstimate(flops=int(flops), bytes_accessed=int(moved), transcendentals=int(exps))


def whole(shape):
    return pl.BlockSpec(shape, lambda i, *_: (0,) * len(shape))


def columns(row, j):
    return pl.ds(pl.multiple_of((row ^ j) * HC, HC), HC)


def shape(dims, kind=BF16):
    return jax.ShapeDtypeStruct(dims, kind)


UB, QB, OB, DB, WIDE = 6144, 6656, 7168, 7296, 7424


def put(ref, start, at, value):
    cols = slice(start, start + value.shape[1])
    number = lax.broadcasted_iota(jnp.int32, (8, value.shape[1]), 0)
    ref[:, cols] = jnp.where(number == at, value, ref[:, cols])


def take(value, at):
    number = lax.broadcasted_iota(jnp.int32, value.shape, 0)
    return jnp.sum(jnp.where(number == at, value, 0.0), axis=0, keepdims=True)


def put_half(ref, start, value):
    cols = slice(start, start + value.shape[1])
    number = lax.broadcasted_iota(jnp.int32, (8, value.shape[1]), 0)
    both = jnp.concatenate([value, value], axis=0)
    ref[:, cols] = jnp.where(number // 4 == pl.program_id(0), both, ref[:, cols])


def unfold(ref, start, width):
    return jnp.concatenate([ref[i : i + 1, start : start + width] for i in range(8)], axis=1)


def prepare_kernel(row_ref, pos_ref, noise, ada, ab, qb, ob, ub, db, pack, silu, cp, sp, frames):
    row = row_ref[0]
    embed = noise[...].astype(F32)
    value = (embed / (1.0 + jnp.exp(-embed))).astype(BF16)
    own = jnp.where(
        row < 2,
        jnp.where(row == 0, value[:, :HC], value[:, HC : 2 * HC]),
        jnp.where(row == 2, value[:, 2 * HC : 3 * HC], value[:, 3 * HC :]),
    )
    silu[...] = own
    pack[:, UB:] = jnp.zeros((FPD, WIDE - UB), F32)
    for segment in range(6):
        cols = slice(segment * D, (segment + 1) * D)
        pack[:, cols] = nn(own, ada[:, cols])
    bias = pl.ds(pl.multiple_of(row * 1536, 512), 1536)
    pack[:, bias] = pack[:, bias] + ab[...].astype(F32)
    for i in range(2):
        at = 2 * row + i
        put(pack, UB, at, ub[:, i * 512 : (i + 1) * 512].astype(F32))
        put(pack, OB, at, ob[:, i * 128 : (i + 1) * 128].astype(F32))
        put(pack, DB, at, db[:, i * 128 : (i + 1) * 128].astype(F32))
    for i in range(3):
        chunk = 3 * row + i
        at = jnp.where(chunk < 4, chunk, chunk - 4)
        second = (chunk >= 4) & (chunk < 8)
        value = qb[:, i * HC : (i + 1) * HC].astype(F32)
        put(pack, QB, jnp.where(second, -1, at), value)
        put(pack, QB + HC, jnp.where(second, at, -1), value)

    def parts(dims):
        lane = lax.broadcasted_iota(jnp.int32, dims, 1)
        index = lane % (HD // 2)
        quarter, eighth = HD // 4, HD // 8
        in_frame = index < quarter
        in_row = (index >= quarter) & (index < quarter + eighth)
        offset = jnp.where(
            in_frame, index, jnp.where(in_row, index - quarter, index - quarter - eighth)
        ).astype(F32)
        length = jnp.where(in_frame, 1.0 * quarter, 1.0 * eighth)
        frequency = jnp.exp(-math.log(10000.0) * offset / length)
        sign = jnp.where(lane % HD < HD // 2, -1.0, 1.0)
        return in_frame, in_row, frequency, sign

    in_frame, in_row, frequency, sign = parts((TOK, HC))
    slot = lax.broadcasted_iota(jnp.int32, (TOK, HC), 0)
    patch = ((slot // PR) ^ row) * PR + slot % PR
    angle = jnp.where(in_row, patch // GRID, patch % GRID).astype(F32) * frequency
    cp[...] = jnp.where(in_frame, 0.0, jnp.cos(angle))
    sp[...] = jnp.where(in_frame, 0.0, jnp.sin(angle) * sign)
    in_frame, _, frequency, sign = parts((16, HC))
    slot = lax.broadcasted_iota(jnp.int32, (16, HC), 0)
    place = pos_ref[0] - PREV + (slot - FPD)
    for f in range(FPD):
        place = jnp.where(slot == f, pos_ref[f], place)
    angle = place.astype(F32) * frequency
    frames[:, :HC] = jnp.where(in_frame, jnp.cos(angle), 0.0)
    frames[:, HC:] = jnp.where(in_frame, jnp.sin(angle) * sign, 0.0)


def prepare(row, places, noise, ada, biases):
    return pl.pallas_call(
        prepare_kernel,
        out_shape=[
            shape((FPD, WIDE), F32),
            shape((FPD, HC)),
            shape((TOK, HC), F32),
            shape((TOK, HC), F32),
            shape((16, 2 * HC), F32),
        ],
        grid_spec=pltpu.PrefetchScalarGridSpec(
            num_scalar_prefetch=2,
            grid=(1,),
            in_specs=[whole((FPD, D)), whole((HC, 6 * D))]
            + [whole((1, b.shape[0])) for b in biases],
            out_specs=[
                whole((FPD, WIDE)),
                whole((FPD, HC)),
                whole((TOK, HC)),
                whole((TOK, HC)),
                whole((16, 2 * HC)),
            ],
        ),
        compiler_params=params(24),
        cost_estimate=cost(2 * 8 * HC * 6 * D, 4 * MB, 4 * TOK * HC),
        name="prepare",
    )(row, places, noise, ada, *[b[None] for b in biases])


def split_heads_kernel(row_ref, q, k, v, p0, p1, p23):
    for j, p in enumerate((p0, p1, p23.at[0], p23.at[1])):

        @pl.when(pl.program_id(0) == j)
        def _():
            p[:, :HC] = q[...]
            p[:, HC : 2 * HC] = k[...]
            p[:, 2 * HC :] = v[...]


def split_heads(row, weight):
    piece = (HC, 3 * HC)
    return pl.pallas_call(
        split_heads_kernel,
        out_shape=[shape(piece), shape(piece), shape((2,) + piece)],
        grid_spec=pltpu.PrefetchScalarGridSpec(
            num_scalar_prefetch=1,
            grid=(4,),
            in_specs=[
                pl.BlockSpec((HC, HC), lambda j, row, s=s: (0, 4 * s + (row[0] ^ j)))
                for s in range(3)
            ],
            out_specs=[whole(piece), whole(piece), whole((2,) + piece)],
        ),
        compiler_params=params(12),
        cost_estimate=cost(0, 3 * MB),
        name="split_heads",
    )(row, weight, weight, weight)


def cosines(cp, sp, frames, at):
    both = frames[pl.ds(at, 1), :]
    return cp[...] + both[:, :HC], sp[...] + both[:, HC:]


def project_kernel(own, row_ref, x0, x1, x2, x3, table, mods, w0, w1, w2, w3, cp, sp, fr, *outs):
    row = row_ref[0]
    f = pl.program_id(0)
    if own:
        h_ref, q_ref, k_ref, v_ref = outs
        first, at, angle = 0, f, f
    else:
        k_ref, v_ref, h_ref = outs
        first, at, angle = HC, f + FPD - PREV, f + FPD
    x = jnp.concatenate([r[0] for r in (x0, x1, x2, x3)], axis=0).astype(F32)
    normal, _ = norm(x)
    shift_row = mods[pl.ds(at, 1), :D]
    scale_row = mods[pl.ds(at, 1), D : 2 * D]
    hidden = (normal * (1.0 + scale_row) + shift_row).astype(BF16)
    where = (0,) if own else ()
    h_ref[where + (slice(None), slice(None))] = hidden
    low, high = table[pl.ds(row, 1), QB : QB + 2 * HC], table[pl.ds(row + 4, 1), QB : QB + HC]
    total = jnp.concatenate([low, high], axis=1)[:, first:]
    for j, w in enumerate((w0, w1, w2, w3)):
        total = total + nn(h_ref[where + (slice(None), columns(row, j))], w[:, first:])
    cosine, sine = cosines(cp, sp, fr, angle)
    if own:
        q_ref[0] = (turn(total[:, :HC], cosine, sine).astype(BF16).astype(F32) * 0.125).astype(BF16)
        total = total[:, HC:]
    k_ref[0] = turn(total[:, :HC], cosine, sine).astype(BF16)
    v_ref[0] = total[:, HC:].astype(BF16)


def project(own, row, xs, table, mods, weights, tables):
    frames = xs[0].shape[0]
    x_spec = pl.BlockSpec((1, PR, D), lambda f, *_: (f, 0, 0))
    out_spec = pl.BlockSpec((1, TOK, HC), lambda f, *_: (f, 0, 0))
    out = shape((frames, TOK, HC))
    if own:
        out_specs = [pl.BlockSpec((1, TOK, D), lambda f, *_: (f, 0, 0)), out_spec, out_spec, out_spec]
        out_shape = [shape((frames, TOK, D)), out, out, out]
        scratch = []
    else:
        out_specs = [out_spec, out_spec]
        out_shape = [out, out]
        scratch = [pltpu.VMEM((TOK, D), BF16)]
    return pl.pallas_call(
        lambda *refs: project_kernel(own, *refs),
        out_shape=out_shape,
        grid_spec=pltpu.PrefetchScalarGridSpec(
            num_scalar_prefetch=1,
            grid=(frames,),
            in_specs=[x_spec] * 4
            + [whole((FPD, WIDE)), whole(mods.shape)]
            + [whole((HC, 3 * HC))] * 4
            + [whole((TOK, HC)), whole((TOK, HC)), whole((16, 2 * HC))],
            out_specs=out_specs,
            scratch_shapes=scratch,
        ),
        compiler_params=params(20),
        cost_estimate=cost(2 * frames * TOK * D * 3 * HC, frames * TOK * D * 4 + 4 * MB),
        name="project_own" if own else "project_prev",
    )(row, *xs, table, mods, *weights, *tables)


def head_lanes():
    return lax.broadcasted_iota(jnp.int32, (TOK, HC), 1) // HD


def spread_queries(q, qs):
    lanes = head_lanes()
    query = q[0]
    for h in range(4):
        qs[pl.ds(h * TOK, TOK), :] = jnp.where(lanes == h, query, jnp.zeros_like(query))


def sweep_scores(low_at, high_at, k, qs, scores, top):
    def one(at, _):
        keys = k[at]
        for h in range(4):
            rows = pl.ds(h * TOK, TOK)
            s = nt(qs[rows, :], keys)
            scores[at - low_at, rows, :] = s
            top[rows, :] = jnp.maximum(top[rows, :], jnp.maximum(s[:, :128], s[:, 128:]))
        return 0

    lax.fori_loop(low_at, high_at, one, 0)
    for h in range(4):
        rows = pl.ds(h * TOK, TOK)
        top[rows, :] = jnp.broadcast_to(jnp.max(top[rows, :], axis=1, keepdims=True), (TOK, 128))


def sweep_values(low_at, high_at, v, scores, top, low, acc):
    low[...] = jnp.zeros_like(low)
    acc[...] = jnp.zeros_like(acc)

    def one(at, _):
        values = v[at]
        for h in range(4):
            rows = pl.ds(h * TOK, TOK)
            p = jnp.exp(scores[at - low_at, rows, :] - jnp.concatenate([top[rows, :]] * 2, axis=1))
            low[rows, :] = low[rows, :] + (p[:, :128] + p[:, 128:])
            acc[rows, :] = acc[rows, :] + nn(p.astype(BF16), values)
        return 0

    lax.fori_loop(low_at, high_at, one, 0)


def attend_own_kernel(pos_ref, q, k, v, mixed, stats, qs, scores, acc, top, low):
    f = pl.program_id(0)
    start = jnp.maximum(f - pos_ref[f], 0)
    spread_queries(q, qs)
    top[...] = jnp.full_like(top, -1e30)
    sweep_scores(start, f + 1, k, qs, scores, top)
    sweep_values(start, f + 1, v, scores, top, low, acc)
    lanes = head_lanes()
    narrow = lax.broadcasted_iota(jnp.int32, (TOK, 128), 1)
    result = jnp.zeros((TOK, HC), F32)
    state = jnp.zeros((TOK, 128), F32)
    for h in range(4):
        rows = pl.ds(h * TOK, TOK)
        result = jnp.where(lanes == h, acc[rows, :], result)
        state = jnp.where(narrow == h, top[rows, :], state)
        state = jnp.where(narrow == 4 + h, jnp.sum(low[rows, :], axis=1, keepdims=True), state)
    mixed[0] = result
    stats[0] = state


def attend_prev_kernel(
    pos_ref, q, k, v, mixed, stats, o0, o1, o23, lse, qs, scores, acc, top, low, result, logs
):
    f = pl.program_id(0)
    count = jnp.maximum(pos_ref[f] - f, 0)
    lanes = head_lanes()
    narrow = lax.broadcasted_iota(jnp.int32, (TOK, 128), 1)
    state = stats[0]

    def finish(part):
        total_mixed = jnp.zeros((TOK, HC), F32)
        total_logs = jnp.zeros((TOK, 128), F32)
        for h in range(4):
            largest, total, value = part(h, state[:, h : h + 1], state[:, 4 + h : 5 + h])
            total_mixed = jnp.where(lanes == h, value / total, total_mixed)
            total_logs = jnp.where(narrow == h, largest + jnp.log(total), total_logs)
        result[...] = total_mixed.astype(BF16)
        logs[...] = total_logs

    @pl.when(count == 0)
    def _():
        finish(lambda h, largest, total: (largest, total, mixed[0]))

    @pl.when(count > 0)
    def _():
        spread_queries(q, qs)
        for h in range(4):
            top[pl.ds(h * TOK, TOK), :] = jnp.broadcast_to(state[:, h : h + 1], (TOK, 128))
        sweep_scores(PREV - count, PREV, k, qs, scores, top)
        sweep_values(PREV - count, PREV, v, scores, top, low, acc)

        def part(h, largest, total):
            rows = pl.ds(h * TOK, TOK)
            most = top[rows, :1]
            fade = jnp.exp(largest - most)
            total = total * fade + jnp.sum(low[rows, :], axis=1, keepdims=True)
            return most, total, mixed[0] * fade + acc[rows, :]

        finish(part)

    lse[0] = logs[...].T[:8]
    o0[0] = result[:PR, :]
    o1[0] = result[PR : 2 * PR, :]
    o23[0, 0] = result[2 * PR : 3 * PR, :]
    o23[1, 0] = result[3 * PR :, :]


def attend(own, places, q, k, v, state=()):
    block = pl.BlockSpec((1, TOK, HC), lambda f, *_: (f, 0, 0))
    narrow = pl.BlockSpec((1, TOK, 128), lambda f, *_: (f, 0, 0))
    piece = pl.BlockSpec((1, PR, HC), lambda f, *_: (f, 0, 0))
    count = FPD if own else PREV
    scratch = [
        pltpu.VMEM((4 * TOK, HC), BF16),
        pltpu.VMEM((8, 4 * TOK, TOK), F32),
        pltpu.VMEM((4 * TOK, HC), F32),
        pltpu.VMEM((4 * TOK, 128), F32),
        pltpu.VMEM((4 * TOK, 128), F32),
    ]
    specs = [block] + [whole((count, TOK, HC))] * 2
    if own:
        out_shape = [shape((FPD, TOK, HC), F32), shape((FPD, TOK, 128), F32)]
        out_specs = [block, narrow]
    else:
        specs += [block, narrow]
        out_shape = [shape((FPD, PR, HC))] * 2 + [
            shape((2, FPD, PR, HC)),
            shape((FPD, 8, TOK), F32),
        ]
        out_specs = [piece] * 2 + [
            pl.BlockSpec((2, 1, PR, HC), lambda f, *_: (0, f, 0, 0)),
            pl.BlockSpec((1, 8, TOK), lambda f, *_: (f, 0, 0)),
        ]
        scratch += [pltpu.VMEM((TOK, HC), BF16), pltpu.VMEM((TOK, 128), F32)]
    return pl.pallas_call(
        attend_own_kernel if own else attend_prev_kernel,
        out_shape=out_shape,
        grid_spec=pltpu.PrefetchScalarGridSpec(
            num_scalar_prefetch=1,
            grid=(FPD,),
            in_specs=specs,
            out_specs=out_specs,
            scratch_shapes=scratch,
        ),
        compiler_params=params(40),
        cost_estimate=cost(
            (30 if own else 12) * 4 * 2 * 2 * TOK**3, 6 * MB, 30 * 4 * TOK * TOK
        ),
        name="attend_own" if own else "attend_prev",
    )(places, q, k, v, *state)


def attend_back_kernel(own, pos_ref, q, k, v, g0, g1, g2, g3, o0, o1, o23, lse, *rest):
    if own:
        cp, sp, fr, before_ref, dq, dk, dv, qs, gs, ks, pl_scr, dl_scr, ds_scr, dq_acc = rest
        dk_acc, dv_acc = dk, dv
    else:
        dq, both_ref, qs, gs, ks, pl_scr, dl_scr, ds_scr, dq_acc, dk_acc, dv_acc = rest
    f = pl.program_id(0)
    place = pos_ref[f]
    lanes = head_lanes()

    @pl.when(f == 0)
    def _():
        for ref in (dk_acc, dv_acc):
            ref[...] = jnp.zeros_like(ref)

    def prelude():
        query = q[0]
        grad = jnp.concatenate([r[0] for r in (g0, g1, g2, g3)], axis=0)
        mixed = jnp.concatenate([o0[0], o1[0], o23[0, 0], o23[1, 0]], axis=0)
        for h in range(4):
            rows = pl.ds(h * TOK, TOK)
            qs[rows, :] = jnp.where(lanes == h, query, jnp.zeros_like(query))
            gs[rows, :] = jnp.where(lanes == h, grad, jnp.zeros_like(grad))
        both = grad.astype(F32) * mixed.astype(F32)
        pick = (
            lax.broadcasted_iota(jnp.int32, (8, HC), 1) // HD
            == lax.broadcasted_iota(jnp.int32, (8, HC), 0)
        ).astype(F32)
        return lax.dot_general(
            pick, both, (((1,), (1,)), ((), ())),
            preferred_element_type=F32, precision=lax.Precision.HIGHEST,
        )

    def step(delta, logs, at):
        keys, values = k[at], v[at]
        for h in range(4):
            rows = pl.ds(h * TOK, TOK)
            ks[rows, :] = jnp.where(lanes == h, keys, jnp.zeros_like(keys))
            p = jnp.exp(nt(keys, qs[rows, :]) - logs[h : h + 1])
            ds = (p * (nt(values, gs[rows, :]) - delta[h : h + 1])).astype(BF16)
            pl_scr[:, rows] = p.astype(BF16)
            dl_scr[:, rows] = ds
            ds_scr[rows, :] = ds
        dv_acc[at] = dv_acc[at] + nn(pl_scr[...], gs[...])
        dk_acc[at] = dk_acc[at] + nn(dl_scr[...], qs[...])
        dq_acc[...] = dq_acc[...] + tn(ds_scr[...], ks[...])

    def sweep(low, high):
        delta = prelude()
        logs = lse[0]
        dq_acc[...] = jnp.zeros_like(dq_acc)

        def one(at, _):
            step(delta, logs, at)
            return 0

        lax.fori_loop(low, high, one, 0)

    if own:
        sweep(jnp.maximum(f - place, 0), f + 1)
        cosine, sine = cosines(cp, sp, fr, f)
        dq[0] = turn((dq_acc[...] + before_ref[0]) * 0.125, cosine, -sine).astype(BF16)
    else:
        count = jnp.maximum(place - f, 0)

        @pl.when(count > 0)
        def _():
            sweep(PREV - count, PREV)
            dq[0] = dq_acc[...]

        @pl.when(count == 0)
        def _():
            dq[0] = jnp.zeros_like(dq_acc)

        @pl.when(f == FPD - 1)
        def _():
            both_ref[0] = dk_acc[...].astype(BF16)
            both_ref[1] = dv_acc[...].astype(BF16)


def attend_back(own, places, q, k, v, grads, mixed, lse, tables=None, before=None):
    block = pl.BlockSpec((1, TOK, HC), lambda f, *_: (f, 0, 0))
    piece = pl.BlockSpec((1, PR, HC), lambda f, *_: (f, 0, 0))
    count = FPD if own else PREV
    wide = pltpu.VMEM((4 * TOK, HC), BF16)
    tall = pltpu.VMEM((TOK, 4 * TOK), BF16)
    scratch = [wide, wide, wide, tall, tall, wide, pltpu.VMEM((TOK, HC), F32)]
    specs = []
    extra = ()
    if own:
        specs = [whole((TOK, HC)), whole((TOK, HC)), whole((16, 2 * HC)), block]
        extra = tuple(tables) + (before,)
    else:
        scratch += [pltpu.VMEM((PREV, TOK, HC), F32)] * 2
    return pl.pallas_call(
        lambda *refs: attend_back_kernel(own, *refs),
        out_shape=[shape((FPD, TOK, HC), BF16 if own else F32)]
        + ([shape((FPD, TOK, HC), F32)] * 2 if own else [shape((2, PREV, TOK, HC))]),
        grid_spec=pltpu.PrefetchScalarGridSpec(
            num_scalar_prefetch=1,
            grid=(FPD,),
            in_specs=[block]
            + [whole((count, TOK, HC))] * 2
            + [piece] * 6
            + [pl.BlockSpec((2, 1, PR, HC), lambda f, *_: (0, f, 0, 0))]
            + [pl.BlockSpec((1, 8, TOK), lambda f, *_: (f, 0, 0))]
            + specs,
            out_specs=[block]
            + ([whole((FPD, TOK, HC))] * 2 if own else [whole((2, PREV, TOK, HC))]),
            scratch_shapes=scratch,
        ),
        compiler_params=params(58),
        cost_estimate=cost(1000 if own else 12 * 4 * 5 * 2 * TOK**3, 1000 if own else 12 * MB),
        name="attend_back_own" if own else "attend_back_prev",
    )(places, q, k, v, *grads, *mixed, lse, *extra)


HALF = 4
RAW = HALF * PR


def flat(ref):
    return ref[...].reshape(RAW, ref.shape[-1])


def frames_of(value):
    return value.reshape(HALF, PR, value.shape[-1])


def segment(table, s):
    both = table[:, s * D : (s + 1) * D]
    return jnp.where(pl.program_id(0) == 0, both[:HALF], both[HALF:])[:, None, :]


def fold(out, start, width, row):
    @pl.when(pl.program_id(0) == 0)
    def _():
        out[:, start : start + width] = jnp.zeros((8, width), F32)

    for i in range(8):
        at = (slice(i, i + 1), slice(start, start + width))
        out[at] = out[at] + row[:, i * width : (i + 1) * width]


def mid_kernel(o0, o1, o2, o3, w0, w1, w2, w3, table, x, cot, branch, middle, hidden, down, dsum):
    total = unfold(table, OB, 128)
    for o, w in zip((o0, o1, o2, o3), (w0, w1, w2, w3)):
        total = total + nn(flat(o), w[...])
    branched = frames_of(total)
    branch[...] = branched
    mid_value = x[...].astype(F32) + segment(table, 2) * branched
    middle[...] = mid_value
    normal, _ = norm(mid_value)
    hidden[...] = (normal * (1.0 + segment(table, 4)) + segment(table, 3)).astype(BF16)
    grad = (segment(table, 5) * cot[...].astype(F32)).astype(BF16)
    down[...] = grad
    fold(dsum, 0, 128, jnp.sum(grad.astype(F32).reshape(RAW, D), axis=0, keepdims=True))


def half_spec(width):
    return pl.BlockSpec((HALF, PR, width), lambda i, *_: (i, 0, 0))


def mid(pieces, weights, table, x, cot):
    return pl.pallas_call(
        mid_kernel,
        out_shape=[
            shape((FPD, PR, D), F32),
            shape((FPD, PR, D), F32),
            shape((FPD, PR, D)),
            shape((FPD, PR, D)),
            shape((8, 128), F32),
        ],
        grid=(FPD // HALF,),
        in_specs=[half_spec(HC)] * 4
        + [whole((HC, D))] * 4
        + [whole((FPD, WIDE)), half_spec(D), half_spec(D)],
        out_specs=[half_spec(D)] * 4 + [whole((8, 128))],
        compiler_params=params(26),
        cost_estimate=cost(2 * 512 * D * D, 12 * MB),
        name="mid",
    )(*pieces, *weights, table, x, cot)


def mid_back_kernel(
    hg, middle, branch, cot, table, w0, w1, w2, w3, usum, dsum, mg, bg, a0, a1, a23, sums
):
    grad = hg[...]
    normal, rate = norm(middle[...])
    put_half(sums, D, jnp.sum(grad, axis=1))
    put_half(sums, 2 * D, jnp.sum(grad * normal, axis=1))
    total = cot[...].astype(F32) + norm_back(normal, rate, grad * (1.0 + segment(table, 4)))
    mg[...] = total
    put_half(sums, 0, jnp.sum(total * branch[...], axis=1))
    low = (segment(table, 2) * total).astype(BF16)
    bg[...] = low
    low = low.reshape(RAW, D)
    sums[:, 3 * D : 3 * D + NB] = usum[...]
    sums[:, 3 * D + NB : 3 * D + NB + 128] = dsum[...]
    fold(sums, 3 * D + NB + 128, 128, jnp.sum(low.astype(F32), axis=0, keepdims=True))
    for j, w in enumerate((w0, w1, w2, w3)):
        value = frames_of(nt(low, w[...]).astype(BF16))
        if j < 2:
            (a0, a1)[j][...] = value
        else:
            a23[j - 2] = value


def mid_back(hg, middle, branch, cot, table, weights, usum, dsum):
    return pl.pallas_call(
        mid_back_kernel,
        out_shape=[shape((FPD, PR, D), F32), shape((FPD, PR, D))]
        + [shape((FPD, PR, HC))] * 2
        + [shape((2, FPD, PR, HC)), shape((8, EARLY), F32)],
        grid=(FPD // HALF,),
        in_specs=[half_spec(D)] * 4
        + [whole((FPD, WIDE))]
        + [whole((HC, D))] * 4
        + [whole((8, NB)), whole((8, 128))],
        out_specs=[half_spec(D)] * 2
        + [half_spec(HC)] * 2
        + [pl.BlockSpec((2, HALF, PR, HC), lambda i: (0, i, 0, 0)), whole((8, EARLY))],
        compiler_params=params(26),
        cost_estimate=cost(2 * 512 * D * D, 12 * MB),
        name="mid_back",
    )(hg, middle, branch, cot, table, *weights, usum, dsum)


NB = 512
STEPS = FF // NB
PER = D // NB
TOKENS = FPD * PR


def block_of(t):
    phase = t // PER
    return ((phase % 2) * 2) ^ (phase // 2)


def up_column(t, row):
    return (row ^ block_of(t)) * PER + t % PER


def down_row(t):
    return block_of(t) * PER + t % PER


def down_spec(j):
    phase = (0, 2, 1, 3)[j]
    return pl.BlockSpec((NB, D), lambda t, row: (jnp.clip(t - phase * PER, 0, PER - 1), 0))


def pick_down(d0, d1, d2, d3):
    phase = pl.program_id(0) // PER
    return jnp.where(
        phase < 2,
        jnp.where(phase == 0, d0[...], d2[...]),
        jnp.where(phase == 2, d1[...], d3[...]),
    )


def feed_kernel(row_ref, h2, dg, u0, u1, u2, u3, table, d0, d1, d2, d3, act, upg, hg, usum):
    row = row_ref[0]
    ups = (u0, u1, u2, u3)
    down = pick_down(d0, d1, d2, d3)
    at = pl.ds(up_column(pl.program_id(0), row), 1)
    u = table[at, UB : UB + NB]
    for j, w in enumerate(ups):
        u = u + nn(h2[:, columns(row, j)], w[...])
    rate = math.sqrt(2.0 / math.pi)
    square = u * u
    half = 0.5 + 0.5 * jnp.tanh(u * (rate + (rate * 0.044715) * square))
    active = u * half
    act[...] = active.astype(BF16)
    slope = half + active * (1.0 - half) * (2.0 * rate + (6.0 * rate * 0.044715) * square)
    grad = (nt(dg[...], down) * slope).astype(BF16)
    upg[...] = grad
    put(usum, 0, up_column(pl.program_id(0), row), jnp.sum(grad.astype(F32), axis=0, keepdims=True))

    @pl.when(pl.program_id(0) == 0)
    def _():
        hg[...] = jnp.zeros_like(hg)

    for j, w in enumerate(ups):
        hg[:, columns(row, j)] = hg[:, columns(row, j)] + nt(grad, w[...])


def feed(row, h2, dg, ups, table, downs):
    tok = whole((TOKENS, D))
    block = pl.BlockSpec((TOKENS, NB), lambda t, row: (0, t))
    return pl.pallas_call(
        feed_kernel,
        out_shape=[
            shape((TOKENS, FF)),
            shape((TOKENS, FF)),
            shape((TOKENS, D), F32),
            shape((8, NB), F32),
        ],
        grid_spec=pltpu.PrefetchScalarGridSpec(
            num_scalar_prefetch=1,
            grid=(STEPS,),
            in_specs=[tok, tok]
            + [pl.BlockSpec((HC, NB), lambda t, row: (0, up_column(t, row[0])))] * 4
            + [whole((FPD, WIDE))]
            + [down_spec(j) for j in range(4)],
            out_specs=[block, block, tok, whole((8, NB))],
        ),
        compiler_params=params(58),
        cost_estimate=cost(3 * 2 * TOKENS * D * FF, 30 * MB, TOKENS * FF),
        name="feed",
    )(row, h2, dg, *ups, table, *downs)


def down_step(da, db, dg, act, part, dn):
    g = pl.program_id(0)
    down = jnp.where(g < PER, da[...], db[...])
    active = act[...]
    dn[...] = dn[...] + nn(active, down)
    part[0] = tn(active, dg[...]).astype(BF16)


def down_send_kernel(dg, act, da, db, part, dn):
    @pl.when(pl.program_id(0) == 0)
    def _():
        dn[...] = jnp.zeros_like(dn)

    down_step(da, db, dg, act, part, dn)


def down_keep_kernel(dg, act, da, db, before, table, middle, cot, part, out, gate, dn):
    @pl.when(pl.program_id(0) == 0)
    def _():
        dn[...] = before[...]

    down_step(da, db, dg, act, part, dn)

    @pl.when(pl.program_id(0) == STEPS // 2 - 1)
    def _():
        bias = unfold(table, DB, 128)
        for f in range(FPD):
            rows = slice(f * PR, (f + 1) * PR)
            value = dn[rows, :] + bias
            out[f] = (middle[f] + table[f : f + 1, 5 * D : 6 * D] * value).astype(BF16)
            gate[f : f + 1, :] = jnp.sum(cot[f].astype(F32) * value, axis=0, keepdims=True)


def down_half(first, dg, act, downs, extra=()):
    tok = whole((TOKENS, D))
    full = whole((FPD, PR, D))
    half = STEPS // 2
    weight = lambda k: pl.BlockSpec((NB, D), lambda g: (jnp.clip(g - k * PER, 0, PER - 1), 0))
    start = half if first else 0
    part = pl.BlockSpec((1, NB, D), lambda g: (g // PER, g % PER, 0))
    out_specs, out_shape, scratch, specs = [part], [shape((2, D, D))], [], []
    if first:
        out_specs += [tok]
        out_shape += [shape((TOKENS, D), F32)]
    else:
        specs = [tok, whole((FPD, WIDE)), full, full]
        out_specs += [full, whole((8, D))]
        out_shape += [shape((FPD, PR, D)), shape((8, D), F32)]
        scratch = [pltpu.VMEM((TOKENS, D), F32)]
    return pl.pallas_call(
        down_send_kernel if first else down_keep_kernel,
        out_shape=out_shape,
        grid=(half,),
        in_specs=[tok, pl.BlockSpec((TOKENS, NB), lambda g: (0, g + start)), weight(0), weight(1)]
        + specs,
        out_specs=out_specs,
        scratch_shapes=scratch,
        compiler_params=params(40),
        cost_estimate=cost(2 * TOKENS * D * FF, 14 * MB),
        name="down_weight_send" if first else "down_weight_keep",
    )(dg, act, *downs, *extra)


def up_weight_kernel(row_ref, h2, upg, uk, us):
    row = row_ref[0]
    grad = upg[...]
    for j, ref in enumerate((uk, us, uk, us)):
        ref[j // 2, 0] = tn(h2[:, columns(row, j)], grad).astype(BF16)


def up_weight_grad(row, h2, upg):
    up_out = pl.BlockSpec(
        (2, 1, HC, NB),
        lambda t, row: (0, up_column(t, row[0]) // PER, 0, up_column(t, row[0]) % PER),
    )
    return pl.pallas_call(
        up_weight_kernel,
        out_shape=[shape((2, 4, HC, D))] * 2,
        grid_spec=pltpu.PrefetchScalarGridSpec(
            num_scalar_prefetch=1,
            grid=(STEPS,),
            in_specs=[whole((TOKENS, D)), pl.BlockSpec((TOKENS, NB), lambda t, row: (0, t))],
            out_specs=[up_out, up_out],
        ),
        compiler_params=params(58),
        cost_estimate=cost(2 * TOKENS * D * FF, 14 * MB),
        name="up_weight_grad",
    )(row, h2, upg)


def out_weight_kernel(t0, t1, t2, t3, bg, keep, send):
    grad = bg[...].reshape(TOKENS, D)
    for j, t in enumerate((t0, t1, t2, t3)):
        ref = (keep, send)[j % 2]
        ref[j // 2] = tn(t[...].reshape(TOKENS, HC), grad).astype(BF16)


def out_weight_grad(pieces, bg):
    return pl.pallas_call(
        out_weight_kernel,
        out_shape=[shape((2, HC, D))] * 2,
        grid=(1,),
        in_specs=[whole((FPD, PR, HC))] * 4 + [whole((FPD, PR, D))],
        out_specs=[whole((2, HC, D))] * 2,
        compiler_params=params(14),
        cost_estimate=cost(2 * TOKENS * D * D, 4 * MB),
        name="out_weight_grad",
    )(*pieces, bg)


CHUNKS = 16
UP_ROWS, OUT_ROWS, DOWN_ROWS = D // CHUNKS, HC // CHUNKS, D // CHUNKS
FIRST = UP_ROWS + OUT_ROWS
ROWS = FIRST + DOWN_ROWS


def core_sum_kernel(ua, ub, da, db, oa, ob, out):
    def both(a, b):
        return (a.astype(F32) + b.astype(F32)).astype(BF16)

    for c in range(4):
        at = c * ROWS
        low, high = c * OUT_ROWS, (c + 1) * OUT_ROWS
        for i in range(4):
            to = at + i * OUT_ROWS
            out[0, to : to + OUT_ROWS] = both(ua[0, i, low:high], ub[0, i, low:high])
        out[0, at + UP_ROWS : at + FIRST] = both(oa[0, low:high], ob[0, low:high])
        low, high = c * DOWN_ROWS, (c + 1) * DOWN_ROWS
        out[0, at + FIRST : at + ROWS] = both(da[0, low:high], db[0, low:high])


def core_sum(up, down, out):
    ups = pl.BlockSpec((1, 4, 4 * OUT_ROWS, D), lambda j, c: (j, 0, c, 0))
    outs = pl.BlockSpec((1, 4 * OUT_ROWS, D), lambda j, c: (j, c, 0))
    downs = pl.BlockSpec((1, 4 * DOWN_ROWS, D), lambda j, c: (j, c, 0))
    return pl.pallas_call(
        core_sum_kernel,
        out_shape=shape((2, CHUNKS * ROWS, D)),
        grid=(2, CHUNKS // 4),
        in_specs=[ups, ups, downs, downs, outs, outs],
        out_specs=pl.BlockSpec((1, 4 * ROWS, D), lambda j, c: (j, c, 0)),
        compiler_params=params(58),
        cost_estimate=cost(1000, 1000),
        name="core_sum",
    )(*up, *down, *out)


def unpack_kernel(total, up, out, down):
    for k in range(4):
        at = k * ROWS
        for i in range(4):
            rows = slice(at + i * OUT_ROWS, at + (i + 1) * OUT_ROWS)
            up[k * OUT_ROWS : (k + 1) * OUT_ROWS, i * D : (i + 1) * D] = total[rows].astype(F32)
        out[k * OUT_ROWS : (k + 1) * OUT_ROWS] = total[at + UP_ROWS : at + FIRST].astype(F32)
        down[k * DOWN_ROWS : (k + 1) * DOWN_ROWS] = total[at + FIRST : at + ROWS].astype(F32)


def unpack(total):
    block = lambda i: (i, 0)
    return pl.pallas_call(
        unpack_kernel,
        out_shape=[shape((HC, FF), F32), shape((HC, D), F32), shape((D, D), F32)],
        grid=(4,),
        in_specs=[pl.BlockSpec((4 * ROWS, D), block)],
        out_specs=[
            pl.BlockSpec((4 * OUT_ROWS, FF), block),
            pl.BlockSpec((4 * OUT_ROWS, D), block),
            pl.BlockSpec((4 * DOWN_ROWS, D), block),
        ],
        compiler_params=params(24),
        cost_estimate=cost(0, 14 * MB),
        name="unpack",
    )(total)


LATE = 3 * D + 2 * HC
EARLY = 3 * D + NB + 256


def arrange_kernel(row_ref, a0, a1, a2, a3, late, far, out):
    row = row_ref[0]
    for j, a in enumerate((a0, a1, a2, a3)):
        for s in range(3):
            lanes = pl.ds(pl.multiple_of(s * D + (row ^ j) * HC, HC), HC)
            out[:, lanes] = a[:, s * HC : (s + 1) * HC]
    both = jnp.concatenate([late[...].astype(F32), far[...].astype(F32)], axis=0)
    out[:, 3 * D :] = both.astype(BF16)


def arrange(row, pieces, late, far):
    rows = pieces[0].shape[0]
    return pl.pallas_call(
        arrange_kernel,
        out_shape=shape((rows, 3 * D + LATE)),
        grid_spec=pltpu.PrefetchScalarGridSpec(
            num_scalar_prefetch=1,
            grid=(1,),
            in_specs=[whole((rows, 3 * HC))] * 4 + [whole((8, LATE))] * 2,
            out_specs=whole((rows, 3 * D + LATE)),
        ),
        compiler_params=params(16),
        cost_estimate=cost(0, 8 * rows * D),
        name="arrange",
    )(row, *pieces, late, far)


def stack_kernel(a0, a1, a2, a3, weights, sums):
    for k, a in enumerate((a0, a1, a2, a3)):
        weights[k] = a[:, : 3 * D]
        sums[k] = a[:, 3 * D :]


def stack(pieces):
    rows, width = pieces[0].shape
    return pl.pallas_call(
        stack_kernel,
        out_shape=[shape((4, rows, 3 * D)), shape((4, rows, LATE))],
        grid=(1,),
        in_specs=[whole((rows, width))] * 4,
        out_specs=[whole((4, rows, 3 * D)), whole((4, rows, LATE))],
        compiler_params=params(16),
        cost_estimate=cost(0, 2 * MB),
        name="stack",
    )(*pieces)


def place_kernel(index_ref, low, high, out):
    for m, a in enumerate((low.at[0], low.at[1], high.at[1], high.at[0])):

        @pl.when(pl.program_id(0) == m)
        def _():
            for k in range(4):
                out[0, index_ref[1] ^ k] = a[k].astype(F32)


def place(index, low, high):
    rows = low.shape[2]
    return pl.pallas_call(
        place_kernel,
        out_shape=shape((4, 4, rows, 3 * D), F32),
        grid_spec=pltpu.PrefetchScalarGridSpec(
            num_scalar_prefetch=1,
            grid=(4,),
            in_specs=[whole(low.shape)] * 2,
            out_specs=pl.BlockSpec((1, 4, rows, 3 * D), lambda i, index: (index[0] ^ i, 0, 0, 0)),
        ),
        compiler_params=params(24),
        cost_estimate=cost(0, 24 * rows * D),
        name="place",
    )(index, low, high).reshape(HC, 3 * D)


def project_back_kernel(row_ref, dq, dk, dv, rk, rv, w0, w1, w2, w3, cp, sp, fr, dp, h0, h2, hs, bsum):
    row = row_ref[0]
    f = pl.program_id(0)
    later = (f > 0).astype(F32)
    keys = dk[0] + later * rk[0, 0].astype(F32)
    values = dv[0] + later * rv[0, 0].astype(F32)
    cosine, sine = cosines(cp, sp, fr, f)
    dp[0, :, :HC] = dq[0]
    dp[0, :, HC : 2 * HC] = turn(keys, cosine, -sine).astype(BF16)
    dp[0, :, 2 * HC :] = values.astype(BF16)
    grad = dp[0]
    sums = jnp.sum(grad.astype(F32), axis=0, keepdims=True)

    @pl.when(f == 0)
    def _():
        bsum[...] = jnp.zeros_like(bsum)

    number = lax.broadcasted_iota(jnp.int32, (8, 2 * HC), 0)
    bsum[...] = bsum[...] + jnp.where(number == row, sums[:, : 2 * HC], 0.0)
    bsum[:, :HC] = bsum[:, :HC] + jnp.where(number[:, :HC] == row + 4, sums[:, 2 * HC :], 0.0)
    for j, w in enumerate((w0, w1, w2, w3)):
        part = nt(grad, w[...]).astype(BF16)
        at = (0, slice(None), columns(row, j))
        h0[at] = part[:PR]
        hs[(0,) + at] = part[PR : 2 * PR]
        h2[at] = part[2 * PR : 3 * PR]
        hs[(1,) + at] = part[3 * PR :]


def project_back(row, dq, dk, dv, returned, weights, tables):
    block = pl.BlockSpec((1, TOK, HC), lambda f, *_: (f, 0, 0))
    late = [
        pl.BlockSpec((1, 1, TOK, HC), lambda f, *_, i=i: (i, jnp.maximum(f - 1, 0), 0, 0))
        for i in range(2)
    ]
    piece = pl.BlockSpec((1, PR, D), lambda f, *_: (f, 0, 0))
    return pl.pallas_call(
        project_back_kernel,
        out_shape=[
            shape((FPD, TOK, 3 * HC)),
            shape((FPD, PR, D)),
            shape((FPD, PR, D)),
            shape((2, FPD, PR, D)),
            shape((8, 2 * HC), F32),
        ],
        grid_spec=pltpu.PrefetchScalarGridSpec(
            num_scalar_prefetch=1,
            grid=(FPD,),
            in_specs=[block] * 3
            + late
            + [whole((HC, 3 * HC))] * 4
            + [whole((TOK, HC)), whole((TOK, HC)), whole((16, 2 * HC))],
            out_specs=[
                pl.BlockSpec((1, TOK, 3 * HC), lambda f, *_: (f, 0, 0)),
                piece,
                piece,
                pl.BlockSpec((2, 1, PR, D), lambda f, *_: (0, f, 0, 0)),
                whole((8, 2 * HC)),
            ],
        ),
        compiler_params=params(20),
        cost_estimate=cost(2 * FPD * TOK * D * 3 * HC, 14 * MB),
        name="project_back",
    )(row, dq, dk, dv, returned, returned, *weights, *tables)


def weight_kernel(row_ref, h, dp, w):
    w[0] = tn(h[...], dp[...]).astype(BF16)


def project_weight(row, hidden, dproj):
    tokens = FPD * TOK
    return pl.pallas_call(
        weight_kernel,
        out_shape=shape((4, HC, 3 * HC)),
        grid_spec=pltpu.PrefetchScalarGridSpec(
            num_scalar_prefetch=1,
            grid=(4,),
            in_specs=[
                pl.BlockSpec((tokens, HC), lambda j, row: (0, row[0] ^ j)),
                whole((tokens, 3 * HC)),
            ],
            out_specs=pl.BlockSpec((1, HC, 3 * HC), lambda j, row: (j, 0, 0)),
        ),
        compiler_params=params(20),
        cost_estimate=cost(2 * tokens * D * 3 * HC, 9 * MB),
        name="project_weight",
    )(row, hidden.reshape(tokens, D), dproj.reshape(tokens, 3 * HC))


def input_back_kernel(x, h0, near, far, table, mg, bsum, gate, out, sums):
    grad = h0[...].astype(F32) + near[0].astype(F32) + far[...].astype(F32)
    normal, rate = norm(x[...].astype(F32))
    put_half(sums, 0, jnp.sum(grad, axis=1))
    put_half(sums, D, jnp.sum(grad * normal, axis=1))
    sums[:, 2 * D : 3 * D] = gate[...]
    sums[:, 3 * D :] = bsum[...]
    out[...] = mg[...] + norm_back(normal, rate, grad * (1.0 + segment(table, 1)))


def input_back(x, h0, near, far, table, mg, bsum, gate):
    return pl.pallas_call(
        input_back_kernel,
        out_shape=[shape((FPD, PR, D), F32), shape((8, LATE), F32)],
        grid=(FPD // HALF,),
        in_specs=[half_spec(D)] * 2
        + [pl.BlockSpec((1, HALF, PR, D), lambda i: (0, i, 0, 0))]
        + [half_spec(D), whole((FPD, WIDE)), half_spec(D), whole((8, 2 * HC)), whole((8, D))],
        out_specs=[half_spec(D), whole((8, LATE))],
        compiler_params=params(20),
        cost_estimate=cost(20 * 512 * D, 10 * MB),
        name="input_back",
    )(x, h0, near, far, table, mg, bsum, gate)


def join_kernel(a0, a1, a2, a3, out):
    for k, a in enumerate((a0, a1, a2, a3)):
        out[2 * k : 2 * k + 2] = a[...]


def join(pieces):
    width = pieces[0].shape[-1]
    return pl.pallas_call(
        join_kernel,
        out_shape=shape((8, 8, width)),
        grid=(1,),
        in_specs=[whole((2, 8, width))] * 4,
        out_specs=whole((8, 8, width)),
        compiler_params=params(16),
        cost_estimate=cost(0, 2 * MB),
        name="join",
    )(*pieces)


def final_kernel(row_ref, *refs):
    row = row_ref[0]
    low, high, *early = refs[:6]
    ada, ab, qb, ob, ub, db, asum = refs[6:]
    late = [low.at[0], low.at[1], high.at[0], high.at[1]]
    early = [early[0], early[3], early[1], early[2]]

    def rows(ref, cols):
        value = ref[:, :, cols].astype(F32)
        return value.reshape(64, value.shape[-1])

    left = [rows(s, slice(EARLY, EARLY + HC)).astype(BF16) for s in early]
    for segment in range(6):
        source, start = ((late, 0), (late, 1), (early, 0), (early, 1), (early, 2), (late, 2))[segment]
        cols = slice(start * D, (start + 1) * D)
        product, total = 0.0, 0.0
        for s, ref in zip(left, source):
            right = rows(ref, cols)
            total = total + jnp.sum(right, axis=0, keepdims=True)
            product = product + tn(s, right.astype(BF16))
        at = segment * D
        ada[:, at : at + D] = product
        asum[0:1, at : at + D] = total

    def fold8(value):
        value = jnp.sum(value, axis=0)
        return value if value.shape[0] == 8 else value[:8] + value[8:]

    def bias(source, start, stop):
        return sum(
            fold8(ref[:, :, start:stop].astype(F32)) for ref in source
        )

    ab[...] = asum[0:1, pl.ds(pl.multiple_of(row * 1536, 512), 1536)]
    folded = bias(late, 3 * D, LATE)
    for i in range(3):
        chunk = 3 * row + i
        at = jnp.where(chunk < 4, chunk, chunk - 4)
        second = (chunk >= 4) & (chunk < 8)
        value = jnp.where(second, folded[:, HC:], folded[:, :HC])
        qb[:, i * HC : (i + 1) * HC] = take(value, at)
    folded = bias(early, 3 * D, EARLY)
    for i in range(2):
        at = 2 * row + i
        ub[:, i * NB : (i + 1) * NB] = take(folded[:, :NB], at)
        db[:, i * 128 : (i + 1) * 128] = take(folded[:, NB : NB + 128], at)
        ob[:, i * 128 : (i + 1) * 128] = take(folded[:, NB + 128 :], at)


def final_sums(row, late, early):
    sizes = (1536, 768, 256, 1024, 256)
    return pl.pallas_call(
        final_kernel,
        out_shape=[shape((HC, 6 * D), F32)] + [shape((1, n), F32) for n in sizes],
        grid_spec=pltpu.PrefetchScalarGridSpec(
            num_scalar_prefetch=1,
            grid=(1,),
            in_specs=[whole((2, 4, 16, LATE))] * 2
            + [whole((8, 8, EARLY + HC))] * 4,
            out_specs=[whole((HC, 6 * D))] + [whole((1, n)) for n in sizes],
            scratch_shapes=[pltpu.VMEM((8, 6 * D), F32)],
        ),
        compiler_params=params(28),
        cost_estimate=cost(2 * 256 * HC * 6 * D, 10 * MB),
        name="final_sums",
    )(row, *late, *early)


def row_sum(value):
    value = value + swap(value, CORE)
    return value + swap(value, DIRECT)


def row_pieces(value):
    return [value, swap(value, CORE), swap(value, DIRECT), swap(value, DIRECT ^ CORE)]


def by_row(pieces, row):
    a, b, c, d = pieces
    odd, high = row % 2 == 1, row >= 2
    a, b = jnp.where(odd, b, a), jnp.where(odd, a, b)
    c, d = jnp.where(odd, d, c), jnp.where(odd, c, d)
    return jnp.stack(
        [
            jnp.where(high, c, a),
            jnp.where(high, d, b),
            jnp.where(high, a, c),
            jnp.where(high, b, d),
        ]
    )


def quarter_rows(value, bit, index, axis):
    rows = value.shape[1] // 4
    at = lambda m: lax.dynamic_slice_in_dim(value, (index[axis] ^ m) * rows, rows, 1)
    return [at(0)] + [swap(at(m), bit * m) for m in (1, 2, 3)]


def add_all(parts):
    return sum(part.astype(F32) for part in parts).astype(BF16)


def exchange_rows(value, bit, index, axis):
    return add_all(quarter_rows(value, bit, index, axis))


def turn_heads(own, beside, across, order=lambda piece: piece):
    across = swap(across, DIRECT)
    return [own, swap(beside, CORE), across[0], swap(order(across)[1], CORE)]


def per_device(
    activations,
    noise_embed,
    frame_position,
    cotangent,
    ada_weight,
    ada_bias,
    qkv_weight,
    qkv_bias,
    out_weight,
    out_bias,
    up_weight,
    up_bias,
    down_weight,
    down_bias,
):
    row = lax.axis_index(("xl", "c")).astype(jnp.int32)
    row_arg = row.reshape(1)
    index = [lax.axis_index("y").astype(jnp.int32), lax.axis_index("z").astype(jnp.int32)]
    index_arg = jnp.stack(index)

    x0 = activations
    x2 = swap(x0, DIRECT)
    x1 = swap(x0, CORE)
    p0 = shift(activations[1:], 1)
    biases = (ada_bias, qkv_bias, out_bias, up_bias, down_bias)
    heads = list(split_heads(row_arg, qkv_weight))
    noise, heads[1] = lax.optimization_barrier((noise_embed, heads[1]))
    part, silu_own, *tables = prepare(row_arg, frame_position, noise, ada_weight, biases)
    across = swap(heads[2], OTHER)
    qkv_pieces = [heads[0], swap(heads[1], CORE), across]
    part = part + swap(part, CORE)
    table = part + swap(part, DIRECT)
    x2, p0, table, *qkv_pieces = lax.optimization_barrier((x2, p0, table, *qkv_pieces))

    qkv_pieces = qkv_pieces[:2] + [qkv_pieces[2][0], swap(qkv_pieces[2][1], CORE)]
    x3 = swap(x2, CORE)
    p2 = swap(p0, DIRECT)
    p1 = swap(p0, CORE)
    before_mods = shift(table[:, : 2 * D], 1)

    out_own = after(out_weight, table)
    outs2 = swap(out_own, OTHER)

    hidden1, q, k, v = project(True, row_arg, (x0, x1, x2, x3), table, table, qkv_pieces, tables)
    outs2, up_own, down_own, q = lax.optimization_barrier((outs2, up_weight, down_weight, q))
    ups2 = swap(up_own, OTHER)
    downs2 = swap(down_own, DIRECT)
    state = attend(True, frame_position, q, k, v)
    p2, before_mods, *state = lax.optimization_barrier((p2, before_mods, *state))
    p3 = swap(p2, CORE)
    kp, vp = project(
        False, row_arg, (p0, p1, p2, p3), table, before_mods, qkv_pieces, tables
    )
    *mixed, lse = attend(False, frame_position, q, kp, vp, state)
    outs2, ups2, downs2, lse = lax.optimization_barrier((outs2, ups2, downs2, lse))
    outs = [out_weight, swap(out_own, CORE), outs2, swap(outs2, CORE)]
    ups = [up_weight, swap(up_own, CORE), ups2, swap(ups2, CORE)]
    downs = [down_weight, swap(down_own, CORE), downs2, swap(downs2, CORE)]
    turned = turn_heads(*mixed)
    branch, middle, hidden2, down_grad, dsum = mid(turned, outs, table, x0, cotangent)
    h2 = hidden2.reshape(TOKENS, D)
    dg = down_grad.reshape(TOKENS, D)
    act, upg, hg, usum = feed(row_arg, h2, dg, ups, table, downs)
    mg, bg, *ag, early = mid_back(
        hg.reshape(FPD, PR, D), middle, branch, cotangent, table, outs, usum, dsum
    )
    late = []
    back = turn_heads(*ag[:2], ag[2], order=lambda piece: late.append(piece) or piece)[:2]

    early = early + swap(early, CORE)
    upg, early, _ = lax.optimization_barrier((upg, early, bg))
    early_far = swap(early, DIRECT)
    uk, us = up_weight_grad(row_arg, h2, upg)
    us = swap(us, CORE)
    dg_later, early_far, uk = lax.optimization_barrier((dg, early_far, uk))
    early = jnp.concatenate([(early + early_far).astype(BF16), silu_own], axis=1)
    early_far = swap(early, FAR)
    ds_part, dn = down_half(True, dg_later, act, (downs[1], downs[3]))
    ds_part_far = swap(ds_part, CORE)
    dn, early, early_far, bg_later, us, far_back, *back = lax.optimization_barrier(
        (dn, early, early_far, bg, us, *late, *back)
    )
    early = jnp.stack([early, early_far])
    early_parts = [early] + [swap(early, m) for m in (16, 32, 48)]
    ok, os = out_weight_grad(turned, bg_later)
    os = swap(os, CORE)
    dk_part, layer_output, gate = down_half(
        False, dg_later, act, (downs[0], downs[2]), (dn, table, middle, cotangent)
    )
    dk_part, early_parts, ds_part_far, os, far_back = lax.optimization_barrier(
        (dk_part, early_parts, ds_part_far, os, far_back)
    )
    back += [far_back[0], swap(far_back[1], CORE)]
    dk_part, back = lax.optimization_barrier((dk_part, back))

    dq_before, both = attend_back(False, frame_position, q, kp, vp, back, mixed, lse)
    returned = shift(both, -1)
    uk, dq_before = lax.optimization_barrier((uk, dq_before))
    packed = core_sum((uk, us), (dk_part, ds_part_far), (ok, os))
    dq_before, packed = lax.optimization_barrier((dq_before, packed))
    scattered = lax.psum_scatter(packed, ("y", "z"), scatter_dimension=1, tiled=True)
    dq, dk, dv = attend_back(
        True, frame_position, q, k, v, back, mixed, lse, tables, dq_before
    )
    early_parts, dq = lax.optimization_barrier((early_parts, dq))
    early = join(early_parts)
    early_all = [early] + [swap(early, m) for m in (4, 8, 12)]
    dq, early = lax.optimization_barrier((dq, early))
    early = early[0].astype(F32)

    dproj, h0, h2_part, send, bsum = project_back(row_arg, dq, dk, dv, returned, qkv_pieces, tables)
    near = swap(send, CORE)
    qkv_parts = project_weight(row_arg, hidden1, dproj)
    far_part = (h2_part.astype(F32) + near[1].astype(F32)).astype(BF16)
    far = swap(far_part, DIRECT)
    far_part, qkv_parts, *early_all = lax.optimization_barrier((far_part, qkv_parts, *early_all))
    quarters = quarter_rows(qkv_parts, 4, index, 0)
    input_grad, late = input_back(x0, h0, near, far, table, mg, bsum, gate)
    late_near = swap(late, CORE)
    late, *quarters = lax.optimization_barrier((late, *quarters))
    quarters = quarter_rows(add_all(quarters), 16, index, 1)
    late = late + late_near
    late_far = swap(late, DIRECT)
    late, *quarters = lax.optimization_barrier((late, *quarters))
    qkv_parts = add_all(quarters)
    qkv_far = swap(qkv_parts, FAR)
    scattered, late, late_far, qkv_parts = lax.optimization_barrier(
        (scattered, late, late_far, qkv_parts)
    )
    late = late + late_far
    late_low = late.astype(BF16)
    late_far = swap(late_low, FAR)
    share_far = swap(scattered[1], DIRECT)
    late_low, qkv_far = lax.optimization_barrier((late_low, qkv_far))
    qkv_parts = add_all([qkv_parts, qkv_far])
    turned = turn_heads(qkv_parts[0], qkv_parts[1], qkv_parts[2:])
    turned, share_far = lax.optimization_barrier((turned, share_far))
    share = scattered[0].astype(F32) + share_far.astype(F32)
    share_far = swap(share.astype(BF16), FAR)
    last = arrange(row_arg, turned, late_low, late_far)

    share, share_far, last = lax.optimization_barrier((share, share_far, last))
    share = (share + share_far.astype(F32)).astype(BF16)
    totals = lax.all_gather(share, ("y", "z"), axis=0, tiled=True)
    weights, sums_late = stack([last] + [swap(last, m) for m in (16, 32, 48)])
    weights = jnp.stack([weights, swap(weights, 4)])
    sums_late = jnp.stack([sums_late, swap(sums_late, 12)])
    weights_far, sums_far = swap(weights, 12), swap(sums_late, 4)
    up_total, out_total, down_total = unpack(totals)
    qkv_total = place(index_arg, weights, weights_far)

    ada_total, *bias_sums = final_sums(row_arg, (sums_late, sums_far), early_all)
    ada_sum, qkv_sum, out_sum, up_sum, down_sum = [b[0] for b in bias_sums]
    mod_own = jnp.concatenate(
        [late[:, : 2 * D], early[:, : 3 * D], late[:, 2 * D : 3 * D]], axis=1
    ).astype(BF16)
    silu_grad = nt(mod_own, ada_weight)
    silu_grad = by_row(row_pieces(silu_grad), row).transpose(1, 0, 2).reshape(FPD, D)
    embed = noise_embed.astype(F32)
    sigma = jax.nn.sigmoid(embed)
    embed_grad = silu_grad * (sigma * (1.0 + embed * (1.0 - sigma)))

    return (
        layer_output,
        input_grad,
        embed_grad,
        ada_total,
        ada_sum,
        qkv_total,
        qkv_sum,
        out_total,
        out_sum,
        up_total,
        up_sum,
        down_total,
        down_sum,
    )


def solution(mesh):
    fine = Mesh(mesh.devices.reshape(2, 4, 4, 2, 2), AXES)
    seq, row = ("xh", "z", "y"), ("xl", "c")
    token, weight, vector = P(seq, row, None), P(row, None), P(row)
    in_specs = (token, P(seq, None), P(seq), token) + (weight, vector) * 5
    out_specs = (token, token, P(seq, None)) + (weight, vector) * 5
    return jax.shard_map(
        per_device, mesh=fine, in_specs=in_specs, out_specs=out_specs, check_vma=False
    )
```
